32 devices in a mesh: shard: 16 (over z, x, core), seq: 2 (over y).
Axes of the slice: x: 2, y: 2, z: 4, core: 2. Of those that a mesh axis runs over, the one named last changes fastest.
Arguments:
- stream: bfloat16 [8192, 1536], P(('shard', 'seq')), may hold values from -6 to 6
- doc_starts: int32 [10], replicated, may hold values from 0 to 8191, as said below
- expert_routes: int32 [8192, 4], P(('shard', 'seq')), may hold values from 0 to 7, all different within a row; in each aligned block of 256 rows (0 to 255, 256 to 511, ...) at most 192 rows name the same one
- attn_gain: bfloat16 [1536], P('shard'), may hold values from 0.5 to 1.5
- w_query: bfloat16 [1536, 1536], P('shard'), may hold values from -0.15625 to 0.15625
- key_projection: bfloat16 [1536, 256], P('shard'), may hold values from -0.15625 to 0.15625
- value_projection: bfloat16 [1536, 256], P('shard'), may hold values from -0.15625 to 0.15625
- w_out: bfloat16 [1536, 1536], P('shard'), may hold values from -3.5 to 3.5
- ffn_gain: bfloat16 [1536], P('shard'), may hold values from 0.5 to 1.5
- w_router: bfloat16 [1536, 8], P('shard'), may hold values from -0.078125 to 0.078125
- w_gate: bfloat16 [8, 1536, 768], P(None, 'shard'), may hold values from -0.15625 to 0.15625
- w_up: bfloat16 [8, 1536, 768], P(None, 'shard'), may hold values from -0.15625 to 0.15625
- w_down: bfloat16 [8, 768, 1536], P(None, 'shard'), may hold values from -1.25 to 1.25
- out_grad: bfloat16 [8192, 1536], P(('shard', 'seq')), may hold values from -6 to 6
Outputs:
- result: bfloat16 [8192, 1536], P(('shard', 'seq'))
- stream_grad: bfloat16 [8192, 1536], P(('shard', 'seq'))
- attn_gain_grad: float32 [1536], P('shard')
- w_query_grad: float32 [1536, 1536], P('shard')
- w_key_grad: float32 [1536, 256], P('shard')
- w_value_grad: float32 [1536, 256], P('shard')
- w_out_grad: float32 [1536, 1536], P('shard')
- ffn_gain_grad: float32 [1536], P('shard')
- w_router_grad: float32 [1536, 8], P('shard')
- w_gate_grad: float32 [8, 1536, 768], P(None, 'shard')
- w_up_grad: float32 [8, 1536, 768], P(None, 'shard')
- w_down_grad: float32 [8, 768, 1536], P(None, 'shard')
The draws below stay inside these ranges and needn't reach their ends.
Inputs may be any that keep to these rules, and one draw needn't show every extreme that they name: `doc_starts`: strictly increasing starts, the first 0; a document runs from its start to the next start or to the stream's end and holds at most 16384 tokens; the last document is the stream's last token alone. `expert_routes`: each row names 4 different experts; among the 256 rows of one device no expert is named by more than 192 rows, and in every draw some expert is named by exactly 192 rows of some device.
All inputs are finite; a program needn't handle non-finite values.
Results may differ from the reference program's by a relative error of at most 0.02.
Values may be sent and summed in bfloat16 or wider, within the bound.
A program may use at most 448 MiB of HBM per device.

```python
import math
import jax
import jax.numpy as jnp
import numpy as np
from jax import lax

MODEL_WIDTH = 1536
QUERY_HEADS = 12
KEY_VALUE_HEADS = 2
HEAD_SIZE = 128
FF = 768
E = 8
TOP = 4
TOK_DEV = 256
MOST = 192
TOKENS = 8192


def draw_doc_starts(key, part):
    key = jax.random.fold_in(key, 7)
    head_key, tail_key = jax.random.split(key)
    head_len = jax.random.randint(head_key, (4,), 1, TOK_DEV // 8 + 1)
    tail_len = jax.random.randint(tail_key, (3,), 1, TOK_DEV // 8 + 1)
    zero_start = jnp.zeros((1,), jnp.int32)
    head_starts = jnp.concatenate([zero_start, jnp.cumsum(head_len).astype(jnp.int32)])
    head_end = jnp.sum(head_len).astype(jnp.int32)
    tail_from = (TOKENS - 1 - jnp.sum(tail_len)).astype(jnp.int32)
    middle_len = tail_from - head_end
    split_start = (head_end + jnp.minimum(16384, middle_len - 1)).reshape(1).astype(jnp.int32)
    tail_starts = tail_from + jnp.concatenate([zero_start, jnp.cumsum(tail_len).astype(jnp.int32)])
    return jnp.concatenate([head_starts, split_start, tail_starts]).astype(jnp.int32)


def block_scale(key, dims, pieces, smallest, high):
    def one(dim, blocks):
        steps = jax.random.uniform(jax.random.fold_in(jax.random.fold_in(key, 6), dim), (blocks,), jnp.float32, smallest / len(pieces), high / len(pieces))
        return jnp.repeat(jnp.exp(steps), dims[dim] // blocks).reshape((-1,) + (1,) * (len(dims) - dim - 1))

    level = one(*pieces[0])
    for cut in pieces[1:]:
        level = level * one(*cut)
    return level


def routed_block(own_key, own, number, rows, count, top, reach, slope):
    order = jax.random.permutation(own_key, count)
    heavy_load, usual = shares(count, rows * top, reach, slope, True), shares(count, rows * top, reach, slope, False)
    places = jnp.arange(count)

    def named(tallies, turn):
        used = int((tallies > 0).sum())
        fixed = max(1, used // 4)
        passed = fixed + (places - fixed + turn * (used - fixed)) % max(1, count - fixed)
        return jnp.zeros((count,), jnp.int32).at[order[jnp.where(places < fixed, places, passed)]].set(jnp.asarray(tallies, jnp.int32))

    tallies = jnp.where(number % 4 == 0, named(heavy_load, number // 4), named(usual, number - number // 4 - 1))
    mixed = jax.random.permutation(jax.random.fold_in(own, 3), count)
    donor, taker = mixed[0:count // 2 * 2:2], mixed[1:count // 2 * 2:2]
    room = jnp.minimum(tallies[donor] - 1, reach - tallies[taker]) // 2
    room = jnp.where((donor == order[0]) | (taker == order[0]) | (tallies[taker] == 0), 0, jnp.maximum(room, 0))
    passed = jax.random.randint(jax.random.fold_in(own, 4), (count // 2,), 0, 1 << 20) % (room + 1)
    tallies = tallies.at[donor].add(-passed).at[taker].add(passed)
    members = jnp.searchsorted(jnp.cumsum(tallies), jnp.arange(rows * top), side="right").astype(jnp.int32)
    table = members.reshape(top, rows).T
    table = table[jax.random.permutation(jax.random.fold_in(own, 1), rows)]
    turn = jax.random.randint(jax.random.fold_in(own, 2), (rows, 1), 0, top)
    return jnp.take_along_axis(table, (jnp.arange(top)[None, :] + turn) % top, axis=1)


def shares(count, total, bound, slope, full):
    portions = [(1 << 20) // math.isqrt(grade ** slope) + 1 for grade in range(1, count + 1)]
    largest = bound if full else min(bound, max(-(-total // count), total * portions[0] // sum(portions)))
    least = 1 if total - largest >= count - 1 else 0
    given, rest = [largest] + [least] * (count - 1), total - largest - least * (count - 1)
    while rest > 0:
        candidates = [i for i in range(1, count) if given[i] < largest] or [i for i in range(1, count) if given[i] < bound]
        mass, remaining = sum([portions[i] for i in candidates]), rest
        for i in candidates:
            more = min(bound - given[i], max(1, remaining * portions[i] // mass), rest)
            given[i] = given[i] + more
            rest = rest - more
    return np.array(given)


def centred(rng, shape, width, reach, shards=(), held_as=jnp.bfloat16):
    array = jax.random.normal(rng, shape, jnp.float32) * width
    if len(shards) > 0:
        array = block_scale(rng, shape, shards, -0.22, 0.18) * array
    return jnp.clip(array, min=-reach, max=reach).astype(held_as)


def setup_inputs(seed: int = 0) -> dict:
    splits = jax.random.split(jax.random.key(seed), 15)
    stream = centred(splits[0], (TOKENS, MODEL_WIDTH), 1.0, 6.0, ((0, 32),))
    doc_starts = draw_doc_starts(jax.random.fold_in(splits[14], 71), 0)
    expert_routes_keys = jax.random.split(jax.random.fold_in(splits[2], 1), TOKENS // TOK_DEV)
    expert_routes_turns = jax.random.permutation(jax.random.fold_in(splits[2], 3), TOKENS // TOK_DEV)
    expert_routes = jax.vmap(lambda own, number: routed_block(jax.random.fold_in(splits[2], 2), own, number, TOK_DEV, E, TOP, MOST, 1))(expert_routes_keys, expert_routes_turns).reshape((TOKENS, TOP))
    attn_gain = jnp.clip(1.0 + 0.1 * jax.random.normal(splits[3], (MODEL_WIDTH,), jnp.float32), 0.5, 1.5).astype(jnp.bfloat16)
    w_query = centred(splits[4], (MODEL_WIDTH, QUERY_HEADS * HEAD_SIZE), MODEL_WIDTH ** -0.5, 0.15625, ((0, 16),))
    key_projection = centred(splits[5], (MODEL_WIDTH, KEY_VALUE_HEADS * HEAD_SIZE), MODEL_WIDTH ** -0.5, 0.15625, ((0, 16),))
    value_projection = centred(splits[6], (MODEL_WIDTH, KEY_VALUE_HEADS * HEAD_SIZE), MODEL_WIDTH ** -0.5, 0.15625, ((0, 16),))
    w_out = centred(splits[7], (QUERY_HEADS * HEAD_SIZE, MODEL_WIDTH), (max(1, 16 * QUERY_HEADS * HEAD_SIZE // TOKENS)) ** -0.5, 3.5, ((0, 16),))
    ffn_gain = jnp.clip(1.0 + 0.1 * jax.random.normal(splits[8], (MODEL_WIDTH,), jnp.float32), 0.5, 1.5).astype(jnp.bfloat16)
    w_router = centred(splits[9], (MODEL_WIDTH, E), (4 * MODEL_WIDTH) ** -0.5, 0.078125, ((0, 16),))
    w_gate = centred(splits[10], (E, MODEL_WIDTH, FF), MODEL_WIDTH ** -0.5, 0.15625, ((1, 16),))
    w_up = centred(splits[11], (E, MODEL_WIDTH, FF), MODEL_WIDTH ** -0.5, 0.15625, ((1, 16),))
    w_down = centred(splits[12], (E, FF, MODEL_WIDTH), (FF // 32) ** -0.5, 1.25, ((1, 16),))
    out_grad = centred(splits[13], (TOKENS, MODEL_WIDTH), 1.0, 6.0, ((0, 32),))
    return dict(stream=stream, doc_starts=doc_starts, expert_routes=expert_routes, attn_gain=attn_gain, w_query=w_query, key_projection=key_projection, value_projection=value_projection, w_out=w_out, ffn_gain=ffn_gain, w_router=w_router, w_gate=w_gate, w_up=w_up, w_down=w_down, out_grad=out_grad)


norm_eps = 1e-06
rope_base = 10000.0
highest = lax.Precision.HIGHEST

@jax.custom_vjp
def reduced_precision(v):
    return lax.optimization_barrier(v.astype(jnp.bfloat16)).astype(jnp.float32)

@jax.custom_vjp
def reduced_backward(v):
    return v

def low_keep(v):
    return (reduced_precision(v), None)

def low_pass(kept, grad):
    return (grad,)

def back_keep(v):
    return (v, None)

def back_low(kept, grad):
    return (reduced_precision(grad),)
reduced_precision.defvjp(low_keep, low_pass)
reduced_backward.defvjp(back_keep, back_low)

def matrix_product(left, right):
    return jnp.dot(left, right, precision=highest, preferred_element_type=jnp.float32)

def rms_scale(values, gain):
    return values * lax.rsqrt(lax.optimization_barrier(jnp.mean(values * values, axis=-1, keepdims=True)) + norm_eps) * gain

def segment_info(tok_index, starts):
    inside = starts[None, :] <= tok_index[:, None]
    segment = lax.optimization_barrier(jnp.sum(inside.astype(jnp.int32), axis=1)) - 1
    doc_first = lax.optimization_barrier(jnp.max(jnp.where(inside, starts[None, :], 0), axis=1))
    return (segment, tok_index - doc_first)

def rope_angles(position, head_width):
    half_width = head_width // 2
    inv_freq = rope_base ** (-(jnp.arange(half_width, dtype=jnp.float32) * 2.0) / head_width)
    return position.astype(jnp.float32)[:, None] * inv_freq[None, :]

def apply_rotary(values, rotary_angle):
    half_width = values.shape[-1] // 2
    cosine = jnp.cos(rotary_angle)[:, None, :]
    sine_part = jnp.sin(rotary_angle)[:, None, :]
    lower, second = (values[..., :half_width], values[..., half_width:])
    return jnp.concatenate([lower * cosine - second * sine_part, second * cosine + lower * sine_part], axis=-1)

def forward(stream, attn_gain, w_query, key_projection, value_projection, w_out, ffn_gain, w_router, w_gate, w_up, w_down, expert_routes, doc_starts):
    count_of_tokens = stream.shape[0]
    tok_index = jnp.arange(count_of_tokens, dtype=jnp.int32)
    segment, position = segment_info(tok_index, doc_starts)
    rotary_angle = rope_angles(position, HEAD_SIZE)
    normalized_input = reduced_precision(rms_scale(stream, attn_gain))
    query_raw = reduced_backward(matrix_product(normalized_input, w_query)).reshape(count_of_tokens, QUERY_HEADS, HEAD_SIZE)
    rotated_query = reduced_backward(reduced_precision(apply_rotary(query_raw, rotary_angle)))
    unrotated_key = reduced_backward(matrix_product(normalized_input, key_projection)).reshape(count_of_tokens, KEY_VALUE_HEADS, HEAD_SIZE)
    key_rows = reduced_backward(reduced_precision(apply_rotary(unrotated_key, rotary_angle)))
    rows_of_values = reduced_backward(reduced_precision(matrix_product(normalized_input, value_projection))).reshape(count_of_tokens, KEY_VALUE_HEADS, HEAD_SIZE)
    rows_per_block = math.gcd(512, count_of_tokens)
    count_of_blocks = count_of_tokens // rows_per_block
    query_group = QUERY_HEADS // KEY_VALUE_HEADS
    score_scale = HEAD_SIZE ** (-0.5)
    blocks_of_queries = rotated_query.reshape(count_of_blocks, rows_per_block, KEY_VALUE_HEADS, query_group, HEAD_SIZE)

    def attend(block_args):
        query_block, block_index, block_segment = block_args
        raw_scores = jnp.einsum('qkgd,tkd->kgqt', query_block, key_rows, precision=highest)
        scores = reduced_backward(raw_scores * score_scale)
        allowed = (tok_index[None, :] <= block_index[:, None]) & (segment[None, :] == block_segment[:, None])
        row_top = lax.optimization_barrier(jnp.max(jnp.where(allowed, scores, -jnp.inf), axis=-1, keepdims=True))
        weights = jnp.exp(jnp.where(allowed, scores - row_top, -jnp.inf))
        row_total = lax.optimization_barrier(jnp.sum(weights, axis=-1, keepdims=True))
        summed = reduced_backward(jnp.einsum('kgqt,tkd->kgqd', reduced_precision(weights), rows_of_values, precision=highest))
        return summed / row_total
    attended = lax.map(jax.checkpoint(attend), (blocks_of_queries, tok_index.reshape(count_of_blocks, rows_per_block), segment.reshape(count_of_blocks, rows_per_block)))
    attended = attended.transpose(0, 3, 1, 2, 4).reshape(count_of_tokens, QUERY_HEADS * HEAD_SIZE)
    mixed_heads = reduced_backward(reduced_precision(attended))
    middle = stream + reduced_backward(matrix_product(mixed_heads, w_out))
    normed_ffn = reduced_precision(rms_scale(middle, ffn_gain))
    logits = reduced_backward(matrix_product(normed_ffn, w_router))
    router_probs = jax.nn.softmax(logits, axis=-1)
    blocks = count_of_tokens // TOK_DEV
    chosen = lax.optimization_barrier(jnp.sum((expert_routes[:, :, None] == jnp.arange(E, dtype=jnp.int32)[None, None, :]).astype(jnp.int32), axis=1))
    chosen_blocks = chosen.reshape(blocks, TOK_DEV, E)
    slot_rank = jnp.cumsum(chosen_blocks, axis=1) - 1
    slot_ids = jnp.arange(MOST, dtype=jnp.int32)
    dispatch = ((slot_rank.transpose(0, 2, 1)[:, :, None, :] == slot_ids[None, None, :, None]) & (chosen_blocks.transpose(0, 2, 1)[:, :, None, :] == 1)).astype(jnp.float32)
    token_gates = (router_probs * chosen.astype(jnp.float32)).reshape(blocks, TOK_DEV, E)
    token_rows = normed_ffn.reshape(blocks, TOK_DEV, MODEL_WIDTH)
    slot_rows = jnp.einsum('bect,btd->becd', dispatch, token_rows, precision=highest)
    slot_gates = jnp.einsum('bect,bte->bec', dispatch, token_gates, precision=highest)
    gate_pre = reduced_backward(jnp.einsum('becd,edf->becf', slot_rows, w_gate, precision=highest))
    up_pre = reduced_backward(jnp.einsum('becd,edf->becf', slot_rows, w_up, precision=highest))
    active = reduced_precision(jax.nn.gelu(gate_pre, approximate=False) * up_pre)
    expert_out = reduced_backward(jnp.einsum('becf,efd->becd', active, w_down, precision=highest))
    mixture = jnp.einsum('bect,becd->btd', dispatch, expert_out * slot_gates[..., None], precision=highest)
    return middle + mixture.reshape(count_of_tokens, MODEL_WIDTH)

def reference(stream, doc_starts, expert_routes, attn_gain, w_query, key_projection, value_projection, w_out, ffn_gain, w_router, w_gate, w_up, w_down, out_grad):
    floats = tuple((array_item.astype(jnp.float32) for array_item in (stream, attn_gain, w_query, key_projection, value_projection, w_out, ffn_gain, w_router, w_gate, w_up, w_down)))

    def apply_layer(*items):
        return forward(*items, expert_routes, doc_starts)
    result, pull_back = jax.vjp(apply_layer, *floats)
    grads = pull_back(out_grad.astype(jnp.float32))
    return (result.astype(jnp.bfloat16), grads[0].astype(jnp.bfloat16), grads[1], grads[2], grads[3], grads[4], grads[5], grads[6], grads[7], grads[8], grads[9], grads[10])
```

```python
import jax
import jax.numpy as jnp
from jax import lax
from jax.experimental import pallas as pl
from jax.experimental.pallas import tpu as pltpu
from jax.sharding import Mesh, PartitionSpec as P

WIDTH = 1536
HEADS = 12
KV_HEADS = 2
HEAD = 128
FF = 768
E = 8
MOST = 192
SEQ = KV_HEADS
GROUP = HEADS // KV_HEADS
INNER = E // SEQ
QCOLS = GROUP * HEAD
QKV = QCOLS + 2 * HEAD
EXTRA = 128
PACK = QKV + EXTRA + WIDTH
EPS = 1e-06
ROPE_BASE = 10000.0
SCALE = HEAD**-0.5
LOG2E = 1.4426950408889634
LN2 = 0.6931471805599453
NEG = -1e30
AXES = ("outer", "inner", "seq")
MESH = pl.DeviceIdType.MESH
NN = (((1,), (0,)), ((), ()))
NT = (((1,), (1,)), ((), ()))
TN = (((0,), (0,)), ((), ()))
BF = jnp.bfloat16
F32 = jnp.float32


def dot(a, b, dims=NN):
    return lax.dot_general(a, b, dims, preferred_element_type=F32)


class Net:
    def __init__(self, depth):
        self.depth = depth
        self.z = lax.axis_index("outer")
        self.i = lax.axis_index("inner")
        self.y = lax.axis_index("seq")
        self.core = lax.rem(self.i, 2)
        self.x = lax.div(self.i, 2)
        self.xp = self.dev(i=lax.rem(self.i + 2, INNER))
        self.cp = self.dev(i=self.i + 1 - 2 * self.core)
        self.yp = self.dev(y=1 - self.y)

    def dev(self, z=None, i=None, y=None):
        return {
            "outer": self.z if z is None else z,
            "inner": self.i if i is None else i,
            "seq": self.y if y is None else y,
        }

    def zoff(self, dz):
        return lax.rem(self.z + dz, self.depth)

    def zpeers(self):
        return [self.dev(z=self.zoff(dz)) for dz in range(1, self.depth)]

    def plane(self):
        out = []
        for di in range(INNER):
            for dy in range(SEQ):
                if di or dy:
                    out.append(
                        self.dev(i=lax.rem(self.i + di, INNER), y=lax.rem(self.y + dy, SEQ))
                    )
        return out


def greet(devices):
    barrier = pltpu.get_barrier_semaphore()
    for device in devices:
        pl.semaphore_signal(barrier, inc=1, device_id=device, device_id_type=MESH)
    pl.semaphore_wait(barrier, len(devices))


def remote(src, dst, ssem, rsem, device):
    return pltpu.make_async_remote_copy(
        src_ref=src, dst_ref=dst, send_sem=ssem, recv_sem=rsem, device_id=device, device_id_type=MESH
    )


class Sends:
    def __init__(self):
        self.items = []

    def start(self, src, dst, ssem, rsem, device):
        copy = remote(src, dst, ssem, rsem, device)
        copy.start()
        self.items.append(copy)

    def finish(self):
        for copy in self.items:
            copy.wait_send()


def arrived(dst, ssem, rsem, device):
    remote(dst, dst, ssem, rsem, device).wait_recv()


def dma_sems(*counts):
    return [pltpu.SemaphoreType.DMA((n,)) for n in counts]


class ShardGather:
    def __init__(self, net, sends, src, out, sems):
        self.net, self.sends, self.src, self.out = net, sends, src, out
        self.sz, self.rz, self.sx, self.rx, self.sc, self.rc = sems

    @staticmethod
    def sems(depth):
        return dma_sems(*([max(depth - 1, 1)] * 2 + [depth] * 2 + [2 * depth] * 2))

    def slot(self, dz, i):
        return self.out.at[lax.rem(self.net.z - dz + self.net.depth, self.net.depth) * INNER + i]

    def begin(self):
        net, me = self.net, self.slot(0, self.net.i)
        for n, device in enumerate(net.zpeers()):
            self.sends.start(self.src, me, self.sz.at[n], self.rz.at[n], device)
        self.sends.start(self.src, me, self.sx.at[0], self.rx.at[0], net.xp)
        self.sends.start(self.src, me, self.sc.at[0], self.rc.at[0], net.cp)

    def end(self):
        net, depth = self.net, self.net.depth
        xi = lax.rem(net.i + 2, INNER)
        for dz in range(1, depth):
            block = self.slot(dz, net.i)
            arrived(block, self.sz.at[dz - 1], self.rz.at[dz - 1], net.zpeers()[dz - 1])
            self.sends.start(block, block, self.sx.at[dz], self.rx.at[dz], net.xp)
            self.sends.start(block, block, self.sc.at[dz], self.rc.at[dz], net.cp)
        for dz in range(depth):
            block = self.slot(dz, xi)
            arrived(block, self.sx.at[dz], self.rx.at[dz], net.xp)
            self.sends.start(
                block, block, self.sc.at[depth + dz], self.rc.at[depth + dz], net.cp
            )
        ci = net.i + 1 - 2 * net.core
        for dz in range(depth):
            arrived(self.slot(dz, ci), self.sc.at[dz], self.rc.at[dz], net.cp)
        for dz in range(depth):
            arrived(
                self.slot(dz, lax.rem(ci + 2, INNER)),
                self.sc.at[depth + dz],
                self.rc.at[depth + dz],
                net.cp,
            )


def hbm():
    return pl.BlockSpec(memory_space=pltpu.HBM)


def vmem():
    return pl.BlockSpec(memory_space=pltpu.VMEM)


def smem():
    return pl.BlockSpec(memory_space=pltpu.SMEM)


def comm_params(cid, limit=56 << 20):
    return pltpu.CompilerParams(
        collective_id=cid, has_side_effects=True, vmem_limit_bytes=limit
    )


def opening(pack, moe, stream, chosen, depth):
    rows = pack.shape[0]

    def kernel(pack_ref, moe_ref, st_ref, ch_ref, pack_out, moe_out, st_out, ch_out, *sems):
        net = Net(depth)
        sends = Sends()
        gather = ShardGather(net, sends, pack_ref, pack_out, sems[:6])
        sm, rm, sy, ry, sp, rp, own = sems[6:]
        locals_ = [
            pltpu.make_async_copy(pack_ref, gather.slot(0, net.i), own.at[0]),
            pltpu.make_async_copy(moe_ref.at[net.i * SEQ + net.y], moe_out.at[net.i], own.at[1]),
            pltpu.make_async_copy(st_ref, st_out.at[net.y], own.at[2]),
            pltpu.make_async_copy(ch_ref, ch_out.at[net.i * SEQ + net.y], own.at[3]),
        ]
        greet(net.zpeers() + net.plane())
        gather.begin()
        sends.start(st_ref, st_out.at[net.y], sy.at[0], ry.at[0], net.yp)
        for n, device in enumerate(net.plane()):
            sends.start(ch_ref, ch_out.at[net.i * SEQ + net.y], sp.at[n], rp.at[n], device)
        for di in range(1, INNER):
            other = lax.rem(net.i + di, INNER)
            sends.start(
                moe_ref.at[other * SEQ + net.y],
                moe_out.at[net.i],
                sm.at[di - 1],
                rm.at[di - 1],
                net.dev(i=other),
            )
        for copy in locals_:
            copy.start()
        gather.end()
        arrived(st_out.at[1 - net.y], sy.at[0], ry.at[0], net.yp)
        n = 0
        for di in range(INNER):
            for dy in range(SEQ):
                if di or dy:
                    frm = lax.rem(net.i - di + INNER, INNER) * SEQ + lax.rem(net.y + dy, SEQ)
                    arrived(ch_out.at[frm], sp.at[n], rp.at[n], net.yp)
                    n += 1
        for di in range(1, INNER):
            frm = lax.rem(net.i - di + INNER, INNER)
            arrived(moe_out.at[frm], sm.at[di - 1], rm.at[di - 1], net.yp)
        sends.finish()
        for copy in locals_:
            copy.wait()

    return pl.pallas_call(
        kernel,
        out_shape=(
            jax.ShapeDtypeStruct((depth * INNER,) + pack.shape, BF),
            jax.ShapeDtypeStruct((INNER,) + moe.shape[1:], BF),
            jax.ShapeDtypeStruct((SEQ,) + stream.shape, BF),
            jax.ShapeDtypeStruct((E,) + chosen.shape, F32),
        ),
        in_specs=[hbm()] * 4,
        out_specs=(hbm(),) * 4,
        scratch_shapes=ShardGather.sems(depth) + dma_sems(3, 3, 1, 1, E - 1, E - 1, 4),
        compiler_params=comm_params(1),
        name="opening",
    )(pack, moe, stream, chosen)


def gather_keys(kv, depth):
    def kernel(src, out, *sems):
        net = Net(depth)
        sends = Sends()
        gather = ShardGather(net, sends, src, out, sems[:6])
        own = pltpu.make_async_copy(src, gather.slot(0, net.i), sems[6].at[0])
        greet(net.zpeers() + [net.xp, net.cp])
        gather.begin()
        own.start()
        gather.end()
        sends.finish()
        own.wait()

    return pl.pallas_call(
        kernel,
        out_shape=jax.ShapeDtypeStruct((depth * INNER,) + kv.shape, BF),
        in_specs=[hbm()],
        out_specs=hbm(),
        scratch_shapes=ShardGather.sems(depth) + dma_sems(1),
        compiler_params=comm_params(2),
        name="gather_keys",
    )(kv)


def gather_plane(rows, depth, cid):
    half = rows.shape[0] // 2

    def kernel(src, out, sx, rx, sy, ry, sc, rc, own):
        net = Net(depth)
        sends = Sends()

        def place(i, y):
            return i * SEQ + y

        xi = lax.rem(net.i + 2, INNER)
        me, xb = place(net.i, net.y), place(xi, net.y)
        yb, db = place(net.i, 1 - net.y), place(xi, 1 - net.y)
        lo, hi = pl.ds(0, half), pl.ds(half, half)
        mine = pltpu.make_async_copy(src, out.at[me], own.at[0])
        greet([net.xp, net.yp, net.cp])
        sends.start(src, out.at[me], sx.at[0], rx.at[0], net.xp)
        sends.start(src, out.at[me], sy.at[0], ry.at[0], net.yp)
        sends.start(src, out.at[me], sc.at[0], rc.at[0], net.cp)
        mine.start()
        arrived(out.at[yb], sy.at[0], ry.at[0], net.yp)
        sends.start(out.at[yb, lo], out.at[yb, lo], sx.at[1], rx.at[1], net.xp)
        sends.start(out.at[yb], out.at[yb], sc.at[1], rc.at[1], net.cp)
        arrived(out.at[xb], sx.at[0], rx.at[0], net.xp)
        sends.start(out.at[xb, hi], out.at[xb, hi], sy.at[1], ry.at[1], net.yp)
        sends.start(out.at[xb], out.at[xb], sc.at[2], rc.at[2], net.cp)
        arrived(out.at[db, lo], sx.at[1], rx.at[1], net.xp)
        sends.start(out.at[db, lo], out.at[db, lo], sc.at[3], rc.at[3], net.cp)
        arrived(out.at[db, hi], sy.at[1], ry.at[1], net.yp)
        sends.start(out.at[db, hi], out.at[db, hi], sc.at[4], rc.at[4], net.cp)
        ci = net.i + 1 - 2 * net.core
        cx = lax.rem(ci + 2, INNER)
        arrived(out.at[place(ci, net.y)], sc.at[0], rc.at[0], net.cp)
        arrived(out.at[place(ci, 1 - net.y)], sc.at[1], rc.at[1], net.cp)
        arrived(out.at[place(cx, net.y)], sc.at[2], rc.at[2], net.cp)
        arrived(out.at[place(cx, 1 - net.y), lo], sc.at[3], rc.at[3], net.cp)
        arrived(out.at[place(cx, 1 - net.y), hi], sc.at[4], rc.at[4], net.cp)
        sends.finish()
        mine.wait()

    return pl.pallas_call(
        kernel,
        out_shape=jax.ShapeDtypeStruct((E,) + rows.shape, BF),
        in_specs=[hbm()],
        out_specs=hbm(),
        scratch_shapes=dma_sems(2, 2, 2, 2, 5, 5, 1),
        compiler_params=comm_params(cid),
        name="gather_plane",
    )(rows)


def add_into(dst, sources, rows, chunk):
    def body(n, carry):
        at = pl.ds(pl.multiple_of(n * chunk, chunk), chunk)
        total = sources[0][at, :].astype(F32)
        for source in sources[1:]:
            total = total + source[at, :].astype(F32)
        dst[at, :] = total.astype(dst.dtype)
        return carry

    lax.fori_loop(0, rows // chunk, body, 0)


def chunk_of(rows):
    for size in (32, 16, 8):
        if rows % size == 0:
            return size
    return rows


def scatter_plane(part, depth):
    rows, cols = part.shape[1:]
    half = rows // 2

    def kernel(part_ref, out, bc, mid, bx, by, second, b2, ssem, rsem):
        net = Net(depth)
        sends = Sends()

        def place(fx, fy, core):
            x = 1 - net.x if fx else net.x
            y = 1 - net.y if fy else net.y
            return (x * 2 + core) * SEQ + y

        greet([net.xp, net.yp, net.cp])
        order = ((1, 1), (1, 0), (0, 1), (0, 0))
        for n, (fx, fy) in enumerate(order):
            sends.start(
                part_ref.at[place(fx, fy, 1 - net.core)], bc.at[n], ssem.at[n], rsem.at[n], net.cp
            )
        ch = chunk_of(half)
        lo, hi = pl.ds(0, half), pl.ds(half, half)
        for n, (fx, fy) in enumerate(order):
            arrived(bc.at[n], ssem.at[n], rsem.at[n], net.cp)
            add_into(mid.at[n], [part_ref.at[place(fx, fy, net.core)], bc.at[n]], rows, ch)
            if n == 0:
                sends.start(mid.at[0, lo], bx.at[0], ssem.at[4], rsem.at[4], net.xp)
                sends.start(mid.at[0, hi], by.at[0], ssem.at[5], rsem.at[5], net.yp)
            if n == 1:
                sends.start(mid.at[1, lo], bx.at[1], ssem.at[6], rsem.at[6], net.xp)
            if n == 2:
                sends.start(mid.at[2, hi], by.at[1], ssem.at[7], rsem.at[7], net.yp)
        arrived(bx.at[0], ssem.at[4], rsem.at[4], net.xp)
        add_into(second.at[0], [mid.at[2, lo], bx.at[0]], half, ch)
        sends.start(second.at[0], b2.at[0], ssem.at[8], rsem.at[8], net.yp)
        arrived(by.at[0], ssem.at[5], rsem.at[5], net.yp)
        add_into(second.at[1], [mid.at[1, hi], by.at[0]], half, ch)
        sends.start(second.at[1], b2.at[1], ssem.at[9], rsem.at[9], net.xp)
        arrived(bx.at[1], ssem.at[6], rsem.at[6], net.xp)
        arrived(by.at[1], ssem.at[7], rsem.at[7], net.yp)
        arrived(b2.at[0], ssem.at[8], rsem.at[8], net.yp)
        add_into(out.at[lo], [mid.at[3, lo], bx.at[1], b2.at[0]], half, ch)
        arrived(b2.at[1], ssem.at[9], rsem.at[9], net.xp)
        add_into(out.at[hi], [mid.at[3, hi], by.at[1], b2.at[1]], half, ch)
        sends.finish()

    return pl.pallas_call(
        kernel,
        out_shape=jax.ShapeDtypeStruct((rows, cols), F32),
        in_specs=[vmem()],
        out_specs=vmem(),
        scratch_shapes=[pltpu.VMEM((4, rows, cols), BF)] * 2
        + [pltpu.VMEM((2, half, cols), BF)] * 4
        + dma_sems(10, 10),
        compiler_params=comm_params(4),
        name="scatter_plane",
    )(part)


class ShardScatter:
    @staticmethod
    def scratch(depth, rows, cols):
        far = max(depth - 1, 1)
        shapes = [(2 * depth, rows, cols)] + [(depth, rows, cols)] * 2 + [(far, rows, cols)] * 2
        return [pltpu.VMEM(s, BF) for s in shapes] + dma_sems(
            2 * depth, 2 * depth, depth, depth, far, far
        )

    def __init__(self, net, sends, part, scratch):
        self.net, self.sends, self.part = net, sends, part
        self.bc, self.sx, self.bx, self.sz, self.bz = scratch[:5]
        self.ssc, self.rsc, self.ssx, self.rsx, self.ssz, self.rsz = scratch[5:]
        depth = net.depth
        self.order = sorted(range(1, depth), key=lambda d: -min(d, depth - d)) + [0]
        self.rows = part.shape[1]
        self.chunk = chunk_of(self.rows)

    def block(self, dz, fx, core):
        x = 1 - self.net.x if fx else self.net.x
        return self.part.at[self.net.zoff(dz) * INNER + x * 2 + core]

    def begin(self):
        net = self.net
        for dz in self.order:
            for fx in (1, 0):
                n = dz * 2 + fx
                self.sends.start(
                    self.block(dz, fx, 1 - net.core),
                    self.bc.at[n],
                    self.ssc.at[n],
                    self.rsc.at[n],
                    net.cp,
                )

    def end(self, out):
        net, sends = self.net, self.sends
        for dz in self.order:
            n = dz * 2 + 1
            arrived(self.bc.at[n], self.ssc.at[n], self.rsc.at[n], net.cp)
            add_into(
                self.sx.at[dz], [self.block(dz, 1, net.core), self.bc.at[n]], self.rows, self.chunk
            )
            sends.start(self.sx.at[dz], self.bx.at[dz], self.ssx.at[dz], self.rsx.at[dz], net.xp)
        for dz in self.order:
            n = dz * 2
            arrived(self.bc.at[n], self.ssc.at[n], self.rsc.at[n], net.cp)
            arrived(self.bx.at[dz], self.ssx.at[dz], self.rsx.at[dz], net.xp)
            terms = [self.block(dz, 0, net.core), self.bc.at[n], self.bx.at[dz]]
            if dz:
                add_into(self.sz.at[dz - 1], terms, self.rows, self.chunk)
                sends.start(
                    self.sz.at[dz - 1],
                    self.bz.at[dz - 1],
                    self.ssz.at[dz - 1],
                    self.rsz.at[dz - 1],
                    net.dev(z=net.zoff(dz)),
                )
            else:
                for far in range(net.depth - 1):
                    arrived(self.bz.at[far], self.ssz.at[far], self.rsz.at[far], net.xp)
                    terms.append(self.bz.at[far])
                add_into(out, terms, self.rows, self.chunk)


def scatter_keys(part, depth):
    rows, cols = part.shape[1:]

    def kernel(part_ref, out, *scratch):
        net = Net(depth)
        sends = Sends()
        greet(net.zpeers() + [net.xp, net.cp])
        work = ShardScatter(net, sends, part_ref, scratch)
        work.begin()
        work.end(out)
        sends.finish()

    return pl.pallas_call(
        kernel,
        out_shape=jax.ShapeDtypeStruct((rows, cols), F32),
        in_specs=[vmem()],
        out_specs=vmem(),
        scratch_shapes=ShardScatter.scratch(depth, rows, cols),
        compiler_params=comm_params(5),
        name="scatter_keys",
    )(part)


def closing(part, moe, depth):
    rows, cols = part.shape[1:]

    def kernel(part_ref, moe_ref, own_out, pair_out, moe_out, low, sm, rm, sy, ry, ls, *scratch):
        net = Net(depth)
        sends = Sends()
        me = net.i * SEQ + net.y
        mine = pltpu.make_async_copy(moe_ref.at[net.i], moe_out.at[me], ls.at[0])
        greet(net.zpeers() + net.plane())
        work = ShardScatter(net, sends, part_ref, scratch)
        work.begin()
        n = 0
        for di in range(INNER):
            for dy in range(SEQ):
                if di or dy:
                    i = lax.rem(net.i + di, INNER)
                    device = net.dev(i=i, y=lax.rem(net.y + dy, SEQ))
                    sends.start(moe_ref.at[i], moe_out.at[me], sm.at[n], rm.at[n], device)
                    n += 1
        mine.start()
        work.end(own_out)
        low[...] = own_out[...].astype(BF)
        sends.start(low, pair_out, sy.at[0], ry.at[0], net.yp)
        n = 0
        for di in range(INNER):
            for dy in range(SEQ):
                if di or dy:
                    frm = lax.rem(net.i - di + INNER, INNER) * SEQ + lax.rem(net.y + dy, SEQ)
                    arrived(moe_out.at[frm], sm.at[n], rm.at[n], net.yp)
                    n += 1
        arrived(pair_out, sy.at[0], ry.at[0], net.yp)
        sends.finish()
        mine.wait()

    return pl.pallas_call(
        kernel,
        out_shape=(
            jax.ShapeDtypeStruct((rows, cols), F32),
            jax.ShapeDtypeStruct((rows, cols), BF),
            jax.ShapeDtypeStruct((E,) + moe.shape[1:], BF),
        ),
        in_specs=[vmem(), hbm()],
        out_specs=(vmem(), vmem(), hbm()),
        scratch_shapes=[pltpu.VMEM((rows, cols), BF)]
        + dma_sems(E - 1, E - 1, 1, 1, 1)
        + ShardScatter.scratch(depth, rows, cols),
        compiler_params=comm_params(6),
        name="closing",
    )(part, moe)


def turn(values, cosine, sine):
    return values * cosine + pltpu.roll(values, HEAD // 2, 1) * sine


def project(stream, gain, weights, cosine, sine):
    rows = stream.shape[0]
    wide = 2 * HEAD

    def kernel(s_ref, g_ref, w_ref, c_ref, n_ref, h_ref, o_ref):
        n = pl.program_id(0)

        @pl.when(n == 0)
        def _():
            x = s_ref[...].astype(F32)
            scale = lax.rsqrt(jnp.mean(x * x, axis=-1, keepdims=True) + EPS)
            h_ref[...] = (x * scale * g_ref[...]).astype(BF)

        r = dot(h_ref[...], w_ref[...])
        first = turn(r[:, :HEAD], c_ref[...], n_ref[...])

        @pl.when(n < 3)
        def _():
            o_ref[:, :HEAD] = (first * (SCALE * LOG2E)).astype(BF)
            second = turn(r[:, HEAD:], c_ref[...], n_ref[...])
            o_ref[:, HEAD:] = (second * (SCALE * LOG2E)).astype(BF)

        @pl.when(n == 3)
        def _():
            o_ref[:, :HEAD] = first.astype(BF)
            o_ref[:, HEAD:] = r[:, HEAD:].astype(BF)

    fixed = lambda shape: pl.BlockSpec(shape, lambda n: (0, 0))
    return pl.pallas_call(
        kernel,
        grid=(QKV // wide,),
        in_specs=[
            fixed((rows, WIDTH)),
            fixed((1, WIDTH)),
            pl.BlockSpec((WIDTH, wide), lambda n: (0, n)),
            fixed((rows, HEAD)),
            fixed((rows, HEAD)),
        ],
        out_specs=(fixed((rows, WIDTH)), pl.BlockSpec((rows, wide), lambda n: (0, n))),
        out_shape=(
            jax.ShapeDtypeStruct((rows, WIDTH), BF),
            jax.ShapeDtypeStruct((rows, QKV), BF),
        ),
        compiler_params=pltpu.CompilerParams(vmem_limit_bytes=32 << 20),
        name="project",
    )(stream, gain, weights, cosine, sine)


def unturn(dq, dkv, cosine, sine):
    rows = dq.shape[0]

    def kernel(dq_ref, dkv_ref, c_ref, n_ref, o_ref):
        c, s = c_ref[...], -n_ref[...]
        for h in range(GROUP):
            at = slice(h * HEAD, (h + 1) * HEAD)
            o_ref[:, at] = turn(dq_ref[:, at].astype(F32), c, s).astype(BF)
        dk = dkv_ref[:, :HEAD].astype(BF).astype(F32)
        o_ref[:, QCOLS : QCOLS + HEAD] = turn(dk, c, s).astype(BF)
        o_ref[:, QCOLS + HEAD :] = dkv_ref[:, HEAD:].astype(BF)

    return pl.pallas_call(
        kernel,
        in_specs=[vmem()] * 4,
        out_specs=vmem(),
        out_shape=jax.ShapeDtypeStruct((rows, QKV), BF),
        compiler_params=pltpu.CompilerParams(vmem_limit_bytes=32 << 20),
        name="unturn",
    )(dq, dkv, cosine, sine)


def attend_forward(q, kv, lo, info, tile=512):
    block = q.shape[1]

    def kernel(info_ref, q_ref, kv_ref, lo_ref, o_ref, m_ref, l_ref, acc, top, total):
        for j in range(2):
            base = info_ref[j] * block
            first = info_ref[2 + j] // tile
            last = (base + block - 1) // tile
            acc[...] = jnp.zeros_like(acc)
            top[...] = jnp.full_like(top, NEG)
            total[...] = jnp.zeros_like(total)

            def step(t, masked):
                start = pl.multiple_of(t * tile, tile)
                k = kv_ref[pl.ds(start, tile), :HEAD]
                vt = kv_ref[pl.ds(start, tile), HEAD:].T
                if masked:
                    key = start + lax.broadcasted_iota(jnp.int32, (tile, block), 0)
                    query = base + lax.broadcasted_iota(jnp.int32, (tile, block), 1)
                    ok = (key <= query) & (key >= lo_ref[j])
                for h in range(GROUP):
                    s = dot(k, q_ref[j, :, h * HEAD : (h + 1) * HEAD], NT)
                    if masked:
                        s = jnp.where(ok, s, NEG)
                    m0 = top[h : h + 1, :]
                    m1 = jnp.maximum(m0, jnp.max(s, axis=0, keepdims=True))
                    p = jnp.exp2(s - m1)
                    f = jnp.exp2(m0 - m1)
                    top[h : h + 1, :] = m1
                    total[h : h + 1, :] = total[h : h + 1, :] * f + jnp.sum(
                        p, axis=0, keepdims=True
                    )
                    acc[h] = acc[h] * f + dot(vt, p.astype(BF))

            free_from = jnp.minimum((info_ref[4 + j] + tile - 1) // tile, last + 1)
            free_to = jnp.maximum(base // tile, free_from)

            def run(a, b, masked):
                lax.fori_loop(a, b, lambda t, c: (step(t, masked), c)[1], 0)

            run(first, free_from, True)
            run(free_from, free_to, False)
            run(jnp.maximum(free_to, first), last + 1, True)
            for h in range(GROUP):
                o_ref[j, :, h * HEAD : (h + 1) * HEAD] = (
                    (acc[h] / total[h : h + 1, :]).T.astype(BF)
                )
            m_ref[j] = top[...]
            l_ref[j] = total[...]

    stat = jax.ShapeDtypeStruct((2, 8, block), F32)
    return pl.pallas_call(
        kernel,
        out_shape=(jax.ShapeDtypeStruct(q.shape, BF), stat, stat),
        in_specs=[smem()] + [vmem()] * 3,
        out_specs=(vmem(),) * 3,
        scratch_shapes=[
            pltpu.VMEM((GROUP, HEAD, block), F32),
            pltpu.VMEM((8, block), F32),
            pltpu.VMEM((8, block), F32),
        ],
        compiler_params=pltpu.CompilerParams(vmem_limit_bytes=48 << 20),
        cost_estimate=pl.CostEstimate(
            flops=int(1e10), bytes_accessed=6 << 20, transcendentals=13 << 20
        ),
        name="attend_forward",
    )(info, q, kv, lo)


def attend_backward(q, kv, lo, info, m, l, dob, ob, tile=512):
    block = q.shape[1]
    keys = kv.shape[0]
    tiles = keys // tile

    def kernel(info_ref, q_ref, kv_ref, lo_ref, m_ref, l_ref, do_ref, ob_ref, dq_ref, dkv_ref, da, dl, acc):
        acc[...] = jnp.zeros_like(acc)
        for j in range(2):
            for h in range(GROUP):
                c = slice(h * HEAD, (h + 1) * HEAD)
                d = do_ref[j, :, c].astype(F32)
                o = ob_ref[j, :, c].astype(F32)
                inv = 1.0 / l_ref[j, h : h + 1, :]
                da[j, h] = (d.T * inv).T.astype(BF)
                dl[j, h : h + 1, :] = -jnp.sum((d * o).T, axis=0, keepdims=True) * inv
        low = jnp.minimum(info_ref[2], info_ref[3]) // tile
        high = (info_ref[1] * block + block - 1) // tile

        def clear(t, carry):
            dkv_ref[pl.ds(pl.multiple_of(t * tile, tile), tile), :] = jnp.zeros((tile, 2 * HEAD), BF)
            return carry

        lax.fori_loop(0, low, clear, 0)
        lax.fori_loop(high + 1, tiles, clear, 0)

        def piece(t, j, masked):
            start = pl.multiple_of(t * tile, tile)
            base = info_ref[j] * block
            k = kv_ref[pl.ds(start, tile), :HEAD]
            v = kv_ref[pl.ds(start, tile), HEAD:]
            kt = k.T
            if masked:
                key = start + lax.broadcasted_iota(jnp.int32, (tile, block), 0)
                query = base + lax.broadcasted_iota(jnp.int32, (tile, block), 1)
                ok = (key <= query) & (key >= lo_ref[j])
            dk = dv = None
            for h in range(GROUP):
                qh = q_ref[j, :, h * HEAD : (h + 1) * HEAD]
                s = dot(k, qh, NT) - m_ref[j, h : h + 1, :]
                if masked:
                    s = jnp.where(ok, s, NEG)
                p = jnp.exp2(s)
                dah = da[j, h]
                dvh = dot(p.astype(BF), dah)
                dp = dot(v, dah, NT) + dl[j, h : h + 1, :]
                ds = (p * dp).astype(BF)
                dkh = dot(ds, qh)
                acc[j, h] += dot(kt, ds)
                dk = dkh if dk is None else dk + dkh
                dv = dvh if dv is None else dv + dvh
            return dk * LN2, dv

        def tile_step(t, carry):
            start = pl.multiple_of(t * tile, tile)
            rows = pl.ds(start, tile)

            def put(j, masked):
                dk, dv = piece(t, j, masked)
                if j == 0:
                    dk = dk + dkv_ref[rows, :HEAD].astype(F32)
                    dv = dv + dkv_ref[rows, HEAD:].astype(F32)
                dkv_ref[rows, :HEAD] = dk.astype(BF)
                dkv_ref[rows, HEAD:] = dv.astype(BF)

            for j in (1, 0):
                base = info_ref[j] * block
                live = (start <= base + block - 1) & (start + tile > info_ref[2 + j])
                free = (start + tile - 1 <= base) & (start >= info_ref[4 + j])
                if j == 1:

                    @pl.when(jnp.logical_not(live))
                    def _():
                        clear(t, 0)

                @pl.when(live & free)
                def _():
                    put(j, False)

                @pl.when(live & jnp.logical_not(free))
                def _():
                    put(j, True)

            return carry

        lax.fori_loop(low, high + 1, tile_step, 0)
        for j in range(2):
            for h in range(GROUP):
                dq_ref[j, :, h * HEAD : (h + 1) * HEAD] = (acc[j, h] * SCALE).T.astype(BF)

    return pl.pallas_call(
        kernel,
        out_shape=(jax.ShapeDtypeStruct(q.shape, BF), jax.ShapeDtypeStruct(kv.shape, BF)),
        in_specs=[smem()] + [vmem()] * 7,
        out_specs=(vmem(),) * 2,
        scratch_shapes=[
            pltpu.VMEM((2, GROUP, block, HEAD), BF),
            pltpu.VMEM((2, 8, block), F32),
            pltpu.VMEM((2, GROUP, HEAD, block), F32),
        ],
        compiler_params=pltpu.CompilerParams(vmem_limit_bytes=60 << 20),
        cost_estimate=pl.CostEstimate(
            flops=int(2.5e10), bytes_accessed=12 << 20, transcendentals=13 << 20
        ),
        name="attend_backward",
    )(info, q, kv, lo, m, l, dob, ob)


def rms_parts(x):
    scale = lax.rsqrt(jnp.mean(x * x, axis=-1, keepdims=True) + EPS)
    return x * scale, scale


def rms_pull(normed, scale, grad, gain):
    inner = grad * gain
    return scale * (inner - normed * jnp.mean(inner * normed, axis=-1, keepdims=True))


def document_first(index, starts):
    return jnp.max(jnp.where(starts <= index[..., None], starts, 0), axis=-1)


def gelu_product(gate_pre, up_pre):
    return jax.nn.gelu(gate_pre, approximate=False) * up_pre


class Zigzag:
    def __init__(self, shards):
        last = 2 * shards - 1
        home = lambda b: b if b < shards else last - b
        self.rows = [
            [(s * 2 + y, home(2 * s + k) * 2 + y) for s in range(shards) for y in range(2)]
            for k in range(2)
        ]
        self.heads = [
            [
                (s * 2 + g, s if (g == 0) == (k == 0) else last - s)
                for s in range(shards)
                for g in range(2)
            ]
            for k in range(2)
        ]

    @staticmethod
    def move(x, pairs, back=False):
        return lax.ppermute(x, AXES, [(b, a) for a, b in pairs] if back else pairs)


def pick(flag, a, b):
    return jnp.where(flag, a, b), jnp.where(flag, b, a)


def experts(h2, out_grad, chosen, router_w, moe_w, rows_in, rows_out, me):
    blocks, tokens = h2.shape[:2]
    logits = dot(h2.reshape(blocks * tokens, WIDTH), router_w)
    probs = jax.nn.softmax(logits, axis=-1)
    mine = (jnp.arange(E) == me).astype(F32)
    named = jnp.sum(chosen * mine[None, :, None], axis=1)
    gate_tok = jnp.sum(probs * mine[None, :], axis=-1).reshape(blocks, tokens) * named
    upper = (jnp.arange(tokens)[:, None] <= jnp.arange(tokens)[None, :]).astype(BF)
    rank = dot(named.astype(BF), upper) - 1.0
    pick_slot = (
        rank[:, None, :] == jnp.arange(MOST, dtype=F32)[None, :, None]
    ) & (named[:, None, :] > 0.5)
    onehot = pick_slot.astype(BF)
    slots = blocks * MOST
    gate = jnp.sum(jnp.where(pick_slot, gate_tok[:, None, :], 0.0), axis=-1).reshape(slots, 1)
    spread = lambda v: lax.dot_general(
        onehot, v, (((2,), (1,)), ((0,), (0,))), preferred_element_type=F32
    )
    collect = lambda v: lax.dot_general(
        onehot, v, (((1,), (1,)), ((0,), (0,))), preferred_element_type=F32
    )
    rows = spread(h2).astype(BF).reshape(slots, WIDTH)
    slot_grad = spread(out_grad).astype(BF).reshape(slots, WIDTH)
    gate_w = moe_w[:, :rows_in, :FF].reshape(WIDTH, FF)
    up_w = moe_w[:, :rows_in, FF:].reshape(WIDTH, FF)
    down_w = moe_w[:, rows_in:, :].reshape(FF, WIDTH)
    gate_pre = dot(rows, gate_w)
    up_pre = dot(rows, up_w)
    active_f, pull = jax.vjp(gelu_product, gate_pre, up_pre)
    active = active_f.astype(BF)
    out = dot(active, down_w)
    slot_gf = slot_grad.astype(F32)
    gate_grad = jnp.sum(slot_gf * out, axis=-1).reshape(blocks, MOST)
    mixture = collect((out * gate).astype(BF).reshape(blocks, MOST, WIDTH)).astype(BF)
    expert_grad = (slot_gf * gate).astype(BF)
    active_grad = dot(expert_grad, down_w, NT)
    g_low, u_low = (v.astype(BF) for v in pull(active_grad))
    back = dot(g_low, gate_w, NT) + dot(u_low, up_w, NT)
    back_tok = collect(back.astype(BF).reshape(blocks, MOST, WIDTH)).astype(BF)
    gate_back = jnp.sum(jnp.where(pick_slot, gate_grad[:, :, None], 0.0), axis=1)
    lanes = (jnp.arange(EXTRA) == me).astype(F32)
    back_tok = jnp.concatenate(
        [back_tok, (gate_back[:, :, None] * lanes[None, None, :]).astype(BF)], axis=-1
    )
    shards = WIDTH // rows_in
    grads = jnp.concatenate(
        [
            jnp.concatenate(
                [
                    dot(rows, g_low, TN).astype(BF).reshape(shards, rows_in, FF),
                    dot(rows, u_low, TN).astype(BF).reshape(shards, rows_in, FF),
                ],
                axis=-1,
            ),
            dot(active, expert_grad, TN).astype(BF).reshape(shards, rows_out, WIDTH),
        ],
        axis=1,
    )
    return mixture, back_tok, grads


def local(depth, stream, doc_starts, routes, attn_gain, w_query, w_key, w_value, w_out, ffn_gain, w_router, w_gate, w_up, w_down, out_grad):
    tokens = stream.shape[0]
    rows_in, rows_out = w_gate.shape[1], w_down.shape[1]
    shards = depth * INNER
    z, i, y = (lax.axis_index(a) for a in AXES)
    shard = z * INNER + i
    own_block = shard * SEQ + y
    me = i * SEQ + y
    zig = Zigzag(shards)

    cut = lambda w, width: lax.dynamic_slice_in_dim(w, y * width, width, 1)
    extra = jnp.concatenate(
        [
            attn_gain[:, None],
            ffn_gain[:, None],
            w_router,
            jnp.zeros((rows_in, EXTRA - 2 - E), BF),
        ],
        axis=1,
    )
    pack = jnp.concatenate(
        [cut(w_query, QCOLS), cut(w_key, HEAD), cut(w_value, HEAD), extra, w_out], axis=1
    )
    moe_pack = jnp.concatenate([jnp.concatenate([w_gate, w_up], axis=2), w_down], axis=1)
    chosen_t = jnp.any(
        routes.T[:, None, :] == jnp.arange(E, dtype=jnp.int32)[None, :, None], axis=0
    ).astype(F32)
    weights, moe_part, stream_pair, chosen_all = opening(pack, moe_pack, stream, chosen_t, depth)
    grad_plane = lax.all_gather(out_grad, ("inner", "seq"), axis=0, tiled=False)
    moe_w = lax.all_gather(moe_part, "outer", axis=0, tiled=True)
    weights = weights.reshape(WIDTH, PACK)
    extra_w = weights[:, QKV : QKV + EXTRA]
    gains = extra_w[:, :2].astype(F32).T
    gain_a, gain_f = gains[0:1], gains[1:2]
    router_w = extra_w[:, 2 : 2 + E]
    qkv_w = weights[:, :QKV]
    out_w = weights[:, QKV + EXTRA :]

    pair_index = shard * SEQ * tokens + jnp.arange(SEQ * tokens, dtype=jnp.int32)
    position = pair_index - document_first(pair_index, doc_starts)
    freq = ROPE_BASE ** (-(jnp.arange(HEAD // 2, dtype=F32) * 2.0) / HEAD)
    angle = position.astype(F32)[:, None] * freq[None, :]
    cos_half, sin_half = jnp.cos(angle), jnp.sin(angle)
    cosine = jnp.concatenate([cos_half, cos_half], axis=1)
    sine = jnp.concatenate([-sin_half, sin_half], axis=1)

    pair = stream_pair.reshape(SEQ * tokens, WIDTH)
    h1, qkv = project(pair, gain_a, qkv_w, cosine, sine)
    even = lax.rem(shard, 2) == 0
    q_pair = qkv[:, :QCOLS].reshape(SEQ, tokens, QCOLS)
    q_low, q_high = pick(even, *(zig.move(q_pair[k], zig.rows[k]) for k in range(2)))
    q = jnp.stack([q_low, q_high])
    kv = gather_keys(qkv[:, QCOLS:], depth).reshape(shards * SEQ * tokens, 2 * HEAD)

    block_ids = jnp.stack([shard, 2 * shards - 1 - shard]).astype(jnp.int32)
    query_index = block_ids[:, None] * tokens + jnp.arange(tokens, dtype=jnp.int32)[None, :]
    lo = document_first(query_index, doc_starts).astype(jnp.int32)
    info = jnp.concatenate([block_ids, lo[:, 0], lo[:, -1], jnp.zeros((2,), jnp.int32)])
    lo = lo[:, None, :]
    ob, top, total = attend_forward(q, kv, lo, info)

    head_zero = y == 0
    ob_a, ob_b = pick(head_zero, ob[0], ob[1])
    low_half = own_block < shards
    half_0, half_1 = pick(
        low_half, zig.move(ob_a, zig.heads[0]), zig.move(ob_b, zig.heads[1])
    )
    mixed = jnp.concatenate([half_0, half_1], axis=1)
    x1 = stream.astype(F32) + dot(mixed, out_w)
    normed, scale = rms_parts(x1)
    h2 = (normed * gain_f).astype(BF)
    h2_plane = gather_plane(h2, depth, 3)

    mixture_part, back_part, moe_grads = experts(
        h2_plane, grad_plane, chosen_all, router_w, moe_w, rows_in, rows_out, me
    )
    back = scatter_plane(back_part, depth)
    mixture = lax.psum_scatter(mixture_part, ("inner", "seq"), scatter_dimension=0, tiled=False)
    moe_own = lax.psum_scatter(
        moe_grads.reshape(depth, INNER, rows_in + rows_out, WIDTH),
        "outer",
        scatter_dimension=0,
        tiled=False,
    )
    result = (x1 + mixture.astype(F32)).astype(BF)

    chosen = chosen_t.T
    probs = jax.nn.softmax(dot(h2, router_w), axis=-1)
    dp = back[:, WIDTH : WIDTH + E] * chosen
    dz = (probs * (dp - jnp.sum(dp * probs, axis=-1, keepdims=True))).astype(BF)
    router_part = dot(h2, dz, TN)
    dh2 = back[:, :WIDTH] + dot(dz, router_w, NT)
    grad_f = out_grad.astype(F32)
    dx1 = grad_f + rms_pull(normed, scale, dh2, gain_f)
    gain_f_part = jnp.sum(dh2 * normed, axis=0)
    dx1_low = dx1.astype(BF)
    out_part = dot(mixed, dx1_low, TN)
    dob = dot(dx1_low, out_w, NT).astype(BF)

    dob_a, dob_b = pick(low_half, dob[:, :QCOLS], dob[:, QCOLS:])
    dob_low, dob_high = pick(
        head_zero,
        zig.move(dob_a, zig.heads[0], True),
        zig.move(dob_b, zig.heads[1], True),
    )
    dob_zig = jnp.stack([dob_low, dob_high])
    dq, dkv_part = attend_backward(q, kv, lo, info, top, total, dob_zig, ob)
    dq_a, dq_b = pick(even, dq[0], dq[1])
    dq_pair = jnp.concatenate(
        [zig.move(dq_a, zig.rows[0], True), zig.move(dq_b, zig.rows[1], True)], axis=0
    )
    dkv = scatter_keys(dkv_part.reshape(shards, SEQ * tokens, 2 * HEAD), depth)
    raw = unturn(dq_pair, dkv, cosine, sine)
    qkv_part = dot(h1, raw, TN)
    dh1 = dot(raw, qkv_w, NT)

    normed_pair, scale_pair = rms_parts(pair.astype(F32))
    gain_a_part = jnp.sum(dh1 * normed_pair, axis=0)
    dh1 = dh1.reshape(SEQ, tokens, WIDTH)
    mine, other = pick(head_zero, dh1[0], dh1[1])
    theirs = lax.ppermute(other.astype(BF), "seq", [(0, 1), (1, 0)])
    normed_s, scale_s = rms_parts(stream.astype(F32))
    stream_grad = (
        dx1 + rms_pull(normed_s, scale_s, mine + theirs.astype(F32), gain_a)
    ).astype(BF)

    small = jnp.concatenate(
        [
            gain_a_part[:, None],
            gain_f_part[:, None],
            router_part,
            jnp.zeros((WIDTH, EXTRA - 2 - E), F32),
        ],
        axis=1,
    )
    dense = jnp.concatenate([qkv_part, small, out_part], axis=1).astype(BF)
    own, peer, moe_out = closing(dense.reshape(shards, rows_in, PACK), moe_own, depth)
    peer = peer.astype(F32)

    def halves(a, b):
        return jnp.concatenate(
            pick(head_zero, own[:, a:b], peer[:, a:b]), axis=1
        )

    both = own[:, QKV:] + peer[:, QKV:]
    moe_out = moe_out.astype(F32)
    return (
        result,
        stream_grad,
        both[:, 0],
        halves(0, QCOLS),
        halves(QCOLS, QCOLS + HEAD),
        halves(QCOLS + HEAD, QKV),
        both[:, EXTRA:],
        both[:, 1],
        both[:, 2 : 2 + E],
        moe_out[:, :rows_in, :FF],
        moe_out[:, :rows_in, FF:],
        moe_out[:, rows_in:, :],
    )


def solution(mesh):
    shards = mesh.shape["shard"]
    depth = shards // INNER
    fine = Mesh(mesh.devices.reshape(depth, INNER, SEQ), AXES)
    shard = ("outer", "inner")
    tokens = P(AXES, None)
    in_specs = (
        tokens,
        P(),
        tokens,
        P(shard),
        P(shard, None),
        P(shard, None),
        P(shard, None),
        P(shard, None),
        P(shard),
        P(shard, None),
        P(None, shard, None),
        P(None, shard, None),
        P(None, shard, None),
        tokens,
    )
    out_specs = (
        tokens,
        tokens,
        P(shard),
        P(shard, None),
        P(shard, None),
        P(shard, None),
        P(shard, None),
        P(shard),
        P(shard, None),
        P(None, shard, None),
        P(None, shard, None),
        P(None, shard, None),
    )

    def run(*args):
        return local(depth, *args)

    return jax.shard_map(run, mesh=fine, in_specs=in_specs, out_specs=out_specs, check_vma=False)
```

```python
import jax
import jax.numpy as jnp
from jax import lax
from jax.experimental import pallas as pl
from jax.experimental.pallas import tpu as pltpu
from jax.sharding import Mesh, PartitionSpec as P

WIDTH = 1536
HEADS = 12
KV_HEADS = 2
HEAD = 128
FF = 768
E = 8
MOST = 192
SEQ = KV_HEADS
GROUP = HEADS // KV_HEADS
INNER = E // SEQ
QCOLS = GROUP * HEAD
QKV = QCOLS + 2 * HEAD
EXTRA = 128
FIRST = QKV + EXTRA
PACK = QKV + EXTRA + WIDTH
EPS = 1e-06
ROPE_BASE = 10000.0
SCALE = HEAD**-0.5
LOG2E = 1.4426950408889634
LN2 = 0.6931471805599453
NEG = -1e30
AXES = ("outer", "inner", "seq")
MESH = pl.DeviceIdType.MESH
NN = (((1,), (0,)), ((), ()))
NT = (((1,), (1,)), ((), ()))
TN = (((0,), (0,)), ((), ()))
BF = jnp.bfloat16
F32 = jnp.float32


def dot(a, b, dims=NN):
    return lax.dot_general(a, b, dims, preferred_element_type=F32)


class Net:
    def __init__(self, depth):
        self.depth = depth
        self.z = lax.axis_index("outer")
        self.i = lax.axis_index("inner")
        self.y = lax.axis_index("seq")
        self.core = lax.rem(self.i, 2)
        self.x = lax.div(self.i, 2)
        self.xp = self.dev(i=lax.rem(self.i + 2, INNER))
        self.cp = self.dev(i=self.i + 1 - 2 * self.core)
        self.yp = self.dev(y=1 - self.y)

    def dev(self, z=None, i=None, y=None):
        return {
            "outer": self.z if z is None else z,
            "inner": self.i if i is None else i,
            "seq": self.y if y is None else y,
        }

    def zoff(self, dz):
        return lax.rem(self.z + dz, self.depth)

    def zpeers(self):
        return [self.dev(z=self.zoff(dz)) for dz in range(1, self.depth)]

    def plane(self):
        out = []
        for di in range(INNER):
            for dy in range(SEQ):
                if di or dy:
                    out.append(
                        self.dev(i=lax.rem(self.i + di, INNER), y=lax.rem(self.y + dy, SEQ))
                    )
        return out


def greet(devices):
    barrier = pltpu.get_barrier_semaphore()
    for device in devices:
        pl.semaphore_signal(barrier, inc=1, device_id=device, device_id_type=MESH)
    pl.semaphore_wait(barrier, len(devices))


def remote(src, dst, ssem, rsem, device):
    return pltpu.make_async_remote_copy(
        src_ref=src, dst_ref=dst, send_sem=ssem, recv_sem=rsem, device_id=device, device_id_type=MESH
    )


class Sends:
    def __init__(self):
        self.items = []

    def start(self, *refs):
        self.later(lambda: refs)

    def later(self, refs):
        remote(*refs()).start()
        self.items.append(refs)

    def finish(self):
        for refs in self.items:
            remote(*refs()).wait_send()


def arrived(dst, ssem, rsem, device):
    remote(dst, dst, ssem, rsem, device).wait_recv()


def dma_sems(*counts):
    return [pltpu.SemaphoreType.DMA((n,)) for n in counts]


class FlatSlots:
    class At:
        def __init__(self, ref, rows):
            self.ref, self.rows = ref, rows

        def __getitem__(self, n):
            return self.ref.at[pl.ds(pl.multiple_of(n * self.rows, self.rows), self.rows)]

    def __init__(self, ref, rows):
        self.at = self.At(ref, rows)


class ShardGather:
    def __init__(self, net, sends, src, out, sems):
        self.net, self.sends, self.src, self.out = net, sends, src, out
        self.sz, self.rz, self.sx, self.rx, self.sc, self.rc = sems
        self.xi = lax.rem(net.i + 2, INNER)

    @staticmethod
    def sems(depth):
        return dma_sems(*([max(depth - 1, 1)] * 2 + [depth] * 2 + [2 * depth] * 2))

    def slot(self, dz, i):
        return self.out.at[lax.rem(self.net.z - dz + self.net.depth, self.net.depth) * INNER + i]

    def begin(self):
        net, me = self.net, self.slot(0, self.net.i)
        for n, device in enumerate(net.zpeers()):
            self.sends.start(self.src, me, self.sz.at[n], self.rz.at[n], device)
        self.sends.start(self.src, me, self.sx.at[0], self.rx.at[0], net.xp)
        self.sends.start(self.src, me, self.sc.at[0], self.rc.at[0], net.cp)

    def pass_on(self, dz, i, ssem, rsem, n, device):
        self.sends.later(
            lambda: (self.slot(dz, i), self.slot(dz, i), ssem.at[n], rsem.at[n], device)
        )

    def after_z(self):
        net = self.net
        for dz in range(1, net.depth):
            block = self.slot(dz, net.i)
            arrived(block, self.sz.at[dz - 1], self.rz.at[dz - 1], net.xp)
            self.pass_on(dz, net.i, self.sx, self.rx, dz, net.xp)
            self.pass_on(dz, net.i, self.sc, self.rc, dz, net.cp)

    def after_x(self):
        net, depth = self.net, self.net.depth
        for dz in range(depth):
            arrived(self.slot(dz, self.xi), self.sx.at[dz], self.rx.at[dz], net.xp)
            self.pass_on(dz, self.xi, self.sc, self.rc, depth + dz, net.cp)

    def last(self):
        net, depth = self.net, self.net.depth
        ci = net.i + 1 - 2 * net.core
        for dz in range(depth):
            arrived(self.slot(dz, ci), self.sc.at[dz], self.rc.at[dz], net.cp)
        for dz in range(depth):
            arrived(
                self.slot(dz, lax.rem(ci + 2, INNER)),
                self.sc.at[depth + dz],
                self.rc.at[depth + dz],
                net.cp,
            )

    def end(self):
        self.after_z()
        self.after_x()
        self.last()

    def one_x(self, dz):
        net, block, n = self.net, self.slot(dz, self.xi), self.net.depth + dz
        arrived(block, self.sx.at[dz], self.rx.at[dz], net.xp)
        remote(block, block, self.sc.at[n], self.rc.at[n], net.cp).start()

    def one_c(self, n, place):
        block = self.out.at[place]
        arrived(block, self.sc.at[n], self.rc.at[n], self.net.cp)

    def sent_loop(self):
        net, depth = self.net, self.net.depth
        for dz in range(depth):
            block = self.slot(dz, self.xi)
            remote(block, block, self.sc.at[depth + dz], self.rc.at[depth + dz], net.cp).wait_send()


def hbm():
    return pl.BlockSpec(memory_space=pltpu.HBM)


def vmem():
    return pl.BlockSpec(memory_space=pltpu.VMEM)


def smem():
    return pl.BlockSpec(memory_space=pltpu.SMEM)


def comm_params(cid, limit=56 << 20):
    return pltpu.CompilerParams(
        collective_id=cid, has_side_effects=True, vmem_limit_bytes=limit
    )


def opening(pack, moe, stream, chosen, depth):
    rows = pack.shape[0]

    def kernel(pack_ref, moe_ref, st_ref, ch_ref, pack_out, moe_out, st_out, ch_out, *sems):
        net = Net(depth)
        sends = Sends()
        gather = ShardGather(net, sends, pack_ref, pack_out, sems[:6])
        sm, rm, sy, ry, sp, rp, own = sems[6:]
        locals_ = [
            pltpu.make_async_copy(pack_ref, gather.slot(0, net.i), own.at[0]),
            pltpu.make_async_copy(moe_ref.at[net.i * SEQ + net.y], moe_out.at[net.i], own.at[1]),
            pltpu.make_async_copy(st_ref, st_out.at[net.y], own.at[2]),
            pltpu.make_async_copy(ch_ref, ch_out.at[net.i * SEQ + net.y], own.at[3]),
        ]
        greet(net.zpeers() + net.plane())
        gather.begin()
        sends.start(st_ref, st_out.at[net.y], sy.at[0], ry.at[0], net.yp)
        for n, device in enumerate(net.plane()):
            sends.start(ch_ref, ch_out.at[net.i * SEQ + net.y], sp.at[n], rp.at[n], device)
        for di in range(1, INNER):
            other = lax.rem(net.i + di, INNER)
            sends.start(
                moe_ref.at[other * SEQ + net.y],
                moe_out.at[net.i],
                sm.at[di - 1],
                rm.at[di - 1],
                net.dev(i=other),
            )
        for copy in locals_:
            copy.start()
        gather.end()
        arrived(st_out.at[1 - net.y], sy.at[0], ry.at[0], net.yp)
        n = 0
        for di in range(INNER):
            for dy in range(SEQ):
                if di or dy:
                    frm = lax.rem(net.i - di + INNER, INNER) * SEQ + lax.rem(net.y + dy, SEQ)
                    arrived(ch_out.at[frm], sp.at[n], rp.at[n], net.yp)
                    n += 1
        for di in range(1, INNER):
            frm = lax.rem(net.i - di + INNER, INNER)
            arrived(moe_out.at[frm], sm.at[di - 1], rm.at[di - 1], net.yp)
        sends.finish()
        for copy in locals_:
            copy.wait()

    return pl.pallas_call(
        kernel,
        out_shape=(
            jax.ShapeDtypeStruct((depth * INNER,) + pack.shape, BF),
            jax.ShapeDtypeStruct((INNER,) + moe.shape[1:], BF),
            jax.ShapeDtypeStruct((SEQ,) + stream.shape, BF),
            jax.ShapeDtypeStruct((E,) + chosen.shape, F32),
        ),
        in_specs=[hbm()] * 4,
        out_specs=(hbm(),) * 4,
        scratch_shapes=ShardGather.sems(depth) + dma_sems(3, 3, 1, 1, E - 1, E - 1, 4),
        compiler_params=comm_params(1),
        name="opening",
    )(pack, moe, stream, chosen)


def gather_keys(kv, depth):
    def kernel(src, out, *sems):
        net = Net(depth)
        sends = Sends()
        gather = ShardGather(net, sends, src, out, sems[:6])
        own = pltpu.make_async_copy(src, gather.slot(0, net.i), sems[6].at[0])
        greet(net.zpeers() + [net.xp, net.cp])
        gather.begin()
        own.start()
        gather.end()
        sends.finish()
        own.wait()

    return pl.pallas_call(
        kernel,
        out_shape=jax.ShapeDtypeStruct((depth * INNER,) + kv.shape, BF),
        in_specs=[hbm()],
        out_specs=hbm(),
        scratch_shapes=ShardGather.sems(depth) + dma_sems(1),
        compiler_params=comm_params(2),
        name="gather_keys",
    )(kv)


def gather_plane(rows, depth, cid):
    half = rows.shape[0] // 2

    def kernel(src, out, sx, rx, sy, ry, sc, rc, own):
        net = Net(depth)
        sends = Sends()

        def place(i, y):
            return i * SEQ + y

        xi = lax.rem(net.i + 2, INNER)
        me, xb = place(net.i, net.y), place(xi, net.y)
        yb, db = place(net.i, 1 - net.y), place(xi, 1 - net.y)
        lo, hi = pl.ds(0, half), pl.ds(half, half)
        mine = pltpu.make_async_copy(src, out.at[me], own.at[0])
        greet([net.xp, net.yp, net.cp])
        sends.start(src, out.at[me], sx.at[0], rx.at[0], net.xp)
        sends.start(src, out.at[me], sy.at[0], ry.at[0], net.yp)
        sends.start(src, out.at[me], sc.at[0], rc.at[0], net.cp)
        mine.start()
        arrived(out.at[yb], sy.at[0], ry.at[0], net.yp)
        sends.start(out.at[yb, lo], out.at[yb, lo], sx.at[1], rx.at[1], net.xp)
        sends.start(out.at[yb], out.at[yb], sc.at[1], rc.at[1], net.cp)
        arrived(out.at[xb], sx.at[0], rx.at[0], net.xp)
        sends.start(out.at[xb, hi], out.at[xb, hi], sy.at[1], ry.at[1], net.yp)
        sends.start(out.at[xb], out.at[xb], sc.at[2], rc.at[2], net.cp)
        arrived(out.at[db, lo], sx.at[1], rx.at[1], net.xp)
        sends.start(out.at[db, lo], out.at[db, lo], sc.at[3], rc.at[3], net.cp)
        arrived(out.at[db, hi], sy.at[1], ry.at[1], net.yp)
        sends.start(out.at[db, hi], out.at[db, hi], sc.at[4], rc.at[4], net.cp)
        ci = net.i + 1 - 2 * net.core
        cx = lax.rem(ci + 2, INNER)
        arrived(out.at[place(ci, net.y)], sc.at[0], rc.at[0], net.cp)
        arrived(out.at[place(ci, 1 - net.y)], sc.at[1], rc.at[1], net.cp)
        arrived(out.at[place(cx, net.y)], sc.at[2], rc.at[2], net.cp)
        arrived(out.at[place(cx, 1 - net.y), lo], sc.at[3], rc.at[3], net.cp)
        arrived(out.at[place(cx, 1 - net.y), hi], sc.at[4], rc.at[4], net.cp)
        sends.finish()
        mine.wait()

    return pl.pallas_call(
        kernel,
        out_shape=jax.ShapeDtypeStruct((E,) + rows.shape, BF),
        in_specs=[hbm()],
        out_specs=hbm(),
        scratch_shapes=dma_sems(2, 2, 2, 2, 5, 5, 1),
        compiler_params=comm_params(cid),
        name="gather_plane",
    )(rows)


def add_into(dst, sources, rows, chunk):
    def body(n, carry):
        at = pl.ds(pl.multiple_of(n * chunk, chunk), chunk)
        total = sources[0][at, :].astype(F32)
        for source in sources[1:]:
            total = total + source[at, :].astype(F32)
        dst[at, :] = total.astype(dst.dtype)
        return carry

    lax.fori_loop(0, rows // chunk, body, 0)


def chunk_of(rows):
    for size in (32, 16, 8):
        if rows % size == 0:
            return size
    return rows


def scatter_plane(part, depth):
    rows, cols = part.shape[1:]
    half = rows // 2

    def kernel(part_ref, out, bc, mid, bx, by, second, b2, ssem, rsem):
        net = Net(depth)
        sends = Sends()

        def place(fx, fy, core):
            x = 1 - net.x if fx else net.x
            y = 1 - net.y if fy else net.y
            return (x * 2 + core) * SEQ + y

        greet([net.xp, net.yp, net.cp])
        order = ((1, 1), (1, 0), (0, 1), (0, 0))
        for n, (fx, fy) in enumerate(order):
            sends.start(
                part_ref.at[place(fx, fy, 1 - net.core)], bc.at[n], ssem.at[n], rsem.at[n], net.cp
            )
        ch = chunk_of(half)
        lo, hi = pl.ds(0, half), pl.ds(half, half)
        for n, (fx, fy) in enumerate(order):
            arrived(bc.at[n], ssem.at[n], rsem.at[n], net.cp)
            add_into(mid.at[n], [part_ref.at[place(fx, fy, net.core)], bc.at[n]], rows, ch)
            if n == 0:
                sends.start(mid.at[0, lo], bx.at[0], ssem.at[4], rsem.at[4], net.xp)
                sends.start(mid.at[0, hi], by.at[0], ssem.at[5], rsem.at[5], net.yp)
            if n == 1:
                sends.start(mid.at[1, lo], bx.at[1], ssem.at[6], rsem.at[6], net.xp)
            if n == 2:
                sends.start(mid.at[2, hi], by.at[1], ssem.at[7], rsem.at[7], net.yp)
        arrived(bx.at[0], ssem.at[4], rsem.at[4], net.xp)
        add_into(second.at[0], [mid.at[2, lo], bx.at[0]], half, ch)
        sends.start(second.at[0], b2.at[0], ssem.at[8], rsem.at[8], net.yp)
        arrived(by.at[0], ssem.at[5], rsem.at[5], net.yp)
        add_into(second.at[1], [mid.at[1, hi], by.at[0]], half, ch)
        sends.start(second.at[1], b2.at[1], ssem.at[9], rsem.at[9], net.xp)
        arrived(bx.at[1], ssem.at[6], rsem.at[6], net.xp)
        arrived(by.at[1], ssem.at[7], rsem.at[7], net.yp)
        arrived(b2.at[0], ssem.at[8], rsem.at[8], net.yp)
        add_into(out.at[lo], [mid.at[3, lo], bx.at[1], b2.at[0]], half, ch)
        arrived(b2.at[1], ssem.at[9], rsem.at[9], net.xp)
        add_into(out.at[hi], [mid.at[3, hi], by.at[1], b2.at[1]], half, ch)
        sends.finish()

    return pl.pallas_call(
        kernel,
        out_shape=jax.ShapeDtypeStruct((rows, cols), F32),
        in_specs=[vmem()],
        out_specs=vmem(),
        scratch_shapes=[pltpu.VMEM((4, rows, cols), BF)] * 2
        + [pltpu.VMEM((2, half, cols), BF)] * 4
        + dma_sems(10, 10),
        compiler_params=comm_params(4),
        name="scatter_plane",
    )(part)


class ShardScatter:
    @staticmethod
    def scratch(depth, rows, cols):
        far = max(depth - 1, 1)
        shapes = [(2 * depth, rows, cols)] + [(depth, rows, cols)] * 2 + [(far, rows, cols)] * 2
        return [pltpu.VMEM(s, BF) for s in shapes] + dma_sems(
            2 * depth, 2 * depth, depth, depth, far, far
        )

    def __init__(self, net, sends, part, scratch):
        self.net, self.sends, self.part = net, sends, part
        self.bc, self.sx, self.bx, self.sz, self.bz = scratch[:5]
        self.ssc, self.rsc, self.ssx, self.rsx, self.ssz, self.rsz = scratch[5:]
        depth = net.depth
        self.order = sorted(range(1, depth), key=lambda d: -min(d, depth - d)) + [0]
        self.rows = part.shape[1]
        self.chunk = chunk_of(self.rows)

    def block(self, dz, fx, core):
        x = 1 - self.net.x if fx else self.net.x
        return self.part.at[self.net.zoff(dz) * INNER + x * 2 + core]

    def begin(self):
        net = self.net
        for dz in self.order:
            for fx in (1, 0):
                n = dz * 2 + fx
                self.sends.start(
                    self.block(dz, fx, 1 - net.core),
                    self.bc.at[n],
                    self.ssc.at[n],
                    self.rsc.at[n],
                    net.cp,
                )

    def end(self, out):
        net, sends = self.net, self.sends
        for dz in self.order:
            n = dz * 2 + 1
            arrived(self.bc.at[n], self.ssc.at[n], self.rsc.at[n], net.cp)
            add_into(
                self.sx.at[dz], [self.block(dz, 1, net.core), self.bc.at[n]], self.rows, self.chunk
            )
            sends.start(self.sx.at[dz], self.bx.at[dz], self.ssx.at[dz], self.rsx.at[dz], net.xp)
        for dz in self.order:
            n = dz * 2
            arrived(self.bc.at[n], self.ssc.at[n], self.rsc.at[n], net.cp)
            arrived(self.bx.at[dz], self.ssx.at[dz], self.rsx.at[dz], net.xp)
            terms = [self.block(dz, 0, net.core), self.bc.at[n], self.bx.at[dz]]
            if dz:
                add_into(self.sz.at[dz - 1], terms, self.rows, self.chunk)
                sends.start(
                    self.sz.at[dz - 1],
                    self.bz.at[dz - 1],
                    self.ssz.at[dz - 1],
                    self.rsz.at[dz - 1],
                    net.dev(z=net.zoff(dz)),
                )
            else:
                for far in range(net.depth - 1):
                    arrived(self.bz.at[far], self.ssz.at[far], self.rsz.at[far], net.xp)
                    terms.append(self.bz.at[far])
                add_into(out, terms, self.rows, self.chunk)


def scatter_keys(part, depth):
    rows, cols = part.shape[1:]

    def kernel(part_ref, out, *scratch):
        net = Net(depth)
        sends = Sends()
        greet(net.zpeers() + [net.xp, net.cp])
        work = ShardScatter(net, sends, part_ref, scratch)
        work.begin()
        work.end(out)
        sends.finish()

    return pl.pallas_call(
        kernel,
        out_shape=jax.ShapeDtypeStruct((rows, cols), F32),
        in_specs=[vmem()],
        out_specs=vmem(),
        scratch_shapes=ShardScatter.scratch(depth, rows, cols),
        compiler_params=comm_params(5),
        name="scatter_keys",
    )(part)


def closing(part, moe, depth):
    rows, cols = part.shape[1:]

    def kernel(part_ref, moe_ref, own_out, pair_out, moe_out, low, sm, rm, sy, ry, ls, *scratch):
        net = Net(depth)
        sends = Sends()
        me = net.i * SEQ + net.y
        mine = pltpu.make_async_copy(moe_ref.at[net.i], moe_out.at[me], ls.at[0])
        greet(net.zpeers() + net.plane())
        work = ShardScatter(net, sends, part_ref, scratch)
        work.begin()
        n = 0
        for di in range(INNER):
            for dy in range(SEQ):
                if di or dy:
                    i = lax.rem(net.i + di, INNER)
                    device = net.dev(i=i, y=lax.rem(net.y + dy, SEQ))
                    sends.start(moe_ref.at[i], moe_out.at[me], sm.at[n], rm.at[n], device)
                    n += 1
        mine.start()
        work.end(own_out)
        low[...] = own_out[...].astype(BF)
        sends.start(low, pair_out, sy.at[0], ry.at[0], net.yp)
        n = 0
        for di in range(INNER):
            for dy in range(SEQ):
                if di or dy:
                    frm = lax.rem(net.i - di + INNER, INNER) * SEQ + lax.rem(net.y + dy, SEQ)
                    arrived(moe_out.at[frm], sm.at[n], rm.at[n], net.yp)
                    n += 1
        arrived(pair_out, sy.at[0], ry.at[0], net.yp)
        sends.finish()
        mine.wait()

    return pl.pallas_call(
        kernel,
        out_shape=(
            jax.ShapeDtypeStruct((rows, cols), F32),
            jax.ShapeDtypeStruct((rows, cols), BF),
            jax.ShapeDtypeStruct((E,) + moe.shape[1:], BF),
        ),
        in_specs=[vmem(), hbm()],
        out_specs=(vmem(), vmem(), hbm()),
        scratch_shapes=[pltpu.VMEM((rows, cols), BF)]
        + dma_sems(E - 1, E - 1, 1, 1, 1)
        + ShardScatter.scratch(depth, rows, cols),
        compiler_params=comm_params(6),
        name="closing",
    )(part, moe)


def turn(values, cosine, sine):
    return values * cosine + pltpu.roll(values, HEAD // 2, 1) * sine


def project(stream, gain, weights, cosine, sine):
    rows = stream.shape[0]
    wide = 2 * HEAD

    def kernel(s_ref, g_ref, w_ref, c_ref, n_ref, h_ref, o_ref):
        n = pl.program_id(0)

        @pl.when(n == 0)
        def _():
            x = s_ref[...].astype(F32)
            scale = lax.rsqrt(jnp.mean(x * x, axis=-1, keepdims=True) + EPS)
            h_ref[...] = (x * scale * g_ref[...]).astype(BF)

        r = dot(h_ref[...], w_ref[...])
        first = turn(r[:, :HEAD], c_ref[...], n_ref[...])

        @pl.when(n < 3)
        def _():
            o_ref[:, :HEAD] = (first * (SCALE * LOG2E)).astype(BF)
            second = turn(r[:, HEAD:], c_ref[...], n_ref[...])
            o_ref[:, HEAD:] = (second * (SCALE * LOG2E)).astype(BF)

        @pl.when(n == 3)
        def _():
            o_ref[:, :HEAD] = first.astype(BF)
            o_ref[:, HEAD:] = r[:, HEAD:].astype(BF)

    fixed = lambda shape: pl.BlockSpec(shape, lambda n: (0, 0))
    return pl.pallas_call(
        kernel,
        grid=(QKV // wide,),
        in_specs=[
            fixed((rows, WIDTH)),
            fixed((1, WIDTH)),
            pl.BlockSpec((WIDTH, wide), lambda n: (0, n)),
            fixed((rows, HEAD)),
            fixed((rows, HEAD)),
        ],
        out_specs=(fixed((rows, WIDTH)), pl.BlockSpec((rows, wide), lambda n: (0, n))),
        out_shape=(
            jax.ShapeDtypeStruct((rows, WIDTH), BF),
            jax.ShapeDtypeStruct((rows, QKV), BF),
        ),
        compiler_params=pltpu.CompilerParams(vmem_limit_bytes=32 << 20),
        name="project",
    )(stream, gain, weights, cosine, sine)


def unturn(dq, dkv, cosine, sine):
    rows = dq.shape[0]

    def kernel(dq_ref, dkv_ref, c_ref, n_ref, o_ref):
        c, s = c_ref[...], -n_ref[...]
        for h in range(GROUP):
            at = slice(h * HEAD, (h + 1) * HEAD)
            o_ref[:, at] = turn(dq_ref[:, at].astype(F32), c, s).astype(BF)
        dk = dkv_ref[:, :HEAD].astype(BF).astype(F32)
        o_ref[:, QCOLS : QCOLS + HEAD] = turn(dk, c, s).astype(BF)
        o_ref[:, QCOLS + HEAD :] = dkv_ref[:, HEAD:].astype(BF)

    return pl.pallas_call(
        kernel,
        in_specs=[vmem()] * 4,
        out_specs=vmem(),
        out_shape=jax.ShapeDtypeStruct((rows, QKV), BF),
        compiler_params=pltpu.CompilerParams(vmem_limit_bytes=32 << 20),
        name="unturn",
    )(dq, dkv, cosine, sine)


def attend_forward(q, kv, lo, info, tile=512):
    block = q.shape[1]

    def kernel(info_ref, q_ref, kv_ref, lo_ref, o_ref, m_ref, l_ref, acc, top, total):
        for j in range(2):
            base = info_ref[j] * block
            first = info_ref[2 + j] // tile
            last = (base + block - 1) // tile
            acc[...] = jnp.zeros_like(acc)
            top[...] = jnp.full_like(top, NEG)
            total[...] = jnp.zeros_like(total)

            def step(t, masked):
                start = pl.multiple_of(t * tile, tile)
                k = kv_ref[pl.ds(start, tile), :HEAD]
                vt = kv_ref[pl.ds(start, tile), HEAD:].T
                if masked:
                    key = start + lax.broadcasted_iota(jnp.int32, (tile, block), 0)
                    query = base + lax.broadcasted_iota(jnp.int32, (tile, block), 1)
                    ok = (key <= query) & (key >= lo_ref[j])
                for h in range(GROUP):
                    s = dot(k, q_ref[j, :, h * HEAD : (h + 1) * HEAD], NT)
                    if masked:
                        s = jnp.where(ok, s, NEG)
                    m0 = top[h : h + 1, :]
                    m1 = jnp.maximum(m0, jnp.max(s, axis=0, keepdims=True))
                    p = jnp.exp2(s - m1)
                    f = jnp.exp2(m0 - m1)
                    top[h : h + 1, :] = m1
                    total[h : h + 1, :] = total[h : h + 1, :] * f + jnp.sum(
                        p, axis=0, keepdims=True
                    )
                    acc[h] = acc[h] * f + dot(vt, p.astype(BF))

            free_from = jnp.minimum((info_ref[4 + j] + tile - 1) // tile, last + 1)
            free_to = jnp.maximum(base // tile, free_from)

            def run(a, b, masked):
                lax.fori_loop(a, b, lambda t, c: (step(t, masked), c)[1], 0)

            run(first, free_from, True)
            run(free_from, free_to, False)
            run(jnp.maximum(free_to, first), last + 1, True)
            for h in range(GROUP):
                o_ref[j, :, h * HEAD : (h + 1) * HEAD] = (
                    (acc[h] / total[h : h + 1, :]).T.astype(BF)
                )
            m_ref[j] = top[...]
            l_ref[j] = total[...]

    stat = jax.ShapeDtypeStruct((2, 8, block), F32)
    return pl.pallas_call(
        kernel,
        out_shape=(jax.ShapeDtypeStruct(q.shape, BF), stat, stat),
        in_specs=[smem()] + [vmem()] * 3,
        out_specs=(vmem(),) * 3,
        scratch_shapes=[
            pltpu.VMEM((GROUP, HEAD, block), F32),
            pltpu.VMEM((8, block), F32),
            pltpu.VMEM((8, block), F32),
        ],
        compiler_params=pltpu.CompilerParams(vmem_limit_bytes=48 << 20),
        cost_estimate=pl.CostEstimate(
            flops=int(1e10), bytes_accessed=6 << 20, transcendentals=13 << 20
        ),
        name="attend_forward",
    )(info, q, kv, lo)


def attend_backward(q, kv, lo, info, m, l, dob, ob, tile=512):
    block = q.shape[1]
    keys = kv.shape[0]
    tiles = keys // tile

    def kernel(info_ref, q_ref, kv_ref, lo_ref, m_ref, l_ref, do_ref, ob_ref, dq_ref, dkv_ref, da, dl, acc):
        acc[...] = jnp.zeros_like(acc)
        for j in range(2):
            for h in range(GROUP):
                c = slice(h * HEAD, (h + 1) * HEAD)
                d = do_ref[j, :, c].astype(F32)
                o = ob_ref[j, :, c].astype(F32)
                inv = 1.0 / l_ref[j, h : h + 1, :]
                da[j, h] = (d.T * inv).T.astype(BF)
                dl[j, h : h + 1, :] = -jnp.sum((d * o).T, axis=0, keepdims=True) * inv
        low = jnp.minimum(info_ref[2], info_ref[3]) // tile
        high = (info_ref[1] * block + block - 1) // tile

        def clear(t, carry):
            dkv_ref[pl.ds(pl.multiple_of(t * tile, tile), tile), :] = jnp.zeros((tile, 2 * HEAD), BF)
            return carry

        lax.fori_loop(0, low, clear, 0)
        lax.fori_loop(high + 1, tiles, clear, 0)

        def piece(t, j, masked):
            start = pl.multiple_of(t * tile, tile)
            base = info_ref[j] * block
            k = kv_ref[pl.ds(start, tile), :HEAD]
            v = kv_ref[pl.ds(start, tile), HEAD:]
            kt = k.T
            if masked:
                key = start + lax.broadcasted_iota(jnp.int32, (tile, block), 0)
                query = base + lax.broadcasted_iota(jnp.int32, (tile, block), 1)
                ok = (key <= query) & (key >= lo_ref[j])
            dk = dv = None
            for h in range(GROUP):
                qh = q_ref[j, :, h * HEAD : (h + 1) * HEAD]
                s = dot(k, qh, NT) - m_ref[j, h : h + 1, :]
                if masked:
                    s = jnp.where(ok, s, NEG)
                p = jnp.exp2(s)
                dah = da[j, h]
                dvh = dot(p.astype(BF), dah)
                dp = dot(v, dah, NT) + dl[j, h : h + 1, :]
                ds = (p * dp).astype(BF)
                dkh = dot(ds, qh)
                acc[j, h] += dot(kt, ds)
                dk = dkh if dk is None else dk + dkh
                dv = dvh if dv is None else dv + dvh
            return dk * LN2, dv

        def tile_step(t, carry):
            start = pl.multiple_of(t * tile, tile)
            rows = pl.ds(start, tile)

            def put(j, masked):
                dk, dv = piece(t, j, masked)
                if j == 0:
                    dk = dk + dkv_ref[rows, :HEAD].astype(F32)
                    dv = dv + dkv_ref[rows, HEAD:].astype(F32)
                dkv_ref[rows, :HEAD] = dk.astype(BF)
                dkv_ref[rows, HEAD:] = dv.astype(BF)

            for j in (1, 0):
                base = info_ref[j] * block
                live = (start <= base + block - 1) & (start + tile > info_ref[2 + j])
                free = (start + tile - 1 <= base) & (start >= info_ref[4 + j])
                if j == 1:

                    @pl.when(jnp.logical_not(live))
                    def _():
                        clear(t, 0)

                @pl.when(live & free)
                def _():
                    put(j, False)

                @pl.when(live & jnp.logical_not(free))
                def _():
                    put(j, True)

            return carry

        lax.fori_loop(low, high + 1, tile_step, 0)
        for j in range(2):
            for h in range(GROUP):
                dq_ref[j, :, h * HEAD : (h + 1) * HEAD] = (acc[j, h] * SCALE).T.astype(BF)

    return pl.pallas_call(
        kernel,
        out_shape=(jax.ShapeDtypeStruct(q.shape, BF), jax.ShapeDtypeStruct(kv.shape, BF)),
        in_specs=[smem()] + [vmem()] * 7,
        out_specs=(vmem(),) * 2,
        scratch_shapes=[
            pltpu.VMEM((2, GROUP, block, HEAD), BF),
            pltpu.VMEM((2, 8, block), F32),
            pltpu.VMEM((2, GROUP, HEAD, block), F32),
        ],
        compiler_params=pltpu.CompilerParams(vmem_limit_bytes=60 << 20),
        cost_estimate=pl.CostEstimate(
            flops=int(2.5e10), bytes_accessed=12 << 20, transcendentals=13 << 20
        ),
        name="attend_backward",
    )(info, q, kv, lo, m, l, dob, ob)


class PlaneGather:
    @staticmethod
    def sems():
        return dma_sems(2, 2, 2, 2, 5, 5)

    def __init__(self, net, sends, src, out, sems, rows):
        self.net, self.sends, self.src, self.out = net, sends, src, out
        self.sx, self.rx, self.sy, self.ry, self.sc, self.rc = sems
        half = rows // 2
        self.lo, self.hi = pl.ds(0, half), pl.ds(half, half)
        xi = lax.rem(net.i + 2, INNER)
        ci = net.i + 1 - 2 * net.core
        cx = lax.rem(ci + 2, INNER)
        place = lambda i, y: i * SEQ + y
        self.me, self.xb = place(net.i, net.y), place(xi, net.y)
        self.yb, self.db = place(net.i, 1 - net.y), place(xi, 1 - net.y)
        self.core_blocks = [place(ci, net.y), place(ci, 1 - net.y), place(cx, net.y)]
        self.core_diag = place(cx, 1 - net.y)

    def begin(self):
        self.begin_y()
        self.begin_x()

    def begin_y(self):
        net, out, src = self.net, self.out, self.src
        self.sends.start(src, out.at[self.me], self.sy.at[0], self.ry.at[0], net.yp)
        self.sends.start(src, out.at[self.me], self.sc.at[0], self.rc.at[0], net.cp)

    def begin_x(self):
        net, out, src = self.net, self.out, self.src
        self.sends.start(src, out.at[self.me], self.sx.at[0], self.rx.at[0], net.xp)

    def pass_on(self, block, part, ssem, rsem, n, device):
        def refs():
            at = self.out.at[block] if part is None else self.out.at[block, part]
            return at, at, ssem.at[n], rsem.at[n], device

        self.sends.later(refs)

    def middle(self):
        net, out = self.net, self.out
        arrived(out.at[self.yb], self.sy.at[0], self.ry.at[0], net.yp)
        self.pass_on(self.yb, self.lo, self.sx, self.rx, 1, net.xp)
        self.pass_on(self.yb, None, self.sc, self.rc, 1, net.cp)
        arrived(out.at[self.xb], self.sx.at[0], self.rx.at[0], net.xp)
        self.pass_on(self.xb, self.hi, self.sy, self.ry, 1, net.yp)
        self.pass_on(self.xb, None, self.sc, self.rc, 2, net.cp)

    def end(self):
        net, out = self.net, self.out
        arrived(out.at[self.db, self.lo], self.sx.at[1], self.rx.at[1], net.xp)
        self.pass_on(self.db, self.lo, self.sc, self.rc, 3, net.cp)
        arrived(out.at[self.db, self.hi], self.sy.at[1], self.ry.at[1], net.yp)
        self.pass_on(self.db, self.hi, self.sc, self.rc, 4, net.cp)

    def last(self):
        net, out = self.net, self.out
        for n, block in enumerate(self.core_blocks):
            arrived(out.at[block], self.sc.at[n], self.rc.at[n], net.cp)
        arrived(out.at[self.core_diag, self.lo], self.sc.at[3], self.rc.at[3], net.cp)
        arrived(out.at[self.core_diag, self.hi], self.sc.at[4], self.rc.at[4], net.cp)


class Route:
    def __init__(self, net, sends_to, comes_from):
        self.net = net
        me = net.z * INNER + net.i
        self.local = (sends_to[0] == me) & (sends_to[1] == net.y)
        self.kept = (comes_from[0] == me) & (comes_from[1] == net.y)
        self.to, self.frm = self.device(sends_to), self.device(comes_from)

    def device(self, place):
        shard, y = place
        return self.net.dev(z=lax.div(shard, INNER), i=lax.rem(shard, INNER), y=y)

    def hello(self):
        @pl.when(jnp.logical_not(self.kept))
        def _():
            pl.semaphore_signal(
                pltpu.get_barrier_semaphore(), inc=1, device_id=self.frm, device_id_type=MESH
            )

        return jnp.where(self.local, 0, 1)

    def send(self, refs):
        @pl.when(self.local)
        def _():
            src, dst, _, _ = refs()
            dst[...] = src[...]

        @pl.when(jnp.logical_not(self.local))
        def _():
            remote(*refs(), self.to).start()

    def sent(self, refs):
        @pl.when(jnp.logical_not(self.local))
        def _():
            remote(*refs(), self.to).wait_send()

    def arrive(self, refs):
        @pl.when(jnp.logical_not(self.kept))
        def _():
            dst, ssem, rsem = refs()
            remote(dst, dst, ssem, rsem, self.to).wait_recv()


class Mirror:
    def __init__(self, net):
        self.net = net
        self.n = net.depth * INNER
        self.last = 2 * self.n - 1
        self.me = net.z * INNER + net.i

    def home(self, block):
        return jnp.where(block < self.n, block, self.last - block)

    def blocks(self):
        return self.me, self.last - self.me

    def slot(self, block):
        return jnp.where(block < self.n, 0, 1)

    def rows_out(self, k):
        block = 2 * self.me + k
        come = self.blocks()[k]
        return Route(
            self.net, (self.home(block), self.net.y), (lax.div(come, 2), self.net.y)
        ), self.slot(block)

    def rows_back(self, k):
        block = self.blocks()[k]
        come = 2 * self.me + k
        return Route(
            self.net, (lax.div(block, 2), self.net.y), (self.home(come), self.net.y)
        ), lax.rem(block, 2)

    def heads_back(self, k):
        block = self.blocks()[k]
        own = 2 * self.me + self.net.y
        return Route(self.net, (lax.div(block, 2), lax.rem(block, 2)), (self.home(own), k))

    def heads_out(self, k):
        own = 2 * self.me + self.net.y
        come = self.blocks()[k]
        return Route(
            self.net, (self.home(own), k), (lax.div(come, 2), lax.rem(come, 2))
        ), self.slot(own)


class Chain:
    @staticmethod
    def sems(depth):
        return dma_sems(*[max(depth - 1, 1) * INNER] * 4)

    def __init__(self, net, out, sems):
        self.net, self.out = net, out
        self.su, self.ru, self.sd, self.rd = sems
        self.steps = (net.depth - 1) * INNER
        self.up = net.dev(z=jnp.minimum(net.z + 1, net.depth - 1))
        self.down = net.dev(z=jnp.maximum(net.z - 1, 0))

    def piece(self, z, q):
        return self.out.at[z * INNER + q]

    def refs(self, hop, q, way):
        net = self.net
        n = (hop + 1) * INNER + q
        z = net.z - 1 - hop if way == 0 else net.z + 1 + hop
        ssem, rsem, device = (
            (self.su.at[n], self.ru.at[n], self.up)
            if way == 0
            else (self.sd.at[n], self.rd.at[n], self.down)
        )
        return self.piece(z, q), ssem, rsem, device

    def begin(self, ready):
        def body(q, carry):
            ready(q)
            for way in range(2):

                @pl.when(self.net.z < self.net.depth - 1 if way == 0 else self.net.z > 0)
                def _():
                    dst, ssem, rsem, device = self.refs(-1, q, way)
                    remote(dst, dst, ssem, rsem, device).start()

            return carry

        lax.fori_loop(0, INNER, body, 0)

    def step(self, n):
        net = self.net
        hop, q = lax.div(n, INNER), lax.rem(n, INNER)
        for way in range(2):
            z = net.z - 1 - hop if way == 0 else net.z + 1 + hop
            here = z >= 0 if way == 0 else z <= net.depth - 1
            further = net.z < net.depth - 1 if way == 0 else net.z > 0

            @pl.when(here)
            def _():
                block = self.piece(z, q)
                if way == 0:
                    arrived(block, self.su.at[n], self.ru.at[n], self.up)
                else:
                    arrived(block, self.sd.at[n], self.rd.at[n], self.down)

            @pl.when(here & further)
            def _():
                dst, ssem, rsem, device = self.refs(hop, q, way)
                remote(dst, dst, ssem, rsem, device).start()

    def run(self, a, b):
        def body(n, carry):
            self.step(n)
            return carry

        lax.fori_loop(a, min(b, self.steps), body, 0)

    def finish(self):
        def body(n, carry):
            hop, q = lax.div(n, INNER) - 1, lax.rem(n, INNER)
            for way in range(2):
                z = self.net.z - 1 - hop if way == 0 else self.net.z + 1 + hop
                here = z >= 0 if way == 0 else z <= self.net.depth - 1
                further = self.net.z < self.net.depth - 1 if way == 0 else self.net.z > 0

                @pl.when(here & further)
                def _():
                    dst, ssem, rsem, device = self.refs(hop, q, way)
                    remote(dst, dst, ssem, rsem, device).wait_send()

            return carry

        lax.fori_loop(0, self.steps, body, 0)


def seg_tile(start, rows, st, en):
    key = start + lax.broadcasted_iota(jnp.int32, (rows, HEAD), 0)
    return ((key >= st) & (key < en)).astype(F32).astype(BF)


def front(stream, pack, moe, chosen, cosine, sine, w_out, out_grad, qseg, starts, depth):
    block = stream.shape[0]
    rows = block * SEQ
    shards = depth * INNER
    part = w_out.shape[0]

    def kernel(
        st_ref, pk_ref, mo_ref, ch_ref, c_ref, n_ref, wo_ref, og_ref, qs_ref, sg_ref,
        s_out, w_full, ch_out, h1_out, q_out, kv_out, o_out, m_out, l_out, mix_out, x1_out, h2_out,
        wf_out, og_out, mo_out,
        qp, acc, top, total, h2_own, gains, own, sq, rq, so, ro, sy, ry, sp, rp, sm, rm, *sems,
    ):
        net = Net(depth)
        sends = Sends()
        mirror = Mirror(net)
        gp = ShardGather(net, sends, pk_ref, FlatSlots(w_full, part), sems[28:34])
        gk = ShardGather(net, sends, None, kv_out, sems[:6])
        gk.src = gk.slot(0, net.i)
        gw = ShardGather(net, sends, wo_ref, FlatSlots(wf_out, part), sems[6:12])
        gg = PlaneGather(net, sends, og_ref, og_out, sems[12:18], block)
        gh = PlaneGather(net, sends, h2_own, h2_out, sems[18:24], block)
        chain = Chain(net, mo_out, sems[24:28])
        rows_out = [mirror.rows_out(k) for k in range(2)]
        heads = [mirror.heads_back(k) for k in range(2)]
        barrier = pltpu.get_barrier_semaphore()
        for device in net.zpeers() + net.plane():
            pl.semaphore_signal(barrier, inc=1, device_id=device, device_id_type=MESH)
        count = depth - 1 + E - 1
        for route in [r for r, _ in rows_out] + heads:
            count = count + route.hello()
        here = lambda y: s_out.at[pl.ds(pl.multiple_of(y * block, block), block)]
        mine_p = pltpu.make_async_copy(pk_ref, gp.slot(0, net.i), own.at[4])
        mine_s = pltpu.make_async_copy(st_ref, here(net.y), own.at[5])
        mine_m = pltpu.make_async_copy(
            mo_ref.at[net.i * SEQ + net.y], mo_out.at[net.z * INNER + net.i], own.at[3]
        )
        mine_c = pltpu.make_async_copy(ch_ref, ch_out.at[net.i * SEQ + net.y], own.at[6])
        mine_g = pltpu.make_async_copy(og_ref, og_out.at[gg.me], own.at[0])
        mine_w = pltpu.make_async_copy(wo_ref, gw.slot(0, net.i), own.at[1])
        for copy in (mine_p, mine_s, mine_m, mine_c, mine_g, mine_w):
            copy.start()
        pl.semaphore_wait(barrier, count)
        gp.begin()
        sends.start(st_ref, here(net.y), sy.at[0], ry.at[0], net.yp)
        for n, device in enumerate(net.plane()):
            sends.start(ch_ref, ch_out.at[net.i * SEQ + net.y], sp.at[n], rp.at[n], device)
        gw.begin()
        gp.end()
        for di in range(1, INNER):
            other = lax.rem(net.i + di, INNER)
            sends.start(
                mo_ref.at[other * SEQ + net.y],
                mo_out.at[net.z * INNER + net.i],
                sm.at[di - 1],
                rm.at[di - 1],
                net.dev(i=other),
            )
        gg.begin_y()

        def moe_ready(q):
            di = lax.rem(net.i - q + INNER, INNER)

            @pl.when(di > 0)
            def _():
                arrived(mo_out.at[net.z * INNER + q], sm.at[di - 1], rm.at[di - 1], net.xp)

        arrived(here(1 - net.y), sy.at[0], ry.at[0], net.yp)
        mine_s.wait()
        mine_p.wait()
        tail = w_full[:, QKV:].astype(F32).T
        gains[...] = tail[:8, :]

        step = 64

        def norm(n, carry):
            at = pl.ds(pl.multiple_of(n * step, step), step)
            x = s_out[at, :].astype(F32)
            scale = lax.rsqrt(jnp.mean(x * x, axis=-1, keepdims=True) + EPS)
            h1_out[at, :] = (x * scale * gains[0:1, :]).astype(BF)
            return carry

        lax.fori_loop(0, rows // step, norm, 0)
        h1 = h1_out[...]
        cos, sin = c_ref[...], n_ref[...]
        r = dot(h1, w_full[:, QCOLS:QKV])
        me = net.z * INNER + net.i
        kv_out[me, :, :HEAD] = turn(r[:, :HEAD], cos, sin).astype(BF)
        kv_out[me, :, HEAD:] = r[:, HEAD:].astype(BF)
        gk.begin()
        for h in range(0, GROUP, 2):
            r = dot(h1, w_full[:, h * HEAD : (h + 2) * HEAD])
            for g in range(2):
                v = turn(r[:, g * HEAD : (g + 1) * HEAD], cos, sin) * (SCALE * LOG2E)
                v = v.astype(BF)
                at = slice((h + g) * HEAD, (h + g + 1) * HEAD)
                qp[0, :, at] = v[:block]
                qp[1, :, at] = v[block:]
        q_refs = [
            lambda k=k: (qp.at[k], q_out.at[rows_out[k][1]], sq.at[k], rq.at[rows_out[k][1]])
            for k in range(2)
        ]
        o_refs = [
            lambda k=k: (o_out.at[k], mix_out.at[net.y], so.at[k], ro.at[net.y]) for k in range(2)
        ]
        for k in range(2):
            rows_out[k][0].send(q_refs[k])
        mine_m.wait()
        mine_w.wait()
        chain.begin(moe_ready)
        gg.begin_x()
        acc[...] = jnp.zeros_like(acc)
        top[...] = jnp.full_like(top, NEG)
        total[...] = jnp.zeros_like(total)
        gk.after_z()
        for k in range(2):
            rows_out[k][0].arrive(lambda: (q_out.at[k], sq.at[k], rq.at[k]))

        low, high = mirror.blocks()
        bases = (low * block, high * block)
        xi = lax.rem(net.i + 2, INNER)
        ci = net.i + 1 - 2 * net.core

        def attend(t, j, masked):
            start = pl.multiple_of(t * rows, rows)
            k = jnp.concatenate(
                [kv_out[t, :, :HEAD], seg_tile(start, rows, sg_ref[0:1, :], sg_ref[1:2, :])], axis=1
            )
            vt = kv_out[t, :, HEAD:].T
            if masked:
                key = start + lax.broadcasted_iota(jnp.int32, (rows, block), 0)
                ok = key <= bases[j] + lax.broadcasted_iota(jnp.int32, (rows, block), 1)
            scores = [
                dot(
                    k,
                    jnp.concatenate(
                        [q_out[j, :, h * HEAD : (h + 1) * HEAD], qs_ref[j]], axis=1
                    ),
                    NT,
                )
                for h in range(GROUP)
            ]
            for h in range(GROUP):
                s = scores[h]
                if masked:
                    s = jnp.where(ok, s, NEG)
                m0 = top[j, h : h + 1, :]
                m1 = jnp.maximum(m0, jnp.max(s, axis=0, keepdims=True))
                p = jnp.exp2(s - m1)
                f = jnp.exp2(m0 - m1)
                top[j, h : h + 1, :] = m1
                total[j, h : h + 1, :] = total[j, h : h + 1, :] * f + jnp.sum(
                    p, axis=0, keepdims=True
                )
                acc[j, h] = acc[j, h] * f + dot(vt, p.astype(BF))

        polled = min((shards - depth) // 2, 2 * INNER - 1, chain.steps)

        def tile(u, carry):
            in_z = u < depth
            in_x = u < 2 * depth
            in_c = u < 3 * depth
            dz = lax.rem(u, depth)
            place = jnp.where(in_z, net.i, jnp.where(in_x, xi, jnp.where(in_c, ci, lax.rem(ci + 2, INNER))))
            t = lax.rem(net.z - dz + depth, depth) * INNER + place

            @pl.when((u >= depth) & in_x)
            def _():
                gk.one_x(dz)

            @pl.when(u >= 2 * depth)
            def _():
                gk.one_c(u - 2 * depth, t)

            @pl.when(u == 2 * depth)
            def _():
                gg.middle()
                gw.after_z()

            @pl.when(u == 3 * depth)
            def _():
                gw.after_x()
                gg.end()

            @pl.when((u >= depth) & (lax.rem(u - depth, 2) == 1) & (u - depth < 2 * polled))
            def _():
                chain.step(lax.div(u - depth, 2))

            for j in (0, 1):
                live = t * rows <= bases[j] + block - 1
                free = t * rows + rows - 1 <= bases[j]

                @pl.when(live & free)
                def _():
                    attend(t, j, False)

                @pl.when(live & jnp.logical_not(free))
                def _():
                    attend(t, j, True)

            return carry

        lax.fori_loop(0, shards, tile, 0)
        gk.sent_loop()
        for j in range(2):
            for h in range(GROUP):
                o_out[j, :, h * HEAD : (h + 1) * HEAD] = (
                    (acc[j, h] / total[j, h : h + 1, :]).T.astype(BF)
                )
        for k in range(2):
            heads[k].send(o_refs[k])
        chain.run(polled, polled + 1)
        m_out[...] = top[...]
        l_out[...] = total[...]
        gw.last()
        gg.last()
        for k in range(2):
            heads[k].arrive(lambda: (mix_out.at[k], so.at[k], ro.at[k]))
        x1 = here(net.y)[...].astype(F32)
        x1 = x1 + dot(mix_out[0], wf_out[:QCOLS, :]) + dot(mix_out[1], wf_out[QCOLS:, :])
        x1_out[...] = x1
        scale = lax.rsqrt(jnp.mean(x1 * x1, axis=-1, keepdims=True) + EPS)
        h2_own[...] = (x1 * scale * gains[1:2, :]).astype(BF)
        mine_h = pltpu.make_async_copy(h2_own, h2_out.at[gh.me], own.at[2])
        gh.begin()
        mine_h.start()
        chain.run(polled + 1, 2 * INNER)
        gh.middle()
        chain.run(2 * INNER, 2 * INNER + 2)
        gh.end()
        chain.run(2 * INNER + 2, chain.steps)
        n = 0
        for di in range(INNER):
            for dy in range(SEQ):
                if di or dy:
                    frm = lax.rem(net.i - di + INNER, INNER) * SEQ + lax.rem(net.y + dy, SEQ)
                    arrived(ch_out.at[frm], sp.at[n], rp.at[n], net.yp)
                    n += 1
        mine_c.wait()
        gh.last()
        for k in range(2):
            rows_out[k][0].sent(q_refs[k])
            heads[k].sent(o_refs[k])
        chain.finish()
        sends.finish()
        mine_g.wait()
        mine_h.wait()

    sds = jax.ShapeDtypeStruct
    stat = sds((2, 8, block), F32)
    heads_shape = sds((2, block, QCOLS), BF)
    return pl.pallas_call(
        kernel,
        out_shape=(
            sds((rows, WIDTH), BF),
            sds((WIDTH, FIRST), BF),
            sds((E,) + chosen.shape, F32),
            sds((rows, WIDTH), BF),
            heads_shape,
            sds((shards, rows, 2 * HEAD), BF),
            heads_shape,
            stat,
            stat,
            heads_shape,
            sds((block, WIDTH), F32),
            sds((E, block, WIDTH), BF),
            sds((WIDTH, WIDTH), BF),
            sds((E, block, WIDTH), BF),
            sds((shards,) + moe.shape[1:], BF),
        ),
        in_specs=[hbm()] * 4 + [vmem()] * 2 + [hbm()] * 2 + [vmem()] * 2,
        out_specs=(vmem(), vmem(), hbm()) + (vmem(),) * 8 + (hbm(), vmem(), hbm(), hbm()),
        scratch_shapes=[
            pltpu.VMEM((2, block, QCOLS), BF),
            pltpu.VMEM((2, GROUP, HEAD, block), F32),
            pltpu.VMEM((2, 8, block), F32),
            pltpu.VMEM((2, 8, block), F32),
            pltpu.VMEM((block, WIDTH), BF),
            pltpu.VMEM((8, WIDTH), F32),
        ]
        + dma_sems(7, 2, 2, 2, 2, 1, 1, E - 1, E - 1, INNER - 1, INNER - 1)
        + ShardGather.sems(depth) * 2
        + PlaneGather.sems() * 2
        + Chain.sems(depth)
        + ShardGather.sems(depth),
        compiler_params=comm_params(7, 60 << 20),
        name="front",
    )(stream, pack, moe, chosen, cosine, sine, w_out, out_grad, qseg, starts)


def rms_parts(x):
    scale = lax.rsqrt(jnp.mean(x * x, axis=-1, keepdims=True) + EPS)
    return x * scale, scale


def rms_pull(normed, scale, grad, gain):
    inner = grad * gain
    return scale * (inner - normed * jnp.mean(inner * normed, axis=-1, keepdims=True))


def document_first(index, starts):
    return jnp.max(jnp.where(starts <= index[..., None], starts, 0), axis=-1)


def gelu_product(gate_pre, up_pre):
    return jax.nn.gelu(gate_pre, approximate=False) * up_pre


class Zigzag:
    def __init__(self, shards):
        last = 2 * shards - 1
        home = lambda b: b if b < shards else last - b
        self.rows = [
            [(s * 2 + y, home(2 * s + k) * 2 + y) for s in range(shards) for y in range(2)]
            for k in range(2)
        ]
        self.heads = [
            [
                (s * 2 + g, s if (g == 0) == (k == 0) else last - s)
                for s in range(shards)
                for g in range(2)
            ]
            for k in range(2)
        ]

    @staticmethod
    def move(x, pairs, back=False):
        return lax.ppermute(x, AXES, [(b, a) for a, b in pairs] if back else pairs)


def pick(flag, a, b):
    return jnp.where(flag, a, b), jnp.where(flag, b, a)


def experts(h2, out_grad, chosen, router_w, moe_w, rows_in, rows_out, me):
    blocks, tokens = h2.shape[:2]
    logits = dot(h2.reshape(blocks * tokens, WIDTH), router_w)
    probs = jax.nn.softmax(logits, axis=-1)
    mine = (jnp.arange(E) == me).astype(F32)
    named = jnp.sum(chosen * mine[None, :, None], axis=1)
    gate_tok = jnp.sum(probs * mine[None, :], axis=-1).reshape(blocks, tokens) * named
    upper = (jnp.arange(tokens)[:, None] <= jnp.arange(tokens)[None, :]).astype(BF)
    rank = dot(named.astype(BF), upper) - 1.0
    pick_slot = (
        rank[:, None, :] == jnp.arange(MOST, dtype=F32)[None, :, None]
    ) & (named[:, None, :] > 0.5)
    onehot = pick_slot.astype(BF)
    slots = blocks * MOST
    gate = jnp.sum(jnp.where(pick_slot, gate_tok[:, None, :], 0.0), axis=-1).reshape(slots, 1)
    spread = lambda v: lax.dot_general(
        onehot, v, (((2,), (1,)), ((0,), (0,))), preferred_element_type=F32
    )
    collect = lambda v: lax.dot_general(
        onehot, v, (((1,), (1,)), ((0,), (0,))), preferred_element_type=F32
    )
    rows = spread(h2).astype(BF).reshape(slots, WIDTH)
    slot_grad = spread(out_grad).astype(BF).reshape(slots, WIDTH)
    gate_w = moe_w[:, :rows_in, :FF].reshape(WIDTH, FF)
    up_w = moe_w[:, :rows_in, FF:].reshape(WIDTH, FF)
    down_w = moe_w[:, rows_in:, :].reshape(FF, WIDTH)
    gate_pre = dot(rows, gate_w)
    up_pre = dot(rows, up_w)
    active_f, pull = jax.vjp(gelu_product, gate_pre, up_pre)
    active = active_f.astype(BF)
    out = dot(active, down_w)
    slot_gf = slot_grad.astype(F32)
    gate_grad = jnp.sum(slot_gf * out, axis=-1).reshape(blocks, MOST)
    mixture = collect((out * gate).astype(BF).reshape(blocks, MOST, WIDTH)).astype(BF)
    expert_grad = (slot_gf * gate).astype(BF)
    active_grad = dot(expert_grad, down_w, NT)
    g_low, u_low = (v.astype(BF) for v in pull(active_grad))
    back = dot(g_low, gate_w, NT) + dot(u_low, up_w, NT)
    back_tok = collect(back.astype(BF).reshape(blocks, MOST, WIDTH)).astype(BF)
    gate_back = jnp.sum(jnp.where(pick_slot, gate_grad[:, :, None], 0.0), axis=1)
    lanes = (jnp.arange(EXTRA) == me).astype(F32)
    back_tok = jnp.concatenate(
        [back_tok, (gate_back[:, :, None] * lanes[None, None, :]).astype(BF)], axis=-1
    )
    shards = WIDTH // rows_in
    grads = jnp.concatenate(
        [
            jnp.concatenate(
                [
                    dot(rows, g_low, TN).astype(BF).reshape(shards, rows_in, FF),
                    dot(rows, u_low, TN).astype(BF).reshape(shards, rows_in, FF),
                ],
                axis=-1,
            ),
            dot(active, expert_grad, TN).astype(BF).reshape(shards, rows_out, WIDTH),
        ],
        axis=1,
    )
    return mixture, back_tok, grads


def local(depth, stream, doc_starts, routes, attn_gain, w_query, w_key, w_value, w_out, ffn_gain, w_router, w_gate, w_up, w_down, out_grad):
    tokens = stream.shape[0]
    rows_in, rows_out = w_gate.shape[1], w_down.shape[1]
    shards = depth * INNER
    z, i, y = (lax.axis_index(a) for a in AXES)
    shard = z * INNER + i
    own_block = shard * SEQ + y
    me = i * SEQ + y
    zig = Zigzag(shards)

    cut = lambda w, width: lax.dynamic_slice_in_dim(w, y * width, width, 1)
    extra = jnp.concatenate(
        [
            attn_gain[:, None],
            ffn_gain[:, None],
            w_router,
            jnp.zeros((rows_in, EXTRA - 2 - E), BF),
        ],
        axis=1,
    )
    pack = jnp.concatenate(
        [cut(w_query, QCOLS), cut(w_key, HEAD), cut(w_value, HEAD), extra], axis=1
    )
    moe_pack = jnp.concatenate([jnp.concatenate([w_gate, w_up], axis=2), w_down], axis=1)
    chosen_t = jnp.any(
        routes.T[:, None, :] == jnp.arange(E, dtype=jnp.int32)[None, :, None], axis=0
    ).astype(F32)
    pair_index = shard * SEQ * tokens + jnp.arange(SEQ * tokens, dtype=jnp.int32)
    position = pair_index - document_first(pair_index, doc_starts)
    freq = ROPE_BASE ** (-(jnp.arange(HEAD // 2, dtype=F32) * 2.0) / HEAD)
    angle = position.astype(F32)[:, None] * freq[None, :]
    cos_half, sin_half = jnp.cos(angle), jnp.sin(angle)
    cosine = jnp.concatenate([cos_half, cos_half], axis=1)
    sine = jnp.concatenate([-sin_half, sin_half], axis=1)

    block_ids = jnp.stack([shard, 2 * shards - 1 - shard]).astype(jnp.int32)
    query_index = block_ids[:, None] * tokens + jnp.arange(tokens, dtype=jnp.int32)[None, :]
    lo = document_first(query_index, doc_starts).astype(jnp.int32)
    info = jnp.concatenate([block_ids, lo[:, 0], lo[:, -1], jnp.zeros((2,), jnp.int32)])
    big = jnp.int32(1 << 30)
    spare = jnp.full((HEAD - doc_starts.shape[0],), big)
    first = jnp.concatenate([doc_starts, spare])
    beyond = jnp.concatenate([doc_starts[1:], spare, big[None]])
    starts = jnp.stack([first, beyond])
    outside = (query_index[..., None] < first) | (query_index[..., None] >= beyond)
    qseg = jnp.where(outside, NEG, 0.0).astype(BF)
    lo = lo[:, None, :]
    (
        pair, weights, chosen_all, h1, q, kv, ob, top, total, mixed, x1, h2_plane, out_w, grad_plane, moe_w,
    ) = front(stream, pack, moe_pack, chosen_t, cosine, sine, w_out, out_grad, qseg, starts, depth)
    extra_w = weights[:, QKV : QKV + EXTRA]
    gains = extra_w[:, :2].astype(F32).T
    gain_a, gain_f = gains[0:1], gains[1:2]
    router_w = extra_w[:, 2 : 2 + E]
    qkv_w = weights[:, :QKV]
    kv = kv.reshape(shards * SEQ * tokens, 2 * HEAD)
    even = lax.rem(shard, 2) == 0
    head_zero = y == 0
    low_half = own_block < shards
    mixed = jnp.concatenate([mixed[0], mixed[1]], axis=1)
    normed, scale = rms_parts(x1)
    h2 = (normed * gain_f).astype(BF)

    mixture_part, back_part, moe_grads = experts(
        h2_plane, grad_plane, chosen_all, router_w, moe_w, rows_in, rows_out, me
    )
    back = scatter_plane(back_part, depth)
    mixture = lax.psum_scatter(mixture_part, ("inner", "seq"), scatter_dimension=0, tiled=False)
    moe_own = lax.psum_scatter(
        moe_grads.reshape(depth, INNER, rows_in + rows_out, WIDTH),
        "outer",
        scatter_dimension=0,
        tiled=False,
    )
    result = (x1 + mixture.astype(F32)).astype(BF)

    chosen = chosen_t.T
    probs = jax.nn.softmax(dot(h2, router_w), axis=-1)
    dp = back[:, WIDTH : WIDTH + E] * chosen
    dz = (probs * (dp - jnp.sum(dp * probs, axis=-1, keepdims=True))).astype(BF)
    router_part = dot(h2, dz, TN)
    dh2 = back[:, :WIDTH] + dot(dz, router_w, NT)
    grad_f = out_grad.astype(F32)
    dx1 = grad_f + rms_pull(normed, scale, dh2, gain_f)
    gain_f_part = jnp.sum(dh2 * normed, axis=0)
    dx1_low = dx1.astype(BF)
    out_part = dot(mixed, dx1_low, TN)
    dob = dot(dx1_low, out_w, NT).astype(BF)

    dob_a, dob_b = pick(low_half, dob[:, :QCOLS], dob[:, QCOLS:])
    dob_low, dob_high = pick(
        head_zero,
        zig.move(dob_a, zig.heads[0], True),
        zig.move(dob_b, zig.heads[1], True),
    )
    dob_zig = jnp.stack([dob_low, dob_high])
    dq, dkv_part = attend_backward(q, kv, lo, info, top, total, dob_zig, ob)
    dq_a, dq_b = pick(even, dq[0], dq[1])
    dq_pair = jnp.concatenate(
        [zig.move(dq_a, zig.rows[0], True), zig.move(dq_b, zig.rows[1], True)], axis=0
    )
    dkv = scatter_keys(dkv_part.reshape(shards, SEQ * tokens, 2 * HEAD), depth)
    raw = unturn(dq_pair, dkv, cosine, sine)
    qkv_part = dot(h1, raw, TN)
    dh1 = dot(raw, qkv_w, NT)

    normed_pair, scale_pair = rms_parts(pair.astype(F32))
    gain_a_part = jnp.sum(dh1 * normed_pair, axis=0)
    dh1 = dh1.reshape(SEQ, tokens, WIDTH)
    mine, other = pick(head_zero, dh1[0], dh1[1])
    theirs = lax.ppermute(other.astype(BF), "seq", [(0, 1), (1, 0)])
    normed_s, scale_s = rms_parts(stream.astype(F32))
    stream_grad = (
        dx1 + rms_pull(normed_s, scale_s, mine + theirs.astype(F32), gain_a)
    ).astype(BF)

    small = jnp.concatenate(
        [
            gain_a_part[:, None],
            gain_f_part[:, None],
            router_part,
            jnp.zeros((WIDTH, EXTRA - 2 - E), F32),
        ],
        axis=1,
    )
    dense = jnp.concatenate([qkv_part, small, out_part], axis=1).astype(BF)
    own, peer, moe_out = closing(dense.reshape(shards, rows_in, PACK), moe_own, depth)
    peer = peer.astype(F32)

    def halves(a, b):
        return jnp.concatenate(
            pick(head_zero, own[:, a:b], peer[:, a:b]), axis=1
        )

    both = own[:, QKV:] + peer[:, QKV:]
    moe_out = moe_out.astype(F32)
    return (
        result,
        stream_grad,
        both[:, 0],
        halves(0, QCOLS),
        halves(QCOLS, QCOLS + HEAD),
        halves(QCOLS + HEAD, QKV),
        both[:, EXTRA:],
        both[:, 1],
        both[:, 2 : 2 + E],
        moe_out[:, :rows_in, :FF],
        moe_out[:, :rows_in, FF:],
        moe_out[:, rows_in:, :],
    )


def solution(mesh):
    shards = mesh.shape["shard"]
    depth = shards // INNER
    fine = Mesh(mesh.devices.reshape(depth, INNER, SEQ), AXES)
    shard = ("outer", "inner")
    tokens = P(AXES, None)
    in_specs = (
        tokens,
        P(),
        tokens,
        P(shard),
        P(shard, None),
        P(shard, None),
        P(shard, None),
        P(shard, None),
        P(shard),
        P(shard, None),
        P(None, shard, None),
        P(None, shard, None),
        P(None, shard, None),
        tokens,
    )
    out_specs = (
        tokens,
        tokens,
        P(shard),
        P(shard, None),
        P(shard, None),
        P(shard, None),
        P(shard, None),
        P(shard),
        P(shard, None),
        P(None, shard, None),
        P(None, shard, None),
        P(None, shard, None),
    )

    def run(*args):
        return local(depth, *args)

    return jax.shard_map(run, mesh=fine, in_specs=in_specs, out_specs=out_specs, check_vma=False)
```

```python
import jax
import jax.numpy as jnp
from jax import lax
from jax.experimental import pallas as pl
from jax.experimental.pallas import tpu as pltpu
from jax.sharding import Mesh, PartitionSpec as P

WIDTH = 1536
HEADS = 12
KV_HEADS = 2
HEAD = 128
FF = 768
E = 8
MOST = 192
SEQ = KV_HEADS
GROUP = HEADS // KV_HEADS
INNER = E // SEQ
QCOLS = GROUP * HEAD
QKV = QCOLS + 2 * HEAD
EXTRA = 128
FIRST = QKV + EXTRA
PACK = QKV + EXTRA + WIDTH
EPS = 1e-06
ROPE_BASE = 10000.0
SCALE = HEAD**-0.5
LOG2E = 1.4426950408889634
LN2 = 0.6931471805599453
NEG = -1e30
AXES = ("outer", "inner", "seq")
MESH = pl.DeviceIdType.MESH
NN = (((1,), (0,)), ((), ()))
NT = (((1,), (1,)), ((), ()))
TN = (((0,), (0,)), ((), ()))
BF = jnp.bfloat16
F32 = jnp.float32


def dot(a, b, dims=NN):
    return lax.dot_general(a, b, dims, preferred_element_type=F32)


class Net:
    def __init__(self, depth):
        self.depth = depth
        self.z = lax.axis_index("outer")
        self.i = lax.axis_index("inner")
        self.y = lax.axis_index("seq")
        self.core = lax.rem(self.i, 2)
        self.x = lax.div(self.i, 2)
        self.xp = self.dev(i=lax.rem(self.i + 2, INNER))
        self.cp = self.dev(i=self.i + 1 - 2 * self.core)
        self.yp = self.dev(y=1 - self.y)

    def dev(self, z=None, i=None, y=None):
        return {
            "outer": self.z if z is None else z,
            "inner": self.i if i is None else i,
            "seq": self.y if y is None else y,
        }

    def zoff(self, dz):
        return lax.rem(self.z + dz, self.depth)

    def zpeers(self):
        return [self.dev(z=self.zoff(dz)) for dz in range(1, self.depth)]

    def plane(self):
        out = []
        for di in range(INNER):
            for dy in range(SEQ):
                if di or dy:
                    out.append(
                        self.dev(i=lax.rem(self.i + di, INNER), y=lax.rem(self.y + dy, SEQ))
                    )
        return out


def greet(devices):
    barrier = pltpu.get_barrier_semaphore()
    for device in devices:
        pl.semaphore_signal(barrier, inc=1, device_id=device, device_id_type=MESH)
    pl.semaphore_wait(barrier, len(devices))


def remote(src, dst, ssem, rsem, device):
    return pltpu.make_async_remote_copy(
        src_ref=src, dst_ref=dst, send_sem=ssem, recv_sem=rsem, device_id=device, device_id_type=MESH
    )


class Sends:
    def __init__(self):
        self.items = []

    def start(self, *refs):
        self.later(lambda: refs)

    def later(self, refs):
        remote(*refs()).start()
        self.items.append(refs)

    def finish(self):
        for refs in self.items:
            remote(*refs()).wait_send()


def arrived(dst, ssem, rsem, device):
    remote(dst, dst, ssem, rsem, device).wait_recv()


def dma_sems(*counts):
    return [pltpu.SemaphoreType.DMA((n,)) for n in counts]


class FlatSlots:
    class At:
        def __init__(self, ref, rows):
            self.ref, self.rows = ref, rows

        def __getitem__(self, n):
            return self.ref.at[pl.ds(pl.multiple_of(n * self.rows, self.rows), self.rows)]

    def __init__(self, ref, rows):
        self.at = self.At(ref, rows)


class ShardGather:
    def __init__(self, net, sends, src, out, sems):
        self.net, self.sends, self.src, self.out = net, sends, src, out
        self.sz, self.rz, self.sx, self.rx, self.sc, self.rc = sems
        self.xi = lax.rem(net.i + 2, INNER)

    @staticmethod
    def sems(depth):
        return dma_sems(*([max(depth - 1, 1)] * 2 + [depth] * 2 + [2 * depth] * 2))

    def slot(self, dz, i):
        return self.out.at[lax.rem(self.net.z - dz + self.net.depth, self.net.depth) * INNER + i]

    def begin(self):
        net, me = self.net, self.slot(0, self.net.i)
        for n, device in enumerate(net.zpeers()):
            self.sends.start(self.src, me, self.sz.at[n], self.rz.at[n], device)
        self.sends.start(self.src, me, self.sx.at[0], self.rx.at[0], net.xp)
        self.sends.start(self.src, me, self.sc.at[0], self.rc.at[0], net.cp)

    def pass_on(self, dz, i, ssem, rsem, n, device):
        self.sends.later(
            lambda: (self.slot(dz, i), self.slot(dz, i), ssem.at[n], rsem.at[n], device)
        )

    def after_z(self):
        net = self.net
        for dz in range(1, net.depth):
            block = self.slot(dz, net.i)
            arrived(block, self.sz.at[dz - 1], self.rz.at[dz - 1], net.xp)
            self.pass_on(dz, net.i, self.sx, self.rx, dz, net.xp)
            self.pass_on(dz, net.i, self.sc, self.rc, dz, net.cp)

    def after_x(self):
        net, depth = self.net, self.net.depth
        for dz in range(depth):
            arrived(self.slot(dz, self.xi), self.sx.at[dz], self.rx.at[dz], net.xp)
            self.pass_on(dz, self.xi, self.sc, self.rc, depth + dz, net.cp)

    def last(self):
        net, depth = self.net, self.net.depth
        ci = net.i + 1 - 2 * net.core
        for dz in range(depth):
            arrived(self.slot(dz, ci), self.sc.at[dz], self.rc.at[dz], net.cp)
        for dz in range(depth):
            arrived(
                self.slot(dz, lax.rem(ci + 2, INNER)),
                self.sc.at[depth + dz],
                self.rc.at[depth + dz],
                net.cp,
            )

    def end(self):
        self.after_z()
        self.after_x()
        self.last()

    def one_x(self, dz):
        net, block, n = self.net, self.slot(dz, self.xi), self.net.depth + dz
        arrived(block, self.sx.at[dz], self.rx.at[dz], net.xp)
        remote(block, block, self.sc.at[n], self.rc.at[n], net.cp).start()

    def one_c(self, n, place):
        block = self.out.at[place]
        arrived(block, self.sc.at[n], self.rc.at[n], self.net.cp)

    def sent_loop(self):
        net, depth = self.net, self.net.depth
        for dz in range(depth):
            block = self.slot(dz, self.xi)
            remote(block, block, self.sc.at[depth + dz], self.rc.at[depth + dz], net.cp).wait_send()


def hbm():
    return pl.BlockSpec(memory_space=pltpu.HBM)


def vmem():
    return pl.BlockSpec(memory_space=pltpu.VMEM)


def smem():
    return pl.BlockSpec(memory_space=pltpu.SMEM)


def comm_params(cid, limit=56 << 20):
    return pltpu.CompilerParams(
        collective_id=cid, has_side_effects=True, vmem_limit_bytes=limit
    )


def add_into(dst, sources, rows, chunk):
    def body(n, carry):
        at = pl.ds(pl.multiple_of(n * chunk, chunk), chunk)
        total = sources[0][at, :].astype(F32)
        for source in sources[1:]:
            total = total + source[at, :].astype(F32)
        dst[at, :] = total.astype(dst.dtype)
        return carry

    lax.fori_loop(0, rows // chunk, body, 0)


def chunk_of(rows):
    for size in (32, 16, 8):
        if rows % size == 0:
            return size
    return rows


def scatter_plane(part, depth):
    rows, cols = part.shape[1:]
    half = rows // 2

    def kernel(part_ref, out, bc, mid, bx, by, second, b2, ssem, rsem):
        net = Net(depth)
        sends = Sends()

        def place(fx, fy, core):
            x = 1 - net.x if fx else net.x
            y = 1 - net.y if fy else net.y
            return (x * 2 + core) * SEQ + y

        greet([net.xp, net.yp, net.cp])
        order = ((1, 1), (1, 0), (0, 1), (0, 0))
        for n, (fx, fy) in enumerate(order):
            sends.start(
                part_ref.at[place(fx, fy, 1 - net.core)], bc.at[n], ssem.at[n], rsem.at[n], net.cp
            )
        ch = chunk_of(half)
        lo, hi = pl.ds(0, half), pl.ds(half, half)
        for n, (fx, fy) in enumerate(order):
            arrived(bc.at[n], ssem.at[n], rsem.at[n], net.cp)
            add_into(mid.at[n], [part_ref.at[place(fx, fy, net.core)], bc.at[n]], rows, ch)
            if n == 0:
                sends.start(mid.at[0, lo], bx.at[0], ssem.at[4], rsem.at[4], net.xp)
                sends.start(mid.at[0, hi], by.at[0], ssem.at[5], rsem.at[5], net.yp)
            if n == 1:
                sends.start(mid.at[1, lo], bx.at[1], ssem.at[6], rsem.at[6], net.xp)
            if n == 2:
                sends.start(mid.at[2, hi], by.at[1], ssem.at[7], rsem.at[7], net.yp)
        arrived(bx.at[0], ssem.at[4], rsem.at[4], net.xp)
        add_into(second.at[0], [mid.at[2, lo], bx.at[0]], half, ch)
        sends.start(second.at[0], b2.at[0], ssem.at[8], rsem.at[8], net.yp)
        arrived(by.at[0], ssem.at[5], rsem.at[5], net.yp)
        add_into(second.at[1], [mid.at[1, hi], by.at[0]], half, ch)
        sends.start(second.at[1], b2.at[1], ssem.at[9], rsem.at[9], net.xp)
        arrived(bx.at[1], ssem.at[6], rsem.at[6], net.xp)
        arrived(by.at[1], ssem.at[7], rsem.at[7], net.yp)
        arrived(b2.at[0], ssem.at[8], rsem.at[8], net.yp)
        add_into(out.at[lo], [mid.at[3, lo], bx.at[1], b2.at[0]], half, ch)
        arrived(b2.at[1], ssem.at[9], rsem.at[9], net.xp)
        add_into(out.at[hi], [mid.at[3, hi], by.at[1], b2.at[1]], half, ch)
        sends.finish()

    return pl.pallas_call(
        kernel,
        out_shape=jax.ShapeDtypeStruct((rows, cols), F32),
        in_specs=[vmem()],
        out_specs=vmem(),
        scratch_shapes=[pltpu.VMEM((4, rows, cols), BF)] * 2
        + [pltpu.VMEM((2, half, cols), BF)] * 4
        + dma_sems(10, 10),
        compiler_params=comm_params(4),
        name="scatter_plane",
    )(part)


class ShardScatter:
    @staticmethod
    def scratch(depth, rows, cols):
        far = max(depth - 1, 1)
        shapes = [(2 * depth, rows, cols)] + [(depth, rows, cols)] * 2 + [(far, rows, cols)] * 2
        return [pltpu.VMEM(s, BF) for s in shapes] + dma_sems(
            2 * depth, 2 * depth, depth, depth, far, far
        )

    def __init__(self, net, sends, part, scratch):
        self.net, self.sends, self.part = net, sends, part
        self.bc, self.sx, self.bx, self.sz, self.bz = scratch[:5]
        self.ssc, self.rsc, self.ssx, self.rsx, self.ssz, self.rsz = scratch[5:]
        depth = net.depth
        self.order = sorted(range(1, depth), key=lambda d: -min(d, depth - d)) + [0]
        self.rows = part.shape[1]
        self.chunk = chunk_of(self.rows)

    def block(self, dz, fx, core):
        x = 1 - self.net.x if fx else self.net.x
        return self.part.at[self.net.zoff(dz) * INNER + x * 2 + core]

    def begin(self):
        net = self.net
        for dz in self.order:
            for fx in (1, 0):
                n = dz * 2 + fx
                self.sends.start(
                    self.block(dz, fx, 1 - net.core),
                    self.bc.at[n],
                    self.ssc.at[n],
                    self.rsc.at[n],
                    net.cp,
                )

    def end(self, out):
        net, sends = self.net, self.sends
        for dz in self.order:
            n = dz * 2 + 1
            arrived(self.bc.at[n], self.ssc.at[n], self.rsc.at[n], net.cp)
            add_into(
                self.sx.at[dz], [self.block(dz, 1, net.core), self.bc.at[n]], self.rows, self.chunk
            )
            sends.start(self.sx.at[dz], self.bx.at[dz], self.ssx.at[dz], self.rsx.at[dz], net.xp)
        for dz in self.order:
            n = dz * 2
            arrived(self.bc.at[n], self.ssc.at[n], self.rsc.at[n], net.cp)
            arrived(self.bx.at[dz], self.ssx.at[dz], self.rsx.at[dz], net.xp)
            terms = [self.block(dz, 0, net.core), self.bc.at[n], self.bx.at[dz]]
            if dz:
                add_into(self.sz.at[dz - 1], terms, self.rows, self.chunk)
                sends.start(
                    self.sz.at[dz - 1],
                    self.bz.at[dz - 1],
                    self.ssz.at[dz - 1],
                    self.rsz.at[dz - 1],
                    net.dev(z=net.zoff(dz)),
                )
            else:
                for far in range(net.depth - 1):
                    arrived(self.bz.at[far], self.ssz.at[far], self.rsz.at[far], net.xp)
                    terms.append(self.bz.at[far])
                add_into(out, terms, self.rows, self.chunk)


def scatter_keys(part, depth, cid):
    rows, cols = part.shape[1:]

    def kernel(part_ref, out, *scratch):
        net = Net(depth)
        sends = Sends()
        greet(net.zpeers() + [net.xp, net.cp])
        work = ShardScatter(net, sends, part_ref, scratch)
        work.begin()
        work.end(out)
        sends.finish()

    return pl.pallas_call(
        kernel,
        out_shape=jax.ShapeDtypeStruct((rows, cols), F32),
        in_specs=[vmem()],
        out_specs=vmem(),
        scratch_shapes=ShardScatter.scratch(depth, rows, cols),
        compiler_params=comm_params(cid),
        name="scatter_keys",
    )(part)


def turn(values, cosine, sine):
    return values * cosine + pltpu.roll(values, HEAD // 2, 1) * sine


def attend_backward(q, kv, lo, info, m, l, dob, ob, tile=512):
    block = q.shape[1]
    keys = kv.shape[0]
    tiles = keys // tile

    def kernel(info_ref, q_ref, kv_ref, lo_ref, m_ref, l_ref, do_ref, ob_ref, dq_ref, dkv_ref, da, dl, acc):
        acc[...] = jnp.zeros_like(acc)
        for j in range(2):
            for h in range(GROUP):
                c = slice(h * HEAD, (h + 1) * HEAD)
                d = do_ref[j, :, c].astype(F32)
                o = ob_ref[j, :, c].astype(F32)
                inv = 1.0 / l_ref[j, h : h + 1, :]
                da[j, h] = (d.T * inv).T.astype(BF)
                dl[j, h : h + 1, :] = -jnp.sum((d * o).T, axis=0, keepdims=True) * inv
        low = jnp.minimum(info_ref[2], info_ref[3]) // tile
        high = (info_ref[1] * block + block - 1) // tile

        def clear(t, carry):
            dkv_ref[pl.ds(pl.multiple_of(t * tile, tile), tile), :] = jnp.zeros((tile, 2 * HEAD), BF)
            return carry

        lax.fori_loop(0, low, clear, 0)
        lax.fori_loop(high + 1, tiles, clear, 0)

        def piece(t, j, masked):
            start = pl.multiple_of(t * tile, tile)
            base = info_ref[j] * block
            k = kv_ref[pl.ds(start, tile), :HEAD]
            v = kv_ref[pl.ds(start, tile), HEAD:]
            kt = k.T
            if masked:
                key = start + lax.broadcasted_iota(jnp.int32, (tile, block), 0)
                query = base + lax.broadcasted_iota(jnp.int32, (tile, block), 1)
                ok = (key <= query) & (key >= lo_ref[j])
            dk = dv = None
            for h in range(GROUP):
                qh = q_ref[j, :, h * HEAD : (h + 1) * HEAD]
                s = dot(k, qh, NT) - m_ref[j, h : h + 1, :]
                if masked:
                    s = jnp.where(ok, s, NEG)
                p = jnp.exp2(s)
                dah = da[j, h]
                dvh = dot(p.astype(BF), dah)
                dp = dot(v, dah, NT) + dl[j, h : h + 1, :]
                ds = (p * dp).astype(BF)
                dkh = dot(ds, qh)
                acc[j, h] += dot(kt, ds)
                dk = dkh if dk is None else dk + dkh
                dv = dvh if dv is None else dv + dvh
            return dk * LN2, dv

        def tile_step(t, carry):
            start = pl.multiple_of(t * tile, tile)
            rows = pl.ds(start, tile)

            def put(j, masked):
                dk, dv = piece(t, j, masked)
                if j == 0:
                    dk = dk + dkv_ref[rows, :HEAD].astype(F32)
                    dv = dv + dkv_ref[rows, HEAD:].astype(F32)
                dkv_ref[rows, :HEAD] = dk.astype(BF)
                dkv_ref[rows, HEAD:] = dv.astype(BF)

            for j in (1, 0):
                base = info_ref[j] * block
                live = (start <= base + block - 1) & (start + tile > info_ref[2 + j])
                free = (start + tile - 1 <= base) & (start >= info_ref[4 + j])
                if j == 1:

                    @pl.when(jnp.logical_not(live))
                    def _():
                        clear(t, 0)

                @pl.when(live & free)
                def _():
                    put(j, False)

                @pl.when(live & jnp.logical_not(free))
                def _():
                    put(j, True)

            return carry

        lax.fori_loop(low, high + 1, tile_step, 0)
        for j in range(2):
            for h in range(GROUP):
                dq_ref[j, :, h * HEAD : (h + 1) * HEAD] = (acc[j, h] * SCALE).T.astype(BF)

    return pl.pallas_call(
        kernel,
        out_shape=(jax.ShapeDtypeStruct(q.shape, BF), jax.ShapeDtypeStruct(kv.shape, BF)),
        in_specs=[smem()] + [vmem()] * 7,
        out_specs=(vmem(),) * 2,
        scratch_shapes=[
            pltpu.VMEM((2, GROUP, block, HEAD), BF),
            pltpu.VMEM((2, 8, block), F32),
            pltpu.VMEM((2, GROUP, HEAD, block), F32),
        ],
        compiler_params=pltpu.CompilerParams(vmem_limit_bytes=60 << 20),
        cost_estimate=pl.CostEstimate(
            flops=int(2.5e10), bytes_accessed=12 << 20, transcendentals=13 << 20
        ),
        name="attend_backward",
    )(info, q, kv, lo, m, l, dob, ob)


class PlaneGather:
    @staticmethod
    def sems():
        return dma_sems(2, 2, 2, 2, 5, 5)

    def __init__(self, net, sends, src, out, sems, rows):
        self.net, self.sends, self.src, self.out = net, sends, src, out
        self.sx, self.rx, self.sy, self.ry, self.sc, self.rc = sems
        half = rows // 2
        self.lo, self.hi = pl.ds(0, half), pl.ds(half, half)
        xi = lax.rem(net.i + 2, INNER)
        ci = net.i + 1 - 2 * net.core
        cx = lax.rem(ci + 2, INNER)
        place = lambda i, y: i * SEQ + y
        self.me, self.xb = place(net.i, net.y), place(xi, net.y)
        self.yb, self.db = place(net.i, 1 - net.y), place(xi, 1 - net.y)
        self.core_blocks = [place(ci, net.y), place(ci, 1 - net.y), place(cx, net.y)]
        self.core_diag = place(cx, 1 - net.y)

    def begin(self):
        self.begin_y()
        self.begin_x()

    def begin_y(self):
        net, out, src = self.net, self.out, self.src
        self.sends.start(src, out.at[self.me], self.sy.at[0], self.ry.at[0], net.yp)
        self.sends.start(src, out.at[self.me], self.sc.at[0], self.rc.at[0], net.cp)

    def begin_x(self):
        net, out, src = self.net, self.out, self.src
        self.sends.start(src, out.at[self.me], self.sx.at[0], self.rx.at[0], net.xp)

    def pass_on(self, block, part, ssem, rsem, n, device):
        def refs():
            at = self.out.at[block] if part is None else self.out.at[block, part]
            return at, at, ssem.at[n], rsem.at[n], device

        self.sends.later(refs)

    def middle(self):
        net, out = self.net, self.out
        arrived(out.at[self.yb], self.sy.at[0], self.ry.at[0], net.yp)
        self.pass_on(self.yb, self.lo, self.sx, self.rx, 1, net.xp)
        self.pass_on(self.yb, None, self.sc, self.rc, 1, net.cp)
        arrived(out.at[self.xb], self.sx.at[0], self.rx.at[0], net.xp)
        self.pass_on(self.xb, self.hi, self.sy, self.ry, 1, net.yp)
        self.pass_on(self.xb, None, self.sc, self.rc, 2, net.cp)

    def end(self):
        net, out = self.net, self.out
        arrived(out.at[self.db, self.lo], self.sx.at[1], self.rx.at[1], net.xp)
        self.pass_on(self.db, self.lo, self.sc, self.rc, 3, net.cp)
        arrived(out.at[self.db, self.hi], self.sy.at[1], self.ry.at[1], net.yp)
        self.pass_on(self.db, self.hi, self.sc, self.rc, 4, net.cp)

    def last(self):
        net, out = self.net, self.out
        for n, block in enumerate(self.core_blocks):
            arrived(out.at[block], self.sc.at[n], self.rc.at[n], net.cp)
        arrived(out.at[self.core_diag, self.lo], self.sc.at[3], self.rc.at[3], net.cp)
        arrived(out.at[self.core_diag, self.hi], self.sc.at[4], self.rc.at[4], net.cp)


class Route:
    def __init__(self, net, sends_to, comes_from):
        self.net = net
        me = net.z * INNER + net.i
        self.local = (sends_to[0] == me) & (sends_to[1] == net.y)
        self.kept = (comes_from[0] == me) & (comes_from[1] == net.y)
        self.to, self.frm = self.device(sends_to), self.device(comes_from)

    def device(self, place):
        shard, y = place
        return self.net.dev(z=lax.div(shard, INNER), i=lax.rem(shard, INNER), y=y)

    def hello(self):
        @pl.when(jnp.logical_not(self.kept))
        def _():
            pl.semaphore_signal(
                pltpu.get_barrier_semaphore(), inc=1, device_id=self.frm, device_id_type=MESH
            )

        return jnp.where(self.local, 0, 1)

    def send(self, refs):
        @pl.when(self.local)
        def _():
            src, dst, _, _ = refs()
            dst[...] = src[...]

        @pl.when(jnp.logical_not(self.local))
        def _():
            remote(*refs(), self.to).start()

    def sent(self, refs):
        @pl.when(jnp.logical_not(self.local))
        def _():
            remote(*refs(), self.to).wait_send()

    def arrive(self, refs):
        @pl.when(jnp.logical_not(self.kept))
        def _():
            dst, ssem, rsem = refs()
            remote(dst, dst, ssem, rsem, self.to).wait_recv()


class Mirror:
    def __init__(self, net):
        self.net = net
        self.n = net.depth * INNER
        self.last = 2 * self.n - 1
        self.me = net.z * INNER + net.i

    def home(self, block):
        return jnp.where(block < self.n, block, self.last - block)

    def blocks(self):
        return self.me, self.last - self.me

    def slot(self, block):
        return jnp.where(block < self.n, 0, 1)

    def rows_out(self, k):
        block = 2 * self.me + k
        come = self.blocks()[k]
        return Route(
            self.net, (self.home(block), self.net.y), (lax.div(come, 2), self.net.y)
        ), self.slot(block)

    def rows_back(self, k):
        block = self.blocks()[k]
        come = 2 * self.me + k
        return Route(
            self.net, (lax.div(block, 2), self.net.y), (self.home(come), self.net.y)
        ), lax.rem(block, 2)

    def heads_back(self, k):
        block = self.blocks()[k]
        own = 2 * self.me + self.net.y
        return Route(self.net, (lax.div(block, 2), lax.rem(block, 2)), (self.home(own), k))

    def heads_out(self, k):
        own = 2 * self.me + self.net.y
        come = self.blocks()[k]
        return Route(
            self.net, (self.home(own), k), (lax.div(come, 2), lax.rem(come, 2))
        ), self.slot(own)


class Chain:
    @staticmethod
    def sems(depth):
        return dma_sems(*[max(depth - 1, 1) * INNER] * 4)

    def __init__(self, net, out, sems):
        self.net, self.out = net, out
        self.su, self.ru, self.sd, self.rd = sems
        self.steps = (net.depth - 1) * INNER
        self.up = net.dev(z=jnp.minimum(net.z + 1, net.depth - 1))
        self.down = net.dev(z=jnp.maximum(net.z - 1, 0))

    def piece(self, z, q):
        return self.out.at[z * INNER + q]

    def refs(self, hop, q, way):
        net = self.net
        n = (hop + 1) * INNER + q
        z = net.z - 1 - hop if way == 0 else net.z + 1 + hop
        ssem, rsem, device = (
            (self.su.at[n], self.ru.at[n], self.up)
            if way == 0
            else (self.sd.at[n], self.rd.at[n], self.down)
        )
        return self.piece(z, q), ssem, rsem, device

    def begin(self, ready):
        def body(q, carry):
            ready(q)
            for way in range(2):

                @pl.when(self.net.z < self.net.depth - 1 if way == 0 else self.net.z > 0)
                def _():
                    dst, ssem, rsem, device = self.refs(-1, q, way)
                    remote(dst, dst, ssem, rsem, device).start()

            return carry

        lax.fori_loop(0, INNER, body, 0)

    def step(self, n):
        net = self.net
        hop, q = lax.div(n, INNER), lax.rem(n, INNER)
        for way in range(2):
            z = net.z - 1 - hop if way == 0 else net.z + 1 + hop
            here = z >= 0 if way == 0 else z <= net.depth - 1
            further = net.z < net.depth - 1 if way == 0 else net.z > 0

            @pl.when(here)
            def _():
                block = self.piece(z, q)
                if way == 0:
                    arrived(block, self.su.at[n], self.ru.at[n], self.up)
                else:
                    arrived(block, self.sd.at[n], self.rd.at[n], self.down)

            @pl.when(here & further)
            def _():
                dst, ssem, rsem, device = self.refs(hop, q, way)
                remote(dst, dst, ssem, rsem, device).start()

    def run(self, a, b):
        def body(n, carry):
            self.step(n)
            return carry

        lax.fori_loop(a, min(b, self.steps), body, 0)

    def finish(self):
        def body(n, carry):
            hop, q = lax.div(n, INNER) - 1, lax.rem(n, INNER)
            for way in range(2):
                z = self.net.z - 1 - hop if way == 0 else self.net.z + 1 + hop
                here = z >= 0 if way == 0 else z <= self.net.depth - 1
                further = self.net.z < self.net.depth - 1 if way == 0 else self.net.z > 0

                @pl.when(here & further)
                def _():
                    dst, ssem, rsem, device = self.refs(hop, q, way)
                    remote(dst, dst, ssem, rsem, device).wait_send()

            return carry

        lax.fori_loop(0, self.steps, body, 0)


def seg_tile(start, rows, st, en):
    key = start + lax.broadcasted_iota(jnp.int32, (rows, HEAD), 0)
    return ((key >= st) & (key < en)).astype(F32).astype(BF)


def front(stream, pack, moe, chosen, cosine, sine, w_out, out_grad, qseg, starts, depth):
    block = stream.shape[0]
    rows = block * SEQ
    shards = depth * INNER
    part = w_out.shape[0]

    def kernel(
        st_ref, pk_ref, mo_ref, ch_ref, c_ref, n_ref, wo_ref, og_ref, qs_ref, sg_ref,
        s_out, w_full, ch_out, h1_out, q_out, kv_out, o_out, m_out, l_out, mix_out, x1_out, h2_out,
        wf_out, og_out, mo_out,
        qp, acc, top, total, h2_own, gains, own, sq, rq, so, ro, sy, ry, sp, rp, sm, rm, *sems,
    ):
        net = Net(depth)
        sends = Sends()
        mirror = Mirror(net)
        gp = ShardGather(net, sends, pk_ref, FlatSlots(w_full, part), sems[28:34])
        gk = ShardGather(net, sends, None, kv_out, sems[:6])
        gk.src = gk.slot(0, net.i)
        gw = ShardGather(net, sends, wo_ref, FlatSlots(wf_out, part), sems[6:12])
        gg = PlaneGather(net, sends, og_ref, og_out, sems[12:18], block)
        gh = PlaneGather(net, sends, h2_own, h2_out, sems[18:24], block)
        chain = Chain(net, mo_out, sems[24:28])
        rows_out = [mirror.rows_out(k) for k in range(2)]
        heads = [mirror.heads_back(k) for k in range(2)]
        barrier = pltpu.get_barrier_semaphore()
        for device in net.zpeers() + net.plane():
            pl.semaphore_signal(barrier, inc=1, device_id=device, device_id_type=MESH)
        count = depth - 1 + E - 1
        for route in [r for r, _ in rows_out] + heads:
            count = count + route.hello()
        here = lambda y: s_out.at[pl.ds(pl.multiple_of(y * block, block), block)]
        mine_p = pltpu.make_async_copy(pk_ref, gp.slot(0, net.i), own.at[4])
        mine_s = pltpu.make_async_copy(st_ref, here(net.y), own.at[5])
        mine_m = pltpu.make_async_copy(
            mo_ref.at[net.i * SEQ + net.y], mo_out.at[net.z * INNER + net.i], own.at[3]
        )
        mine_c = pltpu.make_async_copy(ch_ref, ch_out.at[net.i * SEQ + net.y], own.at[6])
        mine_g = pltpu.make_async_copy(og_ref, og_out.at[gg.me], own.at[0])
        mine_w = pltpu.make_async_copy(wo_ref, gw.slot(0, net.i), own.at[1])
        for copy in (mine_p, mine_s, mine_m, mine_c, mine_g, mine_w):
            copy.start()
        pl.semaphore_wait(barrier, count)
        gp.begin()
        sends.start(st_ref, here(net.y), sy.at[0], ry.at[0], net.yp)
        for n, device in enumerate(net.plane()):
            sends.start(ch_ref, ch_out.at[net.i * SEQ + net.y], sp.at[n], rp.at[n], device)
        gw.begin()
        gp.end()
        for di in range(1, INNER):
            other = lax.rem(net.i + di, INNER)
            sends.start(
                mo_ref.at[other * SEQ + net.y],
                mo_out.at[net.z * INNER + net.i],
                sm.at[di - 1],
                rm.at[di - 1],
                net.dev(i=other),
            )
        gg.begin_y()

        def moe_ready(q):
            di = lax.rem(net.i - q + INNER, INNER)

            @pl.when(di > 0)
            def _():
                arrived(mo_out.at[net.z * INNER + q], sm.at[di - 1], rm.at[di - 1], net.xp)

        arrived(here(1 - net.y), sy.at[0], ry.at[0], net.yp)
        mine_s.wait()
        mine_p.wait()
        tail = w_full[:, QKV:].astype(F32).T
        gains[...] = tail[:8, :]

        step = 64

        def norm(n, carry):
            at = pl.ds(pl.multiple_of(n * step, step), step)
            x = s_out[at, :].astype(F32)
            scale = lax.rsqrt(jnp.mean(x * x, axis=-1, keepdims=True) + EPS)
            h1_out[at, :] = (x * scale * gains[0:1, :]).astype(BF)
            return carry

        lax.fori_loop(0, rows // step, norm, 0)
        h1 = h1_out[...]
        cos, sin = c_ref[...], n_ref[...]
        r = dot(h1, w_full[:, QCOLS:QKV])
        me = net.z * INNER + net.i
        kv_out[me, :, :HEAD] = turn(r[:, :HEAD], cos, sin).astype(BF)
        kv_out[me, :, HEAD:] = r[:, HEAD:].astype(BF)
        gk.begin()
        for h in range(0, GROUP, 2):
            r = dot(h1, w_full[:, h * HEAD : (h + 2) * HEAD])
            for g in range(2):
                v = turn(r[:, g * HEAD : (g + 1) * HEAD], cos, sin) * (SCALE * LOG2E)
                v = v.astype(BF)
                at = slice((h + g) * HEAD, (h + g + 1) * HEAD)
                qp[0, :, at] = v[:block]
                qp[1, :, at] = v[block:]
        q_refs = [
            lambda k=k: (qp.at[k], q_out.at[rows_out[k][1]], sq.at[k], rq.at[rows_out[k][1]])
            for k in range(2)
        ]
        o_refs = [
            lambda k=k: (o_out.at[k], mix_out.at[net.y], so.at[k], ro.at[net.y]) for k in range(2)
        ]
        for k in range(2):
            rows_out[k][0].send(q_refs[k])
        mine_m.wait()
        mine_w.wait()
        chain.begin(moe_ready)
        gg.begin_x()
        acc[...] = jnp.zeros_like(acc)
        top[...] = jnp.full_like(top, NEG)
        total[...] = jnp.zeros_like(total)
        gk.after_z()
        for k in range(2):
            rows_out[k][0].arrive(lambda: (q_out.at[k], sq.at[k], rq.at[k]))

        low, high = mirror.blocks()
        bases = (low * block, high * block)
        xi = lax.rem(net.i + 2, INNER)
        ci = net.i + 1 - 2 * net.core

        def attend(t, j, masked):
            start = pl.multiple_of(t * rows, rows)
            k = jnp.concatenate(
                [kv_out[t, :, :HEAD], seg_tile(start, rows, sg_ref[0:1, :], sg_ref[1:2, :])], axis=1
            )
            vt = kv_out[t, :, HEAD:].T
            if masked:
                key = start + lax.broadcasted_iota(jnp.int32, (rows, block), 0)
                ok = key <= bases[j] + lax.broadcasted_iota(jnp.int32, (rows, block), 1)
            scores = [
                dot(
                    k,
                    jnp.concatenate(
                        [q_out[j, :, h * HEAD : (h + 1) * HEAD], qs_ref[j]], axis=1
                    ),
                    NT,
                )
                for h in range(GROUP)
            ]
            for h in range(GROUP):
                s = scores[h]
                if masked:
                    s = jnp.where(ok, s, NEG)
                m0 = top[j, h : h + 1, :]
                m1 = jnp.maximum(m0, jnp.max(s, axis=0, keepdims=True))
                p = jnp.exp2(s - m1)
                f = jnp.exp2(m0 - m1)
                top[j, h : h + 1, :] = m1
                total[j, h : h + 1, :] = total[j, h : h + 1, :] * f + jnp.sum(
                    p, axis=0, keepdims=True
                )
                acc[j, h] = acc[j, h] * f + dot(vt, p.astype(BF))

        polled = min((shards - depth) // 2, 2 * INNER - 1, chain.steps)

        def tile(u, carry):
            in_z = u < depth
            in_x = u < 2 * depth
            in_c = u < 3 * depth
            dz = lax.rem(u, depth)
            place = jnp.where(in_z, net.i, jnp.where(in_x, xi, jnp.where(in_c, ci, lax.rem(ci + 2, INNER))))
            t = lax.rem(net.z - dz + depth, depth) * INNER + place

            @pl.when((u >= depth) & in_x)
            def _():
                gk.one_x(dz)

            @pl.when(u >= 2 * depth)
            def _():
                gk.one_c(u - 2 * depth, t)

            @pl.when(u == 2 * depth)
            def _():
                gg.middle()
                gw.after_z()

            @pl.when(u == 3 * depth)
            def _():
                gw.after_x()
                gg.end()

            @pl.when((u >= depth) & (lax.rem(u - depth, 2) == 1) & (u - depth < 2 * polled))
            def _():
                chain.step(lax.div(u - depth, 2))

            for j in (0, 1):
                live = t * rows <= bases[j] + block - 1
                free = t * rows + rows - 1 <= bases[j]

                @pl.when(live & free)
                def _():
                    attend(t, j, False)

                @pl.when(live & jnp.logical_not(free))
                def _():
                    attend(t, j, True)

            return carry

        lax.fori_loop(0, shards, tile, 0)
        gk.sent_loop()
        for j in range(2):
            for h in range(GROUP):
                o_out[j, :, h * HEAD : (h + 1) * HEAD] = (
                    (acc[j, h] / total[j, h : h + 1, :]).T.astype(BF)
                )
        for k in range(2):
            heads[k].send(o_refs[k])
        chain.run(polled, polled + 1)
        m_out[...] = top[...]
        l_out[...] = total[...]
        gw.last()
        gg.last()
        for k in range(2):
            heads[k].arrive(lambda: (mix_out.at[k], so.at[k], ro.at[k]))
        x1 = here(net.y)[...].astype(F32)
        x1 = x1 + dot(mix_out[0], wf_out[:QCOLS, :]) + dot(mix_out[1], wf_out[QCOLS:, :])
        x1_out[...] = x1
        scale = lax.rsqrt(jnp.mean(x1 * x1, axis=-1, keepdims=True) + EPS)
        h2_own[...] = (x1 * scale * gains[1:2, :]).astype(BF)
        mine_h = pltpu.make_async_copy(h2_own, h2_out.at[gh.me], own.at[2])
        gh.begin()
        mine_h.start()
        chain.run(polled + 1, 2 * INNER)
        gh.middle()
        chain.run(2 * INNER, 2 * INNER + 2)
        gh.end()
        chain.run(2 * INNER + 2, chain.steps)
        n = 0
        for di in range(INNER):
            for dy in range(SEQ):
                if di or dy:
                    frm = lax.rem(net.i - di + INNER, INNER) * SEQ + lax.rem(net.y + dy, SEQ)
                    arrived(ch_out.at[frm], sp.at[n], rp.at[n], net.yp)
                    n += 1
        mine_c.wait()
        gh.last()
        for k in range(2):
            rows_out[k][0].sent(q_refs[k])
            heads[k].sent(o_refs[k])
        chain.finish()
        sends.finish()
        mine_g.wait()
        mine_h.wait()

    sds = jax.ShapeDtypeStruct
    stat = sds((2, 8, block), F32)
    heads_shape = sds((2, block, QCOLS), BF)
    return pl.pallas_call(
        kernel,
        out_shape=(
            sds((rows, WIDTH), BF),
            sds((WIDTH, FIRST), BF),
            sds((E,) + chosen.shape, F32),
            sds((rows, WIDTH), BF),
            heads_shape,
            sds((shards, rows, 2 * HEAD), BF),
            heads_shape,
            stat,
            stat,
            heads_shape,
            sds((block, WIDTH), F32),
            sds((E, block, WIDTH), BF),
            sds((WIDTH, WIDTH), BF),
            sds((E, block, WIDTH), BF),
            sds((shards,) + moe.shape[1:], BF),
        ),
        in_specs=[hbm()] * 4 + [vmem()] * 2 + [hbm()] * 2 + [vmem()] * 2,
        out_specs=(vmem(), vmem(), hbm()) + (vmem(),) * 8 + (hbm(), vmem(), hbm(), hbm()),
        scratch_shapes=[
            pltpu.VMEM((2, block, QCOLS), BF),
            pltpu.VMEM((2, GROUP, HEAD, block), F32),
            pltpu.VMEM((2, 8, block), F32),
            pltpu.VMEM((2, 8, block), F32),
            pltpu.VMEM((block, WIDTH), BF),
            pltpu.VMEM((8, WIDTH), F32),
        ]
        + dma_sems(7, 2, 2, 2, 2, 1, 1, E - 1, E - 1, INNER - 1, INNER - 1)
        + ShardGather.sems(depth) * 2
        + PlaneGather.sems() * 2
        + Chain.sems(depth)
        + ShardGather.sems(depth),
        compiler_params=comm_params(7, 60 << 20),
        name="front",
    )(stream, pack, moe, chosen, cosine, sine, w_out, out_grad, qseg, starts)


class Tally:
    def __init__(self, net, part, rows, scratch):
        self.net, self.part, self.rows = net, part, rows
        self.bc, self.sx, self.bx, self.sz, self.bz = scratch[:5]
        self.ssc, self.rsc, self.ssx, self.rsx, self.ssz, self.rsz = scratch[5:]
        self.chunk = chunk_of(rows)

    def number(self, dz, fx, core):
        x = jnp.where(fx == 1, 1 - self.net.x, self.net.x)
        return lax.rem(self.net.z + dz, self.net.depth) * INNER + x * 2 + core

    def core_copy(self, dz, fx):
        net, n = self.net, dz * 2 + fx
        src = self.part.at[self.number(dz, fx, 1 - net.core)]
        return remote(src, self.bc.at[n], self.ssc.at[n], self.rsc.at[n], net.cp)

    def x_copy(self, dz):
        return remote(
            self.sx.at[dz], self.bx.at[dz], self.ssx.at[dz], self.rsx.at[dz], self.net.xp
        )

    def z_copy(self, dz):
        n = dz - 1
        device = self.net.dev(z=lax.rem(self.net.z + dz, self.net.depth))
        return remote(self.sz.at[n], self.bz.at[n], self.ssz.at[n], self.rsz.at[n], device)

    def terms(self, dz, fx):
        n = dz * 2 + fx
        arrived(self.bc.at[n], self.ssc.at[n], self.rsc.at[n], self.net.cp)
        return [self.part.at[self.number(dz, fx, self.net.core)], self.bc.at[n]]

    def x_stage(self, dz):
        add_into(self.sx.at[dz], self.terms(dz, 1), self.rows, self.chunk)
        self.x_copy(dz).start()

    def x_terms(self, dz):
        terms = self.terms(dz, 0)
        arrived(self.bx.at[dz], self.ssx.at[dz], self.rsx.at[dz], self.net.xp)
        return terms + [self.bx.at[dz]]

    def z_stage(self, dz):
        add_into(self.sz.at[dz - 1], self.x_terms(dz), self.rows, self.chunk)
        self.z_copy(dz).start()

    def final(self, out):
        terms = self.x_terms(0)
        for n in range(self.net.depth - 1):
            arrived(self.bz.at[n], self.ssz.at[n], self.rsz.at[n], self.net.xp)
            terms.append(self.bz.at[n])
        add_into(out, terms, self.rows, self.chunk)

    def finish(self):
        for dz in range(self.net.depth):
            for fx in range(2):
                self.core_copy(dz, fx).wait_send()
            self.x_copy(dz).wait_send()
            if dz:
                self.z_copy(dz).wait_send()

    def far(self):
        return [d for d in range(1, self.net.depth)] + [0]

    def begin(self):
        for dz in self.far():
            for fx in (1, 0):
                self.core_copy(dz, fx).start()

    def far_stages(self):
        for dz in self.far():
            self.x_stage(dz)

    def near_stages(self):
        for dz in self.far()[:-1]:
            self.z_stage(dz)


def backward(q, kv, qseg, starts, m, l, ob, mixed, dx1, out_w, part_rows, depth):
    block = q.shape[1]
    rows = kv.shape[1]
    shards = depth * INNER

    def kernel(
        q_ref, kv_ref, qs_ref, sg_ref, m_ref, l_ref, ob_ref, mix_ref, dx_ref, wf_ref,
        dq_out, dkv_out, own_out,
        dob, do_ref, da, dl, acc, dqs, dkv, wpart, so, ro, sq, rq, *scratch,
    ):
        net = Net(depth)
        mirror = Mirror(net)
        keys = Tally(net, dkv, rows, scratch[:11])
        outs = Tally(net, wpart, part_rows, scratch[11:])
        heads = [mirror.heads_out(k) for k in range(2)]
        backs = [mirror.rows_back(k) for k in range(2)]
        barrier = pltpu.get_barrier_semaphore()
        for device in net.zpeers() + [net.xp, net.cp]:
            pl.semaphore_signal(barrier, inc=1, device_id=device, device_id_type=MESH)
        count = depth - 1 + 2
        for route, _ in heads + backs:
            count = count + route.hello()
        do_refs = [
            lambda k=k: (dob.at[k], do_ref.at[heads[k][1]], so.at[k], ro.at[heads[k][1]])
            for k in range(2)
        ]
        dq_refs = [
            lambda k=k: (dqs.at[k], dq_out.at[backs[k][1]], sq.at[k], rq.at[backs[k][1]])
            for k in range(2)
        ]
        dx = dx_ref[...]
        for k in range(2):
            dob[k] = dot(dx, wf_ref[k * QCOLS : (k + 1) * QCOLS, :], NT).astype(BF)
        pl.semaphore_wait(barrier, count)
        for k in range(2):
            heads[k][0].send(do_refs[k])
        wide = QCOLS // 2
        for n in range(4):
            cols = slice((n % 2) * wide, (n % 2 + 1) * wide)
            grad = dot(mix_ref[n // 2, :, cols].T, dx).astype(BF)
            for b in range(wide // part_rows):
                wpart[n * (wide // part_rows) + b] = grad[b * part_rows : (b + 1) * part_rows]
        outs.begin()
        acc[...] = jnp.zeros_like(acc)
        for k in range(2):
            heads[k][0].arrive(lambda: (do_ref.at[k], so.at[k], ro.at[k]))
        for j in range(2):
            for h in range(GROUP):
                c = slice(h * HEAD, (h + 1) * HEAD)
                d = do_ref[j, :, c].astype(F32)
                o = ob_ref[j, :, c].astype(F32)
                inv = 1.0 / l_ref[j, h : h + 1, :]
                da[j, h] = (d.T * inv).T.astype(BF)
                dl[j, h : h + 1, :] = -jnp.sum((d * o).T, axis=0, keepdims=True) * inv
        low, high = mirror.blocks()
        bases = (low * block, high * block)

        def piece(t, j, masked):
            start = pl.multiple_of(t * rows, rows)
            k = kv_ref[t, :, :HEAD]
            v = kv_ref[t, :, HEAD:]
            kt = k.T
            k_seg = jnp.concatenate(
                [k, seg_tile(start, rows, sg_ref[0:1, :], sg_ref[1:2, :])], axis=1
            )
            if masked:
                key = start + lax.broadcasted_iota(jnp.int32, (rows, block), 0)
                ok = key <= bases[j] + lax.broadcasted_iota(jnp.int32, (rows, block), 1)
            dk = dv = None
            for h in range(GROUP):
                qh = q_ref[j, :, h * HEAD : (h + 1) * HEAD]
                s = dot(k_seg, jnp.concatenate([qh, qs_ref[j]], axis=1), NT)
                s = s - m_ref[j, h : h + 1, :]
                if masked:
                    s = jnp.where(ok, s, NEG)
                p = jnp.exp2(s)
                dah = da[j, h]
                dvh = dot(p.astype(BF), dah)
                dp = dot(v, dah, NT) + dl[j, h : h + 1, :]
                ds = (p * dp).astype(BF)
                dkh = dot(ds, qh)
                acc[j, h] += dot(kt, ds)
                dk = dkh if dk is None else dk + dkh
                dv = dvh if dv is None else dv + dvh
            return dk * LN2, dv

        def tile(u, carry):
            g, r = lax.div(u, INNER), lax.rem(u, INNER)
            dz = lax.rem(g + 1, depth)
            fx = 1 - lax.div(r, 2)
            other = lax.rem(r, 2) == 0
            t = keys.number(dz, fx, jnp.where(other, 1 - net.core, net.core))

            def put(j, masked):
                dk, dv = piece(t, j, masked)
                if j == 0:
                    dk = dk + dkv[t, :, :HEAD].astype(F32)
                    dv = dv + dkv[t, :, HEAD:].astype(F32)
                dkv[t, :, :HEAD] = dk.astype(BF)
                dkv[t, :, HEAD:] = dv.astype(BF)

            for j in (1, 0):
                live = t * rows <= bases[j] + block - 1
                free = t * rows + rows - 1 <= bases[j]
                if j == 1:

                    @pl.when(jnp.logical_not(live))
                    def _():
                        dkv[t] = jnp.zeros((rows, 2 * HEAD), BF)

                @pl.when(live & free)
                def _():
                    put(j, False)

                @pl.when(live & jnp.logical_not(free))
                def _():
                    put(j, True)

            @pl.when(other)
            def _():
                keys.core_copy(dz, fx).start()

            @pl.when(r == INNER - 1)
            def _():
                keys.x_stage(dz)

            @pl.when((r == INNER - 1) & (g > 0))
            def _():
                keys.z_stage(g)

            @pl.when(u == 2)
            def _():
                outs.far_stages()

            @pl.when(u == shards - INNER)
            def _():
                outs.near_stages()

            return carry

        lax.fori_loop(0, shards, tile, 0)
        for j in range(2):
            for h in range(GROUP):
                dqs[j, :, h * HEAD : (h + 1) * HEAD] = (acc[j, h] * SCALE).T.astype(BF)
        for k in range(2):
            backs[k][0].send(dq_refs[k])
        outs.final(own_out)
        keys.final(dkv_out)
        for k in range(2):
            backs[k][0].arrive(lambda: (dq_out.at[k], sq.at[k], rq.at[k]))
        for k in range(2):
            heads[k][0].sent(do_refs[k])
            backs[k][0].sent(dq_refs[k])
        outs.finish()
        keys.finish()

    sds = jax.ShapeDtypeStruct
    pair = (2, block, QCOLS)
    return pl.pallas_call(
        kernel,
        out_shape=(
            sds(pair, BF),
            sds((rows, 2 * HEAD), F32),
            sds((part_rows, WIDTH), F32),
        ),
        in_specs=[vmem()] * 10,
        out_specs=(vmem(),) * 3,
        scratch_shapes=[
            pltpu.VMEM(pair, BF),
            pltpu.VMEM(pair, BF),
            pltpu.VMEM((2, GROUP, block, HEAD), BF),
            pltpu.VMEM((2, 8, block), F32),
            pltpu.VMEM((2, GROUP, HEAD, block), F32),
            pltpu.VMEM(pair, BF),
            pltpu.VMEM((shards, rows, 2 * HEAD), BF),
            pltpu.VMEM((shards, part_rows, WIDTH), BF),
        ]
        + dma_sems(2, 2, 2, 2)
        + ShardScatter.scratch(depth, rows, 2 * HEAD)
        + ShardScatter.scratch(depth, part_rows, WIDTH),
        compiler_params=comm_params(8, 60 << 20),
        name="backward",
    )(q, kv, qseg, starts, m, l, ob, mixed, dx1, out_w)


def finish_layer(dq, dkv, cosine, sine, h1, weights, pair, small, dx1, gain_a, out_own, moe, depth):
    block = dx1.shape[0]
    rows = pair.shape[0]
    shards = depth * INNER
    part_rows = out_own.shape[0]
    wide = 384

    def kernel(
        dq_ref, dkv_ref, c_ref, n_ref, h1_ref, w_ref, s_ref, sm_ref, dx_ref, ga_ref, oo_ref, moe_ref,
        sg_out, own_out, pair_out, pair_wo, moe_out,
        raw, part, give, take, low, low_wo, sm, rm, sy, ry, ls, *scratch,
    ):
        net = Net(depth)
        sends = Sends()
        me = net.i * SEQ + net.y
        mine = pltpu.make_async_copy(moe_ref.at[net.i], moe_out.at[me], ls.at[0])
        work = Tally(net, part, part_rows, scratch)
        barrier = pltpu.get_barrier_semaphore()
        for device in net.zpeers() + net.plane():
            pl.semaphore_signal(barrier, inc=1, device_id=device, device_id_type=MESH)
        cos, sin = c_ref[...], -n_ref[...]
        for k in range(2):
            at = slice(k * block, (k + 1) * block)
            for h in range(GROUP):
                cols = slice(h * HEAD, (h + 1) * HEAD)
                v = dq_ref[k, :, cols].astype(F32)
                raw[at, cols] = turn(v, cos[at], sin[at]).astype(BF)
        dk = dkv_ref[:, :HEAD].astype(BF).astype(F32)
        raw[:, QCOLS : QCOLS + HEAD] = turn(dk, cos, sin).astype(BF)
        raw[:, QCOLS + HEAD :] = dkv_ref[:, HEAD:].astype(BF)
        pl.semaphore_wait(barrier, depth - 1 + E - 1)
        low_wo[...] = oo_ref[...].astype(BF)
        sends.start(low_wo, pair_wo, sy.at[1], ry.at[1], net.yp)

        def half(y):
            at = pl.ds(pl.multiple_of(y * block, block), block)
            x = s_ref[at, :].astype(F32)
            scale = lax.rsqrt(jnp.mean(x * x, axis=-1, keepdims=True) + EPS)
            grad = dot(raw[at, :], w_ref[:, :QKV], NT)
            return x * scale, scale, grad

        normed, _, grad = half(1 - net.y)
        give[...] = grad.astype(BF)
        sends.start(give, take, sy.at[2], ry.at[2], net.yp)
        gain_part = jnp.sum(grad * normed, axis=0, keepdims=True)
        n = 0
        for di in range(INNER):
            for dy in range(SEQ):
                if di or dy:
                    i = lax.rem(net.i + di, INNER)
                    device = net.dev(i=i, y=lax.rem(net.y + dy, SEQ))
                    sends.start(moe_ref.at[i], moe_out.at[me], sm.at[n], rm.at[n], device)
                    n += 1
        mine.start()
        normed, scale, grad = half(net.y)
        gain_part = gain_part + jnp.sum(grad * normed, axis=0, keepdims=True)
        lanes = lax.broadcasted_iota(jnp.int32, (EXTRA, WIDTH), 0)
        extra = jnp.where(lanes == 0, gain_part, sm_ref[...]).T.astype(BF)
        per = wide // part_rows
        for c in range(WIDTH // wide):
            g = dot(h1_ref[:, c * wide : (c + 1) * wide].T, raw[...]).astype(BF)
            for b in range(per):
                part[c * per + b, :, :QKV] = g[b * part_rows : (b + 1) * part_rows]
                part[c * per + b, :, QKV:] = extra[
                    c * wide + b * part_rows : c * wide + (b + 1) * part_rows
                ]
        work.begin()
        work.far_stages()
        arrived(take, sy.at[2], ry.at[2], net.yp)
        inner = (grad + take[...].astype(F32)) * ga_ref[...]
        pull = scale * (inner - normed * jnp.mean(inner * normed, axis=-1, keepdims=True))
        sg_out[...] = (dx_ref[...] + pull).astype(BF)
        work.near_stages()
        work.final(own_out)
        low[...] = own_out[...].astype(BF)
        sends.start(low, pair_out, sy.at[0], ry.at[0], net.yp)
        n = 0
        for di in range(INNER):
            for dy in range(SEQ):
                if di or dy:
                    frm = lax.rem(net.i - di + INNER, INNER) * SEQ + lax.rem(net.y + dy, SEQ)
                    arrived(moe_out.at[frm], sm.at[n], rm.at[n], net.yp)
                    n += 1
        arrived(pair_wo, sy.at[1], ry.at[1], net.yp)
        arrived(pair_out, sy.at[0], ry.at[0], net.yp)
        sends.finish()
        work.finish()
        mine.wait()

    sds = jax.ShapeDtypeStruct
    return pl.pallas_call(
        kernel,
        out_shape=(
            sds((block, WIDTH), BF),
            sds((part_rows, FIRST), F32),
            sds((part_rows, FIRST), BF),
            sds((part_rows, WIDTH), BF),
            sds((E,) + moe.shape[1:], BF),
        ),
        in_specs=[vmem()] * 11 + [hbm()],
        out_specs=(vmem(),) * 4 + (hbm(),),
        scratch_shapes=[
            pltpu.VMEM((rows, QKV), BF),
            pltpu.VMEM((shards, part_rows, FIRST), BF),
            pltpu.VMEM((block, WIDTH), BF),
            pltpu.VMEM((block, WIDTH), BF),
            pltpu.VMEM((part_rows, FIRST), BF),
            pltpu.VMEM((part_rows, WIDTH), BF),
        ]
        + dma_sems(E - 1, E - 1, 3, 3, 1)
        + ShardScatter.scratch(depth, part_rows, FIRST),
        compiler_params=comm_params(9, 60 << 20),
        name="finish_layer",
    )(dq, dkv, cosine, sine, h1, weights, pair, small, dx1, gain_a, out_own, moe)


def rms_parts(x):
    scale = lax.rsqrt(jnp.mean(x * x, axis=-1, keepdims=True) + EPS)
    return x * scale, scale


def rms_pull(normed, scale, grad, gain):
    inner = grad * gain
    return scale * (inner - normed * jnp.mean(inner * normed, axis=-1, keepdims=True))


def document_first(index, starts):
    return jnp.max(jnp.where(starts <= index[..., None], starts, 0), axis=-1)


def gelu_product(gate_pre, up_pre):
    return jax.nn.gelu(gate_pre, approximate=False) * up_pre


class Zigzag:
    def __init__(self, shards):
        last = 2 * shards - 1
        home = lambda b: b if b < shards else last - b
        self.rows = [
            [(s * 2 + y, home(2 * s + k) * 2 + y) for s in range(shards) for y in range(2)]
            for k in range(2)
        ]
        self.heads = [
            [
                (s * 2 + g, s if (g == 0) == (k == 0) else last - s)
                for s in range(shards)
                for g in range(2)
            ]
            for k in range(2)
        ]

    @staticmethod
    def move(x, pairs, back=False):
        return lax.ppermute(x, AXES, [(b, a) for a, b in pairs] if back else pairs)


def pick(flag, a, b):
    return jnp.where(flag, a, b), jnp.where(flag, b, a)


def experts(h2, out_grad, chosen, router_w, moe_w, rows_in, rows_out, me):
    blocks, tokens = h2.shape[:2]
    logits = dot(h2.reshape(blocks * tokens, WIDTH), router_w)
    probs = jax.nn.softmax(logits, axis=-1)
    mine = (jnp.arange(E) == me).astype(F32)
    named = jnp.sum(chosen * mine[None, :, None], axis=1)
    gate_tok = jnp.sum(probs * mine[None, :], axis=-1).reshape(blocks, tokens) * named
    upper = (jnp.arange(tokens)[:, None] <= jnp.arange(tokens)[None, :]).astype(BF)
    rank = dot(named.astype(BF), upper) - 1.0
    pick_slot = (
        rank[:, None, :] == jnp.arange(MOST, dtype=F32)[None, :, None]
    ) & (named[:, None, :] > 0.5)
    onehot = pick_slot.astype(BF)
    slots = blocks * MOST
    gate = jnp.sum(jnp.where(pick_slot, gate_tok[:, None, :], 0.0), axis=-1).reshape(slots, 1)
    spread = lambda v: lax.dot_general(
        onehot, v, (((2,), (1,)), ((0,), (0,))), preferred_element_type=F32
    )
    collect = lambda v: lax.dot_general(
        onehot, v, (((1,), (1,)), ((0,), (0,))), preferred_element_type=F32
    )
    rows = spread(h2).astype(BF).reshape(slots, WIDTH)
    slot_grad = spread(out_grad).astype(BF).reshape(slots, WIDTH)
    gate_w = moe_w[:, :rows_in, :FF].reshape(WIDTH, FF)
    up_w = moe_w[:, :rows_in, FF:].reshape(WIDTH, FF)
    down_w = moe_w[:, rows_in:, :].reshape(FF, WIDTH)
    gate_pre = dot(rows, gate_w)
    up_pre = dot(rows, up_w)
    active_f, pull = jax.vjp(gelu_product, gate_pre, up_pre)
    active = active_f.astype(BF)
    out = dot(active, down_w)
    slot_gf = slot_grad.astype(F32)
    gate_grad = jnp.sum(slot_gf * out, axis=-1).reshape(blocks, MOST)
    mixture = collect((out * gate).astype(BF).reshape(blocks, MOST, WIDTH)).astype(BF)
    expert_grad = (slot_gf * gate).astype(BF)
    active_grad = dot(expert_grad, down_w, NT)
    g_low, u_low = (v.astype(BF) for v in pull(active_grad))
    back = dot(g_low, gate_w, NT) + dot(u_low, up_w, NT)
    back_tok = collect(back.astype(BF).reshape(blocks, MOST, WIDTH)).astype(BF)
    gate_back = jnp.sum(jnp.where(pick_slot, gate_grad[:, :, None], 0.0), axis=1)
    lanes = (jnp.arange(EXTRA) == me).astype(F32)
    back_tok = jnp.concatenate(
        [back_tok, (gate_back[:, :, None] * lanes[None, None, :]).astype(BF)], axis=-1
    )
    shards = WIDTH // rows_in
    grads = jnp.concatenate(
        [
            jnp.concatenate(
                [
                    dot(rows, g_low, TN).astype(BF).reshape(shards, rows_in, FF),
                    dot(rows, u_low, TN).astype(BF).reshape(shards, rows_in, FF),
                ],
                axis=-1,
            ),
            dot(active, expert_grad, TN).astype(BF).reshape(shards, rows_out, WIDTH),
        ],
        axis=1,
    )
    return mixture, back_tok, grads


def back_apart(zig, q, kv, lo, info, top, total, ob, mixed, dx1, out_w, part_rows, depth):
    z, i, y = (lax.axis_index(a) for a in AXES)
    shards, rows = kv.shape[:2]
    shard = z * INNER + i
    even, head_zero = lax.rem(shard, 2) == 0, y == 0
    dob = dot(dx1, out_w, NT).astype(BF)
    out_part = dot(mixed, dx1, TN).astype(BF).reshape(shards, part_rows, WIDTH)
    out_own = scatter_keys(out_part, depth, 10)
    dob_a, dob_b = pick(shard * SEQ + y < shards, dob[:, :QCOLS], dob[:, QCOLS:])
    dob_zig = jnp.stack(
        pick(
            head_zero,
            zig.move(dob_a, zig.heads[0], True),
            zig.move(dob_b, zig.heads[1], True),
        )
    )
    flat = kv.reshape(shards * rows, 2 * HEAD)
    dq, dkv_part = attend_backward(q, flat, lo, info, top, total, dob_zig, ob)
    dq_a, dq_b = pick(even, dq[0], dq[1])
    dq_pair = jnp.stack([zig.move(dq_a, zig.rows[0], True), zig.move(dq_b, zig.rows[1], True)])
    return dq_pair, scatter_keys(dkv_part.reshape(kv.shape), depth, 5), out_own


def local(depth, stream, doc_starts, routes, attn_gain, w_query, w_key, w_value, w_out, ffn_gain, w_router, w_gate, w_up, w_down, out_grad):
    tokens = stream.shape[0]
    rows_in, rows_out = w_gate.shape[1], w_down.shape[1]
    shards = depth * INNER
    z, i, y = (lax.axis_index(a) for a in AXES)
    shard = z * INNER + i
    me = i * SEQ + y
    zig = Zigzag(shards)

    cut = lambda w, width: lax.dynamic_slice_in_dim(w, y * width, width, 1)
    extra = jnp.concatenate(
        [
            attn_gain[:, None],
            ffn_gain[:, None],
            w_router,
            jnp.zeros((rows_in, EXTRA - 2 - E), BF),
        ],
        axis=1,
    )
    pack = jnp.concatenate(
        [cut(w_query, QCOLS), cut(w_key, HEAD), cut(w_value, HEAD), extra], axis=1
    )
    moe_pack = jnp.concatenate([jnp.concatenate([w_gate, w_up], axis=2), w_down], axis=1)
    chosen_t = jnp.any(
        routes.T[:, None, :] == jnp.arange(E, dtype=jnp.int32)[None, :, None], axis=0
    ).astype(F32)
    pair_index = shard * SEQ * tokens + jnp.arange(SEQ * tokens, dtype=jnp.int32)
    position = pair_index - document_first(pair_index, doc_starts)
    freq = ROPE_BASE ** (-(jnp.arange(HEAD // 2, dtype=F32) * 2.0) / HEAD)
    angle = position.astype(F32)[:, None] * freq[None, :]
    cos_half, sin_half = jnp.cos(angle), jnp.sin(angle)
    cosine = jnp.concatenate([cos_half, cos_half], axis=1)
    sine = jnp.concatenate([-sin_half, sin_half], axis=1)

    block_ids = jnp.stack([shard, 2 * shards - 1 - shard]).astype(jnp.int32)
    query_index = block_ids[:, None] * tokens + jnp.arange(tokens, dtype=jnp.int32)[None, :]
    lo = document_first(query_index, doc_starts).astype(jnp.int32)
    info = jnp.concatenate([block_ids, lo[:, 0], lo[:, -1], jnp.zeros((2,), jnp.int32)])
    big = jnp.int32(1 << 30)
    spare = jnp.full((HEAD - doc_starts.shape[0],), big)
    first = jnp.concatenate([doc_starts, spare])
    beyond = jnp.concatenate([doc_starts[1:], spare, big[None]])
    starts = jnp.stack([first, beyond])
    outside = (query_index[..., None] < first) | (query_index[..., None] >= beyond)
    qseg = jnp.where(outside, NEG, 0.0).astype(BF)
    lo = lo[:, None, :]
    (
        pair, weights, chosen_all, h1, q, kv, ob, top, total, mixed, x1, h2_plane, out_w, grad_plane, moe_w,
    ) = front(stream, pack, moe_pack, chosen_t, cosine, sine, w_out, out_grad, qseg, starts, depth)
    extra_w = weights[:, QKV : QKV + EXTRA]
    gains = extra_w[:, :2].astype(F32).T
    gain_a, gain_f = gains[0:1], gains[1:2]
    router_w = extra_w[:, 2 : 2 + E]
    qkv_w = weights[:, :QKV]
    head_zero = y == 0
    mixed_pair = mixed
    mixed = jnp.concatenate([mixed[0], mixed[1]], axis=1)
    normed, scale = rms_parts(x1)
    h2 = (normed * gain_f).astype(BF)

    mixture_part, back_part, moe_grads = experts(
        h2_plane, grad_plane, chosen_all, router_w, moe_w, rows_in, rows_out, me
    )
    back = scatter_plane(back_part, depth)
    mixture = lax.psum_scatter(mixture_part, ("inner", "seq"), scatter_dimension=0, tiled=False)
    moe_own = lax.psum_scatter(
        moe_grads.reshape(depth, INNER, rows_in + rows_out, WIDTH),
        "outer",
        scatter_dimension=0,
        tiled=False,
    )
    result = (x1 + mixture.astype(F32)).astype(BF)

    chosen = chosen_t.T
    probs = jax.nn.softmax(dot(h2, router_w), axis=-1)
    dp = back[:, WIDTH : WIDTH + E] * chosen
    dz = (probs * (dp - jnp.sum(dp * probs, axis=-1, keepdims=True))).astype(BF)
    router_part = dot(dz, h2, TN)
    dh2 = back[:, :WIDTH] + dot(dz, router_w, NT)
    grad_f = out_grad.astype(F32)
    dx1 = grad_f + rms_pull(normed, scale, dh2, gain_f)
    gain_f_part = jnp.sum(dh2 * normed, axis=0)
    dx1_low = dx1.astype(BF)
    if depth <= 4:
        dq_pair, dkv, out_own = backward(
            q, kv, qseg, starts, top, total, ob, mixed_pair, dx1_low, out_w, rows_in, depth
        )
    else:
        dq_pair, dkv, out_own = back_apart(
            zig, q, kv, lo, info, top, total, ob, mixed, dx1_low, out_w, rows_in, depth
        )
    small = jnp.concatenate(
        [
            jnp.zeros((1, WIDTH), F32),
            gain_f_part[None, :],
            router_part,
            jnp.zeros((EXTRA - 2 - E, WIDTH), F32),
        ],
        axis=0,
    )
    stream_grad, own, peer, peer_out, moe_out = finish_layer(
        dq_pair, dkv, cosine, sine, h1, weights, pair, small, dx1, gain_a, out_own, moe_own, depth
    )
    peer = peer.astype(F32)

    def halves(a, b):
        return jnp.concatenate(pick(head_zero, own[:, a:b], peer[:, a:b]), axis=1)

    both = own[:, QKV:] + peer[:, QKV:]
    moe_out = moe_out.astype(F32)
    return (
        result,
        stream_grad,
        both[:, 0],
        halves(0, QCOLS),
        halves(QCOLS, QCOLS + HEAD),
        halves(QCOLS + HEAD, QKV),
        out_own + peer_out.astype(F32),
        both[:, 1],
        both[:, 2 : 2 + E],
        moe_out[:, :rows_in, :FF],
        moe_out[:, :rows_in, FF:],
        moe_out[:, rows_in:, :],
    )


def solution(mesh):
    shards = mesh.shape["shard"]
    depth = shards // INNER
    fine = Mesh(mesh.devices.reshape(depth, INNER, SEQ), AXES)
    shard = ("outer", "inner")
    tokens = P(AXES, None)
    in_specs = (
        tokens,
        P(),
        tokens,
        P(shard),
        P(shard, None),
        P(shard, None),
        P(shard, None),
        P(shard, None),
        P(shard),
        P(shard, None),
        P(None, shard, None),
        P(None, shard, None),
        P(None, shard, None),
        tokens,
    )
    out_specs = (
        tokens,
        tokens,
        P(shard),
        P(shard, None),
        P(shard, None),
        P(shard, None),
        P(shard, None),
        P(shard),
        P(shard, None),
        P(None, shard, None),
        P(None, shard, None),
        P(None, shard, None),
    )

    def run(*args):
        return local(depth, *args)

    return jax.shard_map(run, mesh=fine, in_specs=in_specs, out_specs=out_specs, check_vma=False)
```

```python
import jax
import jax.numpy as jnp
from jax import lax
from jax.experimental import pallas as pl
from jax.experimental.pallas import tpu as pltpu
from jax.sharding import Mesh, PartitionSpec as P

WIDTH = 1536
HEADS = 12
KV_HEADS = 2
HEAD = 128
FF = 768
E = 8
MOST = 192
SEQ = KV_HEADS
GROUP = HEADS // KV_HEADS
INNER = E // SEQ
QCOLS = GROUP * HEAD
QKV = QCOLS + 2 * HEAD
EXTRA = 128
FIRST = QKV + EXTRA
PACK = QKV + EXTRA + WIDTH
EPS = 1e-06
ROPE_BASE = 10000.0
SCALE = HEAD**-0.5
LOG2E = 1.4426950408889634
LN2 = 0.6931471805599453
NEG = -1e30
AXES = ("outer", "inner", "seq")
MESH = pl.DeviceIdType.MESH
NN = (((1,), (0,)), ((), ()))
NT = (((1,), (1,)), ((), ()))
TN = (((0,), (0,)), ((), ()))
BF = jnp.bfloat16
F32 = jnp.float32


def dot(a, b, dims=NN):
    return lax.dot_general(a, b, dims, preferred_element_type=F32)


class Net:
    def __init__(self, depth):
        self.depth = depth
        self.z = lax.axis_index("outer")
        self.i = lax.axis_index("inner")
        self.y = lax.axis_index("seq")
        self.core = lax.rem(self.i, 2)
        self.x = lax.div(self.i, 2)
        self.xp = self.dev(i=lax.rem(self.i + 2, INNER))
        self.cp = self.dev(i=self.i + 1 - 2 * self.core)
        self.yp = self.dev(y=1 - self.y)

    def dev(self, z=None, i=None, y=None):
        return {
            "outer": self.z if z is None else z,
            "inner": self.i if i is None else i,
            "seq": self.y if y is None else y,
        }

    def zoff(self, dz):
        return lax.rem(self.z + dz, self.depth)

    def zpeers(self):
        return [self.dev(z=self.zoff(dz)) for dz in range(1, self.depth)]

    def plane(self):
        out = []
        for di in range(INNER):
            for dy in range(SEQ):
                if di or dy:
                    out.append(
                        self.dev(i=lax.rem(self.i + di, INNER), y=lax.rem(self.y + dy, SEQ))
                    )
        return out


def greet(devices):
    barrier = pltpu.get_barrier_semaphore()
    for device in devices:
        pl.semaphore_signal(barrier, inc=1, device_id=device, device_id_type=MESH)
    pl.semaphore_wait(barrier, len(devices))


def remote(src, dst, ssem, rsem, device):
    return pltpu.make_async_remote_copy(
        src_ref=src, dst_ref=dst, send_sem=ssem, recv_sem=rsem, device_id=device, device_id_type=MESH
    )


class Sends:
    def __init__(self):
        self.items = []

    def start(self, *refs):
        self.later(lambda: refs)

    def later(self, refs):
        remote(*refs()).start()
        self.items.append(refs)

    def finish(self):
        for refs in self.items:
            remote(*refs()).wait_send()


def arrived(dst, ssem, rsem, device):
    remote(dst, dst, ssem, rsem, device).wait_recv()


def dma_sems(*counts):
    return [pltpu.SemaphoreType.DMA((n,)) for n in counts]


class FlatSlots:
    class At:
        def __init__(self, ref, rows):
            self.ref, self.rows = ref, rows

        def __getitem__(self, n):
            return self.ref.at[pl.ds(pl.multiple_of(n * self.rows, self.rows), self.rows)]

    def __init__(self, ref, rows):
        self.at = self.At(ref, rows)


class ShardGather:
    def __init__(self, net, sends, src, out, sems):
        self.net, self.sends, self.src, self.out = net, sends, src, out
        self.sz, self.rz, self.sx, self.rx, self.sc, self.rc = sems
        self.xi = lax.rem(net.i + 2, INNER)

    @staticmethod
    def sems(depth):
        return dma_sems(*([max(depth - 1, 1)] * 2 + [depth] * 2 + [2 * depth] * 2))

    def slot(self, dz, i):
        return self.out.at[lax.rem(self.net.z - dz + self.net.depth, self.net.depth) * INNER + i]

    def begin(self):
        net, me = self.net, self.slot(0, self.net.i)
        for n, device in enumerate(net.zpeers()):
            self.sends.start(self.src, me, self.sz.at[n], self.rz.at[n], device)
        self.sends.start(self.src, me, self.sx.at[0], self.rx.at[0], net.xp)
        self.sends.start(self.src, me, self.sc.at[0], self.rc.at[0], net.cp)

    def pass_on(self, dz, i, ssem, rsem, n, device):
        self.sends.later(
            lambda: (self.slot(dz, i), self.slot(dz, i), ssem.at[n], rsem.at[n], device)
        )

    def after_z(self):
        net = self.net
        for dz in range(1, net.depth):
            block = self.slot(dz, net.i)
            arrived(block, self.sz.at[dz - 1], self.rz.at[dz - 1], net.xp)
            self.pass_on(dz, net.i, self.sx, self.rx, dz, net.xp)
            self.pass_on(dz, net.i, self.sc, self.rc, dz, net.cp)

    def after_x(self):
        net, depth = self.net, self.net.depth
        for dz in range(depth):
            arrived(self.slot(dz, self.xi), self.sx.at[dz], self.rx.at[dz], net.xp)
            self.pass_on(dz, self.xi, self.sc, self.rc, depth + dz, net.cp)

    def last(self):
        net, depth = self.net, self.net.depth
        ci = net.i + 1 - 2 * net.core
        for dz in range(depth):
            arrived(self.slot(dz, ci), self.sc.at[dz], self.rc.at[dz], net.cp)
        for dz in range(depth):
            arrived(
                self.slot(dz, lax.rem(ci + 2, INNER)),
                self.sc.at[depth + dz],
                self.rc.at[depth + dz],
                net.cp,
            )

    def end(self):
        self.after_z()
        self.after_x()
        self.last()

    def one_x(self, dz):
        net, block, n = self.net, self.slot(dz, self.xi), self.net.depth + dz
        arrived(block, self.sx.at[dz], self.rx.at[dz], net.xp)
        remote(block, block, self.sc.at[n], self.rc.at[n], net.cp).start()

    def one_c(self, n, place):
        block = self.out.at[place]
        arrived(block, self.sc.at[n], self.rc.at[n], self.net.cp)

    def sent_loop(self):
        net, depth = self.net, self.net.depth
        for dz in range(depth):
            block = self.slot(dz, self.xi)
            remote(block, block, self.sc.at[depth + dz], self.rc.at[depth + dz], net.cp).wait_send()


def hbm():
    return pl.BlockSpec(memory_space=pltpu.HBM)


def vmem():
    return pl.BlockSpec(memory_space=pltpu.VMEM)


def smem():
    return pl.BlockSpec(memory_space=pltpu.SMEM)


def comm_params(cid, limit=56 << 20):
    return pltpu.CompilerParams(
        collective_id=cid, has_side_effects=True, vmem_limit_bytes=limit
    )


def add_into(dst, sources, rows, chunk):
    def body(n, carry):
        at = pl.ds(pl.multiple_of(n * chunk, chunk), chunk)
        total = sources[0][at, :].astype(F32)
        for source in sources[1:]:
            total = total + source[at, :].astype(F32)
        dst[at, :] = total.astype(dst.dtype)
        return carry

    lax.fori_loop(0, rows // chunk, body, 0)


def chunk_of(rows):
    for size in (32, 16, 8):
        if rows % size == 0:
            return size
    return rows


class PlaneScatter:
    ORDER = ((1, 1), (1, 0), (0, 1), (0, 0))

    @staticmethod
    def scratch(rows, cols):
        return (
            [pltpu.VMEM((4, rows, cols), BF)] * 2
            + [pltpu.VMEM((2, rows // 2, cols), BF)] * 4
            + dma_sems(10, 10)
        )

    def __init__(self, net, sends, part, rows, scratch):
        self.net, self.sends, self.part, self.rows = net, sends, part, rows
        self.bc, self.mid, self.bx, self.by, self.second, self.b2, self.ss, self.rs = scratch
        self.half = rows // 2
        self.lo, self.hi = pl.ds(0, self.half), pl.ds(self.half, self.half)
        self.chunk = chunk_of(self.half)

    def place(self, fx, fy, core):
        x = 1 - self.net.x if fx else self.net.x
        y = 1 - self.net.y if fy else self.net.y
        return (x * 2 + core) * SEQ + y

    def send(self, src, dst, n, device):
        self.sends.start(src, dst, self.ss.at[n], self.rs.at[n], device)

    def take(self, dst, n):
        arrived(dst, self.ss.at[n], self.rs.at[n], self.net.xp)

    def begin(self):
        net = self.net
        for n, (fx, fy) in enumerate(self.ORDER):
            self.send(self.part.at[self.place(fx, fy, 1 - net.core)], self.bc.at[n], n, net.cp)

    def cores(self):
        net, mid = self.net, self.mid
        for n, (fx, fy) in enumerate(self.ORDER):
            self.take(self.bc.at[n], n)
            own = self.part.at[self.place(fx, fy, net.core)]
            add_into(mid.at[n], [own, self.bc.at[n]], self.rows, self.chunk)
            if n == 0:
                self.send(mid.at[0, self.lo], self.bx.at[0], 4, net.xp)
                self.send(mid.at[0, self.hi], self.by.at[0], 5, net.yp)
            if n == 1:
                self.send(mid.at[1, self.lo], self.bx.at[1], 6, net.xp)
            if n == 2:
                self.send(mid.at[2, self.hi], self.by.at[1], 7, net.yp)

    def turn(self):
        net, mid, second = self.net, self.mid, self.second
        self.take(self.bx.at[0], 4)
        add_into(second.at[0], [mid.at[2, self.lo], self.bx.at[0]], self.half, self.chunk)
        self.send(second.at[0], self.b2.at[0], 8, net.yp)
        self.take(self.by.at[0], 5)
        add_into(second.at[1], [mid.at[1, self.hi], self.by.at[0]], self.half, self.chunk)
        self.send(second.at[1], self.b2.at[1], 9, net.xp)

    def final(self, out, more=()):
        mid = self.mid
        self.take(self.bx.at[1], 6)
        self.take(self.by.at[1], 7)
        for n, (at, got) in enumerate(((self.lo, self.bx), (self.hi, self.by))):
            self.take(self.b2.at[n], 8 + n)
            terms = [mid.at[3, at], got.at[1], self.b2.at[n]] + [m.at[at] for m in more]
            add_into(out.at[at], terms, self.half, self.chunk)


def scatter_plane(part, depth):
    rows, cols = part.shape[1:]

    def kernel(part_ref, out, *scratch):
        net = Net(depth)
        sends = Sends()
        greet([net.xp, net.yp, net.cp])
        work = PlaneScatter(net, sends, part_ref, rows, scratch)
        work.begin()
        work.cores()
        work.turn()
        work.final(out)
        sends.finish()

    return pl.pallas_call(
        kernel,
        out_shape=jax.ShapeDtypeStruct((rows, cols), F32),
        in_specs=[vmem()],
        out_specs=vmem(),
        scratch_shapes=PlaneScatter.scratch(rows, cols),
        compiler_params=comm_params(4),
        name="scatter_plane",
    )(part)


class ShardScatter:
    @staticmethod
    def scratch(depth, rows, cols):
        far = max(depth - 1, 1)
        shapes = [(2 * depth, rows, cols)] + [(depth, rows, cols)] * 2 + [(far, rows, cols)] * 2
        return [pltpu.VMEM(s, BF) for s in shapes] + dma_sems(
            2 * depth, 2 * depth, depth, depth, far, far
        )

    def __init__(self, net, sends, part, scratch):
        self.net, self.sends, self.part = net, sends, part
        self.bc, self.sx, self.bx, self.sz, self.bz = scratch[:5]
        self.ssc, self.rsc, self.ssx, self.rsx, self.ssz, self.rsz = scratch[5:]
        depth = net.depth
        self.order = sorted(range(1, depth), key=lambda d: -min(d, depth - d)) + [0]
        self.rows = part.shape[1]
        self.chunk = chunk_of(self.rows)

    def block(self, dz, fx, core):
        x = 1 - self.net.x if fx else self.net.x
        return self.part.at[self.net.zoff(dz) * INNER + x * 2 + core]

    def begin(self):
        net = self.net
        for dz in self.order:
            for fx in (1, 0):
                n = dz * 2 + fx
                self.sends.start(
                    self.block(dz, fx, 1 - net.core),
                    self.bc.at[n],
                    self.ssc.at[n],
                    self.rsc.at[n],
                    net.cp,
                )

    def end(self, out):
        net, sends = self.net, self.sends
        for dz in self.order:
            n = dz * 2 + 1
            arrived(self.bc.at[n], self.ssc.at[n], self.rsc.at[n], net.cp)
            add_into(
                self.sx.at[dz], [self.block(dz, 1, net.core), self.bc.at[n]], self.rows, self.chunk
            )
            sends.start(self.sx.at[dz], self.bx.at[dz], self.ssx.at[dz], self.rsx.at[dz], net.xp)
        for dz in self.order:
            n = dz * 2
            arrived(self.bc.at[n], self.ssc.at[n], self.rsc.at[n], net.cp)
            arrived(self.bx.at[dz], self.ssx.at[dz], self.rsx.at[dz], net.xp)
            terms = [self.block(dz, 0, net.core), self.bc.at[n], self.bx.at[dz]]
            if dz:
                add_into(self.sz.at[dz - 1], terms, self.rows, self.chunk)
                sends.start(
                    self.sz.at[dz - 1],
                    self.bz.at[dz - 1],
                    self.ssz.at[dz - 1],
                    self.rsz.at[dz - 1],
                    net.dev(z=net.zoff(dz)),
                )
            else:
                for far in range(net.depth - 1):
                    arrived(self.bz.at[far], self.ssz.at[far], self.rsz.at[far], net.xp)
                    terms.append(self.bz.at[far])
                add_into(out, terms, self.rows, self.chunk)


def scatter_keys(part, depth, cid):
    rows, cols = part.shape[1:]

    def kernel(part_ref, out, *scratch):
        net = Net(depth)
        sends = Sends()
        greet(net.zpeers() + [net.xp, net.cp])
        work = ShardScatter(net, sends, part_ref, scratch)
        work.begin()
        work.end(out)
        sends.finish()

    return pl.pallas_call(
        kernel,
        out_shape=jax.ShapeDtypeStruct((rows, cols), F32),
        in_specs=[vmem()],
        out_specs=vmem(),
        scratch_shapes=ShardScatter.scratch(depth, rows, cols),
        compiler_params=comm_params(cid),
        name="scatter_keys",
    )(part)


def turn(values, cosine, sine):
    return values * cosine + pltpu.roll(values, HEAD // 2, 1) * sine


def attend_backward(q, kv, lo, info, m, l, dob, ob, tile=512):
    block = q.shape[1]
    keys = kv.shape[0]
    tiles = keys // tile

    def kernel(info_ref, q_ref, kv_ref, lo_ref, m_ref, l_ref, do_ref, ob_ref, dq_ref, dkv_ref, da, dl, acc):
        acc[...] = jnp.zeros_like(acc)
        for j in range(2):
            for h in range(GROUP):
                c = slice(h * HEAD, (h + 1) * HEAD)
                d = do_ref[j, :, c].astype(F32)
                o = ob_ref[j, :, c].astype(F32)
                inv = 1.0 / l_ref[j, h : h + 1, :]
                da[j, h] = (d.T * inv).T.astype(BF)
                dl[j, h : h + 1, :] = -jnp.sum((d * o).T, axis=0, keepdims=True) * inv
        low = jnp.minimum(info_ref[2], info_ref[3]) // tile
        high = (info_ref[1] * block + block - 1) // tile

        def clear(t, carry):
            dkv_ref[pl.ds(pl.multiple_of(t * tile, tile), tile), :] = jnp.zeros((tile, 2 * HEAD), BF)
            return carry

        lax.fori_loop(0, low, clear, 0)
        lax.fori_loop(high + 1, tiles, clear, 0)

        def piece(t, j, masked):
            start = pl.multiple_of(t * tile, tile)
            base = info_ref[j] * block
            k = kv_ref[pl.ds(start, tile), :HEAD]
            v = kv_ref[pl.ds(start, tile), HEAD:]
            kt = k.T
            if masked:
                key = start + lax.broadcasted_iota(jnp.int32, (tile, block), 0)
                query = base + lax.broadcasted_iota(jnp.int32, (tile, block), 1)
                ok = (key <= query) & (key >= lo_ref[j])
            dk = dv = None
            for h in range(GROUP):
                qh = q_ref[j, :, h * HEAD : (h + 1) * HEAD]
                s = dot(k, qh, NT) - m_ref[j, h : h + 1, :]
                if masked:
                    s = jnp.where(ok, s, NEG)
                p = jnp.exp2(s)
                dah = da[j, h]
                dvh = dot(p.astype(BF), dah)
                dp = dot(v, dah, NT) + dl[j, h : h + 1, :]
                ds = (p * dp).astype(BF)
                dkh = dot(ds, qh)
                acc[j, h] += dot(kt, ds)
                dk = dkh if dk is None else dk + dkh
                dv = dvh if dv is None else dv + dvh
            return dk * LN2, dv

        def tile_step(t, carry):
            start = pl.multiple_of(t * tile, tile)
            rows = pl.ds(start, tile)

            def put(j, masked):
                dk, dv = piece(t, j, masked)
                if j == 0:
                    dk = dk + dkv_ref[rows, :HEAD].astype(F32)
                    dv = dv + dkv_ref[rows, HEAD:].astype(F32)
                dkv_ref[rows, :HEAD] = dk.astype(BF)
                dkv_ref[rows, HEAD:] = dv.astype(BF)

            for j in (1, 0):
                base = info_ref[j] * block
                live = (start <= base + block - 1) & (start + tile > info_ref[2 + j])
                free = (start + tile - 1 <= base) & (start >= info_ref[4 + j])
                if j == 1:

                    @pl.when(jnp.logical_not(live))
                    def _():
                        clear(t, 0)

                @pl.when(live & free)
                def _():
                    put(j, False)

                @pl.when(live & jnp.logical_not(free))
                def _():
                    put(j, True)

            return carry

        lax.fori_loop(low, high + 1, tile_step, 0)
        for j in range(2):
            for h in range(GROUP):
                dq_ref[j, :, h * HEAD : (h + 1) * HEAD] = (acc[j, h] * SCALE).T.astype(BF)

    return pl.pallas_call(
        kernel,
        out_shape=(jax.ShapeDtypeStruct(q.shape, BF), jax.ShapeDtypeStruct(kv.shape, BF)),
        in_specs=[smem()] + [vmem()] * 7,
        out_specs=(vmem(),) * 2,
        scratch_shapes=[
            pltpu.VMEM((2, GROUP, block, HEAD), BF),
            pltpu.VMEM((2, 8, block), F32),
            pltpu.VMEM((2, GROUP, HEAD, block), F32),
        ],
        compiler_params=pltpu.CompilerParams(vmem_limit_bytes=60 << 20),
        cost_estimate=pl.CostEstimate(
            flops=int(2.5e10), bytes_accessed=12 << 20, transcendentals=13 << 20
        ),
        name="attend_backward",
    )(info, q, kv, lo, m, l, dob, ob)


class PlaneGather:
    @staticmethod
    def sems():
        return dma_sems(2, 2, 2, 2, 5, 5)

    def __init__(self, net, sends, src, out, sems, rows):
        self.net, self.sends, self.src, self.out = net, sends, src, out
        self.sx, self.rx, self.sy, self.ry, self.sc, self.rc = sems
        half = rows // 2
        self.lo, self.hi = pl.ds(0, half), pl.ds(half, half)
        xi = lax.rem(net.i + 2, INNER)
        ci = net.i + 1 - 2 * net.core
        cx = lax.rem(ci + 2, INNER)
        place = lambda i, y: i * SEQ + y
        self.me, self.xb = place(net.i, net.y), place(xi, net.y)
        self.yb, self.db = place(net.i, 1 - net.y), place(xi, 1 - net.y)
        self.core_blocks = [place(ci, net.y), place(ci, 1 - net.y), place(cx, net.y)]
        self.core_diag = place(cx, 1 - net.y)

    def begin(self):
        self.begin_y()
        self.begin_x()

    def begin_y(self):
        net, out, src = self.net, self.out, self.src
        self.sends.start(src, out.at[self.me], self.sy.at[0], self.ry.at[0], net.yp)
        self.sends.start(src, out.at[self.me], self.sc.at[0], self.rc.at[0], net.cp)

    def begin_x(self):
        net, out, src = self.net, self.out, self.src
        self.sends.start(src, out.at[self.me], self.sx.at[0], self.rx.at[0], net.xp)

    def pass_on(self, block, part, ssem, rsem, n, device):
        def refs():
            at = self.out.at[block] if part is None else self.out.at[block, part]
            return at, at, ssem.at[n], rsem.at[n], device

        self.sends.later(refs)

    def middle(self):
        net, out = self.net, self.out
        arrived(out.at[self.yb], self.sy.at[0], self.ry.at[0], net.yp)
        self.pass_on(self.yb, self.lo, self.sx, self.rx, 1, net.xp)
        self.pass_on(self.yb, None, self.sc, self.rc, 1, net.cp)
        arrived(out.at[self.xb], self.sx.at[0], self.rx.at[0], net.xp)
        self.pass_on(self.xb, self.hi, self.sy, self.ry, 1, net.yp)
        self.pass_on(self.xb, None, self.sc, self.rc, 2, net.cp)

    def end(self):
        net, out = self.net, self.out
        arrived(out.at[self.db, self.lo], self.sx.at[1], self.rx.at[1], net.xp)
        self.pass_on(self.db, self.lo, self.sc, self.rc, 3, net.cp)
        arrived(out.at[self.db, self.hi], self.sy.at[1], self.ry.at[1], net.yp)
        self.pass_on(self.db, self.hi, self.sc, self.rc, 4, net.cp)

    def last(self):
        net, out = self.net, self.out
        for n, block in enumerate(self.core_blocks):
            arrived(out.at[block], self.sc.at[n], self.rc.at[n], net.cp)
        arrived(out.at[self.core_diag, self.lo], self.sc.at[3], self.rc.at[3], net.cp)
        arrived(out.at[self.core_diag, self.hi], self.sc.at[4], self.rc.at[4], net.cp)


class Route:
    def __init__(self, net, sends_to, comes_from):
        self.net = net
        me = net.z * INNER + net.i
        self.local = (sends_to[0] == me) & (sends_to[1] == net.y)
        self.kept = (comes_from[0] == me) & (comes_from[1] == net.y)
        self.to, self.frm = self.device(sends_to), self.device(comes_from)

    def device(self, place):
        shard, y = place
        return self.net.dev(z=lax.div(shard, INNER), i=lax.rem(shard, INNER), y=y)

    def hello(self):
        @pl.when(jnp.logical_not(self.kept))
        def _():
            pl.semaphore_signal(
                pltpu.get_barrier_semaphore(), inc=1, device_id=self.frm, device_id_type=MESH
            )

        return jnp.where(self.local, 0, 1)

    def send(self, refs):
        @pl.when(self.local)
        def _():
            src, dst, _, _ = refs()
            dst[...] = src[...]

        @pl.when(jnp.logical_not(self.local))
        def _():
            remote(*refs(), self.to).start()

    def sent(self, refs):
        @pl.when(jnp.logical_not(self.local))
        def _():
            remote(*refs(), self.to).wait_send()

    def arrive(self, refs):
        @pl.when(jnp.logical_not(self.kept))
        def _():
            dst, ssem, rsem = refs()
            remote(dst, dst, ssem, rsem, self.to).wait_recv()


class Mirror:
    def __init__(self, net):
        self.net = net
        self.n = net.depth * INNER
        self.last = 2 * self.n - 1
        self.me = net.z * INNER + net.i

    def home(self, block):
        return jnp.where(block < self.n, block, self.last - block)

    def blocks(self):
        return self.me, self.last - self.me

    def slot(self, block):
        return jnp.where(block < self.n, 0, 1)

    def rows_out(self, k):
        block = 2 * self.me + k
        come = self.blocks()[k]
        return Route(
            self.net, (self.home(block), self.net.y), (lax.div(come, 2), self.net.y)
        ), self.slot(block)

    def rows_back(self, k):
        block = self.blocks()[k]
        come = 2 * self.me + k
        return Route(
            self.net, (lax.div(block, 2), self.net.y), (self.home(come), self.net.y)
        ), lax.rem(block, 2)

    def heads_back(self, k):
        block = self.blocks()[k]
        own = 2 * self.me + self.net.y
        return Route(self.net, (lax.div(block, 2), lax.rem(block, 2)), (self.home(own), k))

    def heads_out(self, k):
        own = 2 * self.me + self.net.y
        come = self.blocks()[k]
        return Route(
            self.net, (self.home(own), k), (lax.div(come, 2), lax.rem(come, 2))
        ), self.slot(own)


class Chain:
    @staticmethod
    def sems(depth):
        return dma_sems(*[max(depth - 1, 1) * INNER] * 4)

    def __init__(self, net, out, sems):
        self.net, self.out = net, out
        self.su, self.ru, self.sd, self.rd = sems
        self.steps = (net.depth - 1) * INNER
        self.up = net.dev(z=jnp.minimum(net.z + 1, net.depth - 1))
        self.down = net.dev(z=jnp.maximum(net.z - 1, 0))

    def piece(self, z, q):
        return self.out.at[z * INNER + q]

    def refs(self, hop, q, way):
        net = self.net
        n = (hop + 1) * INNER + q
        z = net.z - 1 - hop if way == 0 else net.z + 1 + hop
        ssem, rsem, device = (
            (self.su.at[n], self.ru.at[n], self.up)
            if way == 0
            else (self.sd.at[n], self.rd.at[n], self.down)
        )
        return self.piece(z, q), ssem, rsem, device

    def begin(self, ready):
        def body(q, carry):
            ready(q)
            for way in range(2):

                @pl.when(self.net.z < self.net.depth - 1 if way == 0 else self.net.z > 0)
                def _():
                    dst, ssem, rsem, device = self.refs(-1, q, way)
                    remote(dst, dst, ssem, rsem, device).start()

            return carry

        lax.fori_loop(0, INNER, body, 0)

    def step(self, n):
        net = self.net
        hop, q = lax.div(n, INNER), lax.rem(n, INNER)
        for way in range(2):
            z = net.z - 1 - hop if way == 0 else net.z + 1 + hop
            here = z >= 0 if way == 0 else z <= net.depth - 1
            further = net.z < net.depth - 1 if way == 0 else net.z > 0

            @pl.when(here)
            def _():
                block = self.piece(z, q)
                if way == 0:
                    arrived(block, self.su.at[n], self.ru.at[n], self.up)
                else:
                    arrived(block, self.sd.at[n], self.rd.at[n], self.down)

            @pl.when(here & further)
            def _():
                dst, ssem, rsem, device = self.refs(hop, q, way)
                remote(dst, dst, ssem, rsem, device).start()

    def run(self, a, b):
        def body(n, carry):
            self.step(n)
            return carry

        lax.fori_loop(a, min(b, self.steps), body, 0)

    def finish(self):
        def body(n, carry):
            hop, q = lax.div(n, INNER) - 1, lax.rem(n, INNER)
            for way in range(2):
                z = self.net.z - 1 - hop if way == 0 else self.net.z + 1 + hop
                here = z >= 0 if way == 0 else z <= self.net.depth - 1
                further = self.net.z < self.net.depth - 1 if way == 0 else self.net.z > 0

                @pl.when(here & further)
                def _():
                    dst, ssem, rsem, device = self.refs(hop, q, way)
                    remote(dst, dst, ssem, rsem, device).wait_send()

            return carry

        lax.fori_loop(0, self.steps, body, 0)


def seg_tile(start, rows, st, en):
    key = start + lax.broadcasted_iota(jnp.int32, (rows, HEAD), 0)
    return ((key >= st) & (key < en)).astype(F32).astype(BF)


def front(stream, pack, moe, chosen, cosine, sine, w_out, out_grad, qseg, starts, depth):
    block = stream.shape[0]
    rows = block * SEQ
    shards = depth * INNER
    part = w_out.shape[0]

    def kernel(
        st_ref, pk_ref, mo_ref, ch_ref, c_ref, n_ref, wo_ref, og_ref, qs_ref, sg_ref,
        s_out, w_full, ch_out, h1_out, q_out, kv_out, o_out, m_out, l_out, mix_out, x1_out, h2_out,
        wf_out, og_out, mo_out,
        qp, acc, top, total, h2_own, gains, own, sq, rq, so, ro, sy, ry, sp, rp, sm, rm, *sems,
    ):
        net = Net(depth)
        sends = Sends()
        mirror = Mirror(net)
        gp = ShardGather(net, sends, pk_ref, FlatSlots(w_full, part), sems[28:34])
        gk = ShardGather(net, sends, None, kv_out, sems[:6])
        gk.src = gk.slot(0, net.i)
        gw = ShardGather(net, sends, wo_ref, FlatSlots(wf_out, part), sems[6:12])
        gg = PlaneGather(net, sends, og_ref, og_out, sems[12:18], block)
        gh = PlaneGather(net, sends, h2_own, h2_out, sems[18:24], block)
        chain = Chain(net, mo_out, sems[24:28])
        rows_out = [mirror.rows_out(k) for k in range(2)]
        heads = [mirror.heads_back(k) for k in range(2)]
        barrier = pltpu.get_barrier_semaphore()
        for device in net.zpeers() + net.plane():
            pl.semaphore_signal(barrier, inc=1, device_id=device, device_id_type=MESH)
        count = depth - 1 + E - 1
        for route in [r for r, _ in rows_out] + heads:
            count = count + route.hello()
        here = lambda y: s_out.at[pl.ds(pl.multiple_of(y * block, block), block)]
        mine_p = pltpu.make_async_copy(pk_ref, gp.slot(0, net.i), own.at[4])
        mine_s = pltpu.make_async_copy(st_ref, here(net.y), own.at[5])
        mine_m = pltpu.make_async_copy(
            mo_ref.at[net.i * SEQ + net.y], mo_out.at[net.z * INNER + net.i], own.at[3]
        )
        mine_c = pltpu.make_async_copy(ch_ref, ch_out.at[net.i * SEQ + net.y], own.at[6])
        mine_g = pltpu.make_async_copy(og_ref, og_out.at[gg.me], own.at[0])
        mine_w = pltpu.make_async_copy(wo_ref, gw.slot(0, net.i), own.at[1])
        for copy in (mine_p, mine_s, mine_m, mine_c, mine_g, mine_w):
            copy.start()
        pl.semaphore_wait(barrier, count)
        gp.begin()
        sends.start(st_ref, here(net.y), sy.at[0], ry.at[0], net.yp)
        for n, device in enumerate(net.plane()):
            sends.start(ch_ref, ch_out.at[net.i * SEQ + net.y], sp.at[n], rp.at[n], device)
        gw.begin()
        gp.end()
        for di in range(1, INNER):
            other = lax.rem(net.i + di, INNER)
            sends.start(
                mo_ref.at[other * SEQ + net.y],
                mo_out.at[net.z * INNER + net.i],
                sm.at[di - 1],
                rm.at[di - 1],
                net.dev(i=other),
            )
        gg.begin_y()

        def moe_ready(q):
            di = lax.rem(net.i - q + INNER, INNER)

            @pl.when(di > 0)
            def _():
                arrived(mo_out.at[net.z * INNER + q], sm.at[di - 1], rm.at[di - 1], net.xp)

        arrived(here(1 - net.y), sy.at[0], ry.at[0], net.yp)
        mine_s.wait()
        mine_p.wait()
        tail = w_full[:, QKV:].astype(F32).T
        gains[...] = tail[:8, :]

        step = 64

        def norm(n, carry):
            at = pl.ds(pl.multiple_of(n * step, step), step)
            x = s_out[at, :].astype(F32)
            scale = lax.rsqrt(jnp.mean(x * x, axis=-1, keepdims=True) + EPS)
            h1_out[at, :] = (x * scale * gains[0:1, :]).astype(BF)
            return carry

        lax.fori_loop(0, rows // step, norm, 0)
        h1 = h1_out[...]
        cos, sin = c_ref[...], n_ref[...]
        r = dot(h1, w_full[:, QCOLS:QKV])
        me = net.z * INNER + net.i
        kv_out[me, :, :HEAD] = turn(r[:, :HEAD], cos, sin).astype(BF)
        kv_out[me, :, HEAD:] = r[:, HEAD:].astype(BF)
        gk.begin()
        for h in range(0, GROUP, 2):
            r = dot(h1, w_full[:, h * HEAD : (h + 2) * HEAD])
            for g in range(2):
                v = turn(r[:, g * HEAD : (g + 1) * HEAD], cos, sin) * (SCALE * LOG2E)
                v = v.astype(BF)
                at = slice((h + g) * HEAD, (h + g + 1) * HEAD)
                qp[0, :, at] = v[:block]
                qp[1, :, at] = v[block:]
        q_refs = [
            lambda k=k: (qp.at[k], q_out.at[rows_out[k][1]], sq.at[k], rq.at[rows_out[k][1]])
            for k in range(2)
        ]
        o_refs = [
            lambda k=k: (o_out.at[k], mix_out.at[net.y], so.at[k], ro.at[net.y]) for k in range(2)
        ]
        for k in range(2):
            rows_out[k][0].send(q_refs[k])
        mine_m.wait()
        mine_w.wait()
        chain.begin(moe_ready)
        gg.begin_x()
        acc[...] = jnp.zeros_like(acc)
        top[...] = jnp.full_like(top, NEG)
        total[...] = jnp.zeros_like(total)
        gk.after_z()
        for k in range(2):
            rows_out[k][0].arrive(lambda: (q_out.at[k], sq.at[k], rq.at[k]))

        low, high = mirror.blocks()
        bases = (low * block, high * block)
        xi = lax.rem(net.i + 2, INNER)
        ci = net.i + 1 - 2 * net.core

        def attend(t, j, masked):
            start = pl.multiple_of(t * rows, rows)
            k = jnp.concatenate(
                [kv_out[t, :, :HEAD], seg_tile(start, rows, sg_ref[0:1, :], sg_ref[1:2, :])], axis=1
            )
            vt = kv_out[t, :, HEAD:].T
            if masked:
                key = start + lax.broadcasted_iota(jnp.int32, (rows, block), 0)
                ok = key <= bases[j] + lax.broadcasted_iota(jnp.int32, (rows, block), 1)
            scores = [
                dot(
                    k,
                    jnp.concatenate(
                        [q_out[j, :, h * HEAD : (h + 1) * HEAD], qs_ref[j]], axis=1
                    ),
                    NT,
                )
                for h in range(GROUP)
            ]
            for h in range(GROUP):
                s = scores[h]
                if masked:
                    s = jnp.where(ok, s, NEG)
                m0 = top[j, h : h + 1, :]
                m1 = jnp.maximum(m0, jnp.max(s, axis=0, keepdims=True))
                p = jnp.exp2(s - m1)
                f = jnp.exp2(m0 - m1)
                top[j, h : h + 1, :] = m1
                total[j, h : h + 1, :] = total[j, h : h + 1, :] * f + jnp.sum(
                    p, axis=0, keepdims=True
                )
                acc[j, h] = acc[j, h] * f + dot(vt, p.astype(BF))

        polled = min((shards - depth) // 2, 2 * INNER - 1, chain.steps)

        def tile(u, carry):
            in_z = u < depth
            in_x = u < 2 * depth
            in_c = u < 3 * depth
            dz = lax.rem(u, depth)
            place = jnp.where(in_z, net.i, jnp.where(in_x, xi, jnp.where(in_c, ci, lax.rem(ci + 2, INNER))))
            t = lax.rem(net.z - dz + depth, depth) * INNER + place

            @pl.when((u >= depth) & in_x)
            def _():
                gk.one_x(dz)

            @pl.when(u >= 2 * depth)
            def _():
                gk.one_c(u - 2 * depth, t)

            @pl.when(u == 2 * depth)
            def _():
                gg.middle()
                gw.after_z()

            @pl.when(u == 3 * depth)
            def _():
                gw.after_x()
                gg.end()

            @pl.when((u >= depth) & (lax.rem(u - depth, 2) == 1) & (u - depth < 2 * polled))
            def _():
                chain.step(lax.div(u - depth, 2))

            for j in (0, 1):
                live = t * rows <= bases[j] + block - 1
                free = t * rows + rows - 1 <= bases[j]

                @pl.when(live & free)
                def _():
                    attend(t, j, False)

                @pl.when(live & jnp.logical_not(free))
                def _():
                    attend(t, j, True)

            return carry

        lax.fori_loop(0, shards, tile, 0)
        gk.sent_loop()
        for j in range(2):
            for h in range(GROUP):
                o_out[j, :, h * HEAD : (h + 1) * HEAD] = (
                    (acc[j, h] / total[j, h : h + 1, :]).T.astype(BF)
                )
        for k in range(2):
            heads[k].send(o_refs[k])
        chain.run(polled, polled + 1)
        m_out[...] = top[...]
        l_out[...] = total[...]
        gw.last()
        gg.last()
        for k in range(2):
            heads[k].arrive(lambda: (mix_out.at[k], so.at[k], ro.at[k]))
        x1 = here(net.y)[...].astype(F32)
        x1 = x1 + dot(mix_out[0], wf_out[:QCOLS, :]) + dot(mix_out[1], wf_out[QCOLS:, :])
        x1_out[...] = x1
        scale = lax.rsqrt(jnp.mean(x1 * x1, axis=-1, keepdims=True) + EPS)
        h2_own[...] = (x1 * scale * gains[1:2, :]).astype(BF)
        mine_h = pltpu.make_async_copy(h2_own, h2_out.at[gh.me], own.at[2])
        gh.begin()
        mine_h.start()
        chain.run(polled + 1, 2 * INNER)
        gh.middle()
        chain.run(2 * INNER, 2 * INNER + 2)
        gh.end()
        chain.run(2 * INNER + 2, chain.steps)
        n = 0
        for di in range(INNER):
            for dy in range(SEQ):
                if di or dy:
                    frm = lax.rem(net.i - di + INNER, INNER) * SEQ + lax.rem(net.y + dy, SEQ)
                    arrived(ch_out.at[frm], sp.at[n], rp.at[n], net.yp)
                    n += 1
        mine_c.wait()
        gh.last()
        for k in range(2):
            rows_out[k][0].sent(q_refs[k])
            heads[k].sent(o_refs[k])
        chain.finish()
        sends.finish()
        mine_g.wait()
        mine_h.wait()

    sds = jax.ShapeDtypeStruct
    stat = sds((2, 8, block), F32)
    heads_shape = sds((2, block, QCOLS), BF)
    return pl.pallas_call(
        kernel,
        out_shape=(
            sds((rows, WIDTH), BF),
            sds((WIDTH, FIRST), BF),
            sds((E,) + chosen.shape, F32),
            sds((rows, WIDTH), BF),
            heads_shape,
            sds((shards, rows, 2 * HEAD), BF),
            heads_shape,
            stat,
            stat,
            heads_shape,
            sds((block, WIDTH), F32),
            sds((E, block, WIDTH), BF),
            sds((WIDTH, WIDTH), BF),
            sds((E, block, WIDTH), BF),
            sds((shards,) + moe.shape[1:], BF),
        ),
        in_specs=[hbm()] * 4 + [vmem()] * 2 + [hbm()] * 2 + [vmem()] * 2,
        out_specs=(vmem(), vmem(), hbm()) + (vmem(),) * 8 + (hbm(), vmem(), hbm(), hbm()),
        scratch_shapes=[
            pltpu.VMEM((2, block, QCOLS), BF),
            pltpu.VMEM((2, GROUP, HEAD, block), F32),
            pltpu.VMEM((2, 8, block), F32),
            pltpu.VMEM((2, 8, block), F32),
            pltpu.VMEM((block, WIDTH), BF),
            pltpu.VMEM((8, WIDTH), F32),
        ]
        + dma_sems(7, 2, 2, 2, 2, 1, 1, E - 1, E - 1, INNER - 1, INNER - 1)
        + ShardGather.sems(depth) * 2
        + PlaneGather.sems() * 2
        + Chain.sems(depth)
        + ShardGather.sems(depth),
        compiler_params=comm_params(7, 60 << 20),
        name="front",
    )(stream, pack, moe, chosen, cosine, sine, w_out, out_grad, qseg, starts)


class Tally:
    def __init__(self, net, part, rows, scratch):
        self.net, self.part, self.rows = net, part, rows
        self.bc, self.sx, self.bx, self.sz, self.bz = scratch[:5]
        self.ssc, self.rsc, self.ssx, self.rsx, self.ssz, self.rsz = scratch[5:]
        self.chunk = chunk_of(rows)

    def number(self, dz, fx, core):
        x = jnp.where(fx == 1, 1 - self.net.x, self.net.x)
        return lax.rem(self.net.z + dz, self.net.depth) * INNER + x * 2 + core

    def core_copy(self, dz, fx):
        net, n = self.net, dz * 2 + fx
        src = self.part.at[self.number(dz, fx, 1 - net.core)]
        return remote(src, self.bc.at[n], self.ssc.at[n], self.rsc.at[n], net.cp)

    def x_copy(self, dz):
        return remote(
            self.sx.at[dz], self.bx.at[dz], self.ssx.at[dz], self.rsx.at[dz], self.net.xp
        )

    def z_copy(self, dz):
        n = dz - 1
        device = self.net.dev(z=lax.rem(self.net.z + dz, self.net.depth))
        return remote(self.sz.at[n], self.bz.at[n], self.ssz.at[n], self.rsz.at[n], device)

    def terms(self, dz, fx):
        n = dz * 2 + fx
        arrived(self.bc.at[n], self.ssc.at[n], self.rsc.at[n], self.net.cp)
        return [self.part.at[self.number(dz, fx, self.net.core)], self.bc.at[n]]

    def x_stage(self, dz):
        add_into(self.sx.at[dz], self.terms(dz, 1), self.rows, self.chunk)
        self.x_copy(dz).start()

    def x_terms(self, dz):
        terms = self.terms(dz, 0)
        arrived(self.bx.at[dz], self.ssx.at[dz], self.rsx.at[dz], self.net.xp)
        return terms + [self.bx.at[dz]]

    def z_stage(self, dz):
        add_into(self.sz.at[dz - 1], self.x_terms(dz), self.rows, self.chunk)
        self.z_copy(dz).start()

    def final(self, out):
        terms = self.x_terms(0)
        for n in range(self.net.depth - 1):
            arrived(self.bz.at[n], self.ssz.at[n], self.rsz.at[n], self.net.xp)
            terms.append(self.bz.at[n])
        add_into(out, terms, self.rows, self.chunk)

    def finish(self):
        for dz in range(self.net.depth):
            for fx in range(2):
                self.core_copy(dz, fx).wait_send()
            self.x_copy(dz).wait_send()
            if dz:
                self.z_copy(dz).wait_send()

    def far(self):
        return [d for d in range(1, self.net.depth)] + [0]

    def begin(self):
        for dz in self.far():
            for fx in (1, 0):
                self.core_copy(dz, fx).start()

    def far_stages(self):
        for dz in self.far():
            self.x_stage(dz)

    def near_stages(self):
        for dz in self.far()[:-1]:
            self.z_stage(dz)


def backward(q, kv, qseg, starts, m, l, ob, mixed, dx1, out_w, part_rows, depth):
    block = q.shape[1]
    rows = kv.shape[1]
    shards = depth * INNER

    def kernel(
        q_ref, kv_ref, qs_ref, sg_ref, m_ref, l_ref, ob_ref, mix_ref, dx_ref, wf_ref,
        dq_out, dkv_out, own_out,
        dob, do_ref, da, dl, acc, dqs, dkv, wpart, wget, so, ro, sq, rq, sw, rw, *scratch,
    ):
        net = Net(depth)
        mirror = Mirror(net)
        keys = Tally(net, dkv, rows, scratch[:11])
        mine = wpart.at[net.y]
        outs = Tally(net, mine, part_rows, scratch[11:])
        quarter = shards // 4

        def pair_copy(n):
            at = pl.ds(n * quarter, quarter)
            return remote(
                wpart.at[1 - net.y, at], wget.at[at], sw.at[n], rw.at[n], net.yp
            )

        def pair_sum():
            for n in range(4):
                at = pl.ds(n * quarter, quarter)
                arrived(wget.at[at], sw.at[n], rw.at[n], net.yp)

                def body(b, carry):
                    add_into(
                        wpart.at[net.y, b], [wpart.at[net.y, b], wget.at[b]], part_rows, outs.chunk
                    )
                    return carry

                lax.fori_loop(n * quarter, (n + 1) * quarter, body, 0)
            outs.begin()

        heads = [mirror.heads_out(k) for k in range(2)]
        backs = [mirror.rows_back(k) for k in range(2)]
        barrier = pltpu.get_barrier_semaphore()
        for device in net.zpeers() + [net.xp, net.cp, net.yp]:
            pl.semaphore_signal(barrier, inc=1, device_id=device, device_id_type=MESH)
        count = depth - 1 + 3
        for route, _ in heads + backs:
            count = count + route.hello()
        do_refs = [
            lambda k=k: (dob.at[k], do_ref.at[heads[k][1]], so.at[k], ro.at[heads[k][1]])
            for k in range(2)
        ]
        dq_refs = [
            lambda k=k: (dqs.at[k], dq_out.at[backs[k][1]], sq.at[k], rq.at[backs[k][1]])
            for k in range(2)
        ]
        dx = dx_ref[...]
        for k in range(2):
            dob[k] = dot(dx, wf_ref[k * QCOLS : (k + 1) * QCOLS, :], NT).astype(BF)
        pl.semaphore_wait(barrier, count)
        for k in range(2):
            heads[k][0].send(do_refs[k])
        wide = QCOLS // 2
        for n in range(4):
            cols = slice((n % 2) * wide, (n % 2 + 1) * wide)
            grad = dot(mix_ref[n // 2, :, cols].T, dx).astype(BF)
            for b in range(wide // part_rows):
                for s in range(SEQ):
                    wpart[s, n * (wide // part_rows) + b] = grad[
                        b * part_rows : (b + 1) * part_rows, s * QCOLS : (s + 1) * QCOLS
                    ]
            pair_copy(n).start()
        acc[...] = jnp.zeros_like(acc)
        for k in range(2):
            heads[k][0].arrive(lambda: (do_ref.at[k], so.at[k], ro.at[k]))
        for j in range(2):
            for h in range(GROUP):
                c = slice(h * HEAD, (h + 1) * HEAD)
                d = do_ref[j, :, c].astype(F32)
                o = ob_ref[j, :, c].astype(F32)
                inv = 1.0 / l_ref[j, h : h + 1, :]
                da[j, h] = (d.T * inv).T.astype(BF)
                dl[j, h : h + 1, :] = -jnp.sum((d * o).T, axis=0, keepdims=True) * inv
        low, high = mirror.blocks()
        bases = (low * block, high * block)

        def piece(t, j, masked):
            start = pl.multiple_of(t * rows, rows)
            k = kv_ref[t, :, :HEAD]
            v = kv_ref[t, :, HEAD:]
            kt = k.T
            k_seg = jnp.concatenate(
                [k, seg_tile(start, rows, sg_ref[0:1, :], sg_ref[1:2, :])], axis=1
            )
            if masked:
                key = start + lax.broadcasted_iota(jnp.int32, (rows, block), 0)
                ok = key <= bases[j] + lax.broadcasted_iota(jnp.int32, (rows, block), 1)
            dk = dv = None
            for h in range(GROUP):
                qh = q_ref[j, :, h * HEAD : (h + 1) * HEAD]
                s = dot(k_seg, jnp.concatenate([qh, qs_ref[j]], axis=1), NT)
                s = s - m_ref[j, h : h + 1, :]
                if masked:
                    s = jnp.where(ok, s, NEG)
                p = jnp.exp2(s)
                dah = da[j, h]
                dvh = dot(p.astype(BF), dah)
                dp = dot(v, dah, NT) + dl[j, h : h + 1, :]
                ds = (p * dp).astype(BF)
                dkh = dot(ds, qh)
                acc[j, h] += dot(kt, ds)
                dk = dkh if dk is None else dk + dkh
                dv = dvh if dv is None else dv + dvh
            return dk * LN2, dv

        def tile(u, carry):
            g, r = lax.div(u, INNER), lax.rem(u, INNER)
            dz = lax.rem(g + 1, depth)
            fx = 1 - lax.div(r, 2)
            other = lax.rem(r, 2) == 0
            t = keys.number(dz, fx, jnp.where(other, 1 - net.core, net.core))

            def put(j, masked):
                dk, dv = piece(t, j, masked)
                if j == 0:
                    dk = dk + dkv[t, :, :HEAD].astype(F32)
                    dv = dv + dkv[t, :, HEAD:].astype(F32)
                dkv[t, :, :HEAD] = dk.astype(BF)
                dkv[t, :, HEAD:] = dv.astype(BF)

            for j in (1, 0):
                live = t * rows <= bases[j] + block - 1
                free = t * rows + rows - 1 <= bases[j]
                if j == 1:

                    @pl.when(jnp.logical_not(live))
                    def _():
                        dkv[t] = jnp.zeros((rows, 2 * HEAD), BF)

                @pl.when(live & free)
                def _():
                    put(j, False)

                @pl.when(live & jnp.logical_not(free))
                def _():
                    put(j, True)

            @pl.when(other)
            def _():
                keys.core_copy(dz, fx).start()

            @pl.when(r == INNER - 1)
            def _():
                keys.x_stage(dz)

            @pl.when((r == INNER - 1) & (g > 0))
            def _():
                keys.z_stage(g)

            @pl.when(u == shards - 7)
            def _():
                pair_sum()

            @pl.when(u == shards - 4)
            def _():
                outs.far_stages()

            @pl.when(u == shards - 1)
            def _():
                outs.near_stages()

            return carry

        lax.fori_loop(0, shards, tile, 0)
        for j in range(2):
            for h in range(GROUP):
                dqs[j, :, h * HEAD : (h + 1) * HEAD] = (acc[j, h] * SCALE).T.astype(BF)
        for k in range(2):
            backs[k][0].send(dq_refs[k])
        outs.final(own_out)
        keys.final(dkv_out)
        for k in range(2):
            backs[k][0].arrive(lambda: (dq_out.at[k], sq.at[k], rq.at[k]))
        for k in range(2):
            heads[k][0].sent(do_refs[k])
            backs[k][0].sent(dq_refs[k])
        for n in range(4):
            pair_copy(n).wait_send()
        outs.finish()
        keys.finish()

    sds = jax.ShapeDtypeStruct
    pair = (2, block, QCOLS)
    return pl.pallas_call(
        kernel,
        out_shape=(
            sds(pair, BF),
            sds((rows, 2 * HEAD), F32),
            sds((part_rows, QCOLS), F32),
        ),
        in_specs=[vmem()] * 10,
        out_specs=(vmem(),) * 3,
        scratch_shapes=[
            pltpu.VMEM(pair, BF),
            pltpu.VMEM(pair, BF),
            pltpu.VMEM((2, GROUP, block, HEAD), BF),
            pltpu.VMEM((2, 8, block), F32),
            pltpu.VMEM((2, GROUP, HEAD, block), F32),
            pltpu.VMEM(pair, BF),
            pltpu.VMEM((shards, rows, 2 * HEAD), BF),
            pltpu.VMEM((SEQ, shards, part_rows, QCOLS), BF),
            pltpu.VMEM((shards, part_rows, QCOLS), BF),
        ]
        + dma_sems(2, 2, 2, 2, 4, 4)
        + ShardScatter.scratch(depth, rows, 2 * HEAD)
        + ShardScatter.scratch(depth, part_rows, QCOLS),
        compiler_params=comm_params(8, 60 << 20),
        name="backward",
    )(q, kv, qseg, starts, m, l, ob, mixed, dx1, out_w)


def finish_layer(
    dq, dkv, cosine, sine, h1, weights, pair, small, dx1, gain_a, out_own, mixture, x1, moe, depth
):
    block = dx1.shape[0]
    rows = pair.shape[0]
    shards = depth * INNER
    part_rows = out_own.shape[0]
    wide = 384

    def kernel(
        dq_ref, dkv_ref, c_ref, n_ref, h1_ref, w_ref, s_ref, sm_ref, dx_ref, ga_ref, oo_ref, mx_ref, x1_ref, moe_ref,
        res_out, sg_out, own_out, pair_out, pair_wo, moe_out,
        raw, part, give, take, low, low_wo, sm, rm, sy, ry, ls, *scratch,
    ):
        net = Net(depth)
        sends = Sends()
        me = net.i * SEQ + net.y
        mine = pltpu.make_async_copy(moe_ref.at[net.i], moe_out.at[me], ls.at[0])
        work = Tally(net, part, part_rows, scratch[:11])
        mix = PlaneScatter(net, sends, mx_ref, block, scratch[11:])
        barrier = pltpu.get_barrier_semaphore()
        for device in net.zpeers() + net.plane():
            pl.semaphore_signal(barrier, inc=1, device_id=device, device_id_type=MESH)
        pl.semaphore_wait(barrier, depth - 1 + E - 1)
        mix.begin()
        for di in range(1, INNER):
            i = lax.rem(net.i + di, INNER)
            sends.start(
                moe_ref.at[i], moe_out.at[me], sm.at[di], rm.at[di], net.dev(i=i)
            )
        sends.start(moe_ref.at[net.i], moe_out.at[me], sm.at[0], rm.at[0], net.yp)
        mine.start()
        cos, sin = c_ref[...], -n_ref[...]
        for k in range(2):
            at = slice(k * block, (k + 1) * block)
            for h in range(GROUP):
                cols = slice(h * HEAD, (h + 1) * HEAD)
                v = dq_ref[k, :, cols].astype(F32)
                raw[at, cols] = turn(v, cos[at], sin[at]).astype(BF)
        dk = dkv_ref[:, :HEAD].astype(BF).astype(F32)
        raw[:, QCOLS : QCOLS + HEAD] = turn(dk, cos, sin).astype(BF)
        raw[:, QCOLS + HEAD :] = dkv_ref[:, HEAD:].astype(BF)
        mix.cores()
        low_wo[...] = oo_ref[...].astype(BF)
        sends.start(low_wo, pair_wo, sy.at[1], ry.at[1], net.yp)

        def half(y):
            at = pl.ds(pl.multiple_of(y * block, block), block)
            x = s_ref[at, :].astype(F32)
            scale = lax.rsqrt(jnp.mean(x * x, axis=-1, keepdims=True) + EPS)
            grad = dot(raw[at, :], w_ref[:, :QKV], NT)
            return x * scale, scale, grad

        normed, _, grad = half(1 - net.y)
        give[...] = grad.astype(BF)
        sends.start(give, take, sy.at[2], ry.at[2], net.yp)
        gain_part = jnp.sum(grad * normed, axis=0, keepdims=True)
        normed, scale, grad = half(net.y)
        gain_part = gain_part + jnp.sum(grad * normed, axis=0, keepdims=True)
        lanes = lax.broadcasted_iota(jnp.int32, (EXTRA, WIDTH), 0)
        extra = jnp.where(lanes == 0, gain_part, sm_ref[...]).T.astype(BF)
        per = wide // part_rows
        for c in range(WIDTH // wide):
            g = dot(h1_ref[:, c * wide : (c + 1) * wide].T, raw[...]).astype(BF)
            for b in range(per):
                part[c * per + b, :, :QKV] = g[b * part_rows : (b + 1) * part_rows]
                part[c * per + b, :, QKV:] = extra[
                    c * wide + b * part_rows : c * wide + (b + 1) * part_rows
                ]
        work.begin()
        work.far_stages()
        mix.turn()
        for di in range(1, INNER):
            got = moe_out.at[lax.rem(net.i - di + INNER, INNER) * SEQ + net.y]
            arrived(got, sm.at[di], rm.at[di], net.yp)
            sends.start(got, got, sm.at[INNER - 1 + di], rm.at[INNER - 1 + di], net.yp)
        arrived(take, sy.at[2], ry.at[2], net.yp)
        inner = (grad + take[...].astype(F32)) * ga_ref[...]
        pull = scale * (inner - normed * jnp.mean(inner * normed, axis=-1, keepdims=True))
        sg_out[...] = (dx_ref[...] + pull).astype(BF)
        work.near_stages()
        work.final(own_out)
        low[...] = own_out[...].astype(BF)
        sends.start(low, pair_out, sy.at[0], ry.at[0], net.yp)
        mix.final(res_out, [x1_ref])
        for di in range(INNER):
            n = INNER - 1 + di if di else 0
            got = moe_out.at[lax.rem(net.i - di + INNER, INNER) * SEQ + 1 - net.y]
            arrived(got, sm.at[n], rm.at[n], net.yp)
        arrived(pair_wo, sy.at[1], ry.at[1], net.yp)
        arrived(pair_out, sy.at[0], ry.at[0], net.yp)
        sends.finish()
        work.finish()
        mine.wait()

    sds = jax.ShapeDtypeStruct
    return pl.pallas_call(
        kernel,
        out_shape=(
            sds((block, WIDTH), BF),
            sds((block, WIDTH), BF),
            sds((part_rows, FIRST), F32),
            sds((part_rows, FIRST), BF),
            sds((part_rows, QCOLS), BF),
            sds((E,) + moe.shape[1:], BF),
        ),
        in_specs=[vmem()] * 13 + [hbm()],
        out_specs=(vmem(),) * 5 + (hbm(),),
        scratch_shapes=[
            pltpu.VMEM((rows, QKV), BF),
            pltpu.VMEM((shards, part_rows, FIRST), BF),
            pltpu.VMEM((block, WIDTH), BF),
            pltpu.VMEM((block, WIDTH), BF),
            pltpu.VMEM((part_rows, FIRST), BF),
            pltpu.VMEM((part_rows, QCOLS), BF),
        ]
        + dma_sems(2 * INNER - 1, 2 * INNER - 1, 3, 3, 1)
        + ShardScatter.scratch(depth, part_rows, FIRST)
        + PlaneScatter.scratch(block, WIDTH),
        compiler_params=comm_params(9, 60 << 20),
        name="finish_layer",
    )(dq, dkv, cosine, sine, h1, weights, pair, small, dx1, gain_a, out_own, mixture, x1, moe)


def run_expert(h2, out_grad, onehot, gate, lane, moe_w, rows_in, rows_out):
    blocks, tokens = h2.shape[:2]
    slots = onehot.shape[1]
    shards = moe_w.shape[0]
    pairs = 2
    steps = blocks // pairs
    wide = WIDTH + EXTRA

    def kernel(
        h_ref, g_ref, oh_ref, gt_ref, ln_ref, w_ref, mix_out, back_out, grads_out,
        gu_w, dn_w, gu_acc, dn_acc, rows, slot_g, stage, wsem, gsem,
    ):
        step = pl.program_id(0)

        def weight_copies():
            for n in range(shards):
                yield pltpu.make_async_copy(
                    w_ref.at[n, pl.ds(0, rows_in)], gu_w.at[pl.ds(n * rows_in, rows_in)], wsem.at[n]
                )
                yield pltpu.make_async_copy(
                    w_ref.at[n, pl.ds(rows_in, rows_out)],
                    dn_w.at[pl.ds(n * rows_out, rows_out)],
                    wsem.at[shards + n],
                )

        @pl.when(step == 0)
        def _():
            for copy in weight_copies():
                copy.start()
            gu_acc[...] = jnp.zeros_like(gu_acc)
            dn_acc[...] = jnp.zeros_like(dn_acc)
            for copy in weight_copies():
                copy.wait()

        for b in range(pairs):
            at = slice(b * slots, (b + 1) * slots)
            rows[at, :] = dot(oh_ref[b], h_ref[b]).astype(BF)
            slot_g[at, :] = dot(oh_ref[b], g_ref[b]).astype(BF)
        gate_col = gt_ref[...].reshape(pairs * slots, 1)
        both = dot(rows[...], gu_w[...])
        pre, up = both[:, :FF], both[:, FF:]
        phi = 0.5 * (1.0 + lax.erf(pre * (0.5**0.5)))
        slope = phi + pre * jnp.exp(-0.5 * pre * pre) * 0.3989422804014327
        gelu = pre * phi
        active = (gelu * up).astype(BF)
        grad = slot_g[...]
        out = dot(active, dn_w[...])
        gate_grad = jnp.sum(grad.astype(F32) * out, axis=-1, keepdims=True)
        mixed = (out * gate_col).astype(BF)
        expert_grad = (grad.astype(F32) * gate_col).astype(BF)
        active_grad = dot(expert_grad, dn_w[...], NT)
        low = jnp.concatenate(
            [(active_grad * up * slope).astype(BF), (active_grad * gelu).astype(BF)], axis=1
        )
        back = dot(low, gu_w[...], NT).astype(BF)
        back = jnp.concatenate([back, (gate_grad * ln_ref[...]).astype(BF)], axis=1)
        for b in range(pairs):
            at = slice(b * slots, (b + 1) * slots)
            spread = oh_ref[b].T
            mix_out[b] = dot(spread, mixed[at]).astype(BF)
            back_out[b] = dot(spread, back[at]).astype(BF)
        gu_acc[...] += dot(rows[...].T, low)
        dn_acc[...] += dot(active.T, expert_grad)

        @pl.when(step == steps - 1)
        def _():
            def copy(n, slot):
                return pltpu.make_async_copy(stage.at[slot], grads_out.at[n], gsem.at[slot])

            for n in range(shards):
                slot = n % 2
                if n >= 2:
                    copy(n - 2, slot).wait()
                stage[slot, :rows_in, :] = gu_acc[n * rows_in : (n + 1) * rows_in, :].astype(BF)
                stage[slot, rows_in:, :] = dn_acc[n * rows_out : (n + 1) * rows_out, :].astype(BF)
                copy(n, slot).start()
            for n in range(shards - 2, shards):
                copy(n, n % 2).wait()

    sds = jax.ShapeDtypeStruct
    block = lambda *shape: pl.BlockSpec((pairs,) + shape, lambda n: (n,) + (0,) * len(shape))
    return pl.pallas_call(
        kernel,
        grid=(steps,),
        out_shape=(
            sds((blocks, tokens, WIDTH), BF),
            sds((blocks, tokens, wide), BF),
            sds(moe_w.shape, BF),
        ),
        in_specs=[
            block(tokens, WIDTH),
            block(tokens, WIDTH),
            block(slots, tokens),
            block(slots, 1),
            pl.BlockSpec((1, EXTRA), lambda n: (0, 0)),
            hbm(),
        ],
        out_specs=(block(tokens, WIDTH), block(tokens, wide), hbm()),
        scratch_shapes=[
            pltpu.VMEM((WIDTH, 2 * FF), BF),
            pltpu.VMEM((FF, WIDTH), BF),
            pltpu.VMEM((WIDTH, 2 * FF), F32),
            pltpu.VMEM((FF, WIDTH), F32),
            pltpu.VMEM((pairs * slots, WIDTH), BF),
            pltpu.VMEM((pairs * slots, WIDTH), BF),
            pltpu.VMEM((2, rows_in + rows_out, WIDTH), BF),
        ]
        + dma_sems(2 * shards, 2),
        compiler_params=pltpu.CompilerParams(
            vmem_limit_bytes=60 << 20, dimension_semantics=("arbitrary",)
        ),
        cost_estimate=pl.CostEstimate(
            flops=int(3.8e10), bytes_accessed=40 << 20, transcendentals=4 << 20
        ),
        name="run_expert",
    )(h2, out_grad, onehot, gate, lane, moe_w)


def rms_parts(x):
    scale = lax.rsqrt(jnp.mean(x * x, axis=-1, keepdims=True) + EPS)
    return x * scale, scale


def rms_pull(normed, scale, grad, gain):
    inner = grad * gain
    return scale * (inner - normed * jnp.mean(inner * normed, axis=-1, keepdims=True))


def document_first(index, starts):
    return jnp.max(jnp.where(starts <= index[..., None], starts, 0), axis=-1)


def gelu_product(gate_pre, up_pre):
    return jax.nn.gelu(gate_pre, approximate=False) * up_pre


class Zigzag:
    def __init__(self, shards):
        last = 2 * shards - 1
        home = lambda b: b if b < shards else last - b
        self.rows = [
            [(s * 2 + y, home(2 * s + k) * 2 + y) for s in range(shards) for y in range(2)]
            for k in range(2)
        ]
        self.heads = [
            [
                (s * 2 + g, s if (g == 0) == (k == 0) else last - s)
                for s in range(shards)
                for g in range(2)
            ]
            for k in range(2)
        ]

    @staticmethod
    def move(x, pairs, back=False):
        return lax.ppermute(x, AXES, [(b, a) for a, b in pairs] if back else pairs)


def pick(flag, a, b):
    return jnp.where(flag, a, b), jnp.where(flag, b, a)


def experts(h2, out_grad, chosen, router_w, moe_w, rows_in, rows_out, me):
    blocks, tokens = h2.shape[:2]
    logits = dot(h2.reshape(blocks * tokens, WIDTH), router_w)
    probs = jax.nn.softmax(logits, axis=-1)
    mine = (jnp.arange(E) == me).astype(F32)
    named = jnp.sum(chosen * mine[None, :, None], axis=1)
    gate_tok = jnp.sum(probs * mine[None, :], axis=-1).reshape(blocks, tokens) * named
    upper = (jnp.arange(tokens)[:, None] <= jnp.arange(tokens)[None, :]).astype(BF)
    rank = dot(named.astype(BF), upper) - 1.0
    pick_slot = (
        rank[:, None, :] == jnp.arange(MOST, dtype=F32)[None, :, None]
    ) & (named[:, None, :] > 0.5)
    onehot = pick_slot.astype(BF)
    slots = blocks * MOST
    gate = jnp.sum(jnp.where(pick_slot, gate_tok[:, None, :], 0.0), axis=-1)
    if rows_in % 16 == 0 and rows_out % 16 == 0:
        lane = (jnp.arange(EXTRA) == me).astype(F32)[None, :]
        return run_expert(
            h2, out_grad, onehot, gate[:, :, None], lane, moe_w, rows_in, rows_out
        )
    gate = gate.reshape(slots, 1)
    spread = lambda v: lax.dot_general(
        onehot, v, (((2,), (1,)), ((0,), (0,))), preferred_element_type=F32
    )
    collect = lambda v: lax.dot_general(
        onehot, v, (((1,), (1,)), ((0,), (0,))), preferred_element_type=F32
    )
    rows = spread(h2).astype(BF).reshape(slots, WIDTH)
    slot_grad = spread(out_grad).astype(BF).reshape(slots, WIDTH)
    gate_w = moe_w[:, :rows_in, :FF].reshape(WIDTH, FF)
    up_w = moe_w[:, :rows_in, FF:].reshape(WIDTH, FF)
    down_w = moe_w[:, rows_in:, :].reshape(FF, WIDTH)
    gate_pre = dot(rows, gate_w)
    up_pre = dot(rows, up_w)
    active_f, pull = jax.vjp(gelu_product, gate_pre, up_pre)
    active = active_f.astype(BF)
    out = dot(active, down_w)
    slot_gf = slot_grad.astype(F32)
    gate_grad = jnp.sum(slot_gf * out, axis=-1).reshape(blocks, MOST)
    mixture = collect((out * gate).astype(BF).reshape(blocks, MOST, WIDTH)).astype(BF)
    expert_grad = (slot_gf * gate).astype(BF)
    active_grad = dot(expert_grad, down_w, NT)
    g_low, u_low = (v.astype(BF) for v in pull(active_grad))
    back = dot(g_low, gate_w, NT) + dot(u_low, up_w, NT)
    back_tok = collect(back.astype(BF).reshape(blocks, MOST, WIDTH)).astype(BF)
    gate_back = jnp.sum(jnp.where(pick_slot, gate_grad[:, :, None], 0.0), axis=1)
    lanes = (jnp.arange(EXTRA) == me).astype(F32)
    back_tok = jnp.concatenate(
        [back_tok, (gate_back[:, :, None] * lanes[None, None, :]).astype(BF)], axis=-1
    )
    shards = WIDTH // rows_in
    grads = jnp.concatenate(
        [
            jnp.concatenate(
                [
                    dot(rows, g_low, TN).astype(BF).reshape(shards, rows_in, FF),
                    dot(rows, u_low, TN).astype(BF).reshape(shards, rows_in, FF),
                ],
                axis=-1,
            ),
            dot(active, expert_grad, TN).astype(BF).reshape(shards, rows_out, WIDTH),
        ],
        axis=1,
    )
    return mixture, back_tok, grads


def back_apart(zig, q, kv, lo, info, top, total, ob, mixed, dx1, out_w, part_rows, depth):
    z, i, y = (lax.axis_index(a) for a in AXES)
    shards, rows = kv.shape[:2]
    shard = z * INNER + i
    even, head_zero = lax.rem(shard, 2) == 0, y == 0
    dob = dot(dx1, out_w, NT).astype(BF)
    out_part = dot(mixed, dx1, TN).astype(BF)
    keep, give = pick(head_zero, out_part[:, :QCOLS], out_part[:, QCOLS:])
    keep = keep.astype(F32) + lax.ppermute(give, "seq", [(0, 1), (1, 0)]).astype(F32)
    out_own = scatter_keys(keep.astype(BF).reshape(shards, part_rows, QCOLS), depth, 10)
    dob_a, dob_b = pick(shard * SEQ + y < shards, dob[:, :QCOLS], dob[:, QCOLS:])
    dob_zig = jnp.stack(
        pick(
            head_zero,
            zig.move(dob_a, zig.heads[0], True),
            zig.move(dob_b, zig.heads[1], True),
        )
    )
    flat = kv.reshape(shards * rows, 2 * HEAD)
    dq, dkv_part = attend_backward(q, flat, lo, info, top, total, dob_zig, ob)
    dq_a, dq_b = pick(even, dq[0], dq[1])
    dq_pair = jnp.stack([zig.move(dq_a, zig.rows[0], True), zig.move(dq_b, zig.rows[1], True)])
    return dq_pair, scatter_keys(dkv_part.reshape(kv.shape), depth, 5), out_own


def local(depth, stream, doc_starts, routes, attn_gain, w_query, w_key, w_value, w_out, ffn_gain, w_router, w_gate, w_up, w_down, out_grad):
    tokens = stream.shape[0]
    rows_in, rows_out = w_gate.shape[1], w_down.shape[1]
    shards = depth * INNER
    z, i, y = (lax.axis_index(a) for a in AXES)
    shard = z * INNER + i
    me = i * SEQ + y
    zig = Zigzag(shards)

    cut = lambda w, width: lax.dynamic_slice_in_dim(w, y * width, width, 1)
    extra = jnp.concatenate(
        [
            attn_gain[:, None],
            ffn_gain[:, None],
            w_router,
            jnp.zeros((rows_in, EXTRA - 2 - E), BF),
        ],
        axis=1,
    )
    pack = jnp.concatenate(
        [cut(w_query, QCOLS), cut(w_key, HEAD), cut(w_value, HEAD), extra], axis=1
    )
    moe_pack = jnp.concatenate([jnp.concatenate([w_gate, w_up], axis=2), w_down], axis=1)
    chosen_t = jnp.any(
        routes.T[:, None, :] == jnp.arange(E, dtype=jnp.int32)[None, :, None], axis=0
    ).astype(F32)
    pair_index = shard * SEQ * tokens + jnp.arange(SEQ * tokens, dtype=jnp.int32)
    position = pair_index - document_first(pair_index, doc_starts)
    freq = ROPE_BASE ** (-(jnp.arange(HEAD // 2, dtype=F32) * 2.0) / HEAD)
    angle = position.astype(F32)[:, None] * freq[None, :]
    cos_half, sin_half = jnp.cos(angle), jnp.sin(angle)
    cosine = jnp.concatenate([cos_half, cos_half], axis=1)
    sine = jnp.concatenate([-sin_half, sin_half], axis=1)

    block_ids = jnp.stack([shard, 2 * shards - 1 - shard]).astype(jnp.int32)
    query_index = block_ids[:, None] * tokens + jnp.arange(tokens, dtype=jnp.int32)[None, :]
    lo = document_first(query_index, doc_starts).astype(jnp.int32)
    info = jnp.concatenate([block_ids, lo[:, 0], lo[:, -1], jnp.zeros((2,), jnp.int32)])
    big = jnp.int32(1 << 30)
    spare = jnp.full((HEAD - doc_starts.shape[0],), big)
    first = jnp.concatenate([doc_starts, spare])
    beyond = jnp.concatenate([doc_starts[1:], spare, big[None]])
    starts = jnp.stack([first, beyond])
    outside = (query_index[..., None] < first) | (query_index[..., None] >= beyond)
    qseg = jnp.where(outside, NEG, 0.0).astype(BF)
    lo = lo[:, None, :]
    (
        pair, weights, chosen_all, h1, q, kv, ob, top, total, mixed, x1, h2_plane, out_w, grad_plane, moe_w,
    ) = front(stream, pack, moe_pack, chosen_t, cosine, sine, w_out, out_grad, qseg, starts, depth)
    extra_w = weights[:, QKV : QKV + EXTRA]
    gains = extra_w[:, :2].astype(F32).T
    gain_a, gain_f = gains[0:1], gains[1:2]
    router_w = extra_w[:, 2 : 2 + E]
    qkv_w = weights[:, :QKV]
    head_zero = y == 0
    mixed_pair = mixed
    mixed = jnp.concatenate([mixed[0], mixed[1]], axis=1)
    normed, scale = rms_parts(x1)
    h2 = (normed * gain_f).astype(BF)

    mixture_part, back_part, moe_grads = experts(
        h2_plane, grad_plane, chosen_all, router_w, moe_w, rows_in, rows_out, me
    )
    back = scatter_plane(back_part, depth)
    moe_own = lax.psum_scatter(
        moe_grads.reshape(depth, INNER, rows_in + rows_out, WIDTH),
        "outer",
        scatter_dimension=0,
        tiled=False,
    )

    chosen = chosen_t.T
    probs = jax.nn.softmax(dot(h2, router_w), axis=-1)
    dp = back[:, WIDTH : WIDTH + E] * chosen
    dz = (probs * (dp - jnp.sum(dp * probs, axis=-1, keepdims=True))).astype(BF)
    router_part = dot(dz, h2, TN)
    dh2 = back[:, :WIDTH] + dot(dz, router_w, NT)
    grad_f = out_grad.astype(F32)
    dx1 = grad_f + rms_pull(normed, scale, dh2, gain_f)
    gain_f_part = jnp.sum(dh2 * normed, axis=0)
    dx1_low = dx1.astype(BF)
    if depth <= 4:
        dq_pair, dkv, out_own = backward(
            q, kv, qseg, starts, top, total, ob, mixed_pair, dx1_low, out_w, rows_in, depth
        )
    else:
        dq_pair, dkv, out_own = back_apart(
            zig, q, kv, lo, info, top, total, ob, mixed, dx1_low, out_w, rows_in, depth
        )
    small = jnp.concatenate(
        [
            jnp.zeros((1, WIDTH), F32),
            gain_f_part[None, :],
            router_part,
            jnp.zeros((EXTRA - 2 - E, WIDTH), F32),
        ],
        axis=0,
    )
    result, stream_grad, own, peer, peer_out, moe_out = finish_layer(
        dq_pair,
        dkv,
        cosine,
        sine,
        h1,
        weights,
        pair,
        small,
        dx1,
        gain_a,
        out_own,
        mixture_part,
        x1,
        moe_own,
        depth,
    )
    peer = peer.astype(F32)

    def halves(a, b):
        return jnp.concatenate(pick(head_zero, own[:, a:b], peer[:, a:b]), axis=1)

    both = own[:, QKV:] + peer[:, QKV:]
    moe_out = moe_out.astype(F32)
    return (
        result,
        stream_grad,
        both[:, 0],
        halves(0, QCOLS),
        halves(QCOLS, QCOLS + HEAD),
        halves(QCOLS + HEAD, QKV),
        jnp.concatenate(pick(head_zero, out_own, peer_out.astype(F32)), axis=1),
        both[:, 1],
        both[:, 2 : 2 + E],
        moe_out[:, :rows_in, :FF],
        moe_out[:, :rows_in, FF:],
        moe_out[:, rows_in:, :],
    )


def solution(mesh):
    shards = mesh.shape["shard"]
    depth = shards // INNER
    fine = Mesh(mesh.devices.reshape(depth, INNER, SEQ), AXES)
    shard = ("outer", "inner")
    tokens = P(AXES, None)
    in_specs = (
        tokens,
        P(),
        tokens,
        P(shard),
        P(shard, None),
        P(shard, None),
        P(shard, None),
        P(shard, None),
        P(shard),
        P(shard, None),
        P(None, shard, None),
        P(None, shard, None),
        P(None, shard, None),
        tokens,
    )
    out_specs = (
        tokens,
        tokens,
        P(shard),
        P(shard, None),
        P(shard, None),
        P(shard, None),
        P(shard, None),
        P(shard),
        P(shard, None),
        P(None, shard, None),
        P(None, shard, None),
        P(None, shard, None),
    )

    def run(*args):
        return local(depth, *args)

    return jax.shard_map(run, mesh=fine, in_specs=in_specs, out_specs=out_specs, check_vma=False)
```

```python
import jax
import jax.numpy as jnp
from jax import lax
from jax.experimental import pallas as pl
from jax.experimental.pallas import tpu as pltpu
from jax.sharding import Mesh, PartitionSpec as P

WIDTH = 1536
HEADS = 12
KV_HEADS = 2
HEAD = 128
FF = 768
E = 8
MOST = 192
SEQ = KV_HEADS
GROUP = HEADS // KV_HEADS
INNER = E // SEQ
QCOLS = GROUP * HEAD
QKV = QCOLS + 2 * HEAD
EXTRA = 128
FIRST = QKV + EXTRA
PACK = QKV + EXTRA + WIDTH
EPS = 1e-06
ROPE_BASE = 10000.0
SCALE = HEAD**-0.5
LOG2E = 1.4426950408889634
LN2 = 0.6931471805599453
NEG = -1e30
AXES = ("outer", "inner", "seq")
MESH = pl.DeviceIdType.MESH
NN = (((1,), (0,)), ((), ()))
NT = (((1,), (1,)), ((), ()))
TN = (((0,), (0,)), ((), ()))
BF = jnp.bfloat16
F32 = jnp.float32


def dot(a, b, dims=NN):
    return lax.dot_general(a, b, dims, preferred_element_type=F32)


class Net:
    def __init__(self, depth):
        self.depth = depth
        self.z = lax.axis_index("outer")
        self.i = lax.axis_index("inner")
        self.y = lax.axis_index("seq")
        self.core = lax.rem(self.i, 2)
        self.x = lax.div(self.i, 2)
        self.xp = self.dev(i=lax.rem(self.i + 2, INNER))
        self.cp = self.dev(i=self.i + 1 - 2 * self.core)
        self.yp = self.dev(y=1 - self.y)

    def dev(self, z=None, i=None, y=None):
        return {
            "outer": self.z if z is None else z,
            "inner": self.i if i is None else i,
            "seq": self.y if y is None else y,
        }

    def zoff(self, dz):
        return lax.rem(self.z + dz, self.depth)

    def zpeers(self):
        return [self.dev(z=self.zoff(dz)) for dz in range(1, self.depth)]

    def plane(self):
        out = []
        for di in range(INNER):
            for dy in range(SEQ):
                if di or dy:
                    out.append(
                        self.dev(i=lax.rem(self.i + di, INNER), y=lax.rem(self.y + dy, SEQ))
                    )
        return out


def greet(devices):
    barrier = pltpu.get_barrier_semaphore()
    for device in devices:
        pl.semaphore_signal(barrier, inc=1, device_id=device, device_id_type=MESH)
    pl.semaphore_wait(barrier, len(devices))


def remote(src, dst, ssem, rsem, device):
    return pltpu.make_async_remote_copy(
        src_ref=src, dst_ref=dst, send_sem=ssem, recv_sem=rsem, device_id=device, device_id_type=MESH
    )


class Sends:
    def __init__(self):
        self.items = []

    def start(self, *refs):
        self.later(lambda: refs)

    def later(self, refs):
        remote(*refs()).start()
        self.items.append(refs)

    def finish(self):
        for refs in self.items:
            remote(*refs()).wait_send()


def arrived(dst, ssem, rsem, device):
    remote(dst, dst, ssem, rsem, device).wait_recv()


def dma_sems(*counts):
    return [pltpu.SemaphoreType.DMA((n,)) for n in counts]


class FlatSlots:
    class At:
        def __init__(self, ref, rows):
            self.ref, self.rows = ref, rows

        def __getitem__(self, n):
            return self.ref.at[pl.ds(pl.multiple_of(n * self.rows, self.rows), self.rows)]

    def __init__(self, ref, rows):
        self.at = self.At(ref, rows)


class ShardGather:
    def __init__(self, net, sends, src, out, sems):
        self.net, self.sends, self.src, self.out = net, sends, src, out
        self.sz, self.rz, self.sx, self.rx, self.sc, self.rc = sems
        self.xi = lax.rem(net.i + 2, INNER)

    @staticmethod
    def sems(depth):
        return dma_sems(*([max(depth - 1, 1)] * 2 + [depth] * 2 + [2 * depth] * 2))

    def slot(self, dz, i):
        return self.out.at[lax.rem(self.net.z - dz + self.net.depth, self.net.depth) * INNER + i]

    def begin(self):
        net, me = self.net, self.slot(0, self.net.i)
        for n, device in enumerate(net.zpeers()):
            self.sends.start(self.src, me, self.sz.at[n], self.rz.at[n], device)
        self.sends.start(self.src, me, self.sx.at[0], self.rx.at[0], net.xp)
        self.sends.start(self.src, me, self.sc.at[0], self.rc.at[0], net.cp)

    def pass_on(self, dz, i, ssem, rsem, n, device):
        self.sends.later(
            lambda: (self.slot(dz, i), self.slot(dz, i), ssem.at[n], rsem.at[n], device)
        )

    def after_z(self):
        net = self.net
        for dz in range(1, net.depth):
            block = self.slot(dz, net.i)
            arrived(block, self.sz.at[dz - 1], self.rz.at[dz - 1], net.xp)
            self.pass_on(dz, net.i, self.sx, self.rx, dz, net.xp)
            self.pass_on(dz, net.i, self.sc, self.rc, dz, net.cp)

    def after_x(self):
        net, depth = self.net, self.net.depth
        for dz in range(depth):
            arrived(self.slot(dz, self.xi), self.sx.at[dz], self.rx.at[dz], net.xp)
            self.pass_on(dz, self.xi, self.sc, self.rc, depth + dz, net.cp)

    def last(self):
        net, depth = self.net, self.net.depth
        ci = net.i + 1 - 2 * net.core
        for dz in range(depth):
            arrived(self.slot(dz, ci), self.sc.at[dz], self.rc.at[dz], net.cp)
        for dz in range(depth):
            arrived(
                self.slot(dz, lax.rem(ci + 2, INNER)),
                self.sc.at[depth + dz],
                self.rc.at[depth + dz],
                net.cp,
            )

    def end(self):
        self.after_z()
        self.after_x()
        self.last()

    def one_x(self, dz):
        net, block, n = self.net, self.slot(dz, self.xi), self.net.depth + dz
        arrived(block, self.sx.at[dz], self.rx.at[dz], net.xp)
        remote(block, block, self.sc.at[n], self.rc.at[n], net.cp).start()

    def one_c(self, n, place):
        block = self.out.at[place]
        arrived(block, self.sc.at[n], self.rc.at[n], self.net.cp)

    def sent_loop(self):
        net, depth = self.net, self.net.depth
        for dz in range(depth):
            block = self.slot(dz, self.xi)
            remote(block, block, self.sc.at[depth + dz], self.rc.at[depth + dz], net.cp).wait_send()


def hbm():
    return pl.BlockSpec(memory_space=pltpu.HBM)


def vmem():
    return pl.BlockSpec(memory_space=pltpu.VMEM)


def smem():
    return pl.BlockSpec(memory_space=pltpu.SMEM)


def comm_params(cid, limit=56 << 20):
    return pltpu.CompilerParams(
        collective_id=cid, has_side_effects=True, vmem_limit_bytes=limit
    )


def add_into(dst, sources, rows, chunk):
    def body(n, carry):
        at = pl.ds(pl.multiple_of(n * chunk, chunk), chunk)
        total = sources[0][at, :].astype(F32)
        for source in sources[1:]:
            total = total + source[at, :].astype(F32)
        dst[at, :] = total.astype(dst.dtype)
        return carry

    lax.fori_loop(0, rows // chunk, body, 0)


def chunk_of(rows):
    for size in (32, 16, 8):
        if rows % size == 0:
            return size
    return rows


class PlaneScatter:
    ORDER = ((1, 1), (1, 0), (0, 1), (0, 0))

    @staticmethod
    def scratch(rows, cols):
        return (
            [pltpu.VMEM((4, rows, cols), BF)] * 2
            + [pltpu.VMEM((2, rows // 2, cols), BF)] * 4
            + dma_sems(10, 10)
        )

    def __init__(self, net, sends, part, rows, scratch):
        self.net, self.sends, self.part, self.rows = net, sends, part, rows
        self.bc, self.mid, self.bx, self.by, self.second, self.b2, self.ss, self.rs = scratch
        self.half = rows // 2
        self.lo, self.hi = pl.ds(0, self.half), pl.ds(self.half, self.half)
        self.chunk = chunk_of(self.half)

    def place(self, fx, fy, core):
        x = 1 - self.net.x if fx else self.net.x
        y = 1 - self.net.y if fy else self.net.y
        return (x * 2 + core) * SEQ + y

    def send(self, src, dst, n, device):
        self.sends.later(lambda: (src(), dst(), self.ss.at[n], self.rs.at[n], device))

    def take(self, dst, n):
        arrived(dst, self.ss.at[n], self.rs.at[n], self.net.xp)

    def begin(self):
        net = self.net
        for n, (fx, fy) in enumerate(self.ORDER):
            src = lambda fx=fx, fy=fy: self.part.at[self.place(fx, fy, 1 - net.core)]
            self.send(src, lambda n=n: self.bc.at[n], n, net.cp)

    def cores(self):
        net, mid = self.net, self.mid
        for n, (fx, fy) in enumerate(self.ORDER):
            self.take(self.bc.at[n], n)
            own = self.part.at[self.place(fx, fy, net.core)]
            add_into(mid.at[n], [own, self.bc.at[n]], self.rows, self.chunk)
            if n == 0:
                self.send(lambda: mid.at[0, self.lo], lambda: self.bx.at[0], 4, net.xp)
                self.send(lambda: mid.at[0, self.hi], lambda: self.by.at[0], 5, net.yp)
            if n == 1:
                self.send(lambda: mid.at[1, self.lo], lambda: self.bx.at[1], 6, net.xp)
            if n == 2:
                self.send(lambda: mid.at[2, self.hi], lambda: self.by.at[1], 7, net.yp)

    def turn(self):
        net, mid, second = self.net, self.mid, self.second
        self.take(self.bx.at[0], 4)
        add_into(second.at[0], [mid.at[2, self.lo], self.bx.at[0]], self.half, self.chunk)
        self.send(lambda: second.at[0], lambda: self.b2.at[0], 8, net.yp)
        self.take(self.by.at[0], 5)
        add_into(second.at[1], [mid.at[1, self.hi], self.by.at[0]], self.half, self.chunk)
        self.send(lambda: second.at[1], lambda: self.b2.at[1], 9, net.xp)

    def final(self, out, more=()):
        mid = self.mid
        self.take(self.bx.at[1], 6)
        self.take(self.by.at[1], 7)
        for n, (at, got) in enumerate(((self.lo, self.bx), (self.hi, self.by))):
            self.take(self.b2.at[n], 8 + n)
            terms = [mid.at[3, at], got.at[1], self.b2.at[n]] + [m.at[at] for m in more]
            add_into(out.at[at], terms, self.half, self.chunk)


def scatter_plane(part, depth):
    rows, cols = part.shape[1:]

    def kernel(part_ref, out, *scratch):
        net = Net(depth)
        sends = Sends()
        greet([net.xp, net.yp, net.cp])
        work = PlaneScatter(net, sends, part_ref, rows, scratch)
        work.begin()
        work.cores()
        work.turn()
        work.final(out)
        sends.finish()

    return pl.pallas_call(
        kernel,
        out_shape=jax.ShapeDtypeStruct((rows, cols), F32),
        in_specs=[vmem()],
        out_specs=vmem(),
        scratch_shapes=PlaneScatter.scratch(rows, cols),
        compiler_params=comm_params(4),
        name="scatter_plane",
    )(part)


class ShardScatter:
    @staticmethod
    def scratch(depth, rows, cols):
        far = max(depth - 1, 1)
        shapes = [(2 * depth, rows, cols)] + [(depth, rows, cols)] * 2 + [(far, rows, cols)] * 2
        return [pltpu.VMEM(s, BF) for s in shapes] + dma_sems(
            2 * depth, 2 * depth, depth, depth, far, far
        )

    def __init__(self, net, sends, part, scratch):
        self.net, self.sends, self.part = net, sends, part
        self.bc, self.sx, self.bx, self.sz, self.bz = scratch[:5]
        self.ssc, self.rsc, self.ssx, self.rsx, self.ssz, self.rsz = scratch[5:]
        depth = net.depth
        self.order = sorted(range(1, depth), key=lambda d: -min(d, depth - d)) + [0]
        self.rows = part.shape[1]
        self.chunk = chunk_of(self.rows)

    def block(self, dz, fx, core):
        x = 1 - self.net.x if fx else self.net.x
        return self.part.at[self.net.zoff(dz) * INNER + x * 2 + core]

    def begin(self):
        net = self.net
        for dz in self.order:
            for fx in (1, 0):
                n = dz * 2 + fx
                self.sends.start(
                    self.block(dz, fx, 1 - net.core),
                    self.bc.at[n],
                    self.ssc.at[n],
                    self.rsc.at[n],
                    net.cp,
                )

    def end(self, out):
        net, sends = self.net, self.sends
        for dz in self.order:
            n = dz * 2 + 1
            arrived(self.bc.at[n], self.ssc.at[n], self.rsc.at[n], net.cp)
            add_into(
                self.sx.at[dz], [self.block(dz, 1, net.core), self.bc.at[n]], self.rows, self.chunk
            )
            sends.start(self.sx.at[dz], self.bx.at[dz], self.ssx.at[dz], self.rsx.at[dz], net.xp)
        for dz in self.order:
            n = dz * 2
            arrived(self.bc.at[n], self.ssc.at[n], self.rsc.at[n], net.cp)
            arrived(self.bx.at[dz], self.ssx.at[dz], self.rsx.at[dz], net.xp)
            terms = [self.block(dz, 0, net.core), self.bc.at[n], self.bx.at[dz]]
            if dz:
                add_into(self.sz.at[dz - 1], terms, self.rows, self.chunk)
                sends.start(
                    self.sz.at[dz - 1],
                    self.bz.at[dz - 1],
                    self.ssz.at[dz - 1],
                    self.rsz.at[dz - 1],
                    net.dev(z=net.zoff(dz)),
                )
            else:
                for far in range(net.depth - 1):
                    arrived(self.bz.at[far], self.ssz.at[far], self.rsz.at[far], net.xp)
                    terms.append(self.bz.at[far])
                add_into(out, terms, self.rows, self.chunk)


def scatter_keys(part, depth, cid):
    rows, cols = part.shape[1:]

    def kernel(part_ref, out, *scratch):
        net = Net(depth)
        sends = Sends()
        greet(net.zpeers() + [net.xp, net.cp])
        work = ShardScatter(net, sends, part_ref, scratch)
        work.begin()
        work.end(out)
        sends.finish()

    return pl.pallas_call(
        kernel,
        out_shape=jax.ShapeDtypeStruct((rows, cols), F32),
        in_specs=[vmem()],
        out_specs=vmem(),
        scratch_shapes=ShardScatter.scratch(depth, rows, cols),
        compiler_params=comm_params(cid),
        name="scatter_keys",
    )(part)


def turn(values, cosine, sine):
    return values * cosine + pltpu.roll(values, HEAD // 2, 1) * sine


def attend_backward(q, kv, lo, info, m, l, dob, ob, tile=512):
    block = q.shape[1]
    keys = kv.shape[0]
    tiles = keys // tile

    def kernel(info_ref, q_ref, kv_ref, lo_ref, m_ref, l_ref, do_ref, ob_ref, dq_ref, dkv_ref, da, dl, acc):
        acc[...] = jnp.zeros_like(acc)
        for j in range(2):
            for h in range(GROUP):
                c = slice(h * HEAD, (h + 1) * HEAD)
                d = do_ref[j, :, c].astype(F32)
                o = ob_ref[j, :, c].astype(F32)
                inv = 1.0 / l_ref[j, h : h + 1, :]
                da[j, h] = (d.T * inv).T.astype(BF)
                dl[j, h : h + 1, :] = -jnp.sum((d * o).T, axis=0, keepdims=True) * inv
        low = jnp.minimum(info_ref[2], info_ref[3]) // tile
        high = (info_ref[1] * block + block - 1) // tile

        def clear(t, carry):
            dkv_ref[pl.ds(pl.multiple_of(t * tile, tile), tile), :] = jnp.zeros((tile, 2 * HEAD), BF)
            return carry

        lax.fori_loop(0, low, clear, 0)
        lax.fori_loop(high + 1, tiles, clear, 0)

        def piece(t, j, masked):
            start = pl.multiple_of(t * tile, tile)
            base = info_ref[j] * block
            k = kv_ref[pl.ds(start, tile), :HEAD]
            v = kv_ref[pl.ds(start, tile), HEAD:]
            kt = k.T
            if masked:
                key = start + lax.broadcasted_iota(jnp.int32, (tile, block), 0)
                query = base + lax.broadcasted_iota(jnp.int32, (tile, block), 1)
                ok = (key <= query) & (key >= lo_ref[j])
            dk = dv = None
            for h in range(GROUP):
                qh = q_ref[j, :, h * HEAD : (h + 1) * HEAD]
                s = dot(k, qh, NT) - m_ref[j, h : h + 1, :]
                if masked:
                    s = jnp.where(ok, s, NEG)
                p = jnp.exp2(s)
                dah = da[j, h]
                dvh = dot(p.astype(BF), dah)
                dp = dot(v, dah, NT) + dl[j, h : h + 1, :]
                ds = (p * dp).astype(BF)
                dkh = dot(ds, qh)
                acc[j, h] += dot(kt, ds)
                dk = dkh if dk is None else dk + dkh
                dv = dvh if dv is None else dv + dvh
            return dk * LN2, dv

        def tile_step(t, carry):
            start = pl.multiple_of(t * tile, tile)
            rows = pl.ds(start, tile)

            def put(j, masked):
                dk, dv = piece(t, j, masked)
                if j == 0:
                    dk = dk + dkv_ref[rows, :HEAD].astype(F32)
                    dv = dv + dkv_ref[rows, HEAD:].astype(F32)
                dkv_ref[rows, :HEAD] = dk.astype(BF)
                dkv_ref[rows, HEAD:] = dv.astype(BF)

            for j in (1, 0):
                base = info_ref[j] * block
                live = (start <= base + block - 1) & (start + tile > info_ref[2 + j])
                free = (start + tile - 1 <= base) & (start >= info_ref[4 + j])
                if j == 1:

                    @pl.when(jnp.logical_not(live))
                    def _():
                        clear(t, 0)

                @pl.when(live & free)
                def _():
                    put(j, False)

                @pl.when(live & jnp.logical_not(free))
                def _():
                    put(j, True)

            return carry

        lax.fori_loop(low, high + 1, tile_step, 0)
        for j in range(2):
            for h in range(GROUP):
                dq_ref[j, :, h * HEAD : (h + 1) * HEAD] = (acc[j, h] * SCALE).T.astype(BF)

    return pl.pallas_call(
        kernel,
        out_shape=(jax.ShapeDtypeStruct(q.shape, BF), jax.ShapeDtypeStruct(kv.shape, BF)),
        in_specs=[smem()] + [vmem()] * 7,
        out_specs=(vmem(),) * 2,
        scratch_shapes=[
            pltpu.VMEM((2, GROUP, block, HEAD), BF),
            pltpu.VMEM((2, 8, block), F32),
            pltpu.VMEM((2, GROUP, HEAD, block), F32),
        ],
        compiler_params=pltpu.CompilerParams(vmem_limit_bytes=60 << 20),
        cost_estimate=pl.CostEstimate(
            flops=int(2.5e10), bytes_accessed=12 << 20, transcendentals=13 << 20
        ),
        name="attend_backward",
    )(info, q, kv, lo, m, l, dob, ob)


class PlaneGather:
    @staticmethod
    def sems():
        return dma_sems(2, 2, 2, 2, 5, 5)

    def __init__(self, net, sends, src, out, sems, rows):
        self.net, self.sends, self.src, self.out = net, sends, src, out
        self.sx, self.rx, self.sy, self.ry, self.sc, self.rc = sems
        half = rows // 2
        self.lo, self.hi = pl.ds(0, half), pl.ds(half, half)
        xi = lax.rem(net.i + 2, INNER)
        ci = net.i + 1 - 2 * net.core
        cx = lax.rem(ci + 2, INNER)
        place = lambda i, y: i * SEQ + y
        self.me, self.xb = place(net.i, net.y), place(xi, net.y)
        self.yb, self.db = place(net.i, 1 - net.y), place(xi, 1 - net.y)
        self.core_blocks = [place(ci, net.y), place(ci, 1 - net.y), place(cx, net.y)]
        self.core_diag = place(cx, 1 - net.y)

    def begin(self):
        self.begin_y()
        self.begin_x()

    def begin_y(self):
        net, out, src = self.net, self.out, self.src
        self.sends.start(src, out.at[self.me], self.sy.at[0], self.ry.at[0], net.yp)
        self.sends.start(src, out.at[self.me], self.sc.at[0], self.rc.at[0], net.cp)

    def begin_x(self):
        net, out, src = self.net, self.out, self.src
        self.sends.start(src, out.at[self.me], self.sx.at[0], self.rx.at[0], net.xp)

    def pass_on(self, block, part, ssem, rsem, n, device):
        def refs():
            at = self.out.at[block] if part is None else self.out.at[block, part]
            return at, at, ssem.at[n], rsem.at[n], device

        self.sends.later(refs)

    def middle(self):
        net, out = self.net, self.out
        arrived(out.at[self.yb], self.sy.at[0], self.ry.at[0], net.yp)
        self.pass_on(self.yb, self.lo, self.sx, self.rx, 1, net.xp)
        self.pass_on(self.yb, None, self.sc, self.rc, 1, net.cp)
        arrived(out.at[self.xb], self.sx.at[0], self.rx.at[0], net.xp)
        self.pass_on(self.xb, self.hi, self.sy, self.ry, 1, net.yp)
        self.pass_on(self.xb, None, self.sc, self.rc, 2, net.cp)

    def end(self):
        net, out = self.net, self.out
        arrived(out.at[self.db, self.lo], self.sx.at[1], self.rx.at[1], net.xp)
        self.pass_on(self.db, self.lo, self.sc, self.rc, 3, net.cp)
        arrived(out.at[self.db, self.hi], self.sy.at[1], self.ry.at[1], net.yp)
        self.pass_on(self.db, self.hi, self.sc, self.rc, 4, net.cp)

    def last(self):
        net, out = self.net, self.out
        for n, block in enumerate(self.core_blocks):
            arrived(out.at[block], self.sc.at[n], self.rc.at[n], net.cp)
        arrived(out.at[self.core_diag, self.lo], self.sc.at[3], self.rc.at[3], net.cp)
        arrived(out.at[self.core_diag, self.hi], self.sc.at[4], self.rc.at[4], net.cp)


class Route:
    def __init__(self, net, sends_to, comes_from):
        self.net = net
        me = net.z * INNER + net.i
        self.local = (sends_to[0] == me) & (sends_to[1] == net.y)
        self.kept = (comes_from[0] == me) & (comes_from[1] == net.y)
        self.to, self.frm = self.device(sends_to), self.device(comes_from)

    def device(self, place):
        shard, y = place
        return self.net.dev(z=lax.div(shard, INNER), i=lax.rem(shard, INNER), y=y)

    def hello(self):
        @pl.when(jnp.logical_not(self.kept))
        def _():
            pl.semaphore_signal(
                pltpu.get_barrier_semaphore(), inc=1, device_id=self.frm, device_id_type=MESH
            )

        return jnp.where(self.local, 0, 1)

    def send(self, refs):
        @pl.when(self.local)
        def _():
            src, dst, _, _ = refs()
            dst[...] = src[...]

        @pl.when(jnp.logical_not(self.local))
        def _():
            remote(*refs(), self.to).start()

    def sent(self, refs):
        @pl.when(jnp.logical_not(self.local))
        def _():
            remote(*refs(), self.to).wait_send()

    def arrive(self, refs):
        @pl.when(jnp.logical_not(self.kept))
        def _():
            dst, ssem, rsem = refs()
            remote(dst, dst, ssem, rsem, self.to).wait_recv()


class Mirror:
    def __init__(self, net):
        self.net = net
        self.n = net.depth * INNER
        self.last = 2 * self.n - 1
        self.me = net.z * INNER + net.i

    def home(self, block):
        return jnp.where(block < self.n, block, self.last - block)

    def blocks(self):
        return self.me, self.last - self.me

    def slot(self, block):
        return jnp.where(block < self.n, 0, 1)

    def rows_out(self, k):
        block = 2 * self.me + k
        come = self.blocks()[k]
        return Route(
            self.net, (self.home(block), self.net.y), (lax.div(come, 2), self.net.y)
        ), self.slot(block)

    def rows_back(self, k):
        block = self.blocks()[k]
        come = 2 * self.me + k
        return Route(
            self.net, (lax.div(block, 2), self.net.y), (self.home(come), self.net.y)
        ), lax.rem(block, 2)

    def heads_back(self, k):
        block = self.blocks()[k]
        own = 2 * self.me + self.net.y
        return Route(self.net, (lax.div(block, 2), lax.rem(block, 2)), (self.home(own), k))

    def heads_out(self, k):
        own = 2 * self.me + self.net.y
        come = self.blocks()[k]
        return Route(
            self.net, (self.home(own), k), (lax.div(come, 2), lax.rem(come, 2))
        ), self.slot(own)


class Chain:
    @staticmethod
    def sems(depth):
        return dma_sems(*[max(depth - 1, 1) * INNER] * 4)

    def __init__(self, net, out, sems):
        self.net, self.out = net, out
        self.su, self.ru, self.sd, self.rd = sems
        self.steps = (net.depth - 1) * INNER
        self.up = net.dev(z=jnp.minimum(net.z + 1, net.depth - 1))
        self.down = net.dev(z=jnp.maximum(net.z - 1, 0))

    def piece(self, z, q):
        return self.out.at[z * INNER + q]

    def refs(self, hop, q, way):
        net = self.net
        n = (hop + 1) * INNER + q
        z = net.z - 1 - hop if way == 0 else net.z + 1 + hop
        ssem, rsem, device = (
            (self.su.at[n], self.ru.at[n], self.up)
            if way == 0
            else (self.sd.at[n], self.rd.at[n], self.down)
        )
        return self.piece(z, q), ssem, rsem, device

    def begin(self, ready):
        def body(q, carry):
            ready(q)
            for way in range(2):

                @pl.when(self.net.z < self.net.depth - 1 if way == 0 else self.net.z > 0)
                def _():
                    dst, ssem, rsem, device = self.refs(-1, q, way)
                    remote(dst, dst, ssem, rsem, device).start()

            return carry

        lax.fori_loop(0, INNER, body, 0)

    def step(self, n):
        net = self.net
        hop, q = lax.div(n, INNER), lax.rem(n, INNER)
        for way in range(2):
            z = net.z - 1 - hop if way == 0 else net.z + 1 + hop
            here = z >= 0 if way == 0 else z <= net.depth - 1
            further = net.z < net.depth - 1 if way == 0 else net.z > 0

            @pl.when(here)
            def _():
                block = self.piece(z, q)
                if way == 0:
                    arrived(block, self.su.at[n], self.ru.at[n], self.up)
                else:
                    arrived(block, self.sd.at[n], self.rd.at[n], self.down)

            @pl.when(here & further)
            def _():
                dst, ssem, rsem, device = self.refs(hop, q, way)
                remote(dst, dst, ssem, rsem, device).start()

    def run(self, a, b):
        def body(n, carry):
            self.step(n)
            return carry

        lax.fori_loop(a, min(b, self.steps), body, 0)

    def finish(self):
        def body(n, carry):
            hop, q = lax.div(n, INNER) - 1, lax.rem(n, INNER)
            for way in range(2):
                z = self.net.z - 1 - hop if way == 0 else self.net.z + 1 + hop
                here = z >= 0 if way == 0 else z <= self.net.depth - 1
                further = self.net.z < self.net.depth - 1 if way == 0 else self.net.z > 0

                @pl.when(here & further)
                def _():
                    dst, ssem, rsem, device = self.refs(hop, q, way)
                    remote(dst, dst, ssem, rsem, device).wait_send()

            return carry

        lax.fori_loop(0, self.steps, body, 0)


def seg_tile(start, rows, st, en):
    key = start + lax.broadcasted_iota(jnp.int32, (rows, HEAD), 0)
    return ((key >= st) & (key < en)).astype(F32).astype(BF)


def front(stream, pack, moe, chosen, cosine, sine, w_out, out_grad, qseg, starts, depth):
    block = stream.shape[0]
    rows = block * SEQ
    shards = depth * INNER
    part = w_out.shape[0]

    def kernel(
        st_ref, pk_ref, mo_ref, ch_ref, c_ref, n_ref, wo_ref, og_ref, qs_ref, sg_ref,
        s_out, w_full, ch_out, h1_out, q_out, kv_out, o_out, m_out, l_out, mix_out, x1_out, h2_out,
        wf_out, og_out, mo_out,
        qp, acc, top, total, h2_own, gains, own, sq, rq, so, ro, sy, ry, sp, rp, sm, rm, *sems,
    ):
        net = Net(depth)
        sends = Sends()
        mirror = Mirror(net)
        gp = ShardGather(net, sends, pk_ref, FlatSlots(w_full, part), sems[28:34])
        gk = ShardGather(net, sends, None, kv_out, sems[:6])
        gk.src = gk.slot(0, net.i)
        gw = ShardGather(net, sends, wo_ref, FlatSlots(wf_out, part), sems[6:12])
        gg = PlaneGather(net, sends, og_ref, og_out, sems[12:18], block)
        gh = PlaneGather(net, sends, h2_own, h2_out, sems[18:24], block)
        chain = Chain(net, mo_out, sems[24:28])
        rows_out = [mirror.rows_out(k) for k in range(2)]
        heads = [mirror.heads_back(k) for k in range(2)]
        barrier = pltpu.get_barrier_semaphore()
        for device in net.zpeers() + net.plane():
            pl.semaphore_signal(barrier, inc=1, device_id=device, device_id_type=MESH)
        count = depth - 1 + E - 1
        for route in [r for r, _ in rows_out] + heads:
            count = count + route.hello()
        here = lambda y: s_out.at[pl.ds(pl.multiple_of(y * block, block), block)]
        mine_p = pltpu.make_async_copy(pk_ref, gp.slot(0, net.i), own.at[4])
        mine_s = pltpu.make_async_copy(st_ref, here(net.y), own.at[5])
        mine_m = pltpu.make_async_copy(
            mo_ref.at[net.i * SEQ + net.y], mo_out.at[net.z * INNER + net.i], own.at[3]
        )
        mine_c = pltpu.make_async_copy(ch_ref, ch_out.at[net.i * SEQ + net.y], own.at[6])
        mine_g = pltpu.make_async_copy(og_ref, og_out.at[gg.me], own.at[0])
        mine_w = pltpu.make_async_copy(wo_ref, gw.slot(0, net.i), own.at[1])
        for copy in (mine_p, mine_s, mine_m, mine_c, mine_g, mine_w):
            copy.start()
        pl.semaphore_wait(barrier, count)
        gp.begin()
        sends.start(st_ref, here(net.y), sy.at[0], ry.at[0], net.yp)
        for n, device in enumerate(net.plane()):
            sends.start(ch_ref, ch_out.at[net.i * SEQ + net.y], sp.at[n], rp.at[n], device)
        gw.begin()
        gp.end()
        for di in range(1, INNER):
            other = lax.rem(net.i + di, INNER)
            sends.start(
                mo_ref.at[other * SEQ + net.y],
                mo_out.at[net.z * INNER + net.i],
                sm.at[di - 1],
                rm.at[di - 1],
                net.dev(i=other),
            )
        gg.begin_y()

        def moe_ready(q):
            di = lax.rem(net.i - q + INNER, INNER)

            @pl.when(di > 0)
            def _():
                arrived(mo_out.at[net.z * INNER + q], sm.at[di - 1], rm.at[di - 1], net.xp)

        arrived(here(1 - net.y), sy.at[0], ry.at[0], net.yp)
        mine_s.wait()
        mine_p.wait()
        tail = w_full[:, QKV:].astype(F32).T
        gains[...] = tail[:8, :]

        step = 64

        def norm(n, carry):
            at = pl.ds(pl.multiple_of(n * step, step), step)
            x = s_out[at, :].astype(F32)
            scale = lax.rsqrt(jnp.mean(x * x, axis=-1, keepdims=True) + EPS)
            h1_out[at, :] = (x * scale * gains[0:1, :]).astype(BF)
            return carry

        lax.fori_loop(0, rows // step, norm, 0)
        h1 = h1_out[...]
        cos, sin = c_ref[...], n_ref[...]
        r = dot(h1, w_full[:, QCOLS:QKV])
        me = net.z * INNER + net.i
        kv_out[me, :, :HEAD] = turn(r[:, :HEAD], cos, sin).astype(BF)
        kv_out[me, :, HEAD:] = r[:, HEAD:].astype(BF)
        gk.begin()
        for h in range(0, GROUP, 2):
            r = dot(h1, w_full[:, h * HEAD : (h + 2) * HEAD])
            for g in range(2):
                v = turn(r[:, g * HEAD : (g + 1) * HEAD], cos, sin) * (SCALE * LOG2E)
                v = v.astype(BF)
                at = slice((h + g) * HEAD, (h + g + 1) * HEAD)
                qp[0, :, at] = v[:block]
                qp[1, :, at] = v[block:]
        q_refs = [
            lambda k=k: (qp.at[k], q_out.at[rows_out[k][1]], sq.at[k], rq.at[rows_out[k][1]])
            for k in range(2)
        ]
        o_refs = [
            lambda k=k: (o_out.at[k], mix_out.at[net.y], so.at[k], ro.at[net.y]) for k in range(2)
        ]
        for k in range(2):
            rows_out[k][0].send(q_refs[k])
        mine_m.wait()
        mine_w.wait()
        chain.begin(moe_ready)
        gg.begin_x()
        acc[...] = jnp.zeros_like(acc)
        top[...] = jnp.full_like(top, NEG)
        total[...] = jnp.zeros_like(total)
        gk.after_z()
        for k in range(2):
            rows_out[k][0].arrive(lambda: (q_out.at[k], sq.at[k], rq.at[k]))

        low, high = mirror.blocks()
        bases = (low * block, high * block)
        xi = lax.rem(net.i + 2, INNER)
        ci = net.i + 1 - 2 * net.core

        def attend(t, j, masked):
            start = pl.multiple_of(t * rows, rows)
            k = jnp.concatenate(
                [kv_out[t, :, :HEAD], seg_tile(start, rows, sg_ref[0:1, :], sg_ref[1:2, :])], axis=1
            )
            vt = kv_out[t, :, HEAD:].T
            if masked:
                key = start + lax.broadcasted_iota(jnp.int32, (rows, block), 0)
                ok = key <= bases[j] + lax.broadcasted_iota(jnp.int32, (rows, block), 1)
            scores = [
                dot(
                    k,
                    jnp.concatenate(
                        [q_out[j, :, h * HEAD : (h + 1) * HEAD], qs_ref[j]], axis=1
                    ),
                    NT,
                )
                for h in range(GROUP)
            ]
            for h in range(GROUP):
                s = scores[h]
                if masked:
                    s = jnp.where(ok, s, NEG)
                m0 = top[j, h : h + 1, :]
                m1 = jnp.maximum(m0, jnp.max(s, axis=0, keepdims=True))
                p = jnp.exp2(s - m1)
                f = jnp.exp2(m0 - m1)
                top[j, h : h + 1, :] = m1
                total[j, h : h + 1, :] = total[j, h : h + 1, :] * f + jnp.sum(
                    p, axis=0, keepdims=True
                )
                acc[j, h] = acc[j, h] * f + dot(vt, p.astype(BF))

        polled = min((shards - depth) // 2, 2 * INNER - 1, chain.steps)

        def tile(u, carry):
            in_z = u < depth
            in_x = u < 2 * depth
            in_c = u < 3 * depth
            dz = lax.rem(u, depth)
            place = jnp.where(in_z, net.i, jnp.where(in_x, xi, jnp.where(in_c, ci, lax.rem(ci + 2, INNER))))
            t = lax.rem(net.z - dz + depth, depth) * INNER + place

            @pl.when((u >= depth) & in_x)
            def _():
                gk.one_x(dz)

            @pl.when(u >= 2 * depth)
            def _():
                gk.one_c(u - 2 * depth, t)

            @pl.when(u == 2 * depth)
            def _():
                gg.middle()
                gw.after_z()

            @pl.when(u == 3 * depth)
            def _():
                gw.after_x()
                gg.end()

            @pl.when((u >= depth) & (lax.rem(u - depth, 2) == 1) & (u - depth < 2 * polled))
            def _():
                chain.step(lax.div(u - depth, 2))

            for j in (0, 1):
                live = t * rows <= bases[j] + block - 1
                free = t * rows + rows - 1 <= bases[j]

                @pl.when(live & free)
                def _():
                    attend(t, j, False)

                @pl.when(live & jnp.logical_not(free))
                def _():
                    attend(t, j, True)

            return carry

        lax.fori_loop(0, shards, tile, 0)
        gk.sent_loop()
        for j in range(2):
            for h in range(GROUP):
                o_out[j, :, h * HEAD : (h + 1) * HEAD] = (
                    (acc[j, h] / total[j, h : h + 1, :]).T.astype(BF)
                )
        for k in range(2):
            heads[k].send(o_refs[k])
        chain.run(polled, polled + 1)
        m_out[...] = top[...]
        l_out[...] = total[...]
        gw.last()
        gg.last()
        for k in range(2):
            heads[k].arrive(lambda: (mix_out.at[k], so.at[k], ro.at[k]))
        x1 = here(net.y)[...].astype(F32)
        x1 = x1 + dot(mix_out[0], wf_out[:QCOLS, :]) + dot(mix_out[1], wf_out[QCOLS:, :])
        x1_out[...] = x1
        scale = lax.rsqrt(jnp.mean(x1 * x1, axis=-1, keepdims=True) + EPS)
        h2_own[...] = (x1 * scale * gains[1:2, :]).astype(BF)
        mine_h = pltpu.make_async_copy(h2_own, h2_out.at[gh.me], own.at[2])
        gh.begin()
        mine_h.start()
        chain.run(polled + 1, 2 * INNER)
        gh.middle()
        chain.run(2 * INNER, 2 * INNER + 2)
        gh.end()
        chain.run(2 * INNER + 2, chain.steps)
        n = 0
        for di in range(INNER):
            for dy in range(SEQ):
                if di or dy:
                    frm = lax.rem(net.i - di + INNER, INNER) * SEQ + lax.rem(net.y + dy, SEQ)
                    arrived(ch_out.at[frm], sp.at[n], rp.at[n], net.yp)
                    n += 1
        mine_c.wait()
        gh.last()
        for k in range(2):
            rows_out[k][0].sent(q_refs[k])
            heads[k].sent(o_refs[k])
        chain.finish()
        sends.finish()
        mine_g.wait()
        mine_h.wait()

    sds = jax.ShapeDtypeStruct
    stat = sds((2, 8, block), F32)
    heads_shape = sds((2, block, QCOLS), BF)
    return pl.pallas_call(
        kernel,
        out_shape=(
            sds((rows, WIDTH), BF),
            sds((WIDTH, FIRST), BF),
            sds((E,) + chosen.shape, F32),
            sds((rows, WIDTH), BF),
            heads_shape,
            sds((shards, rows, 2 * HEAD), BF),
            heads_shape,
            stat,
            stat,
            heads_shape,
            sds((block, WIDTH), F32),
            sds((E, block, WIDTH), BF),
            sds((WIDTH, WIDTH), BF),
            sds((E, block, WIDTH), BF),
            sds((shards,) + moe.shape[1:], BF),
        ),
        in_specs=[hbm()] * 4 + [vmem()] * 2 + [hbm()] * 2 + [vmem()] * 2,
        out_specs=(vmem(), vmem(), hbm()) + (vmem(),) * 8 + (hbm(), vmem(), hbm(), hbm()),
        scratch_shapes=[
            pltpu.VMEM((2, block, QCOLS), BF),
            pltpu.VMEM((2, GROUP, HEAD, block), F32),
            pltpu.VMEM((2, 8, block), F32),
            pltpu.VMEM((2, 8, block), F32),
            pltpu.VMEM((block, WIDTH), BF),
            pltpu.VMEM((8, WIDTH), F32),
        ]
        + dma_sems(7, 2, 2, 2, 2, 1, 1, E - 1, E - 1, INNER - 1, INNER - 1)
        + ShardGather.sems(depth) * 2
        + PlaneGather.sems() * 2
        + Chain.sems(depth)
        + ShardGather.sems(depth),
        compiler_params=comm_params(7, 60 << 20),
        name="front",
    )(stream, pack, moe, chosen, cosine, sine, w_out, out_grad, qseg, starts)


class Tally:
    def __init__(self, net, part, rows, scratch):
        self.net, self.part, self.rows = net, part, rows
        self.bc, self.sx, self.bx, self.sz, self.bz = scratch[:5]
        self.ssc, self.rsc, self.ssx, self.rsx, self.ssz, self.rsz = scratch[5:]
        self.chunk = chunk_of(rows)

    def number(self, dz, fx, core):
        x = jnp.where(fx == 1, 1 - self.net.x, self.net.x)
        return lax.rem(self.net.z + dz, self.net.depth) * INNER + x * 2 + core

    def core_copy(self, dz, fx):
        net, n = self.net, dz * 2 + fx
        src = self.part.at[self.number(dz, fx, 1 - net.core)]
        return remote(src, self.bc.at[n], self.ssc.at[n], self.rsc.at[n], net.cp)

    def x_copy(self, dz):
        return remote(
            self.sx.at[dz], self.bx.at[dz], self.ssx.at[dz], self.rsx.at[dz], self.net.xp
        )

    def z_copy(self, dz):
        n = dz - 1
        device = self.net.dev(z=lax.rem(self.net.z + dz, self.net.depth))
        return remote(self.sz.at[n], self.bz.at[n], self.ssz.at[n], self.rsz.at[n], device)

    def terms(self, dz, fx):
        n = dz * 2 + fx
        arrived(self.bc.at[n], self.ssc.at[n], self.rsc.at[n], self.net.cp)
        return [self.part.at[self.number(dz, fx, self.net.core)], self.bc.at[n]]

    def x_stage(self, dz):
        add_into(self.sx.at[dz], self.terms(dz, 1), self.rows, self.chunk)
        self.x_copy(dz).start()

    def x_terms(self, dz):
        terms = self.terms(dz, 0)
        arrived(self.bx.at[dz], self.ssx.at[dz], self.rsx.at[dz], self.net.xp)
        return terms + [self.bx.at[dz]]

    def z_stage(self, dz):
        add_into(self.sz.at[dz - 1], self.x_terms(dz), self.rows, self.chunk)
        self.z_copy(dz).start()

    def final(self, out):
        terms = self.x_terms(0)
        for n in range(self.net.depth - 1):
            arrived(self.bz.at[n], self.ssz.at[n], self.rsz.at[n], self.net.xp)
            terms.append(self.bz.at[n])
        add_into(out, terms, self.rows, self.chunk)

    def finish(self):
        for dz in range(self.net.depth):
            for fx in range(2):
                self.core_copy(dz, fx).wait_send()
            self.x_copy(dz).wait_send()
            if dz:
                self.z_copy(dz).wait_send()

    def far(self):
        return [d for d in range(1, self.net.depth)] + [0]

    def begin(self):
        for dz in self.far():
            for fx in (1, 0):
                self.core_copy(dz, fx).start()

    def far_stages(self):
        for dz in self.far():
            self.x_stage(dz)

    def near_stages(self):
        for dz in self.far()[:-1]:
            self.z_stage(dz)


def backward(q, kv, qseg, starts, m, l, ob, mixed, dx1, out_w, mixture, part_rows, depth):
    block = q.shape[1]
    rows = kv.shape[1]
    shards = depth * INNER

    def kernel(
        q_ref, kv_ref, qs_ref, sg_ref, m_ref, l_ref, ob_ref, mix_ref, dx_ref, wf_ref, mx_ref,
        dq_out, dkv_out, own_out, sum_out,
        dob, do_ref, da, dl, acc, dqs, dkv, wpart, wget, so, ro, sq, rq, sw, rw, *scratch,
    ):
        net = Net(depth)
        mirror = Mirror(net)
        keys = Tally(net, dkv, rows, scratch[:11])
        mine = wpart.at[net.y]
        outs = Tally(net, mine, part_rows, scratch[11:22])
        sends = Sends()
        plane = PlaneScatter(net, sends, mx_ref, block, scratch[22:])
        quarter = shards // 4

        def pair_copy(n):
            at = pl.ds(n * quarter, quarter)
            return remote(
                wpart.at[1 - net.y, at], wget.at[at], sw.at[n], rw.at[n], net.yp
            )

        def pair_sum():
            for n in range(4):
                at = pl.ds(n * quarter, quarter)
                arrived(wget.at[at], sw.at[n], rw.at[n], net.yp)

                def body(b, carry):
                    add_into(
                        wpart.at[net.y, b], [wpart.at[net.y, b], wget.at[b]], part_rows, outs.chunk
                    )
                    return carry

                lax.fori_loop(n * quarter, (n + 1) * quarter, body, 0)
            outs.begin()

        heads = [mirror.heads_out(k) for k in range(2)]
        backs = [mirror.rows_back(k) for k in range(2)]
        barrier = pltpu.get_barrier_semaphore()
        for device in net.zpeers() + [net.xp, net.cp, net.yp]:
            pl.semaphore_signal(barrier, inc=1, device_id=device, device_id_type=MESH)
        count = depth - 1 + 3
        for route, _ in heads + backs:
            count = count + route.hello()
        do_refs = [
            lambda k=k: (dob.at[k], do_ref.at[heads[k][1]], so.at[k], ro.at[heads[k][1]])
            for k in range(2)
        ]
        dq_refs = [
            lambda k=k: (dqs.at[k], dq_out.at[backs[k][1]], sq.at[k], rq.at[backs[k][1]])
            for k in range(2)
        ]
        dx = dx_ref[...]
        for k in range(2):
            dob[k] = dot(dx, wf_ref[k * QCOLS : (k + 1) * QCOLS, :], NT).astype(BF)
        pl.semaphore_wait(barrier, count)
        for k in range(2):
            heads[k][0].send(do_refs[k])
        plane.begin()
        wide = QCOLS // 2
        for n in range(4):
            cols = slice((n % 2) * wide, (n % 2 + 1) * wide)
            grad = dot(mix_ref[n // 2, :, cols].T, dx).astype(BF)
            for b in range(wide // part_rows):
                for s in range(SEQ):
                    wpart[s, n * (wide // part_rows) + b] = grad[
                        b * part_rows : (b + 1) * part_rows, s * QCOLS : (s + 1) * QCOLS
                    ]
            pair_copy(n).start()
        acc[...] = jnp.zeros_like(acc)
        plane.cores()
        for k in range(2):
            heads[k][0].arrive(lambda: (do_ref.at[k], so.at[k], ro.at[k]))
        for j in range(2):
            for h in range(GROUP):
                c = slice(h * HEAD, (h + 1) * HEAD)
                d = do_ref[j, :, c].astype(F32)
                o = ob_ref[j, :, c].astype(F32)
                inv = 1.0 / l_ref[j, h : h + 1, :]
                da[j, h] = (d.T * inv).T.astype(BF)
                dl[j, h : h + 1, :] = -jnp.sum((d * o).T, axis=0, keepdims=True) * inv
        low, high = mirror.blocks()
        bases = (low * block, high * block)

        def piece(t, j, masked):
            start = pl.multiple_of(t * rows, rows)
            k = kv_ref[t, :, :HEAD]
            v = kv_ref[t, :, HEAD:]
            kt = k.T
            k_seg = jnp.concatenate(
                [k, seg_tile(start, rows, sg_ref[0:1, :], sg_ref[1:2, :])], axis=1
            )
            if masked:
                key = start + lax.broadcasted_iota(jnp.int32, (rows, block), 0)
                ok = key <= bases[j] + lax.broadcasted_iota(jnp.int32, (rows, block), 1)
            dk = dv = None
            for h in range(GROUP):
                qh = q_ref[j, :, h * HEAD : (h + 1) * HEAD]
                s = dot(k_seg, jnp.concatenate([qh, qs_ref[j]], axis=1), NT)
                s = s - m_ref[j, h : h + 1, :]
                if masked:
                    s = jnp.where(ok, s, NEG)
                p = jnp.exp2(s)
                dah = da[j, h]
                dvh = dot(p.astype(BF), dah)
                dp = dot(v, dah, NT) + dl[j, h : h + 1, :]
                ds = (p * dp).astype(BF)
                dkh = dot(ds, qh)
                acc[j, h] += dot(kt, ds)
                dk = dkh if dk is None else dk + dkh
                dv = dvh if dv is None else dv + dvh
            return dk * LN2, dv

        def tile(u, carry):
            g, r = lax.div(u, INNER), lax.rem(u, INNER)
            dz = lax.rem(g + 1, depth)
            fx = 1 - lax.div(r, 2)
            other = lax.rem(r, 2) == 0
            t = keys.number(dz, fx, jnp.where(other, 1 - net.core, net.core))

            def put(j, masked):
                dk, dv = piece(t, j, masked)
                if j == 0:
                    dk = dk + dkv[t, :, :HEAD].astype(F32)
                    dv = dv + dkv[t, :, HEAD:].astype(F32)
                dkv[t, :, :HEAD] = dk.astype(BF)
                dkv[t, :, HEAD:] = dv.astype(BF)

            for j in (1, 0):
                live = t * rows <= bases[j] + block - 1
                free = t * rows + rows - 1 <= bases[j]
                if j == 1:

                    @pl.when(jnp.logical_not(live))
                    def _():
                        dkv[t] = jnp.zeros((rows, 2 * HEAD), BF)

                @pl.when(live & free)
                def _():
                    put(j, False)

                @pl.when(live & jnp.logical_not(free))
                def _():
                    put(j, True)

            @pl.when(other)
            def _():
                keys.core_copy(dz, fx).start()

            @pl.when(r == INNER - 1)
            def _():
                keys.x_stage(dz)

            @pl.when((r == INNER - 1) & (g > 0))
            def _():
                keys.z_stage(g)

            @pl.when(u == shards // 2 - 2)
            def _():
                plane.turn()

            @pl.when(u == shards - 7)
            def _():
                pair_sum()

            @pl.when(u == shards - 4)
            def _():
                outs.far_stages()

            @pl.when(u == shards - 1)
            def _():
                outs.near_stages()

            return carry

        lax.fori_loop(0, shards, tile, 0)
        for j in range(2):
            for h in range(GROUP):
                dqs[j, :, h * HEAD : (h + 1) * HEAD] = (acc[j, h] * SCALE).T.astype(BF)
        for k in range(2):
            backs[k][0].send(dq_refs[k])
        plane.final(sum_out)
        outs.final(own_out)
        keys.final(dkv_out)
        for k in range(2):
            backs[k][0].arrive(lambda: (dq_out.at[k], sq.at[k], rq.at[k]))
        for k in range(2):
            heads[k][0].sent(do_refs[k])
            backs[k][0].sent(dq_refs[k])
        for n in range(4):
            pair_copy(n).wait_send()
        sends.finish()
        outs.finish()
        keys.finish()

    sds = jax.ShapeDtypeStruct
    pair = (2, block, QCOLS)
    return pl.pallas_call(
        kernel,
        out_shape=(
            sds(pair, BF),
            sds((rows, 2 * HEAD), F32),
            sds((part_rows, QCOLS), F32),
            sds((block, WIDTH), BF),
        ),
        in_specs=[vmem()] * 11,
        out_specs=(vmem(),) * 4,
        scratch_shapes=[
            pltpu.VMEM(pair, BF),
            pltpu.VMEM(pair, BF),
            pltpu.VMEM((2, GROUP, block, HEAD), BF),
            pltpu.VMEM((2, 8, block), F32),
            pltpu.VMEM((2, GROUP, HEAD, block), F32),
            pltpu.VMEM(pair, BF),
            pltpu.VMEM((shards, rows, 2 * HEAD), BF),
            pltpu.VMEM((SEQ, shards, part_rows, QCOLS), BF),
            pltpu.VMEM((shards, part_rows, QCOLS), BF),
        ]
        + dma_sems(2, 2, 2, 2, 4, 4)
        + ShardScatter.scratch(depth, rows, 2 * HEAD)
        + ShardScatter.scratch(depth, part_rows, QCOLS)
        + PlaneScatter.scratch(block, WIDTH),
        compiler_params=comm_params(8, 60 << 20),
        name="backward",
    )(q, kv, qseg, starts, m, l, ob, mixed, dx1, out_w, mixture)


def finish_layer(
    dq, dkv, cosine, sine, h1, weights, pair, small, dx1, gain_a, out_own, moe, depth
):
    block = dx1.shape[0]
    rows = pair.shape[0]
    shards = depth * INNER
    part_rows = out_own.shape[0]
    wide = 384

    def kernel(
        dq_ref, dkv_ref, c_ref, n_ref, h1_ref, w_ref, s_ref, sm_ref, dx_ref, ga_ref, oo_ref, moe_ref,
        sg_out, own_out, pair_out, pair_wo, moe_out,
        raw, part, give, take, low, low_wo, sm, rm, sy, ry, ls, *scratch,
    ):
        net = Net(depth)
        sends = Sends()
        me = net.i * SEQ + net.y
        mine = pltpu.make_async_copy(moe_ref.at[net.i], moe_out.at[me], ls.at[0])
        work = Tally(net, part, part_rows, scratch)
        barrier = pltpu.get_barrier_semaphore()
        for device in net.zpeers() + net.plane():
            pl.semaphore_signal(barrier, inc=1, device_id=device, device_id_type=MESH)
        pl.semaphore_wait(barrier, depth - 1 + E - 1)
        for di in range(1, INNER):
            i = lax.rem(net.i + di, INNER)
            sends.start(
                moe_ref.at[i], moe_out.at[me], sm.at[di], rm.at[di], net.dev(i=i)
            )
        sends.start(moe_ref.at[net.i], moe_out.at[me], sm.at[0], rm.at[0], net.yp)
        mine.start()
        cos, sin = c_ref[...], -n_ref[...]
        for k in range(2):
            at = slice(k * block, (k + 1) * block)
            for h in range(GROUP):
                cols = slice(h * HEAD, (h + 1) * HEAD)
                v = dq_ref[k, :, cols].astype(F32)
                raw[at, cols] = turn(v, cos[at], sin[at]).astype(BF)
        dk = dkv_ref[:, :HEAD].astype(BF).astype(F32)
        raw[:, QCOLS : QCOLS + HEAD] = turn(dk, cos, sin).astype(BF)
        raw[:, QCOLS + HEAD :] = dkv_ref[:, HEAD:].astype(BF)
        low_wo[...] = oo_ref[...].astype(BF)
        sends.start(low_wo, pair_wo, sy.at[1], ry.at[1], net.yp)

        def half(y):
            at = pl.ds(pl.multiple_of(y * block, block), block)
            x = s_ref[at, :].astype(F32)
            scale = lax.rsqrt(jnp.mean(x * x, axis=-1, keepdims=True) + EPS)
            grad = dot(raw[at, :], w_ref[:, :QKV], NT)
            return x * scale, scale, grad

        normed, _, grad = half(1 - net.y)
        give[...] = grad.astype(BF)
        sends.start(give, take, sy.at[2], ry.at[2], net.yp)
        gain_part = jnp.sum(grad * normed, axis=0, keepdims=True)
        normed, scale, grad = half(net.y)
        gain_part = gain_part + jnp.sum(grad * normed, axis=0, keepdims=True)
        lanes = lax.broadcasted_iota(jnp.int32, (EXTRA, WIDTH), 0)
        extra = jnp.where(lanes == 0, gain_part, sm_ref[...]).T.astype(BF)
        per = wide // part_rows
        for c in range(WIDTH // wide):
            g = dot(h1_ref[:, c * wide : (c + 1) * wide].T, raw[...]).astype(BF)
            for b in range(per):
                part[c * per + b, :, :QKV] = g[b * part_rows : (b + 1) * part_rows]
                part[c * per + b, :, QKV:] = extra[
                    c * wide + b * part_rows : c * wide + (b + 1) * part_rows
                ]
        work.begin()
        work.far_stages()
        for di in range(1, INNER):
            got = moe_out.at[lax.rem(net.i - di + INNER, INNER) * SEQ + net.y]
            arrived(got, sm.at[di], rm.at[di], net.yp)
            sends.start(got, got, sm.at[INNER - 1 + di], rm.at[INNER - 1 + di], net.yp)
        arrived(take, sy.at[2], ry.at[2], net.yp)
        inner = (grad + take[...].astype(F32)) * ga_ref[...]
        pull = scale * (inner - normed * jnp.mean(inner * normed, axis=-1, keepdims=True))
        sg_out[...] = (dx_ref[...] + pull).astype(BF)
        work.near_stages()
        work.final(own_out)
        low[...] = own_out[...].astype(BF)
        sends.start(low, pair_out, sy.at[0], ry.at[0], net.yp)
        for di in range(INNER):
            n = INNER - 1 + di if di else 0
            got = moe_out.at[lax.rem(net.i - di + INNER, INNER) * SEQ + 1 - net.y]
            arrived(got, sm.at[n], rm.at[n], net.yp)
        arrived(pair_wo, sy.at[1], ry.at[1], net.yp)
        arrived(pair_out, sy.at[0], ry.at[0], net.yp)
        sends.finish()
        work.finish()
        mine.wait()

    sds = jax.ShapeDtypeStruct
    return pl.pallas_call(
        kernel,
        out_shape=(
            sds((block, WIDTH), BF),
            sds((part_rows, FIRST), F32),
            sds((part_rows, FIRST), BF),
            sds((part_rows, QCOLS), BF),
            sds((E,) + moe.shape[1:], BF),
        ),
        in_specs=[vmem()] * 11 + [hbm()],
        out_specs=(vmem(),) * 4 + (hbm(),),
        scratch_shapes=[
            pltpu.VMEM((rows, QKV), BF),
            pltpu.VMEM((shards, part_rows, FIRST), BF),
            pltpu.VMEM((block, WIDTH), BF),
            pltpu.VMEM((block, WIDTH), BF),
            pltpu.VMEM((part_rows, FIRST), BF),
            pltpu.VMEM((part_rows, QCOLS), BF),
        ]
        + dma_sems(2 * INNER - 1, 2 * INNER - 1, 3, 3, 1)
        + ShardScatter.scratch(depth, part_rows, FIRST),
        compiler_params=comm_params(9, 60 << 20),
        name="finish_layer",
    )(dq, dkv, cosine, sine, h1, weights, pair, small, dx1, gain_a, out_own, moe)


def run_expert(h2, out_grad, onehot, gate, lane, moe_w, rows_in, rows_out):
    blocks, tokens = h2.shape[:2]
    slots = onehot.shape[1]
    shards = moe_w.shape[0]
    pairs = 2
    steps = blocks // pairs
    wide = WIDTH + EXTRA

    def kernel(
        h_ref, g_ref, oh_ref, gt_ref, ln_ref, w_ref, mix_out, back_out, grads_out,
        gu_w, dn_w, gu_acc, dn_acc, rows, slot_g, stage, wsem, gsem,
    ):
        step = pl.program_id(0)

        def weight_copies():
            for n in range(shards):
                yield pltpu.make_async_copy(
                    w_ref.at[n, pl.ds(0, rows_in)], gu_w.at[pl.ds(n * rows_in, rows_in)], wsem.at[n]
                )
                yield pltpu.make_async_copy(
                    w_ref.at[n, pl.ds(rows_in, rows_out)],
                    dn_w.at[pl.ds(n * rows_out, rows_out)],
                    wsem.at[shards + n],
                )

        @pl.when(step == 0)
        def _():
            for copy in weight_copies():
                copy.start()
            gu_acc[...] = jnp.zeros_like(gu_acc)
            dn_acc[...] = jnp.zeros_like(dn_acc)
            for copy in weight_copies():
                copy.wait()

        for b in range(pairs):
            at = slice(b * slots, (b + 1) * slots)
            rows[at, :] = dot(oh_ref[b], h_ref[b]).astype(BF)
            slot_g[at, :] = dot(oh_ref[b], g_ref[b]).astype(BF)
        gate_col = gt_ref[...].reshape(pairs * slots, 1)
        both = dot(rows[...], gu_w[...])
        pre, up = both[:, :FF], both[:, FF:]
        phi = 0.5 * (1.0 + lax.erf(pre * (0.5**0.5)))
        slope = phi + pre * jnp.exp(-0.5 * pre * pre) * 0.3989422804014327
        gelu = pre * phi
        active = (gelu * up).astype(BF)
        grad = slot_g[...]
        out = dot(active, dn_w[...])
        gate_grad = jnp.sum(grad.astype(F32) * out, axis=-1, keepdims=True)
        mixed = (out * gate_col).astype(BF)
        expert_grad = (grad.astype(F32) * gate_col).astype(BF)
        active_grad = dot(expert_grad, dn_w[...], NT)
        low = jnp.concatenate(
            [(active_grad * up * slope).astype(BF), (active_grad * gelu).astype(BF)], axis=1
        )
        back = dot(low, gu_w[...], NT).astype(BF)
        back = jnp.concatenate([back, (gate_grad * ln_ref[...]).astype(BF)], axis=1)
        for b in range(pairs):
            at = slice(b * slots, (b + 1) * slots)
            spread = oh_ref[b].T
            mix_out[b] = dot(spread, mixed[at]).astype(BF)
            back_out[b] = dot(spread, back[at]).astype(BF)
        gu_acc[...] += dot(rows[...].T, low)
        dn_acc[...] += dot(active.T, expert_grad)

        @pl.when(step == steps - 1)
        def _():
            def copy(n, slot):
                return pltpu.make_async_copy(stage.at[slot], grads_out.at[n], gsem.at[slot])

            for n in range(shards):
                slot = n % 2
                if n >= 2:
                    copy(n - 2, slot).wait()
                stage[slot, :rows_in, :] = gu_acc[n * rows_in : (n + 1) * rows_in, :].astype(BF)
                stage[slot, rows_in:, :] = dn_acc[n * rows_out : (n + 1) * rows_out, :].astype(BF)
                copy(n, slot).start()
            for n in range(shards - 2, shards):
                copy(n, n % 2).wait()

    sds = jax.ShapeDtypeStruct
    block = lambda *shape: pl.BlockSpec((pairs,) + shape, lambda n: (n,) + (0,) * len(shape))
    return pl.pallas_call(
        kernel,
        grid=(steps,),
        out_shape=(
            sds((blocks, tokens, WIDTH), BF),
            sds((blocks, tokens, wide), BF),
            sds(moe_w.shape, BF),
        ),
        in_specs=[
            block(tokens, WIDTH),
            block(tokens, WIDTH),
            block(slots, tokens),
            block(slots, 1),
            pl.BlockSpec((1, EXTRA), lambda n: (0, 0)),
            hbm(),
        ],
        out_specs=(block(tokens, WIDTH), block(tokens, wide), hbm()),
        scratch_shapes=[
            pltpu.VMEM((WIDTH, 2 * FF), BF),
            pltpu.VMEM((FF, WIDTH), BF),
            pltpu.VMEM((WIDTH, 2 * FF), F32),
            pltpu.VMEM((FF, WIDTH), F32),
            pltpu.VMEM((pairs * slots, WIDTH), BF),
            pltpu.VMEM((pairs * slots, WIDTH), BF),
            pltpu.VMEM((2, rows_in + rows_out, WIDTH), BF),
        ]
        + dma_sems(2 * shards, 2),
        compiler_params=pltpu.CompilerParams(
            vmem_limit_bytes=60 << 20, dimension_semantics=("arbitrary",)
        ),
        cost_estimate=pl.CostEstimate(
            flops=int(3.8e10), bytes_accessed=40 << 20, transcendentals=4 << 20
        ),
        name="run_expert",
    )(h2, out_grad, onehot, gate, lane, moe_w)


def rms_parts(x):
    scale = lax.rsqrt(jnp.mean(x * x, axis=-1, keepdims=True) + EPS)
    return x * scale, scale


def rms_pull(normed, scale, grad, gain):
    inner = grad * gain
    return scale * (inner - normed * jnp.mean(inner * normed, axis=-1, keepdims=True))


def document_first(index, starts):
    return jnp.max(jnp.where(starts <= index[..., None], starts, 0), axis=-1)


def gelu_product(gate_pre, up_pre):
    return jax.nn.gelu(gate_pre, approximate=False) * up_pre


class Zigzag:
    def __init__(self, shards):
        last = 2 * shards - 1
        home = lambda b: b if b < shards else last - b
        self.rows = [
            [(s * 2 + y, home(2 * s + k) * 2 + y) for s in range(shards) for y in range(2)]
            for k in range(2)
        ]
        self.heads = [
            [
                (s * 2 + g, s if (g == 0) == (k == 0) else last - s)
                for s in range(shards)
                for g in range(2)
            ]
            for k in range(2)
        ]

    @staticmethod
    def move(x, pairs, back=False):
        return lax.ppermute(x, AXES, [(b, a) for a, b in pairs] if back else pairs)


def pick(flag, a, b):
    return jnp.where(flag, a, b), jnp.where(flag, b, a)


def experts(h2, out_grad, chosen, router_w, moe_w, rows_in, rows_out, me):
    blocks, tokens = h2.shape[:2]
    logits = dot(h2.reshape(blocks * tokens, WIDTH), router_w)
    probs = jax.nn.softmax(logits, axis=-1)
    mine = (jnp.arange(E) == me).astype(F32)
    named = jnp.sum(chosen * mine[None, :, None], axis=1)
    gate_tok = jnp.sum(probs * mine[None, :], axis=-1).reshape(blocks, tokens) * named
    upper = (jnp.arange(tokens)[:, None] <= jnp.arange(tokens)[None, :]).astype(BF)
    rank = dot(named.astype(BF), upper) - 1.0
    pick_slot = (
        rank[:, None, :] == jnp.arange(MOST, dtype=F32)[None, :, None]
    ) & (named[:, None, :] > 0.5)
    onehot = pick_slot.astype(BF)
    slots = blocks * MOST
    gate = jnp.sum(jnp.where(pick_slot, gate_tok[:, None, :], 0.0), axis=-1)
    if rows_in % 16 == 0 and rows_out % 16 == 0:
        lane = (jnp.arange(EXTRA) == me).astype(F32)[None, :]
        return run_expert(
            h2, out_grad, onehot, gate[:, :, None], lane, moe_w, rows_in, rows_out
        )
    gate = gate.reshape(slots, 1)
    spread = lambda v: lax.dot_general(
        onehot, v, (((2,), (1,)), ((0,), (0,))), preferred_element_type=F32
    )
    collect = lambda v: lax.dot_general(
        onehot, v, (((1,), (1,)), ((0,), (0,))), preferred_element_type=F32
    )
    rows = spread(h2).astype(BF).reshape(slots, WIDTH)
    slot_grad = spread(out_grad).astype(BF).reshape(slots, WIDTH)
    gate_w = moe_w[:, :rows_in, :FF].reshape(WIDTH, FF)
    up_w = moe_w[:, :rows_in, FF:].reshape(WIDTH, FF)
    down_w = moe_w[:, rows_in:, :].reshape(FF, WIDTH)
    gate_pre = dot(rows, gate_w)
    up_pre = dot(rows, up_w)
    active_f, pull = jax.vjp(gelu_product, gate_pre, up_pre)
    active = active_f.astype(BF)
    out = dot(active, down_w)
    slot_gf = slot_grad.astype(F32)
    gate_grad = jnp.sum(slot_gf * out, axis=-1).reshape(blocks, MOST)
    mixture = collect((out * gate).astype(BF).reshape(blocks, MOST, WIDTH)).astype(BF)
    expert_grad = (slot_gf * gate).astype(BF)
    active_grad = dot(expert_grad, down_w, NT)
    g_low, u_low = (v.astype(BF) for v in pull(active_grad))
    back = dot(g_low, gate_w, NT) + dot(u_low, up_w, NT)
    back_tok = collect(back.astype(BF).reshape(blocks, MOST, WIDTH)).astype(BF)
    gate_back = jnp.sum(jnp.where(pick_slot, gate_grad[:, :, None], 0.0), axis=1)
    lanes = (jnp.arange(EXTRA) == me).astype(F32)
    back_tok = jnp.concatenate(
        [back_tok, (gate_back[:, :, None] * lanes[None, None, :]).astype(BF)], axis=-1
    )
    shards = WIDTH // rows_in
    grads = jnp.concatenate(
        [
            jnp.concatenate(
                [
                    dot(rows, g_low, TN).astype(BF).reshape(shards, rows_in, FF),
                    dot(rows, u_low, TN).astype(BF).reshape(shards, rows_in, FF),
                ],
                axis=-1,
            ),
            dot(active, expert_grad, TN).astype(BF).reshape(shards, rows_out, WIDTH),
        ],
        axis=1,
    )
    return mixture, back_tok, grads


def back_apart(zig, q, kv, lo, info, top, total, ob, mixed, dx1, out_w, part_rows, depth):
    z, i, y = (lax.axis_index(a) for a in AXES)
    shards, rows = kv.shape[:2]
    shard = z * INNER + i
    even, head_zero = lax.rem(shard, 2) == 0, y == 0
    dob = dot(dx1, out_w, NT).astype(BF)
    out_part = dot(mixed, dx1, TN).astype(BF)
    keep, give = pick(head_zero, out_part[:, :QCOLS], out_part[:, QCOLS:])
    keep = keep.astype(F32) + lax.ppermute(give, "seq", [(0, 1), (1, 0)]).astype(F32)
    out_own = scatter_keys(keep.astype(BF).reshape(shards, part_rows, QCOLS), depth, 10)
    dob_a, dob_b = pick(shard * SEQ + y < shards, dob[:, :QCOLS], dob[:, QCOLS:])
    dob_zig = jnp.stack(
        pick(
            head_zero,
            zig.move(dob_a, zig.heads[0], True),
            zig.move(dob_b, zig.heads[1], True),
        )
    )
    flat = kv.reshape(shards * rows, 2 * HEAD)
    dq, dkv_part = attend_backward(q, flat, lo, info, top, total, dob_zig, ob)
    dq_a, dq_b = pick(even, dq[0], dq[1])
    dq_pair = jnp.stack([zig.move(dq_a, zig.rows[0], True), zig.move(dq_b, zig.rows[1], True)])
    return dq_pair, scatter_keys(dkv_part.reshape(kv.shape), depth, 5), out_own


def local(depth, stream, doc_starts, routes, attn_gain, w_query, w_key, w_value, w_out, ffn_gain, w_router, w_gate, w_up, w_down, out_grad):
    tokens = stream.shape[0]
    rows_in, rows_out = w_gate.shape[1], w_down.shape[1]
    shards = depth * INNER
    z, i, y = (lax.axis_index(a) for a in AXES)
    shard = z * INNER + i
    me = i * SEQ + y
    zig = Zigzag(shards)

    cut = lambda w, width: lax.dynamic_slice_in_dim(w, y * width, width, 1)
    extra = jnp.concatenate(
        [
            attn_gain[:, None],
            ffn_gain[:, None],
            w_router,
            jnp.zeros((rows_in, EXTRA - 2 - E), BF),
        ],
        axis=1,
    )
    pack = jnp.concatenate(
        [cut(w_query, QCOLS), cut(w_key, HEAD), cut(w_value, HEAD), extra], axis=1
    )
    moe_pack = jnp.concatenate([jnp.concatenate([w_gate, w_up], axis=2), w_down], axis=1)
    chosen_t = jnp.any(
        routes.T[:, None, :] == jnp.arange(E, dtype=jnp.int32)[None, :, None], axis=0
    ).astype(F32)
    pair_index = shard * SEQ * tokens + jnp.arange(SEQ * tokens, dtype=jnp.int32)
    position = pair_index - document_first(pair_index, doc_starts)
    freq = ROPE_BASE ** (-(jnp.arange(HEAD // 2, dtype=F32) * 2.0) / HEAD)
    angle = position.astype(F32)[:, None] * freq[None, :]
    cos_half, sin_half = jnp.cos(angle), jnp.sin(angle)
    cosine = jnp.concatenate([cos_half, cos_half], axis=1)
    sine = jnp.concatenate([-sin_half, sin_half], axis=1)

    block_ids = jnp.stack([shard, 2 * shards - 1 - shard]).astype(jnp.int32)
    query_index = block_ids[:, None] * tokens + jnp.arange(tokens, dtype=jnp.int32)[None, :]
    lo = document_first(query_index, doc_starts).astype(jnp.int32)
    info = jnp.concatenate([block_ids, lo[:, 0], lo[:, -1], jnp.zeros((2,), jnp.int32)])
    big = jnp.int32(1 << 30)
    spare = jnp.full((HEAD - doc_starts.shape[0],), big)
    first = jnp.concatenate([doc_starts, spare])
    beyond = jnp.concatenate([doc_starts[1:], spare, big[None]])
    starts = jnp.stack([first, beyond])
    outside = (query_index[..., None] < first) | (query_index[..., None] >= beyond)
    qseg = jnp.where(outside, NEG, 0.0).astype(BF)
    lo = lo[:, None, :]
    (
        pair, weights, chosen_all, h1, q, kv, ob, top, total, mixed, x1, h2_plane, out_w, grad_plane, moe_w,
    ) = front(stream, pack, moe_pack, chosen_t, cosine, sine, w_out, out_grad, qseg, starts, depth)
    extra_w = lax.optimization_barrier(weights[:, QKV : QKV + EXTRA])
    gains = extra_w[:, :2].astype(F32).T
    gain_a, gain_f = gains[0:1], gains[1:2]
    router_w = extra_w[:, 2 : 2 + E]
    qkv_w = weights[:, :QKV]
    head_zero = y == 0
    mixed_pair = mixed
    mixed = jnp.concatenate([mixed[0], mixed[1]], axis=1)
    normed, scale = rms_parts(x1)
    h2 = (normed * gain_f).astype(BF)

    mixture_part, back_part, moe_grads = experts(
        h2_plane, grad_plane, chosen_all, router_w, moe_w, rows_in, rows_out, me
    )
    back = scatter_plane(back_part, depth)
    moe_own = lax.psum_scatter(
        moe_grads.reshape(depth, INNER, rows_in + rows_out, WIDTH),
        "outer",
        scatter_dimension=0,
        tiled=False,
    )

    chosen = chosen_t.T
    probs = jax.nn.softmax(dot(h2, router_w), axis=-1)
    dp = back[:, WIDTH : WIDTH + E] * chosen
    dz = (probs * (dp - jnp.sum(dp * probs, axis=-1, keepdims=True))).astype(BF)
    router_part = dot(dz, h2, TN)
    dh2 = back[:, :WIDTH] + dot(dz, router_w, NT)
    grad_f = out_grad.astype(F32)
    dx1 = grad_f + rms_pull(normed, scale, dh2, gain_f)
    gain_f_part = jnp.sum(dh2 * normed, axis=0)
    dx1_low = dx1.astype(BF)
    if depth <= 4:
        dq_pair, dkv, out_own, mixture = backward(
            q, kv, qseg, starts, top, total, ob, mixed_pair, dx1_low, out_w, mixture_part, rows_in, depth
        )
    else:
        dq_pair, dkv, out_own = back_apart(
            zig, q, kv, lo, info, top, total, ob, mixed, dx1_low, out_w, rows_in, depth
        )
        mixture = lax.psum_scatter(mixture_part, ("inner", "seq"), scatter_dimension=0, tiled=False)
    result = (x1 + mixture.astype(F32)).astype(BF)
    small = jnp.concatenate(
        [
            jnp.zeros((1, WIDTH), F32),
            gain_f_part[None, :],
            router_part,
            jnp.zeros((EXTRA - 2 - E, WIDTH), F32),
        ],
        axis=0,
    )
    stream_grad, own, peer, peer_out, moe_out = finish_layer(
        dq_pair,
        dkv,
        cosine,
        sine,
        h1,
        weights,
        pair,
        small,
        dx1,
        gain_a,
        out_own,
        moe_own,
        depth,
    )
    peer = peer.astype(F32)

    def halves(a, b):
        return jnp.concatenate(pick(head_zero, own[:, a:b], peer[:, a:b]), axis=1)

    both = own[:, QKV:] + peer[:, QKV:]
    moe_out = moe_out.astype(F32)
    return (
        result,
        stream_grad,
        both[:, 0],
        halves(0, QCOLS),
        halves(QCOLS, QCOLS + HEAD),
        halves(QCOLS + HEAD, QKV),
        jnp.concatenate(pick(head_zero, out_own, peer_out.astype(F32)), axis=1),
        both[:, 1],
        both[:, 2 : 2 + E],
        moe_out[:, :rows_in, :FF],
        moe_out[:, :rows_in, FF:],
        moe_out[:, rows_in:, :],
    )


def solution(mesh):
    shards = mesh.shape["shard"]
    depth = shards // INNER
    fine = Mesh(mesh.devices.reshape(depth, INNER, SEQ), AXES)
    shard = ("outer", "inner")
    tokens = P(AXES, None)
    in_specs = (
        tokens,
        P(),
        tokens,
        P(shard),
        P(shard, None),
        P(shard, None),
        P(shard, None),
        P(shard, None),
        P(shard),
        P(shard, None),
        P(None, shard, None),
        P(None, shard, None),
        P(None, shard, None),
        tokens,
    )
    out_specs = (
        tokens,
        tokens,
        P(shard),
        P(shard, None),
        P(shard, None),
        P(shard, None),
        P(shard, None),
        P(shard),
        P(shard, None),
        P(None, shard, None),
        P(None, shard, None),
        P(None, shard, None),
    )

    def run(*args):
        return local(depth, *args)

    return jax.shard_map(run, mesh=fine, in_specs=in_specs, out_specs=out_specs, check_vma=False)
```

```python
import jax
import jax.numpy as jnp
from jax import lax
from jax.experimental import pallas as pl
from jax.experimental.pallas import tpu as pltpu
from jax.sharding import Mesh, PartitionSpec as P

WIDTH = 1536
HEADS = 12
KV_HEADS = 2
HEAD = 128
FF = 768
E = 8
MOST = 192
SEQ = KV_HEADS
GROUP = HEADS // KV_HEADS
INNER = E // SEQ
QCOLS = GROUP * HEAD
QKV = QCOLS + 2 * HEAD
EXTRA = 128
FIRST = QKV + EXTRA
PACK = QKV + EXTRA + WIDTH
EPS = 1e-06
ROPE_BASE = 10000.0
SCALE = HEAD**-0.5
LOG2E = 1.4426950408889634
LN2 = 0.6931471805599453
NEG = -1e30
AXES = ("outer", "inner", "seq")
MESH = pl.DeviceIdType.MESH
NN = (((1,), (0,)), ((), ()))
NT = (((1,), (1,)), ((), ()))
TN = (((0,), (0,)), ((), ()))
BF = jnp.bfloat16
F32 = jnp.float32


def dot(a, b, dims=NN):
    return lax.dot_general(a, b, dims, preferred_element_type=F32)


class Net:
    def __init__(self, depth):
        self.depth = depth
        self.z = lax.axis_index("outer")
        self.i = lax.axis_index("inner")
        self.y = lax.axis_index("seq")
        self.core = lax.rem(self.i, 2)
        self.x = lax.div(self.i, 2)
        self.xp = self.dev(i=lax.rem(self.i + 2, INNER))
        self.cp = self.dev(i=self.i + 1 - 2 * self.core)
        self.yp = self.dev(y=1 - self.y)

    def dev(self, z=None, i=None, y=None):
        return {
            "outer": self.z if z is None else z,
            "inner": self.i if i is None else i,
            "seq": self.y if y is None else y,
        }

    def zoff(self, dz):
        return lax.rem(self.z + dz, self.depth)

    def zpeers(self):
        return [self.dev(z=self.zoff(dz)) for dz in range(1, self.depth)]

    def plane(self):
        out = []
        for di in range(INNER):
            for dy in range(SEQ):
                if di or dy:
                    out.append(
                        self.dev(i=lax.rem(self.i + di, INNER), y=lax.rem(self.y + dy, SEQ))
                    )
        return out


def greet(devices):
    barrier = pltpu.get_barrier_semaphore()
    for device in devices:
        pl.semaphore_signal(barrier, inc=1, device_id=device, device_id_type=MESH)
    pl.semaphore_wait(barrier, len(devices))


def remote(src, dst, ssem, rsem, device):
    return pltpu.make_async_remote_copy(
        src_ref=src, dst_ref=dst, send_sem=ssem, recv_sem=rsem, device_id=device, device_id_type=MESH
    )


class Sends:
    def __init__(self):
        self.items = []

    def start(self, *refs):
        self.later(lambda: refs)

    def later(self, refs):
        remote(*refs()).start()
        self.items.append(refs)

    def finish(self):
        for refs in self.items:
            remote(*refs()).wait_send()


def arrived(dst, ssem, rsem, device):
    remote(dst, dst, ssem, rsem, device).wait_recv()


def dma_sems(*counts):
    return [pltpu.SemaphoreType.DMA((n,)) for n in counts]


class FlatSlots:
    class At:
        def __init__(self, ref, rows):
            self.ref, self.rows = ref, rows

        def __getitem__(self, n):
            return self.ref.at[pl.ds(pl.multiple_of(n * self.rows, self.rows), self.rows)]

    def __init__(self, ref, rows):
        self.at = self.At(ref, rows)


class ShardGather:
    def __init__(self, net, sends, src, out, sems):
        self.net, self.sends, self.src, self.out = net, sends, src, out
        self.sz, self.rz, self.sx, self.rx, self.sc, self.rc = sems
        self.xi = lax.rem(net.i + 2, INNER)

    @staticmethod
    def sems(depth):
        return dma_sems(*([max(depth - 1, 1)] * 2 + [depth] * 2 + [2 * depth] * 2))

    def slot(self, dz, i):
        return self.out.at[lax.rem(self.net.z - dz + self.net.depth, self.net.depth) * INNER + i]

    def begin(self):
        net, me = self.net, self.slot(0, self.net.i)
        for n, device in enumerate(net.zpeers()):
            self.sends.start(self.src, me, self.sz.at[n], self.rz.at[n], device)
        self.sends.start(self.src, me, self.sx.at[0], self.rx.at[0], net.xp)
        self.sends.start(self.src, me, self.sc.at[0], self.rc.at[0], net.cp)

    def pass_on(self, dz, i, ssem, rsem, n, device):
        self.sends.later(
            lambda: (self.slot(dz, i), self.slot(dz, i), ssem.at[n], rsem.at[n], device)
        )

    def after_z(self):
        net = self.net
        for dz in range(1, net.depth):
            block = self.slot(dz, net.i)
            arrived(block, self.sz.at[dz - 1], self.rz.at[dz - 1], net.xp)
            self.pass_on(dz, net.i, self.sx, self.rx, dz, net.xp)
            self.pass_on(dz, net.i, self.sc, self.rc, dz, net.cp)

    def after_x(self):
        net, depth = self.net, self.net.depth
        for dz in range(depth):
            arrived(self.slot(dz, self.xi), self.sx.at[dz], self.rx.at[dz], net.xp)
            self.pass_on(dz, self.xi, self.sc, self.rc, depth + dz, net.cp)

    def last(self):
        net, depth = self.net, self.net.depth
        ci = net.i + 1 - 2 * net.core
        for dz in range(depth):
            arrived(self.slot(dz, ci), self.sc.at[dz], self.rc.at[dz], net.cp)
        for dz in range(depth):
            arrived(
                self.slot(dz, lax.rem(ci + 2, INNER)),
                self.sc.at[depth + dz],
                self.rc.at[depth + dz],
                net.cp,
            )

    def end(self):
        self.after_z()
        self.after_x()
        self.last()

    def one_x(self, dz):
        net, block, n = self.net, self.slot(dz, self.xi), self.net.depth + dz
        arrived(block, self.sx.at[dz], self.rx.at[dz], net.xp)
        remote(block, block, self.sc.at[n], self.rc.at[n], net.cp).start()

    def one_c(self, n, place):
        block = self.out.at[place]
        arrived(block, self.sc.at[n], self.rc.at[n], self.net.cp)

    def sent_loop(self):
        net, depth = self.net, self.net.depth
        for dz in range(depth):
            block = self.slot(dz, self.xi)
            remote(block, block, self.sc.at[depth + dz], self.rc.at[depth + dz], net.cp).wait_send()


def hbm():
    return pl.BlockSpec(memory_space=pltpu.HBM)


def vmem():
    return pl.BlockSpec(memory_space=pltpu.VMEM)


def smem():
    return pl.BlockSpec(memory_space=pltpu.SMEM)


def comm_params(cid, limit=56 << 20):
    return pltpu.CompilerParams(
        collective_id=cid, has_side_effects=True, vmem_limit_bytes=limit
    )


def add_into(dst, sources, rows, chunk):
    def body(n, carry):
        at = pl.ds(pl.multiple_of(n * chunk, chunk), chunk)
        total = sources[0][at, :].astype(F32)
        for source in sources[1:]:
            total = total + source[at, :].astype(F32)
        dst[at, :] = total.astype(dst.dtype)
        return carry

    lax.fori_loop(0, rows // chunk, body, 0)


def chunk_of(rows):
    for size in (32, 16, 8):
        if rows % size == 0:
            return size
    return rows


class PlaneScatter:
    ORDER = ((1, 1), (1, 0), (0, 1), (0, 0))

    @staticmethod
    def scratch(rows, cols):
        return (
            [pltpu.VMEM((4, rows, cols), BF)] * 2
            + [pltpu.VMEM((2, rows // 2, cols), BF)] * 4
            + dma_sems(10, 10)
        )

    def __init__(self, net, sends, part, rows, scratch):
        self.net, self.sends, self.part, self.rows = net, sends, part, rows
        self.bc, self.mid, self.bx, self.by, self.second, self.b2, self.ss, self.rs = scratch
        self.half = rows // 2
        self.lo, self.hi = pl.ds(0, self.half), pl.ds(self.half, self.half)
        self.chunk = chunk_of(self.half)

    def place(self, fx, fy, core):
        x = 1 - self.net.x if fx else self.net.x
        y = 1 - self.net.y if fy else self.net.y
        return (x * 2 + core) * SEQ + y

    def send(self, src, dst, n, device):
        self.sends.later(lambda: (src(), dst(), self.ss.at[n], self.rs.at[n], device))

    def take(self, dst, n):
        arrived(dst, self.ss.at[n], self.rs.at[n], self.net.xp)

    def begin(self):
        net = self.net
        for n, (fx, fy) in enumerate(self.ORDER):
            src = lambda fx=fx, fy=fy: self.part.at[self.place(fx, fy, 1 - net.core)]
            self.send(src, lambda n=n: self.bc.at[n], n, net.cp)

    def cores(self):
        net, mid = self.net, self.mid
        for n, (fx, fy) in enumerate(self.ORDER):
            self.take(self.bc.at[n], n)
            own = self.part.at[self.place(fx, fy, net.core)]
            add_into(mid.at[n], [own, self.bc.at[n]], self.rows, self.chunk)
            if n == 0:
                self.send(lambda: mid.at[0, self.lo], lambda: self.bx.at[0], 4, net.xp)
                self.send(lambda: mid.at[0, self.hi], lambda: self.by.at[0], 5, net.yp)
            if n == 1:
                self.send(lambda: mid.at[1, self.lo], lambda: self.bx.at[1], 6, net.xp)
            if n == 2:
                self.send(lambda: mid.at[2, self.hi], lambda: self.by.at[1], 7, net.yp)

    def turn(self):
        net, mid, second = self.net, self.mid, self.second
        self.take(self.bx.at[0], 4)
        add_into(second.at[0], [mid.at[2, self.lo], self.bx.at[0]], self.half, self.chunk)
        self.send(lambda: second.at[0], lambda: self.b2.at[0], 8, net.yp)
        self.take(self.by.at[0], 5)
        add_into(second.at[1], [mid.at[1, self.hi], self.by.at[0]], self.half, self.chunk)
        self.send(lambda: second.at[1], lambda: self.b2.at[1], 9, net.xp)

    def final(self, out, more=()):
        mid = self.mid
        self.take(self.bx.at[1], 6)
        self.take(self.by.at[1], 7)
        for n, (at, got) in enumerate(((self.lo, self.bx), (self.hi, self.by))):
            self.take(self.b2.at[n], 8 + n)
            terms = [mid.at[3, at], got.at[1], self.b2.at[n]] + [m.at[at] for m in more]
            add_into(out.at[at], terms, self.half, self.chunk)


def scatter_plane(part, depth):
    rows, cols = part.shape[1:]

    def kernel(part_ref, out, *scratch):
        net = Net(depth)
        sends = Sends()
        greet([net.xp, net.yp, net.cp])
        work = PlaneScatter(net, sends, part_ref, rows, scratch)
        work.begin()
        work.cores()
        work.turn()
        work.final(out)
        sends.finish()

    return pl.pallas_call(
        kernel,
        out_shape=jax.ShapeDtypeStruct((rows, cols), F32),
        in_specs=[vmem()],
        out_specs=vmem(),
        scratch_shapes=PlaneScatter.scratch(rows, cols),
        compiler_params=comm_params(4),
        name="scatter_plane",
    )(part)


class ShardScatter:
    @staticmethod
    def scratch(depth, rows, cols):
        far = max(depth - 1, 1)
        shapes = [(2 * depth, rows, cols)] + [(depth, rows, cols)] * 2 + [(far, rows, cols)] * 2
        return [pltpu.VMEM(s, BF) for s in shapes] + dma_sems(
            2 * depth, 2 * depth, depth, depth, far, far
        )

    def __init__(self, net, sends, part, scratch):
        self.net, self.sends, self.part = net, sends, part
        self.bc, self.sx, self.bx, self.sz, self.bz = scratch[:5]
        self.ssc, self.rsc, self.ssx, self.rsx, self.ssz, self.rsz = scratch[5:]
        depth = net.depth
        self.order = sorted(range(1, depth), key=lambda d: -min(d, depth - d)) + [0]
        self.rows = part.shape[1]
        self.chunk = chunk_of(self.rows)

    def block(self, dz, fx, core):
        x = 1 - self.net.x if fx else self.net.x
        return self.part.at[self.net.zoff(dz) * INNER + x * 2 + core]

    def begin(self):
        net = self.net
        for dz in self.order:
            for fx in (1, 0):
                n = dz * 2 + fx
                self.sends.start(
                    self.block(dz, fx, 1 - net.core),
                    self.bc.at[n],
                    self.ssc.at[n],
                    self.rsc.at[n],
                    net.cp,
                )

    def end(self, out):
        net, sends = self.net, self.sends
        for dz in self.order:
            n = dz * 2 + 1
            arrived(self.bc.at[n], self.ssc.at[n], self.rsc.at[n], net.cp)
            add_into(
                self.sx.at[dz], [self.block(dz, 1, net.core), self.bc.at[n]], self.rows, self.chunk
            )
            sends.start(self.sx.at[dz], self.bx.at[dz], self.ssx.at[dz], self.rsx.at[dz], net.xp)
        for dz in self.order:
            n = dz * 2
            arrived(self.bc.at[n], self.ssc.at[n], self.rsc.at[n], net.cp)
            arrived(self.bx.at[dz], self.ssx.at[dz], self.rsx.at[dz], net.xp)
            terms = [self.block(dz, 0, net.core), self.bc.at[n], self.bx.at[dz]]
            if dz:
                add_into(self.sz.at[dz - 1], terms, self.rows, self.chunk)
                sends.start(
                    self.sz.at[dz - 1],
                    self.bz.at[dz - 1],
                    self.ssz.at[dz - 1],
                    self.rsz.at[dz - 1],
                    net.dev(z=net.zoff(dz)),
                )
            else:
                for far in range(net.depth - 1):
                    arrived(self.bz.at[far], self.ssz.at[far], self.rsz.at[far], net.xp)
                    terms.append(self.bz.at[far])
                add_into(out, terms, self.rows, self.chunk)


def scatter_keys(part, depth, cid):
    rows, cols = part.shape[1:]

    def kernel(part_ref, out, *scratch):
        net = Net(depth)
        sends = Sends()
        greet(net.zpeers() + [net.xp, net.cp])
        work = ShardScatter(net, sends, part_ref, scratch)
        work.begin()
        work.end(out)
        sends.finish()

    return pl.pallas_call(
        kernel,
        out_shape=jax.ShapeDtypeStruct((rows, cols), F32),
        in_specs=[vmem()],
        out_specs=vmem(),
        scratch_shapes=ShardScatter.scratch(depth, rows, cols),
        compiler_params=comm_params(cid),
        name="scatter_keys",
    )(part)


def turn(values, cosine, sine):
    return values * cosine + pltpu.roll(values, HEAD // 2, 1) * sine


def attend_backward(q, kv, lo, info, m, l, dob, ob, tile=512):
    block = q.shape[1]
    keys = kv.shape[0]
    tiles = keys // tile

    def kernel(info_ref, q_ref, kv_ref, lo_ref, m_ref, l_ref, do_ref, ob_ref, dq_ref, dkv_ref, da, dl, acc):
        acc[...] = jnp.zeros_like(acc)
        for j in range(2):
            for h in range(GROUP):
                c = slice(h * HEAD, (h + 1) * HEAD)
                d = do_ref[j, :, c].astype(F32)
                o = ob_ref[j, :, c].astype(F32)
                inv = 1.0 / l_ref[j, h : h + 1, :]
                da[j, h] = (d.T * inv).T.astype(BF)
                dl[j, h : h + 1, :] = -jnp.sum((d * o).T, axis=0, keepdims=True) * inv
        low = jnp.minimum(info_ref[2], info_ref[3]) // tile
        high = (info_ref[1] * block + block - 1) // tile

        def clear(t, carry):
            dkv_ref[pl.ds(pl.multiple_of(t * tile, tile), tile), :] = jnp.zeros((tile, 2 * HEAD), BF)
            return carry

        lax.fori_loop(0, low, clear, 0)
        lax.fori_loop(high + 1, tiles, clear, 0)

        def piece(t, j, masked):
            start = pl.multiple_of(t * tile, tile)
            base = info_ref[j] * block
            k = kv_ref[pl.ds(start, tile), :HEAD]
            v = kv_ref[pl.ds(start, tile), HEAD:]
            kt = k.T
            if masked:
                key = start + lax.broadcasted_iota(jnp.int32, (tile, block), 0)
                query = base + lax.broadcasted_iota(jnp.int32, (tile, block), 1)
                ok = (key <= query) & (key >= lo_ref[j])
            dk = dv = None
            for h in range(GROUP):
                qh = q_ref[j, :, h * HEAD : (h + 1) * HEAD]
                s = dot(k, qh, NT) - m_ref[j, h : h + 1, :]
                if masked:
                    s = jnp.where(ok, s, NEG)
                p = jnp.exp2(s)
                dah = da[j, h]
                dvh = dot(p.astype(BF), dah)
                dp = dot(v, dah, NT) + dl[j, h : h + 1, :]
                ds = (p * dp).astype(BF)
                dkh = dot(ds, qh)
                acc[j, h] += dot(kt, ds)
                dk = dkh if dk is None else dk + dkh
                dv = dvh if dv is None else dv + dvh
            return dk * LN2, dv

        def tile_step(t, carry):
            start = pl.multiple_of(t * tile, tile)
            rows = pl.ds(start, tile)

            def put(j, masked):
                dk, dv = piece(t, j, masked)
                if j == 0:
                    dk = dk + dkv_ref[rows, :HEAD].astype(F32)
                    dv = dv + dkv_ref[rows, HEAD:].astype(F32)
                dkv_ref[rows, :HEAD] = dk.astype(BF)
                dkv_ref[rows, HEAD:] = dv.astype(BF)

            for j in (1, 0):
                base = info_ref[j] * block
                live = (start <= base + block - 1) & (start + tile > info_ref[2 + j])
                free = (start + tile - 1 <= base) & (start >= info_ref[4 + j])
                if j == 1:

                    @pl.when(jnp.logical_not(live))
                    def _():
                        clear(t, 0)

                @pl.when(live & free)
                def _():
                    put(j, False)

                @pl.when(live & jnp.logical_not(free))
                def _():
                    put(j, True)

            return carry

        lax.fori_loop(low, high + 1, tile_step, 0)
        for j in range(2):
            for h in range(GROUP):
                dq_ref[j, :, h * HEAD : (h + 1) * HEAD] = (acc[j, h] * SCALE).T.astype(BF)

    return pl.pallas_call(
        kernel,
        out_shape=(jax.ShapeDtypeStruct(q.shape, BF), jax.ShapeDtypeStruct(kv.shape, BF)),
        in_specs=[smem()] + [vmem()] * 7,
        out_specs=(vmem(),) * 2,
        scratch_shapes=[
            pltpu.VMEM((2, GROUP, block, HEAD), BF),
            pltpu.VMEM((2, 8, block), F32),
            pltpu.VMEM((2, GROUP, HEAD, block), F32),
        ],
        compiler_params=pltpu.CompilerParams(vmem_limit_bytes=60 << 20),
        cost_estimate=pl.CostEstimate(
            flops=int(2.5e10), bytes_accessed=12 << 20, transcendentals=13 << 20
        ),
        name="attend_backward",
    )(info, q, kv, lo, m, l, dob, ob)


class PlaneGather:
    @staticmethod
    def sems():
        return dma_sems(2, 2, 2, 2, 5, 5)

    def __init__(self, net, sends, src, out, sems, rows):
        self.net, self.sends, self.src, self.out = net, sends, src, out
        self.sx, self.rx, self.sy, self.ry, self.sc, self.rc = sems
        half = rows // 2
        self.lo, self.hi = pl.ds(0, half), pl.ds(half, half)
        xi = lax.rem(net.i + 2, INNER)
        ci = net.i + 1 - 2 * net.core
        cx = lax.rem(ci + 2, INNER)
        place = lambda i, y: i * SEQ + y
        self.me, self.xb = place(net.i, net.y), place(xi, net.y)
        self.yb, self.db = place(net.i, 1 - net.y), place(xi, 1 - net.y)
        self.core_blocks = [place(ci, net.y), place(ci, 1 - net.y), place(cx, net.y)]
        self.core_diag = place(cx, 1 - net.y)

    def begin(self):
        self.begin_y()
        self.begin_x()

    def begin_y(self):
        net, out, src = self.net, self.out, self.src
        self.sends.start(src, out.at[self.me], self.sy.at[0], self.ry.at[0], net.yp)
        self.sends.start(src, out.at[self.me], self.sc.at[0], self.rc.at[0], net.cp)

    def begin_x(self):
        net, out, src = self.net, self.out, self.src
        self.sends.start(src, out.at[self.me], self.sx.at[0], self.rx.at[0], net.xp)

    def pass_on(self, block, part, ssem, rsem, n, device):
        def refs():
            at = self.out.at[block] if part is None else self.out.at[block, part]
            return at, at, ssem.at[n], rsem.at[n], device

        self.sends.later(refs)

    def middle(self):
        net, out = self.net, self.out
        arrived(out.at[self.yb], self.sy.at[0], self.ry.at[0], net.yp)
        self.pass_on(self.yb, self.lo, self.sx, self.rx, 1, net.xp)
        self.pass_on(self.yb, None, self.sc, self.rc, 1, net.cp)
        arrived(out.at[self.xb], self.sx.at[0], self.rx.at[0], net.xp)
        self.pass_on(self.xb, self.hi, self.sy, self.ry, 1, net.yp)
        self.pass_on(self.xb, None, self.sc, self.rc, 2, net.cp)

    def end(self):
        net, out = self.net, self.out
        arrived(out.at[self.db, self.lo], self.sx.at[1], self.rx.at[1], net.xp)
        self.pass_on(self.db, self.lo, self.sc, self.rc, 3, net.cp)
        arrived(out.at[self.db, self.hi], self.sy.at[1], self.ry.at[1], net.yp)
        self.pass_on(self.db, self.hi, self.sc, self.rc, 4, net.cp)

    def last(self):
        net, out = self.net, self.out
        for n, block in enumerate(self.core_blocks):
            arrived(out.at[block], self.sc.at[n], self.rc.at[n], net.cp)
        arrived(out.at[self.core_diag, self.lo], self.sc.at[3], self.rc.at[3], net.cp)
        arrived(out.at[self.core_diag, self.hi], self.sc.at[4], self.rc.at[4], net.cp)


class Route:
    def __init__(self, net, sends_to, comes_from):
        self.net = net
        me = net.z * INNER + net.i
        self.local = (sends_to[0] == me) & (sends_to[1] == net.y)
        self.kept = (comes_from[0] == me) & (comes_from[1] == net.y)
        self.to, self.frm = self.device(sends_to), self.device(comes_from)

    def device(self, place):
        shard, y = place
        return self.net.dev(z=lax.div(shard, INNER), i=lax.rem(shard, INNER), y=y)

    def hello(self):
        @pl.when(jnp.logical_not(self.kept))
        def _():
            pl.semaphore_signal(
                pltpu.get_barrier_semaphore(), inc=1, device_id=self.frm, device_id_type=MESH
            )

        return jnp.where(self.local, 0, 1)

    def send(self, refs):
        @pl.when(self.local)
        def _():
            src, dst, _, _ = refs()
            dst[...] = src[...]

        @pl.when(jnp.logical_not(self.local))
        def _():
            remote(*refs(), self.to).start()

    def sent(self, refs):
        @pl.when(jnp.logical_not(self.local))
        def _():
            remote(*refs(), self.to).wait_send()

    def arrive(self, refs):
        @pl.when(jnp.logical_not(self.kept))
        def _():
            dst, ssem, rsem = refs()
            remote(dst, dst, ssem, rsem, self.to).wait_recv()


class Mirror:
    def __init__(self, net):
        self.net = net
        self.n = net.depth * INNER
        self.last = 2 * self.n - 1
        self.me = net.z * INNER + net.i

    def home(self, block):
        return jnp.where(block < self.n, block, self.last - block)

    def blocks(self):
        return self.me, self.last - self.me

    def slot(self, block):
        return jnp.where(block < self.n, 0, 1)

    def rows_out(self, k):
        block = 2 * self.me + k
        come = self.blocks()[k]
        return Route(
            self.net, (self.home(block), self.net.y), (lax.div(come, 2), self.net.y)
        ), self.slot(block)

    def rows_back(self, k):
        block = self.blocks()[k]
        come = 2 * self.me + k
        return Route(
            self.net, (lax.div(block, 2), self.net.y), (self.home(come), self.net.y)
        ), lax.rem(block, 2)

    def heads_back(self, k):
        block = self.blocks()[k]
        own = 2 * self.me + self.net.y
        return Route(self.net, (lax.div(block, 2), lax.rem(block, 2)), (self.home(own), k))

    def heads_out(self, k):
        own = 2 * self.me + self.net.y
        come = self.blocks()[k]
        return Route(
            self.net, (self.home(own), k), (lax.div(come, 2), lax.rem(come, 2))
        ), self.slot(own)


class Chain:
    @staticmethod
    def sems(depth):
        return dma_sems(*[max(depth - 1, 1) * INNER] * 4)

    def __init__(self, net, out, sems):
        self.net, self.out = net, out
        self.su, self.ru, self.sd, self.rd = sems
        self.steps = (net.depth - 1) * INNER
        self.up = net.dev(z=jnp.minimum(net.z + 1, net.depth - 1))
        self.down = net.dev(z=jnp.maximum(net.z - 1, 0))

    def piece(self, z, q):
        return self.out.at[z * INNER + q]

    def refs(self, hop, q, way):
        net = self.net
        n = (hop + 1) * INNER + q
        z = net.z - 1 - hop if way == 0 else net.z + 1 + hop
        ssem, rsem, device = (
            (self.su.at[n], self.ru.at[n], self.up)
            if way == 0
            else (self.sd.at[n], self.rd.at[n], self.down)
        )
        return self.piece(z, q), ssem, rsem, device

    def begin(self, ready):
        def body(q, carry):
            ready(q)
            for way in range(2):

                @pl.when(self.net.z < self.net.depth - 1 if way == 0 else self.net.z > 0)
                def _():
                    dst, ssem, rsem, device = self.refs(-1, q, way)
                    remote(dst, dst, ssem, rsem, device).start()

            return carry

        lax.fori_loop(0, INNER, body, 0)

    def step(self, n):
        net = self.net
        hop, q = lax.div(n, INNER), lax.rem(n, INNER)
        for way in range(2):
            z = net.z - 1 - hop if way == 0 else net.z + 1 + hop
            here = z >= 0 if way == 0 else z <= net.depth - 1
            further = net.z < net.depth - 1 if way == 0 else net.z > 0

            @pl.when(here)
            def _():
                block = self.piece(z, q)
                if way == 0:
                    arrived(block, self.su.at[n], self.ru.at[n], self.up)
                else:
                    arrived(block, self.sd.at[n], self.rd.at[n], self.down)

            @pl.when(here & further)
            def _():
                dst, ssem, rsem, device = self.refs(hop, q, way)
                remote(dst, dst, ssem, rsem, device).start()

    def run(self, a, b):
        def body(n, carry):
            self.step(n)
            return carry

        lax.fori_loop(a, min(b, self.steps), body, 0)

    def finish(self):
        def body(n, carry):
            hop, q = lax.div(n, INNER) - 1, lax.rem(n, INNER)
            for way in range(2):
                z = self.net.z - 1 - hop if way == 0 else self.net.z + 1 + hop
                here = z >= 0 if way == 0 else z <= self.net.depth - 1
                further = self.net.z < self.net.depth - 1 if way == 0 else self.net.z > 0

                @pl.when(here & further)
                def _():
                    dst, ssem, rsem, device = self.refs(hop, q, way)
                    remote(dst, dst, ssem, rsem, device).wait_send()

            return carry

        lax.fori_loop(0, self.steps, body, 0)


def seg_tile(start, rows, st, en):
    key = start + lax.broadcasted_iota(jnp.int32, (rows, HEAD), 0)
    return ((key >= st) & (key < en)).astype(F32).astype(BF)


def front(stream, pack, moe, chosen, cosine, sine, w_out, out_grad, qseg, starts, depth):
    block = stream.shape[0]
    rows = block * SEQ
    shards = depth * INNER
    part = w_out.shape[0]

    def kernel(
        st_ref, pk_ref, mo_ref, ch_ref, c_ref, n_ref, wo_ref, og_ref, qs_ref, sg_ref,
        s_out, w_full, ch_out, h1_out, q_out, kv_out, o_out, m_out, l_out, mix_out, x1_out, h2_out,
        wf_out, og_out, mo_out,
        qp, acc, top, total, h2_own, gains, own, sq, rq, so, ro, sy, ry, sp, rp, sm, rm, *sems,
    ):
        net = Net(depth)
        sends = Sends()
        mirror = Mirror(net)
        gp = ShardGather(net, sends, pk_ref, FlatSlots(w_full, part), sems[28:34])
        gk = ShardGather(net, sends, None, kv_out, sems[:6])
        gk.src = gk.slot(0, net.i)
        gw = ShardGather(net, sends, wo_ref, FlatSlots(wf_out, part), sems[6:12])
        gg = PlaneGather(net, sends, og_ref, og_out, sems[12:18], block)
        gh = PlaneGather(net, sends, h2_own, h2_out, sems[18:24], block)
        chain = Chain(net, mo_out, sems[24:28])
        rows_out = [mirror.rows_out(k) for k in range(2)]
        heads = [mirror.heads_back(k) for k in range(2)]
        barrier = pltpu.get_barrier_semaphore()
        for device in net.zpeers() + net.plane():
            pl.semaphore_signal(barrier, inc=1, device_id=device, device_id_type=MESH)
        count = depth - 1 + E - 1
        for route in [r for r, _ in rows_out] + heads:
            count = count + route.hello()
        here = lambda y: s_out.at[pl.ds(pl.multiple_of(y * block, block), block)]
        mine_p = pltpu.make_async_copy(pk_ref, gp.slot(0, net.i), own.at[4])
        mine_s = pltpu.make_async_copy(st_ref, here(net.y), own.at[5])
        mine_m = pltpu.make_async_copy(
            mo_ref.at[net.i * SEQ + net.y], mo_out.at[net.z * INNER + net.i], own.at[3]
        )
        mine_c = pltpu.make_async_copy(ch_ref, ch_out.at[net.i * SEQ + net.y], own.at[6])
        mine_g = pltpu.make_async_copy(og_ref, og_out.at[gg.me], own.at[0])
        mine_w = pltpu.make_async_copy(wo_ref, gw.slot(0, net.i), own.at[1])
        for copy in (mine_p, mine_s, mine_m, mine_c, mine_g, mine_w):
            copy.start()
        pl.semaphore_wait(barrier, count)
        gp.begin()
        sends.start(st_ref, here(net.y), sy.at[0], ry.at[0], net.yp)
        for n, device in enumerate(net.plane()):
            sends.start(ch_ref, ch_out.at[net.i * SEQ + net.y], sp.at[n], rp.at[n], device)
        gw.begin()
        gp.end()
        for di in range(1, INNER):
            other = lax.rem(net.i + di, INNER)
            sends.start(
                mo_ref.at[other * SEQ + net.y],
                mo_out.at[net.z * INNER + net.i],
                sm.at[di - 1],
                rm.at[di - 1],
                net.dev(i=other),
            )
        gg.begin_y()

        def moe_ready(q):
            di = lax.rem(net.i - q + INNER, INNER)

            @pl.when(di > 0)
            def _():
                arrived(mo_out.at[net.z * INNER + q], sm.at[di - 1], rm.at[di - 1], net.xp)

        arrived(here(1 - net.y), sy.at[0], ry.at[0], net.yp)
        mine_s.wait()
        mine_p.wait()
        tail = w_full[:, QKV:].astype(F32).T
        gains[...] = tail[:8, :]

        step = 64

        def norm(n, carry):
            at = pl.ds(pl.multiple_of(n * step, step), step)
            x = s_out[at, :].astype(F32)
            scale = lax.rsqrt(jnp.mean(x * x, axis=-1, keepdims=True) + EPS)
            h1_out[at, :] = (x * scale * gains[0:1, :]).astype(BF)
            return carry

        lax.fori_loop(0, rows // step, norm, 0)
        h1 = h1_out[...]
        cos, sin = c_ref[...], n_ref[...]
        r = dot(h1, w_full[:, QCOLS:QKV])
        me = net.z * INNER + net.i
        kv_out[me, :, :HEAD] = turn(r[:, :HEAD], cos, sin).astype(BF)
        kv_out[me, :, HEAD:] = r[:, HEAD:].astype(BF)
        gk.begin()
        for h in range(0, GROUP, 2):
            r = dot(h1, w_full[:, h * HEAD : (h + 2) * HEAD])
            for g in range(2):
                v = turn(r[:, g * HEAD : (g + 1) * HEAD], cos, sin) * (SCALE * LOG2E)
                v = v.astype(BF)
                at = slice((h + g) * HEAD, (h + g + 1) * HEAD)
                qp[0, :, at] = v[:block]
                qp[1, :, at] = v[block:]
        q_refs = [
            lambda k=k: (qp.at[k], q_out.at[rows_out[k][1]], sq.at[k], rq.at[rows_out[k][1]])
            for k in range(2)
        ]
        o_refs = [
            lambda k=k: (o_out.at[k], mix_out.at[net.y], so.at[k], ro.at[net.y]) for k in range(2)
        ]
        for k in range(2):
            rows_out[k][0].send(q_refs[k])
        mine_m.wait()
        mine_w.wait()
        chain.begin(moe_ready)
        gg.begin_x()
        acc[...] = jnp.zeros_like(acc)
        top[...] = jnp.full_like(top, NEG)
        total[...] = jnp.zeros_like(total)
        gk.after_z()
        for k in range(2):
            rows_out[k][0].arrive(lambda: (q_out.at[k], sq.at[k], rq.at[k]))

        low, high = mirror.blocks()
        bases = (low * block, high * block)
        xi = lax.rem(net.i + 2, INNER)
        ci = net.i + 1 - 2 * net.core

        def attend(t, j, masked):
            start = pl.multiple_of(t * rows, rows)
            k = jnp.concatenate(
                [kv_out[t, :, :HEAD], seg_tile(start, rows, sg_ref[0:1, :], sg_ref[1:2, :])], axis=1
            )
            vt = kv_out[t, :, HEAD:].T
            if masked:
                key = start + lax.broadcasted_iota(jnp.int32, (rows, block), 0)
                ok = key <= bases[j] + lax.broadcasted_iota(jnp.int32, (rows, block), 1)
            scores = [
                dot(
                    k,
                    jnp.concatenate(
                        [q_out[j, :, h * HEAD : (h + 1) * HEAD], qs_ref[j]], axis=1
                    ),
                    NT,
                )
                for h in range(GROUP)
            ]
            for h in range(GROUP):
                s = scores[h]
                if masked:
                    s = jnp.where(ok, s, NEG)
                m0 = top[j, h : h + 1, :]
                m1 = jnp.maximum(m0, jnp.max(s, axis=0, keepdims=True))
                p = jnp.exp2(s - m1)
                f = jnp.exp2(m0 - m1)
                top[j, h : h + 1, :] = m1
                total[j, h : h + 1, :] = total[j, h : h + 1, :] * f + jnp.sum(
                    p, axis=0, keepdims=True
                )
                acc[j, h] = acc[j, h] * f + dot(vt, p.astype(BF))

        polled = min((shards - depth) // 2, 2 * INNER - 1, chain.steps)

        def tile(u, carry):
            in_z = u < depth
            in_x = u < 2 * depth
            in_c = u < 3 * depth
            dz = lax.rem(u, depth)
            place = jnp.where(in_z, net.i, jnp.where(in_x, xi, jnp.where(in_c, ci, lax.rem(ci + 2, INNER))))
            t = lax.rem(net.z - dz + depth, depth) * INNER + place

            @pl.when((u >= depth) & in_x)
            def _():
                gk.one_x(dz)

            @pl.when(u >= 2 * depth)
            def _():
                gk.one_c(u - 2 * depth, t)

            @pl.when(u == 2 * depth)
            def _():
                gg.middle()
                gw.after_z()

            @pl.when(u == 3 * depth)
            def _():
                gw.after_x()
                gg.end()

            @pl.when((u >= depth) & (lax.rem(u - depth, 2) == 1) & (u - depth < 2 * polled))
            def _():
                chain.step(lax.div(u - depth, 2))

            for j in (0, 1):
                live = t * rows <= bases[j] + block - 1
                free = t * rows + rows - 1 <= bases[j]

                @pl.when(live & free)
                def _():
                    attend(t, j, False)

                @pl.when(live & jnp.logical_not(free))
                def _():
                    attend(t, j, True)

            return carry

        lax.fori_loop(0, shards, tile, 0)
        gk.sent_loop()
        for j in range(2):
            for h in range(GROUP):
                o_out[j, :, h * HEAD : (h + 1) * HEAD] = (
                    (acc[j, h] / total[j, h : h + 1, :]).T.astype(BF)
                )
        for k in range(2):
            heads[k].send(o_refs[k])
        chain.run(polled, polled + 1)
        m_out[...] = top[...]
        l_out[...] = total[...]
        gw.last()
        gg.last()
        for k in range(2):
            heads[k].arrive(lambda: (mix_out.at[k], so.at[k], ro.at[k]))
        x1 = here(net.y)[...].astype(F32)
        x1 = x1 + dot(mix_out[0], wf_out[:QCOLS, :]) + dot(mix_out[1], wf_out[QCOLS:, :])
        x1_out[...] = x1
        scale = lax.rsqrt(jnp.mean(x1 * x1, axis=-1, keepdims=True) + EPS)
        h2_own[...] = (x1 * scale * gains[1:2, :]).astype(BF)
        mine_h = pltpu.make_async_copy(h2_own, h2_out.at[gh.me], own.at[2])
        gh.begin()
        mine_h.start()
        chain.run(polled + 1, 2 * INNER)
        gh.middle()
        chain.run(2 * INNER, 2 * INNER + 2)
        gh.end()
        chain.run(2 * INNER + 2, chain.steps)
        n = 0
        for di in range(INNER):
            for dy in range(SEQ):
                if di or dy:
                    frm = lax.rem(net.i - di + INNER, INNER) * SEQ + lax.rem(net.y + dy, SEQ)
                    arrived(ch_out.at[frm], sp.at[n], rp.at[n], net.yp)
                    n += 1
        mine_c.wait()
        gh.last()
        for k in range(2):
            rows_out[k][0].sent(q_refs[k])
            heads[k].sent(o_refs[k])
        chain.finish()
        sends.finish()
        mine_g.wait()
        mine_h.wait()

    sds = jax.ShapeDtypeStruct
    stat = sds((2, 8, block), F32)
    heads_shape = sds((2, block, QCOLS), BF)
    return pl.pallas_call(
        kernel,
        out_shape=(
            sds((rows, WIDTH), BF),
            sds((WIDTH, FIRST), BF),
            sds((E,) + chosen.shape, F32),
            sds((rows, WIDTH), BF),
            heads_shape,
            sds((shards, rows, 2 * HEAD), BF),
            heads_shape,
            stat,
            stat,
            heads_shape,
            sds((block, WIDTH), F32),
            sds((E, block, WIDTH), BF),
            sds((WIDTH, WIDTH), BF),
            sds((E, block, WIDTH), BF),
            sds((shards,) + moe.shape[1:], BF),
        ),
        in_specs=[hbm()] * 4 + [vmem()] * 2 + [hbm()] * 2 + [vmem()] * 2,
        out_specs=(vmem(), vmem(), hbm()) + (vmem(),) * 8 + (hbm(), vmem(), hbm(), hbm()),
        scratch_shapes=[
            pltpu.VMEM((2, block, QCOLS), BF),
            pltpu.VMEM((2, GROUP, HEAD, block), F32),
            pltpu.VMEM((2, 8, block), F32),
            pltpu.VMEM((2, 8, block), F32),
            pltpu.VMEM((block, WIDTH), BF),
            pltpu.VMEM((8, WIDTH), F32),
        ]
        + dma_sems(7, 2, 2, 2, 2, 1, 1, E - 1, E - 1, INNER - 1, INNER - 1)
        + ShardGather.sems(depth) * 2
        + PlaneGather.sems() * 2
        + Chain.sems(depth)
        + ShardGather.sems(depth),
        compiler_params=comm_params(7, 60 << 20),
        name="front",
    )(stream, pack, moe, chosen, cosine, sine, w_out, out_grad, qseg, starts)


class Tally:
    def __init__(self, net, part, rows, scratch):
        self.net, self.part, self.rows = net, part, rows
        self.bc, self.sx, self.bx, self.sz, self.bz = scratch[:5]
        self.ssc, self.rsc, self.ssx, self.rsx, self.ssz, self.rsz = scratch[5:]
        self.chunk = chunk_of(rows)

    def number(self, dz, fx, core):
        x = jnp.where(fx == 1, 1 - self.net.x, self.net.x)
        return lax.rem(self.net.z + dz, self.net.depth) * INNER + x * 2 + core

    def core_copy(self, dz, fx):
        net, n = self.net, dz * 2 + fx
        src = self.part.at[self.number(dz, fx, 1 - net.core)]
        return remote(src, self.bc.at[n], self.ssc.at[n], self.rsc.at[n], net.cp)

    def x_copy(self, dz):
        return remote(
            self.sx.at[dz], self.bx.at[dz], self.ssx.at[dz], self.rsx.at[dz], self.net.xp
        )

    def z_copy(self, dz):
        n = dz - 1
        device = self.net.dev(z=lax.rem(self.net.z + dz, self.net.depth))
        return remote(self.sz.at[n], self.bz.at[n], self.ssz.at[n], self.rsz.at[n], device)

    def terms(self, dz, fx):
        n = dz * 2 + fx
        arrived(self.bc.at[n], self.ssc.at[n], self.rsc.at[n], self.net.cp)
        return [self.part.at[self.number(dz, fx, self.net.core)], self.bc.at[n]]

    def x_stage(self, dz):
        add_into(self.sx.at[dz], self.terms(dz, 1), self.rows, self.chunk)
        self.x_copy(dz).start()

    def x_terms(self, dz):
        terms = self.terms(dz, 0)
        arrived(self.bx.at[dz], self.ssx.at[dz], self.rsx.at[dz], self.net.xp)
        return terms + [self.bx.at[dz]]

    def z_stage(self, dz):
        add_into(self.sz.at[dz - 1], self.x_terms(dz), self.rows, self.chunk)
        self.z_copy(dz).start()

    def final(self, out):
        terms = self.x_terms(0)
        for n in range(self.net.depth - 1):
            arrived(self.bz.at[n], self.ssz.at[n], self.rsz.at[n], self.net.xp)
            terms.append(self.bz.at[n])
        add_into(out, terms, self.rows, self.chunk)

    def finish(self):
        for dz in range(self.net.depth):
            for fx in range(2):
                self.core_copy(dz, fx).wait_send()
            self.x_copy(dz).wait_send()
            if dz:
                self.z_copy(dz).wait_send()

    def far(self):
        return [d for d in range(1, self.net.depth)] + [0]

    def begin(self):
        for dz in self.far():
            for fx in (1, 0):
                self.core_copy(dz, fx).start()

    def far_stages(self):
        for dz in self.far():
            self.x_stage(dz)

    def near_stages(self):
        for dz in self.far()[:-1]:
            self.z_stage(dz)


def backward(q, kv, qseg, starts, m, l, ob, mixed, dx1, out_w, mixture, part_rows, depth):
    block = q.shape[1]
    rows = kv.shape[1]
    shards = depth * INNER

    def kernel(
        q_ref, kv_ref, qs_ref, sg_ref, m_ref, l_ref, ob_ref, mix_ref, dx_ref, wf_ref, mx_ref,
        dq_out, dkv_out, own_out, sum_out,
        dob, do_ref, da, dl, acc, dqs, dkv, wpart, wget, so, ro, sq, rq, sw, rw, *scratch,
    ):
        net = Net(depth)
        mirror = Mirror(net)
        keys = Tally(net, dkv, rows, scratch[:11])
        mine = wpart.at[net.y]
        outs = Tally(net, mine, part_rows, scratch[11:22])
        sends = Sends()
        plane = PlaneScatter(net, sends, mx_ref, block, scratch[22:])
        quarter = shards // 4

        def pair_copy(n):
            at = pl.ds(n * quarter, quarter)
            return remote(
                wpart.at[1 - net.y, at], wget.at[at], sw.at[n], rw.at[n], net.yp
            )

        def pair_sum():
            for n in range(4):
                at = pl.ds(n * quarter, quarter)
                arrived(wget.at[at], sw.at[n], rw.at[n], net.yp)

                def body(b, carry):
                    add_into(
                        wpart.at[net.y, b], [wpart.at[net.y, b], wget.at[b]], part_rows, outs.chunk
                    )
                    return carry

                lax.fori_loop(n * quarter, (n + 1) * quarter, body, 0)
            outs.begin()

        heads = [mirror.heads_out(k) for k in range(2)]
        backs = [mirror.rows_back(k) for k in range(2)]
        barrier = pltpu.get_barrier_semaphore()
        for device in net.zpeers() + [net.xp, net.cp, net.yp]:
            pl.semaphore_signal(barrier, inc=1, device_id=device, device_id_type=MESH)
        count = depth - 1 + 3
        for route, _ in heads + backs:
            count = count + route.hello()
        do_refs = [
            lambda k=k: (dob.at[k], do_ref.at[heads[k][1]], so.at[k], ro.at[heads[k][1]])
            for k in range(2)
        ]
        dq_refs = [
            lambda k=k: (dqs.at[k], dq_out.at[backs[k][1]], sq.at[k], rq.at[backs[k][1]])
            for k in range(2)
        ]
        dx = dx_ref[...]
        for k in range(2):
            dob[k] = dot(dx, wf_ref[k * QCOLS : (k + 1) * QCOLS, :], NT).astype(BF)
        pl.semaphore_wait(barrier, count)
        for k in range(2):
            heads[k][0].send(do_refs[k])
        plane.begin()
        wide = QCOLS // 2
        for n in range(4):
            cols = slice((n % 2) * wide, (n % 2 + 1) * wide)
            grad = dot(mix_ref[n // 2, :, cols].T, dx).astype(BF)
            for b in range(wide // part_rows):
                for s in range(SEQ):
                    wpart[s, n * (wide // part_rows) + b] = grad[
                        b * part_rows : (b + 1) * part_rows, s * QCOLS : (s + 1) * QCOLS
                    ]
            pair_copy(n).start()
        acc[...] = jnp.zeros_like(acc)
        plane.cores()
        for k in range(2):
            heads[k][0].arrive(lambda: (do_ref.at[k], so.at[k], ro.at[k]))
        for j in range(2):
            for h in range(GROUP):
                c = slice(h * HEAD, (h + 1) * HEAD)
                d = do_ref[j, :, c].astype(F32)
                o = ob_ref[j, :, c].astype(F32)
                inv = 1.0 / l_ref[j, h : h + 1, :]
                da[j, h] = (d.T * inv).T.astype(BF)
                dl[j, h : h + 1, :] = -jnp.sum((d * o).T, axis=0, keepdims=True) * inv
        low, high = mirror.blocks()
        bases = (low * block, high * block)

        def piece(t, j, masked):
            start = pl.multiple_of(t * rows, rows)
            k = kv_ref[t, :, :HEAD]
            v = kv_ref[t, :, HEAD:]
            kt = k.T
            k_seg = jnp.concatenate(
                [k, seg_tile(start, rows, sg_ref[0:1, :], sg_ref[1:2, :])], axis=1
            )
            if masked:
                key = start + lax.broadcasted_iota(jnp.int32, (rows, block), 0)
                ok = key <= bases[j] + lax.broadcasted_iota(jnp.int32, (rows, block), 1)
            dk = dv = None
            for h in range(GROUP):
                qh = q_ref[j, :, h * HEAD : (h + 1) * HEAD]
                s = dot(k_seg, jnp.concatenate([qh, qs_ref[j]], axis=1), NT)
                s = s - m_ref[j, h : h + 1, :]
                if masked:
                    s = jnp.where(ok, s, NEG)
                p = jnp.exp2(s)
                dah = da[j, h]
                dvh = dot(p.astype(BF), dah)
                dp = dot(v, dah, NT) + dl[j, h : h + 1, :]
                ds = (p * dp).astype(BF)
                dkh = dot(ds, qh)
                acc[j, h] += dot(kt, ds)
                dk = dkh if dk is None else dk + dkh
                dv = dvh if dv is None else dv + dvh
            return dk * LN2, dv

        def tile(u, carry):
            g, r = lax.div(u, INNER), lax.rem(u, INNER)
            dz = lax.rem(g + 1, depth)
            fx = 1 - lax.div(r, 2)
            other = lax.rem(r, 2) == 0
            t = keys.number(dz, fx, jnp.where(other, 1 - net.core, net.core))

            def put(j, masked):
                dk, dv = piece(t, j, masked)
                if j == 0:
                    dk = dk + dkv[t, :, :HEAD].astype(F32)
                    dv = dv + dkv[t, :, HEAD:].astype(F32)
                dkv[t, :, :HEAD] = dk.astype(BF)
                dkv[t, :, HEAD:] = dv.astype(BF)

            for j in (1, 0):
                live = t * rows <= bases[j] + block - 1
                free = t * rows + rows - 1 <= bases[j]
                if j == 1:

                    @pl.when(jnp.logical_not(live))
                    def _():
                        dkv[t] = jnp.zeros((rows, 2 * HEAD), BF)

                @pl.when(live & free)
                def _():
                    put(j, False)

                @pl.when(live & jnp.logical_not(free))
                def _():
                    put(j, True)

            @pl.when(other)
            def _():
                keys.core_copy(dz, fx).start()

            @pl.when(r == INNER - 1)
            def _():
                keys.x_stage(dz)

            @pl.when((r == INNER - 1) & (g > 0))
            def _():
                keys.z_stage(g)

            @pl.when(u == shards // 2 - 2)
            def _():
                plane.turn()

            @pl.when(u == shards - 7)
            def _():
                pair_sum()

            @pl.when(u == shards - 4)
            def _():
                outs.far_stages()

            @pl.when(u == shards - 1)
            def _():
                outs.near_stages()

            return carry

        lax.fori_loop(0, shards, tile, 0)
        for j in range(2):
            for h in range(GROUP):
                dqs[j, :, h * HEAD : (h + 1) * HEAD] = (acc[j, h] * SCALE).T.astype(BF)
        for k in range(2):
            backs[k][0].send(dq_refs[k])
        plane.final(sum_out)
        outs.final(own_out)
        keys.final(dkv_out)
        for k in range(2):
            backs[k][0].arrive(lambda: (dq_out.at[k], sq.at[k], rq.at[k]))
        for k in range(2):
            heads[k][0].sent(do_refs[k])
            backs[k][0].sent(dq_refs[k])
        for n in range(4):
            pair_copy(n).wait_send()
        sends.finish()
        outs.finish()
        keys.finish()

    sds = jax.ShapeDtypeStruct
    pair = (2, block, QCOLS)
    return pl.pallas_call(
        kernel,
        out_shape=(
            sds(pair, BF),
            sds((rows, 2 * HEAD), F32),
            sds((part_rows, QCOLS), F32),
            sds((block, WIDTH), BF),
        ),
        in_specs=[vmem()] * 11,
        out_specs=(vmem(),) * 4,
        scratch_shapes=[
            pltpu.VMEM(pair, BF),
            pltpu.VMEM(pair, BF),
            pltpu.VMEM((2, GROUP, block, HEAD), BF),
            pltpu.VMEM((2, 8, block), F32),
            pltpu.VMEM((2, GROUP, HEAD, block), F32),
            pltpu.VMEM(pair, BF),
            pltpu.VMEM((shards, rows, 2 * HEAD), BF),
            pltpu.VMEM((SEQ, shards, part_rows, QCOLS), BF),
            pltpu.VMEM((shards, part_rows, QCOLS), BF),
        ]
        + dma_sems(2, 2, 2, 2, 4, 4)
        + ShardScatter.scratch(depth, rows, 2 * HEAD)
        + ShardScatter.scratch(depth, part_rows, QCOLS)
        + PlaneScatter.scratch(block, WIDTH),
        compiler_params=comm_params(8, 60 << 20),
        name="backward",
    )(q, kv, qseg, starts, m, l, ob, mixed, dx1, out_w, mixture)


def finish_layer(
    dq, dkv, cosine, sine, h1, weights, pair, small, dx1, gain_a, out_own, moe, depth
):
    block = dx1.shape[0]
    rows = pair.shape[0]
    shards = depth * INNER
    part_rows = out_own.shape[0]
    wide = 384

    def kernel(
        dq_ref, dkv_ref, c_ref, n_ref, h1_ref, w_ref, s_ref, sm_ref, dx_ref, ga_ref, oo_ref, moe_ref,
        sg_out, own_out, pair_out, pair_wo, moe_out,
        raw, part, give, take, low, low_wo, sm, rm, sy, ry, ls, *scratch,
    ):
        net = Net(depth)
        sends = Sends()
        me = net.i * SEQ + net.y
        mine = pltpu.make_async_copy(moe_ref.at[net.i], moe_out.at[me], ls.at[0])
        work = Tally(net, part, part_rows, scratch)
        barrier = pltpu.get_barrier_semaphore()
        for device in net.zpeers() + net.plane():
            pl.semaphore_signal(barrier, inc=1, device_id=device, device_id_type=MESH)
        pl.semaphore_wait(barrier, depth - 1 + E - 1)
        for di in range(1, INNER):
            i = lax.rem(net.i + di, INNER)
            sends.start(
                moe_ref.at[i], moe_out.at[me], sm.at[di], rm.at[di], net.dev(i=i)
            )
        sends.start(moe_ref.at[net.i], moe_out.at[me], sm.at[0], rm.at[0], net.yp)
        mine.start()
        cos, sin = c_ref[...], -n_ref[...]
        for k in range(2):
            at = slice(k * block, (k + 1) * block)
            for h in range(GROUP):
                cols = slice(h * HEAD, (h + 1) * HEAD)
                v = dq_ref[k, :, cols].astype(F32)
                raw[at, cols] = turn(v, cos[at], sin[at]).astype(BF)
        dk = dkv_ref[:, :HEAD].astype(BF).astype(F32)
        raw[:, QCOLS : QCOLS + HEAD] = turn(dk, cos, sin).astype(BF)
        raw[:, QCOLS + HEAD :] = dkv_ref[:, HEAD:].astype(BF)
        low_wo[...] = oo_ref[...].astype(BF)
        sends.start(low_wo, pair_wo, sy.at[1], ry.at[1], net.yp)

        def half(y):
            at = pl.ds(pl.multiple_of(y * block, block), block)
            x = s_ref[at, :].astype(F32)
            scale = lax.rsqrt(jnp.mean(x * x, axis=-1, keepdims=True) + EPS)
            grad = dot(raw[at, :], w_ref[:, :QKV], NT)
            return x * scale, scale, grad

        normed, _, grad = half(1 - net.y)
        give[...] = grad.astype(BF)
        sends.start(give, take, sy.at[2], ry.at[2], net.yp)
        gain_part = jnp.sum(grad * normed, axis=0, keepdims=True)
        normed, scale, grad = half(net.y)
        gain_part = gain_part + jnp.sum(grad * normed, axis=0, keepdims=True)
        lanes = lax.broadcasted_iota(jnp.int32, (EXTRA, WIDTH), 0)
        extra = jnp.where(lanes == 0, gain_part, sm_ref[...]).T.astype(BF)
        per = wide // part_rows
        for c in range(WIDTH // wide):
            g = dot(h1_ref[:, c * wide : (c + 1) * wide].T, raw[...]).astype(BF)
            for b in range(per):
                part[c * per + b, :, :QKV] = g[b * part_rows : (b + 1) * part_rows]
                part[c * per + b, :, QKV:] = extra[
                    c * wide + b * part_rows : c * wide + (b + 1) * part_rows
                ]
        work.begin()
        work.far_stages()
        for di in range(1, INNER):
            got = moe_out.at[lax.rem(net.i - di + INNER, INNER) * SEQ + net.y]
            arrived(got, sm.at[di], rm.at[di], net.yp)
            sends.start(got, got, sm.at[INNER - 1 + di], rm.at[INNER - 1 + di], net.yp)
        arrived(take, sy.at[2], ry.at[2], net.yp)
        inner = (grad + take[...].astype(F32)) * ga_ref[...]
        pull = scale * (inner - normed * jnp.mean(inner * normed, axis=-1, keepdims=True))
        sg_out[...] = (dx_ref[...] + pull).astype(BF)
        work.near_stages()
        work.final(own_out)
        low[...] = own_out[...].astype(BF)
        sends.start(low, pair_out, sy.at[0], ry.at[0], net.yp)
        for di in range(INNER):
            n = INNER - 1 + di if di else 0
            got = moe_out.at[lax.rem(net.i - di + INNER, INNER) * SEQ + 1 - net.y]
            arrived(got, sm.at[n], rm.at[n], net.yp)
        arrived(pair_wo, sy.at[1], ry.at[1], net.yp)
        arrived(pair_out, sy.at[0], ry.at[0], net.yp)
        sends.finish()
        work.finish()
        mine.wait()

    sds = jax.ShapeDtypeStruct
    return pl.pallas_call(
        kernel,
        out_shape=(
            sds((block, WIDTH), BF),
            sds((part_rows, FIRST), F32),
            sds((part_rows, FIRST), BF),
            sds((part_rows, QCOLS), BF),
            sds((E,) + moe.shape[1:], BF),
        ),
        in_specs=[vmem()] * 11 + [hbm()],
        out_specs=(vmem(),) * 4 + (hbm(),),
        scratch_shapes=[
            pltpu.VMEM((rows, QKV), BF),
            pltpu.VMEM((shards, part_rows, FIRST), BF),
            pltpu.VMEM((block, WIDTH), BF),
            pltpu.VMEM((block, WIDTH), BF),
            pltpu.VMEM((part_rows, FIRST), BF),
            pltpu.VMEM((part_rows, QCOLS), BF),
        ]
        + dma_sems(2 * INNER - 1, 2 * INNER - 1, 3, 3, 1)
        + ShardScatter.scratch(depth, part_rows, FIRST),
        compiler_params=comm_params(9, 60 << 20),
        name="finish_layer",
    )(dq, dkv, cosine, sine, h1, weights, pair, small, dx1, gain_a, out_own, moe)


def run_expert(h2, out_grad, onehot, gate, lane, moe_w, rows_in, rows_out):
    blocks, tokens = h2.shape[:2]
    slots = onehot.shape[1]
    shards = moe_w.shape[0]
    pairs = 2
    steps = blocks // pairs
    wide = WIDTH + EXTRA

    def kernel(
        h_ref, g_ref, oh_ref, gt_ref, ln_ref, w_ref, mix_out, back_out, grads_out,
        gu_w, dn_w, gu_acc, dn_acc, rows, slot_g, stage, wsem, gsem,
    ):
        step = pl.program_id(0)

        def weight_copies():
            for n in range(shards):
                yield pltpu.make_async_copy(
                    w_ref.at[n, pl.ds(0, rows_in)], gu_w.at[pl.ds(n * rows_in, rows_in)], wsem.at[n]
                )
                yield pltpu.make_async_copy(
                    w_ref.at[n, pl.ds(rows_in, rows_out)],
                    dn_w.at[pl.ds(n * rows_out, rows_out)],
                    wsem.at[shards + n],
                )

        @pl.when(step == 0)
        def _():
            for copy in weight_copies():
                copy.start()
            gu_acc[...] = jnp.zeros_like(gu_acc)
            dn_acc[...] = jnp.zeros_like(dn_acc)

        for b in range(pairs):
            at = slice(b * slots, (b + 1) * slots)
            rows[at, :] = dot(oh_ref[b], h_ref[b]).astype(BF)
            slot_g[at, :] = dot(oh_ref[b], g_ref[b]).astype(BF)

        @pl.when(step == 0)
        def _():
            for copy in weight_copies():
                copy.wait()

        gate_col = gt_ref[...].reshape(pairs * slots, 1)
        both = dot(rows[...], gu_w[...])
        pre, up = both[:, :FF], both[:, FF:]
        phi = 0.5 * (1.0 + lax.erf(pre * (0.5**0.5)))
        slope = phi + pre * jnp.exp(-0.5 * pre * pre) * 0.3989422804014327
        gelu = pre * phi
        active = (gelu * up).astype(BF)
        grad = slot_g[...]
        out = dot(active, dn_w[...])
        gate_grad = jnp.sum(grad.astype(F32) * out, axis=-1, keepdims=True)
        mixed = (out * gate_col).astype(BF)
        expert_grad = (grad.astype(F32) * gate_col).astype(BF)
        active_grad = dot(expert_grad, dn_w[...], NT)
        low = jnp.concatenate(
            [(active_grad * up * slope).astype(BF), (active_grad * gelu).astype(BF)], axis=1
        )
        back = dot(low, gu_w[...], NT).astype(BF)
        back = jnp.concatenate([back, (gate_grad * ln_ref[...]).astype(BF)], axis=1)
        for b in range(pairs):
            at = slice(b * slots, (b + 1) * slots)
            spread = oh_ref[b].T
            mix_out[b] = dot(spread, mixed[at]).astype(BF)
            back_out[b] = dot(spread, back[at]).astype(BF)
        gu_acc[...] += dot(rows[...].T, low)
        dn_acc[...] += dot(active.T, expert_grad)

        @pl.when(step == steps - 1)
        def _():
            def copy(n, slot):
                return pltpu.make_async_copy(stage.at[slot], grads_out.at[n], gsem.at[slot])

            for n in range(shards):
                slot = n % 2
                if n >= 2:
                    copy(n - 2, slot).wait()
                stage[slot, :rows_in, :] = gu_acc[n * rows_in : (n + 1) * rows_in, :].astype(BF)
                stage[slot, rows_in:, :] = dn_acc[n * rows_out : (n + 1) * rows_out, :].astype(BF)
                copy(n, slot).start()
            for n in range(shards - 2, shards):
                copy(n, n % 2).wait()

    sds = jax.ShapeDtypeStruct
    block = lambda *shape: pl.BlockSpec((pairs,) + shape, lambda n: (n,) + (0,) * len(shape))
    return pl.pallas_call(
        kernel,
        grid=(steps,),
        out_shape=(
            sds((blocks, tokens, WIDTH), BF),
            sds((blocks, tokens, wide), BF),
            sds(moe_w.shape, BF),
        ),
        in_specs=[
            block(tokens, WIDTH),
            block(tokens, WIDTH),
            block(slots, tokens),
            block(slots, 1),
            pl.BlockSpec((1, EXTRA), lambda n: (0, 0)),
            hbm(),
        ],
        out_specs=(block(tokens, WIDTH), block(tokens, wide), hbm()),
        scratch_shapes=[
            pltpu.VMEM((WIDTH, 2 * FF), BF),
            pltpu.VMEM((FF, WIDTH), BF),
            pltpu.VMEM((WIDTH, 2 * FF), F32),
            pltpu.VMEM((FF, WIDTH), F32),
            pltpu.VMEM((pairs * slots, WIDTH), BF),
            pltpu.VMEM((pairs * slots, WIDTH), BF),
            pltpu.VMEM((2, rows_in + rows_out, WIDTH), BF),
        ]
        + dma_sems(2 * shards, 2),
        compiler_params=pltpu.CompilerParams(
            vmem_limit_bytes=60 << 20, dimension_semantics=("arbitrary",)
        ),
        cost_estimate=pl.CostEstimate(
            flops=int(3.8e10), bytes_accessed=40 << 20, transcendentals=4 << 20
        ),
        name="run_expert",
    )(h2, out_grad, onehot, gate, lane, moe_w)


def rms_parts(x):
    scale = lax.rsqrt(jnp.mean(x * x, axis=-1, keepdims=True) + EPS)
    return x * scale, scale


def rms_pull(normed, scale, grad, gain):
    inner = grad * gain
    return scale * (inner - normed * jnp.mean(inner * normed, axis=-1, keepdims=True))


def document_first(index, starts):
    return jnp.max(jnp.where(starts <= index[..., None], starts, 0), axis=-1)


def gelu_product(gate_pre, up_pre):
    return jax.nn.gelu(gate_pre, approximate=False) * up_pre


class Zigzag:
    def __init__(self, shards):
        last = 2 * shards - 1
        home = lambda b: b if b < shards else last - b
        self.rows = [
            [(s * 2 + y, home(2 * s + k) * 2 + y) for s in range(shards) for y in range(2)]
            for k in range(2)
        ]
        self.heads = [
            [
                (s * 2 + g, s if (g == 0) == (k == 0) else last - s)
                for s in range(shards)
                for g in range(2)
            ]
            for k in range(2)
        ]

    @staticmethod
    def move(x, pairs, back=False):
        return lax.ppermute(x, AXES, [(b, a) for a, b in pairs] if back else pairs)


def pick(flag, a, b):
    return jnp.where(flag, a, b), jnp.where(flag, b, a)


def experts(h2, out_grad, chosen, router_w, moe_w, rows_in, rows_out, me):
    blocks, tokens = h2.shape[:2]
    logits = dot(h2.reshape(blocks * tokens, WIDTH), router_w)
    probs = jax.nn.softmax(logits, axis=-1)
    mine = (jnp.arange(E) == me).astype(F32)
    named = jnp.sum(chosen * mine[None, :, None], axis=1)
    gate_tok = jnp.sum(probs * mine[None, :], axis=-1).reshape(blocks, tokens) * named
    upper = (jnp.arange(tokens)[:, None] <= jnp.arange(tokens)[None, :]).astype(BF)
    rank = dot(named.astype(BF), upper) - 1.0
    pick_slot = (
        rank[:, None, :] == jnp.arange(MOST, dtype=F32)[None, :, None]
    ) & (named[:, None, :] > 0.5)
    onehot = pick_slot.astype(BF)
    slots = blocks * MOST
    gate = jnp.sum(jnp.where(pick_slot, gate_tok[:, None, :], 0.0), axis=-1)
    if rows_in % 16 == 0 and rows_out % 16 == 0:
        lane = (jnp.arange(EXTRA) == me).astype(F32)[None, :]
        return run_expert(
            h2, out_grad, onehot, gate[:, :, None], lane, moe_w, rows_in, rows_out
        )
    gate = gate.reshape(slots, 1)
    spread = lambda v: lax.dot_general(
        onehot, v, (((2,), (1,)), ((0,), (0,))), preferred_element_type=F32
    )
    collect = lambda v: lax.dot_general(
        onehot, v, (((1,), (1,)), ((0,), (0,))), preferred_element_type=F32
    )
    rows = spread(h2).astype(BF).reshape(slots, WIDTH)
    slot_grad = spread(out_grad).astype(BF).reshape(slots, WIDTH)
    gate_w = moe_w[:, :rows_in, :FF].reshape(WIDTH, FF)
    up_w = moe_w[:, :rows_in, FF:].reshape(WIDTH, FF)
    down_w = moe_w[:, rows_in:, :].reshape(FF, WIDTH)
    gate_pre = dot(rows, gate_w)
    up_pre = dot(rows, up_w)
    active_f, pull = jax.vjp(gelu_product, gate_pre, up_pre)
    active = active_f.astype(BF)
    out = dot(active, down_w)
    slot_gf = slot_grad.astype(F32)
    gate_grad = jnp.sum(slot_gf * out, axis=-1).reshape(blocks, MOST)
    mixture = collect((out * gate).astype(BF).reshape(blocks, MOST, WIDTH)).astype(BF)
    expert_grad = (slot_gf * gate).astype(BF)
    active_grad = dot(expert_grad, down_w, NT)
    g_low, u_low = (v.astype(BF) for v in pull(active_grad))
    back = dot(g_low, gate_w, NT) + dot(u_low, up_w, NT)
    back_tok = collect(back.astype(BF).reshape(blocks, MOST, WIDTH)).astype(BF)
    gate_back = jnp.sum(jnp.where(pick_slot, gate_grad[:, :, None], 0.0), axis=1)
    lanes = (jnp.arange(EXTRA) == me).astype(F32)
    back_tok = jnp.concatenate(
        [back_tok, (gate_back[:, :, None] * lanes[None, None, :]).astype(BF)], axis=-1
    )
    shards = WIDTH // rows_in
    grads = jnp.concatenate(
        [
            jnp.concatenate(
                [
                    dot(rows, g_low, TN).astype(BF).reshape(shards, rows_in, FF),
                    dot(rows, u_low, TN).astype(BF).reshape(shards, rows_in, FF),
                ],
                axis=-1,
            ),
            dot(active, expert_grad, TN).astype(BF).reshape(shards, rows_out, WIDTH),
        ],
        axis=1,
    )
    return mixture, back_tok, grads


def back_apart(zig, q, kv, lo, info, top, total, ob, mixed, dx1, out_w, part_rows, depth):
    z, i, y = (lax.axis_index(a) for a in AXES)
    shards, rows = kv.shape[:2]
    shard = z * INNER + i
    even, head_zero = lax.rem(shard, 2) == 0, y == 0
    dob = dot(dx1, out_w, NT).astype(BF)
    out_part = dot(mixed, dx1, TN).astype(BF)
    keep, give = pick(head_zero, out_part[:, :QCOLS], out_part[:, QCOLS:])
    keep = keep.astype(F32) + lax.ppermute(give, "seq", [(0, 1), (1, 0)]).astype(F32)
    out_own = scatter_keys(keep.astype(BF).reshape(shards, part_rows, QCOLS), depth, 10)
    dob_a, dob_b = pick(shard * SEQ + y < shards, dob[:, :QCOLS], dob[:, QCOLS:])
    dob_zig = jnp.stack(
        pick(
            head_zero,
            zig.move(dob_a, zig.heads[0], True),
            zig.move(dob_b, zig.heads[1], True),
        )
    )
    flat = kv.reshape(shards * rows, 2 * HEAD)
    dq, dkv_part = attend_backward(q, flat, lo, info, top, total, dob_zig, ob)
    dq_a, dq_b = pick(even, dq[0], dq[1])
    dq_pair = jnp.stack([zig.move(dq_a, zig.rows[0], True), zig.move(dq_b, zig.rows[1], True)])
    return dq_pair, scatter_keys(dkv_part.reshape(kv.shape), depth, 5), out_own


def local(depth, stream, doc_starts, routes, attn_gain, w_query, w_key, w_value, w_out, ffn_gain, w_router, w_gate, w_up, w_down, out_grad):
    tokens = stream.shape[0]
    rows_in, rows_out = w_gate.shape[1], w_down.shape[1]
    shards = depth * INNER
    z, i, y = (lax.axis_index(a) for a in AXES)
    shard = z * INNER + i
    me = i * SEQ + y
    zig = Zigzag(shards)

    cut = lambda w, width: lax.dynamic_slice_in_dim(w, y * width, width, 1)
    extra = jnp.concatenate(
        [
            attn_gain[:, None],
            ffn_gain[:, None],
            w_router,
            jnp.zeros((rows_in, EXTRA - 2 - E), BF),
        ],
        axis=1,
    )
    pack = jnp.concatenate(
        [cut(w_query, QCOLS), cut(w_key, HEAD), cut(w_value, HEAD), extra], axis=1
    )
    moe_pack = jnp.concatenate([jnp.concatenate([w_gate, w_up], axis=2), w_down], axis=1)
    chosen_t = jnp.any(
        routes.T[:, None, :] == jnp.arange(E, dtype=jnp.int32)[None, :, None], axis=0
    ).astype(F32)
    pair_index = shard * SEQ * tokens + jnp.arange(SEQ * tokens, dtype=jnp.int32)
    position = pair_index - document_first(pair_index, doc_starts)
    freq = ROPE_BASE ** (-(jnp.arange(HEAD // 2, dtype=F32) * 2.0) / HEAD)
    angle = position.astype(F32)[:, None] * freq[None, :]
    cos_half, sin_half = jnp.cos(angle), jnp.sin(angle)
    cosine = jnp.concatenate([cos_half, cos_half], axis=1)
    sine = jnp.concatenate([-sin_half, sin_half], axis=1)

    block_ids = jnp.stack([shard, 2 * shards - 1 - shard]).astype(jnp.int32)
    query_index = block_ids[:, None] * tokens + jnp.arange(tokens, dtype=jnp.int32)[None, :]
    lo = document_first(query_index, doc_starts).astype(jnp.int32)
    info = jnp.concatenate([block_ids, lo[:, 0], lo[:, -1], jnp.zeros((2,), jnp.int32)])
    big = jnp.int32(1 << 30)
    spare = jnp.full((HEAD - doc_starts.shape[0],), big)
    first = jnp.concatenate([doc_starts, spare])
    beyond = jnp.concatenate([doc_starts[1:], spare, big[None]])
    starts = jnp.stack([first, beyond])
    outside = (query_index[..., None] < first) | (query_index[..., None] >= beyond)
    qseg = jnp.where(outside, NEG, 0.0).astype(BF)
    lo = lo[:, None, :]
    (
        pair, weights, chosen_all, h1, q, kv, ob, top, total, mixed, x1, h2_plane, out_w, grad_plane, moe_w,
    ) = front(stream, pack, moe_pack, chosen_t, cosine, sine, w_out, out_grad, qseg, starts, depth)
    extra_w = lax.optimization_barrier(weights[:, QKV : QKV + EXTRA])
    gains = extra_w[:, :2].astype(F32).T
    gain_a, gain_f = gains[0:1], gains[1:2]
    router_w = extra_w[:, 2 : 2 + E]
    qkv_w = weights[:, :QKV]
    head_zero = y == 0
    mixed_pair = mixed
    mixed = jnp.concatenate([mixed[0], mixed[1]], axis=1)
    normed, scale = rms_parts(x1)
    h2 = (normed * gain_f).astype(BF)

    mixture_part, back_part, moe_grads = experts(
        h2_plane, grad_plane, chosen_all, router_w, moe_w, rows_in, rows_out, me
    )
    back = scatter_plane(back_part, depth)
    moe_own = lax.psum_scatter(
        moe_grads.reshape(depth, INNER, rows_in + rows_out, WIDTH),
        "outer",
        scatter_dimension=0,
        tiled=False,
    )

    chosen = chosen_t.T
    probs = jax.nn.softmax(dot(h2, router_w), axis=-1)
    dp = back[:, WIDTH : WIDTH + E] * chosen
    dz = (probs * (dp - jnp.sum(dp * probs, axis=-1, keepdims=True))).astype(BF)
    router_part = dot(dz, h2, TN)
    dh2 = back[:, :WIDTH] + dot(dz, router_w, NT)
    grad_f = out_grad.astype(F32)
    dx1 = grad_f + rms_pull(normed, scale, dh2, gain_f)
    gain_f_part = jnp.sum(dh2 * normed, axis=0)
    dx1_low = dx1.astype(BF)
    if depth <= 4:
        dq_pair, dkv, out_own, mixture = backward(
            q, kv, qseg, starts, top, total, ob, mixed_pair, dx1_low, out_w, mixture_part, rows_in, depth
        )
    else:
        dq_pair, dkv, out_own = back_apart(
            zig, q, kv, lo, info, top, total, ob, mixed, dx1_low, out_w, rows_in, depth
        )
        mixture = lax.psum_scatter(mixture_part, ("inner", "seq"), scatter_dimension=0, tiled=False)
    result = (x1 + mixture.astype(F32)).astype(BF)
    small = jnp.concatenate(
        [
            jnp.zeros((1, WIDTH), F32),
            gain_f_part[None, :],
            router_part,
            jnp.zeros((EXTRA - 2 - E, WIDTH), F32),
        ],
        axis=0,
    )
    stream_grad, own, peer, peer_out, moe_out = finish_layer(
        dq_pair,
        dkv,
        cosine,
        sine,
        h1,
        weights,
        pair,
        small,
        dx1,
        gain_a,
        out_own,
        moe_own,
        depth,
    )
    peer = peer.astype(F32)

    def halves(a, b):
        return jnp.concatenate(pick(head_zero, own[:, a:b], peer[:, a:b]), axis=1)

    both = own[:, QKV:] + peer[:, QKV:]
    moe_out = moe_out.astype(F32)
    return (
        result,
        stream_grad,
        both[:, 0],
        halves(0, QCOLS),
        halves(QCOLS, QCOLS + HEAD),
        halves(QCOLS + HEAD, QKV),
        jnp.concatenate(pick(head_zero, out_own, peer_out.astype(F32)), axis=1),
        both[:, 1],
        both[:, 2 : 2 + E],
        moe_out[:, :rows_in, :FF],
        moe_out[:, :rows_in, FF:],
        moe_out[:, rows_in:, :],
    )


def solution(mesh):
    shards = mesh.shape["shard"]
    depth = shards // INNER
    fine = Mesh(mesh.devices.reshape(depth, INNER, SEQ), AXES)
    shard = ("outer", "inner")
    tokens = P(AXES, None)
    in_specs = (
        tokens,
        P(),
        tokens,
        P(shard),
        P(shard, None),
        P(shard, None),
        P(shard, None),
        P(shard, None),
        P(shard),
        P(shard, None),
        P(None, shard, None),
        P(None, shard, None),
        P(None, shard, None),
        tokens,
    )
    out_specs = (
        tokens,
        tokens,
        P(shard),
        P(shard, None),
        P(shard, None),
        P(shard, None),
        P(shard, None),
        P(shard),
        P(shard, None),
        P(None, shard, None),
        P(None, shard, None),
        P(None, shard, None),
    )

    def run(*args):
        return local(depth, *args)

    return jax.shard_map(run, mesh=fine, in_specs=in_specs, out_specs=out_specs, check_vma=False)
```
